32 devices in a mesh: ctx: 8 (over y, x, core), fsdp: 4 (over z).
Axes of the slice: x: 2, y: 2, z: 4, core: 2. Of those that a mesh axis runs over, the one named last changes fastest.
Arguments:
- tokens: bfloat16 [6144, 1536], P(('ctx', 'fsdp')), may hold values from -6 to 6
- out_grad: bfloat16 [6144, 1536], P(('ctx', 'fsdp')), may hold values from -6 to 6
- pair_table: int32 [4, 8], P('fsdp'), may hold values from 0 to 7, each once within a row
- attn_gain: bfloat16 [1536], P(('ctx', 'fsdp')), may hold values from 0.099609375 to 1.8984375
- w_query: bfloat16 [1536, 1536], P(('ctx', 'fsdp')), may hold values from -0.15625 to 0.15625
- w_key: bfloat16 [1536, 768], P(('ctx', 'fsdp')), may hold values from -0.15625 to 0.15625
- w_value: bfloat16 [1536, 768], P(('ctx', 'fsdp')), may hold values from -0.15625 to 0.15625
- w_out: bfloat16 [1536, 1536], P(('ctx', 'fsdp')), may hold values from -2 to 2
- mlp_gain: bfloat16 [1536], P(('ctx', 'fsdp')), may hold values from 0.099609375 to 1.8984375
- w_gate: bfloat16 [1536, 4096], P(None, ('ctx', 'fsdp')), may hold values from -0.15625 to 0.15625
- w_up: bfloat16 [1536, 4096], P(None, ('ctx', 'fsdp')), may hold values from -0.15625 to 0.15625
- w_down: bfloat16 [4096, 1536], P(('ctx', 'fsdp')), may hold values from -0.09375 to 0.09375
Outputs:
- mixed: bfloat16 [6144, 1536], P(('ctx', 'fsdp'))
- tokens_grad: bfloat16 [6144, 1536], P(('ctx', 'fsdp'))
- attn_gain_grad: float32 [1536], P(('ctx', 'fsdp'))
- w_query_grad: float32 [1536, 1536], P(('ctx', 'fsdp'))
- w_key_grad: float32 [1536, 768], P(('ctx', 'fsdp'))
- w_value_grad: float32 [1536, 768], P(('ctx', 'fsdp'))
- w_out_grad: float32 [1536, 1536], P(('ctx', 'fsdp'))
- mlp_gain_grad: float32 [1536], P(('ctx', 'fsdp'))
- w_gate_grad: float32 [1536, 4096], P(None, ('ctx', 'fsdp'))
- w_up_grad: float32 [1536, 4096], P(None, ('ctx', 'fsdp'))
- w_down_grad: float32 [4096, 1536], P(('ctx', 'fsdp'))
The draws below stay inside these ranges and needn't reach their ends.
Inputs may be any that keep to these rules, and one draw needn't show every extreme that they name: Each row of pair_table lists every block pair 0 to 7 once; pair p stands for the blocks p and 15 - p of 96 tokens of a sequence.
All inputs are finite; a program needn't handle non-finite values.
Results may differ from the reference program's by a relative error of at most 0.017.
Values may be sent and summed in bfloat16 or wider, within the bound.
A program may use at most 320 MiB of HBM per device.

```python
import math
import jax
import jax.numpy as jnp
from jax import lax

D = 1536
HEADS = 16
KV_HEADS = 8
HEAD_DIM = 96
FF = 4096
TOK_DEV = 192
LEN = 1536
TOKENS = 6144
N_CTX = 8
N_FSDP = 4


def raised(array, own_key, source, target, parts, factor):
    def block_of(position):
        return (jnp.arange(array.shape[position]) // (array.shape[position] // parts)).reshape((-1,) + (1,) * (array.ndim - 1 - position))

    first = jax.random.permutation(own_key, parts)[block_of(target)]
    far = (block_of(target) + parts // 2) % parts
    return jnp.where((block_of(source) == first) | (block_of(source) == far), factor * array, array)


def shard_levels(stream_key, shape, cuts, smallest, top_value):
    level, own = 1.0, jax.random.fold_in(stream_key, 6)
    for position, blocks in cuts:
        draws = jnp.exp(jax.random.uniform(jax.random.fold_in(own, position), (blocks,), jnp.float32, smallest / len(cuts), top_value / len(cuts)))
        level = level * jnp.repeat(draws, shape[position] // blocks).reshape([-1 if axis == position else 1 for axis in range(len(shape))])
    return level


def bell_draw(rng, extent, deviation, limit, shards=(), held_as=jnp.bfloat16):
    entries = deviation * jax.random.normal(rng, extent, jnp.float32)
    if shards:
        entries = entries * shard_levels(rng, extent, shards, -0.22, 0.18)
    return jnp.clip(entries, -limit, limit).astype(held_as)


def heavy_noise(key, shape, width, limit, cuts, heavy, held_as=jnp.bfloat16):
    values = width * jax.random.normal(key, shape, jnp.float32)
    if cuts:
        values = values * shard_levels(key, shape, cuts, -0.22, 0.18)
    return jnp.clip(raised(values, jax.random.fold_in(key, 3), *heavy), -limit, limit).astype(held_as)


def setup_inputs(seed: int = 0) -> dict:
    streams_of = jax.random.split(jax.random.key(seed), 13)
    tokens = heavy_noise(streams_of[0], (TOKENS, D), 1.0, 6.0, ((0, 32),), (0, 1, 32, 2.75))
    out_grad = bell_draw(streams_of[1], (TOKENS, D), 1.0, 6.0, ((0, 32),))
    pair_table = jax.vmap(lambda own: jax.random.permutation(own, N_CTX))(jax.random.split(streams_of[2], N_FSDP)).reshape((N_FSDP, N_CTX)).astype(jnp.int32)
    attn_gain = jnp.clip(1.0 + 0.18 * jax.random.normal(streams_of[3], (D,), jnp.float32), 0.099609375, 1.8984375).astype(jnp.bfloat16)
    w_query = bell_draw(streams_of[4], (D, HEADS * HEAD_DIM), D ** -0.5, 0.15625, ((0, 32),))
    w_key = bell_draw(streams_of[5], (D, KV_HEADS * HEAD_DIM), D ** -0.5, 0.15625, ((0, 32),))
    w_value = bell_draw(streams_of[6], (D, KV_HEADS * HEAD_DIM), D ** -0.5, 0.15625, ((0, 32),))
    w_out = bell_draw(streams_of[7], (HEADS * HEAD_DIM, D), (max(1, 8 * HEADS * HEAD_DIM // LEN)) ** -0.5, 2.0, ((0, 32),))
    mlp_gain = jnp.clip(1.0 + 0.18 * jax.random.normal(streams_of[8], (D,), jnp.float32), 0.099609375, 1.8984375).astype(jnp.bfloat16)
    w_gate = bell_draw(streams_of[9], (D, FF), D ** -0.5, 0.15625, ((1, 32),))
    w_up = bell_draw(streams_of[10], (D, FF), D ** -0.5, 0.15625, ((1, 32),))
    w_down = bell_draw(streams_of[11], (FF, D), FF ** -0.5, 0.09375, ((0, 32),))
    return {"tokens": tokens, "out_grad": out_grad, "pair_table": pair_table, "attn_gain": attn_gain, "w_query": w_query, "w_key": w_key, "w_value": w_value, "w_out": w_out, "mlp_gain": mlp_gain, "w_gate": w_gate, "w_up": w_up, "w_down": w_down}


EPS = 1e-05
THETA = 100000.0
HIGH = lax.Precision.HIGHEST

@jax.custom_vjp
def low(v):
    return lax.optimization_barrier(v.astype(jnp.bfloat16)).astype(jnp.float32)

@jax.custom_vjp
def low_back(v):
    return v

def low_keep(v):
    return (low(v), None)

def low_pass(kept, grad):
    return (grad,)

def back_keep(v):
    return (v, None)

def back_low(kept, grad):
    return (low(grad),)
low.defvjp(low_keep, low_pass)
low_back.defvjp(back_keep, back_low)

def rotate(values_in, positions, direction):
    half_dim = values_in.shape[-1] // 2
    freqs = THETA ** (-(jnp.arange(half_dim, dtype=jnp.float32) * 2.0 / values_in.shape[-1]))
    angle = positions.astype(jnp.float32)[:, None] * freqs[None, :]
    cosine = jnp.cos(angle)[:, None, :]
    sine = direction * jnp.sin(angle)[:, None, :]
    first_half = values_in[..., :half_dim]
    second_half = values_in[..., half_dim:]
    return jnp.concatenate([first_half * cosine - second_half * sine, second_half * cosine + first_half * sine], axis=-1)

def attend(queries, keys, values, positions):
    seq_len = queries.shape[0]
    query_block = math.gcd(seq_len, 256)
    group_size = HEADS // KV_HEADS
    score_scale = HEAD_DIM ** (-0.5)

    def one_block(inputs):
        query_tile, query_pos = inputs
        grouped = query_tile.reshape(query_block, KV_HEADS, group_size, HEAD_DIM)
        scores = jnp.einsum('tkgd,skd->kgts', grouped, keys, precision=HIGH) * score_scale
        scores = low_back(scores)
        visible = positions[None, :] <= query_pos[:, None]
        scores = jnp.where(visible[None, None], scores, -jnp.inf)
        weights = low(jax.nn.softmax(scores, axis=-1))
        result = jnp.einsum('kgts,skd->tkgd', weights, values, precision=HIGH)
        return result.reshape(query_block, HEADS * HEAD_DIM)
    tiles = queries.reshape(seq_len // query_block, query_block, HEADS, HEAD_DIM)
    pos_tiles = positions.reshape(seq_len // query_block, query_block)
    result = lax.map(jax.checkpoint(one_block), (tiles, pos_tiles))
    return result.reshape(seq_len, HEADS * HEAD_DIM)

def layer(params, resid_in, positions):
    attn_gain, w_query, w_key, w_value, w_out, mlp_gain, w_gate, w_up, w_down = params
    seq_len = resid_in.shape[0]
    inv_one = lax.rsqrt(lax.optimization_barrier(jnp.mean(resid_in * resid_in, axis=-1, keepdims=True)) + EPS)
    normed_in = low(resid_in * inv_one * attn_gain)
    query_lin = low_back(jnp.dot(normed_in, w_query, precision=HIGH))
    key_lin = low_back(jnp.dot(normed_in, w_key, precision=HIGH))
    value_lin = low_back(jnp.dot(normed_in, w_value, precision=HIGH))
    queries = low(rotate(query_lin.reshape(seq_len, HEADS, HEAD_DIM), positions, 1.0))
    keys = low(rotate(key_lin.reshape(seq_len, KV_HEADS, HEAD_DIM), positions, 1.0))
    values = low(value_lin.reshape(seq_len, KV_HEADS, HEAD_DIM))
    attn_out = low(low_back(attend(queries, keys, values, positions)))
    resid_mid = resid_in + low_back(jnp.dot(attn_out, w_out, precision=HIGH))
    inv_two = lax.rsqrt(lax.optimization_barrier(jnp.mean(resid_mid * resid_mid, axis=-1, keepdims=True)) + EPS)
    normed_mid = low(resid_mid * inv_two * mlp_gain)
    gate = low_back(jnp.dot(normed_mid, w_gate, precision=HIGH))
    up_proj = low_back(jnp.dot(normed_mid, w_up, precision=HIGH))
    hidden = low(jax.nn.silu(gate) * up_proj)
    return resid_mid + low_back(jnp.dot(hidden, w_down, precision=HIGH))

def reference(tokens, out_grad, pair_table, attn_gain, w_query, w_key, w_value, w_out, mlp_gain, w_gate, w_up, w_down):
    half_rows = TOK_DEV // 2
    offsets = jnp.arange(TOK_DEV, dtype=jnp.int32)[None, None, :]
    pair_index = pair_table.astype(jnp.int32)[:, :, None]
    early = pair_index * half_rows + offsets
    late = (2 * N_CTX - 1 - pair_index) * half_rows + offsets - half_rows
    positions = jnp.where(offsets < half_rows, early, late).reshape(N_FSDP, LEN).astype(jnp.int32)

    def arrange(array_in):
        return array_in.astype(jnp.float32).reshape(N_CTX, N_FSDP, TOK_DEV, D).transpose(1, 0, 2, 3).reshape(N_FSDP, LEN, D)

    def restore(array_in):
        return array_in.reshape(N_FSDP, N_CTX, TOK_DEV, D).transpose(1, 0, 2, 3).reshape(TOKENS, D).astype(jnp.bfloat16)
    params = tuple((weight.astype(jnp.float32) for weight in (attn_gain, w_query, w_key, w_value, w_out, mlp_gain, w_gate, w_up, w_down)))
    sequences = arrange(tokens)
    cotangent = arrange(out_grad)

    def forward(params, sequences):

        def one_sequence(carry, inputs):
            return (carry, jax.checkpoint(layer)(params, inputs[0], inputs[1]))
        return lax.scan(one_sequence, jnp.zeros((), jnp.float32), (sequences, positions))[1]
    outputs, pullback = jax.vjp(forward, params, sequences)
    param_grads, input_grads = pullback(cotangent)
    return (restore(outputs), restore(input_grads), param_grads[0], param_grads[1], param_grads[2], param_grads[3], param_grads[4], param_grads[5], param_grads[6], param_grads[7], param_grads[8])
```

```python
import functools
import math

import jax
import jax.numpy as jnp
import numpy as np
from jax import lax
from jax.experimental import pallas as pl
from jax.experimental.pallas import tpu as pltpu
from jax.sharding import PartitionSpec as P

HEADS = 16
KV_HEADS = 8
HEAD_DIM = 96
FEED_WIDTH = 4096


EPS = 1e-05
THETA = 100000.0
NEG_FILL = -1e30


def rotate(values_in, positions, direction):
    half_dim = values_in.shape[-1] // 2
    freqs = THETA ** (-(jnp.arange(half_dim, dtype=jnp.float32) * 2.0 / values_in.shape[-1]))
    angle = positions.astype(jnp.float32)[:, None] * freqs[None, :]
    cosine = jnp.cos(angle)[:, None, :]
    sine = direction * jnp.sin(angle)[:, None, :]
    first_half = values_in[..., :half_dim]
    second_half = values_in[..., half_dim:]
    return jnp.concatenate(
        [first_half * cosine - second_half * sine, second_half * cosine + first_half * sine],
        axis=-1,
    )


def place_rows(pair_index, tok_rows, block_count):
    half_rows = tok_rows // 2
    offsets = jnp.arange(tok_rows, dtype=jnp.int32)
    early = pair_index * half_rows + offsets
    late = (block_count - 1 - pair_index) * half_rows + offsets - half_rows
    return jnp.where(offsets < half_rows, early, late)


def rms_scale(values_in):
    return lax.rsqrt(jnp.mean(values_in * values_in, axis=-1, keepdims=True) + EPS)


def norm_back(grad_normed, normed, inv_rms, gain):
    scaled = grad_normed * gain
    return inv_rms * (scaled - normed * jnp.mean(scaled * normed, axis=-1, keepdims=True))


def local(
    tokens,
    out_grad,
    pair_table,
    attn_gain,
    w_query,
    w_key,
    w_value,
    w_out,
    mlp_gain,
    w_gate,
    w_up,
    w_down,
):
    tok_rows = tokens.shape[0]
    half_rows = tok_rows // 2
    ctx_count = lax.axis_size("ctx")
    half_count = 2 * ctx_count
    pair_row = pair_table[0]
    my_pos = place_rows(pair_row[lax.axis_index("ctx")], tok_rows, half_count)
    half_blocks = jnp.stack([pair_row, half_count - 1 - pair_row], axis=1).reshape(-1)
    block_ids = jnp.arange(half_count, dtype=jnp.int32)
    inverse = jnp.sum(
        jnp.where(half_blocks[None, :] == block_ids[:, None], block_ids[None, :], 0), axis=1
    )
    group_size = HEADS // KV_HEADS
    score_scale = HEAD_DIM ** (-0.5)
    query_width = HEADS * HEAD_DIM
    kv_width = KV_HEADS * HEAD_DIM
    w_query_all, w_key_all, w_value_all, w_out_all, gain_first, gain_second = (
        lax.all_gather(w_query, ("ctx", "fsdp"), axis=0, tiled=True),
        lax.all_gather(w_key, ("ctx", "fsdp"), axis=0, tiled=True),
        lax.all_gather(w_value, ("ctx", "fsdp"), axis=0, tiled=True),
        lax.all_gather(w_out, ("ctx", "fsdp"), axis=0, tiled=True),
        lax.all_gather(attn_gain, ("ctx", "fsdp"), axis=0, tiled=True),
        lax.all_gather(mlp_gain, ("ctx", "fsdp"), axis=0, tiled=True),
    )
    gain_one = gain_first.astype(jnp.float32)
    gain_two = gain_second.astype(jnp.float32)
    resid_in = tokens.astype(jnp.float32)
    inv_one = rms_scale(resid_in)
    normed_one = resid_in * inv_one
    normed_in = (normed_one * gain_one).astype(jnp.bfloat16)
    query_lin = jnp.dot(normed_in, w_query_all, preferred_element_type=jnp.float32)
    key_lin = jnp.dot(normed_in, w_key_all, preferred_element_type=jnp.float32)
    value_lin = jnp.dot(normed_in, w_value_all, preferred_element_type=jnp.float32)
    query_rot = rotate(query_lin.reshape(tok_rows, HEADS, HEAD_DIM), my_pos, 1.0).astype(
        jnp.bfloat16
    )
    key_rot = (
        rotate(key_lin.reshape(tok_rows, KV_HEADS, HEAD_DIM), my_pos, 1.0)
        .astype(jnp.bfloat16)
        .reshape(tok_rows, kv_width)
    )
    value_low = value_lin.astype(jnp.bfloat16)
    keys_got, values_got = (
        lax.all_gather(key_rot, "ctx", axis=0, tiled=True),
        lax.all_gather(value_low, "ctx", axis=0, tiled=True),
    )
    seq_len = keys_got.shape[0]
    keys_all = jnp.take(keys_got.reshape(half_count, half_rows, kv_width), inverse, axis=0).reshape(
        seq_len, kv_width
    )
    values_all = jnp.take(
        values_got.reshape(half_count, half_rows, kv_width), inverse, axis=0
    ).reshape(seq_len, kv_width)
    key_pos = jnp.arange(seq_len, dtype=jnp.int32)
    key_block = math.gcd(seq_len, 512)
    live_blocks = jnp.max(my_pos) // key_block + 1
    query_grp = query_rot.reshape(tok_rows, KV_HEADS, group_size, HEAD_DIM)

    def block_scores(block_index):
        first_row = block_index * key_block
        key_tile = lax.dynamic_slice_in_dim(keys_all, first_row, key_block, 0).reshape(
            key_block, KV_HEADS, HEAD_DIM
        )
        value_tile = lax.dynamic_slice_in_dim(values_all, first_row, key_block, 0).reshape(
            key_block, KV_HEADS, HEAD_DIM
        )
        scores = (
            jnp.einsum("tkgd,skd->kgts", query_grp, key_tile, preferred_element_type=jnp.float32)
            * score_scale
        )
        visible = (
            lax.dynamic_slice_in_dim(key_pos, first_row, key_block, 0)[None, :] <= my_pos[:, None]
        )
        return (scores, visible, key_tile, value_tile)

    def stats_step(block_index, carry):
        run_max, run_sum = carry
        scores, visible, key_tile, value_tile = block_scores(block_index)
        masked = jnp.where(visible, scores, NEG_FILL)
        new_max = jnp.maximum(run_max, jnp.max(masked, axis=-1))
        weights = jnp.where(visible, jnp.exp(masked - new_max[..., None]), 0.0)
        return (new_max, run_sum * jnp.exp(run_max - new_max) + jnp.sum(weights, axis=-1))

    start_max = jnp.full((KV_HEADS, group_size, tok_rows), NEG_FILL, jnp.float32)
    run_max, run_sum = lax.fori_loop(
        0, live_blocks, stats_step, (start_max, jnp.zeros_like(start_max))
    )
    log_total = run_max + jnp.log(run_sum)

    def probs(scores, visible):
        return jnp.where(visible, jnp.exp(scores - log_total[..., None]), 0.0)

    def output_step(block_index, accum):
        scores, visible, key_tile, value_tile = block_scores(block_index)
        prob_low = probs(scores, visible).astype(jnp.bfloat16)
        return accum + jnp.einsum(
            "kgts,skd->kgtd", prob_low, value_tile, preferred_element_type=jnp.float32
        )

    attn_acc = lax.fori_loop(
        0,
        live_blocks,
        output_step,
        jnp.zeros((KV_HEADS, group_size, tok_rows, HEAD_DIM), jnp.float32),
    )
    attn_low = attn_acc.transpose(2, 0, 1, 3).reshape(tok_rows, query_width).astype(jnp.bfloat16)
    resid_mid = resid_in + jnp.dot(attn_low, w_out_all, preferred_element_type=jnp.float32)
    inv_two = rms_scale(resid_mid)
    normed_two = resid_mid * inv_two
    normed_mid = (normed_two * gain_two).astype(jnp.bfloat16)
    w_gate_part, w_up_part, w_down_part = (
        lax.all_gather(w_gate, ("ctx", "fsdp"), axis=1, tiled=True),
        lax.all_gather(w_up, ("ctx", "fsdp"), axis=1, tiled=True),
        lax.all_gather(w_down, ("ctx", "fsdp"), axis=0, tiled=True),
    )
    gate_lin = jnp.dot(normed_mid, w_gate_part, preferred_element_type=jnp.float32)
    up_lin = jnp.dot(normed_mid, w_up_part, preferred_element_type=jnp.float32)
    sigma = jax.nn.sigmoid(gate_lin)
    activated = gate_lin * sigma
    hidden_low = (activated * up_lin).astype(jnp.bfloat16)
    mlp_branch = jnp.dot(hidden_low, w_down_part, preferred_element_type=jnp.float32)
    mixed = (resid_mid + mlp_branch).astype(jnp.bfloat16)
    grad_top = out_grad.astype(jnp.float32)
    d_down = jnp.einsum("tf,td->fd", hidden_low, out_grad, preferred_element_type=jnp.float32)
    grad_hidden = jnp.einsum("td,fd->tf", out_grad, w_down_part, preferred_element_type=jnp.float32)
    grad_gate = (grad_hidden * up_lin * sigma * (1.0 + gate_lin * (1.0 - sigma))).astype(
        jnp.bfloat16
    )
    grad_up = (grad_hidden * activated).astype(jnp.bfloat16)
    d_gate = jnp.einsum("td,tf->df", normed_mid, grad_gate, preferred_element_type=jnp.float32)
    d_up = jnp.einsum("td,tf->df", normed_mid, grad_up, preferred_element_type=jnp.float32)
    grad_normed_mid = jnp.einsum(
        "tf,df->td", grad_gate, w_gate_part, preferred_element_type=jnp.float32
    ) + jnp.einsum("tf,df->td", grad_up, w_up_part, preferred_element_type=jnp.float32)
    gate_grad_out, up_grad_out, down_grad_out = (
        lax.psum_scatter(d_gate, ("ctx", "fsdp"), scatter_dimension=1, tiled=True),
        lax.psum_scatter(d_up, ("ctx", "fsdp"), scatter_dimension=1, tiled=True),
        lax.psum_scatter(d_down, ("ctx", "fsdp"), scatter_dimension=0, tiled=True),
    )
    d_gain_two = jnp.sum(grad_normed_mid * normed_two, axis=0)
    grad_mid = grad_top + norm_back(grad_normed_mid, normed_two, inv_two, gain_two)
    grad_mid_low = grad_mid.astype(jnp.bfloat16)
    d_out = jnp.einsum("tq,td->qd", attn_low, grad_mid_low, preferred_element_type=jnp.float32)
    grad_attn_low = jnp.einsum(
        "td,qd->tq", grad_mid_low, w_out_all, preferred_element_type=jnp.float32
    ).astype(jnp.bfloat16)
    grad_heads = grad_attn_low.reshape(tok_rows, KV_HEADS, group_size, HEAD_DIM).transpose(
        1, 2, 0, 3
    )
    row_delta = jnp.sum(grad_heads.astype(jnp.float32) * attn_acc, axis=-1)

    def back_step(block_index, carry):
        grad_query, grad_keys, grad_values = carry
        scores, visible, key_tile, value_tile = block_scores(block_index)
        prob_full = probs(scores, visible)
        prob_low = prob_full.astype(jnp.bfloat16)
        grad_prob = jnp.einsum(
            "kgtd,skd->kgts", grad_heads, value_tile, preferred_element_type=jnp.float32
        )
        grad_score = (prob_full * (grad_prob - row_delta[..., None])).astype(jnp.bfloat16)
        grad_query = grad_query + score_scale * jnp.einsum(
            "kgts,skd->kgtd", grad_score, key_tile, preferred_element_type=jnp.float32
        )
        key_part = score_scale * jnp.einsum(
            "kgts,tkgd->skd", grad_score, query_grp, preferred_element_type=jnp.float32
        )
        value_part = jnp.einsum(
            "kgts,kgtd->skd", prob_low, grad_heads, preferred_element_type=jnp.float32
        )
        first_row = block_index * key_block
        grad_keys = lax.dynamic_update_slice_in_dim(
            grad_keys, key_part.reshape(key_block, kv_width), first_row, 0
        )
        grad_values = lax.dynamic_update_slice_in_dim(
            grad_values, value_part.reshape(key_block, kv_width), first_row, 0
        )
        return (grad_query, grad_keys, grad_values)

    empty_keys = jnp.zeros((seq_len, kv_width), jnp.float32)
    grad_query, grad_keys, grad_values = lax.fori_loop(
        0,
        live_blocks,
        back_step,
        (
            jnp.zeros((KV_HEADS, group_size, tok_rows, HEAD_DIM), jnp.float32),
            empty_keys,
            empty_keys,
        ),
    )
    keys_back = jnp.take(
        grad_keys.reshape(half_count, half_rows, kv_width), half_blocks, axis=0
    ).reshape(seq_len, kv_width)
    values_back = jnp.take(
        grad_values.reshape(half_count, half_rows, kv_width), half_blocks, axis=0
    ).reshape(seq_len, kv_width)
    own_keys, own_values = (
        lax.psum_scatter(
            keys_back.astype(jnp.bfloat16), "ctx", scatter_dimension=0, tiled=True
        ).astype(jnp.float32),
        lax.psum_scatter(
            values_back.astype(jnp.bfloat16), "ctx", scatter_dimension=0, tiled=True
        ).astype(jnp.float32),
    )
    grad_query_lin = rotate(
        grad_query.transpose(2, 0, 1, 3).reshape(tok_rows, HEADS, HEAD_DIM), my_pos, -1.0
    )
    grad_query_low = grad_query_lin.reshape(tok_rows, query_width).astype(jnp.bfloat16)
    grad_key_lin = rotate(own_keys.reshape(tok_rows, KV_HEADS, HEAD_DIM), my_pos, -1.0)
    grad_key_low = grad_key_lin.reshape(tok_rows, kv_width).astype(jnp.bfloat16)
    grad_value_low = own_values.astype(jnp.bfloat16)
    d_query = jnp.einsum("td,tq->dq", normed_in, grad_query_low, preferred_element_type=jnp.float32)
    d_key = jnp.einsum("td,tq->dq", normed_in, grad_key_low, preferred_element_type=jnp.float32)
    d_value = jnp.einsum("td,tq->dq", normed_in, grad_value_low, preferred_element_type=jnp.float32)
    grad_normed_in = (
        jnp.einsum("tq,dq->td", grad_query_low, w_query_all, preferred_element_type=jnp.float32)
        + jnp.einsum("tq,dq->td", grad_key_low, w_key_all, preferred_element_type=jnp.float32)
        + jnp.einsum("tq,dq->td", grad_value_low, w_value_all, preferred_element_type=jnp.float32)
    )
    d_gain_one = jnp.sum(grad_normed_in * normed_one, axis=0)
    grad_input = grad_mid + norm_back(grad_normed_in, normed_one, inv_one, gain_one)
    query_grad_out, key_grad_out, value_grad_out, out_grad_out, gain_one_out, gain_two_out = (
        lax.psum_scatter(d_query, ("ctx", "fsdp"), scatter_dimension=0, tiled=True),
        lax.psum_scatter(d_key, ("ctx", "fsdp"), scatter_dimension=0, tiled=True),
        lax.psum_scatter(d_value, ("ctx", "fsdp"), scatter_dimension=0, tiled=True),
        lax.psum_scatter(d_out, ("ctx", "fsdp"), scatter_dimension=0, tiled=True),
        lax.psum_scatter(d_gain_one, ("ctx", "fsdp"), scatter_dimension=0, tiled=True),
        lax.psum_scatter(d_gain_two, ("ctx", "fsdp"), scatter_dimension=0, tiled=True),
    )
    return (
        mixed,
        grad_input.astype(jnp.bfloat16),
        gain_one_out,
        query_grad_out,
        key_grad_out,
        value_grad_out,
        out_grad_out,
        gain_two_out,
        gate_grad_out,
        up_grad_out,
        down_grad_out,
    )


BF = jnp.bfloat16
F32 = jnp.float32
MESH = pl.DeviceIdType.MESH
HEAD_PAD = 128
LOG2E = 1.4426950408889634
VMEM_LIMIT = 58 * 2**20
NT = (((1,), (1,)), ((), ()))
TN = (((0,), (0,)), ((), ()))


def dot(a, b, dims=(((1,), (0,)), ((), ()))):
    return lax.dot_general(a, b, dims, preferred_element_type=F32)


class Place:
    def __init__(self, n_ctx, n_fsdp):
        self.n_ctx, self.n_fsdp = n_ctx, n_fsdp
        self.c, self.f = lax.axis_index("ctx"), lax.axis_index("fsdp")
        core = lax.rem(self.c, 2)
        step_x = 2 - 4 * lax.rem(lax.div(self.c, 2), 2)
        step_y = 4 - 8 * lax.div(self.c, 4)
        self.other = 1 - 2 * core
        self.s = self.c + self.other
        self.a = self.c + step_x * (1 - core) + step_y * core
        self.b = self.c + step_x * core + step_y * (1 - core)
        self.d = self.c + step_x + step_y

    def ctx_peer(self, j):
        return lax.rem(self.c + j, self.n_ctx)

    def ctx_source(self, j):
        return lax.rem(self.c + self.n_ctx - j, self.n_ctx)

    def fsdp_peer(self, j):
        return lax.rem(self.f + j, self.n_fsdp)

    def fsdp_source(self, j):
        return lax.rem(self.f + self.n_fsdp - j, self.n_fsdp)

    def greet(self, everyone):
        barrier = pltpu.get_barrier_semaphore()
        if everyone:
            mates = [(self.ctx_peer(j), self.f) for j in range(1, self.n_ctx)]
            mates += [(self.c, self.fsdp_peer(j)) for j in range(1, self.n_fsdp)]
        else:
            mates = [(self.s, self.f), (self.a, self.f), (self.b, self.f)]
        for mate in mates:
            pl.semaphore_signal(barrier, inc=1, device_id=mate, device_id_type=MESH)
        pl.semaphore_wait(barrier, len(mates))


def remote(src, dst, send, recv, device):
    return pltpu.make_async_remote_copy(
        src_ref=src, dst_ref=dst, send_sem=send, recv_sem=recv, device_id=device, device_id_type=MESH
    )


class PlaneGather:
    COUNT = 7

    def __init__(self, at, own, blocks, sems):
        self.at, self.own, self.blocks = at, own, blocks
        self.send, self.recv = sems
        self.started = []

    def copy(self, i, src, slot, mate):
        cp = remote(src, self.blocks.at[slot], self.send.at[i], self.recv.at[i], (mate, self.at.f))
        cp.start()
        self.started.append(cp)

    def wait(self, i, slot):
        block = self.blocks.at[slot]
        remote(block, block, self.send.at[i], self.recv.at[i], (self.at.s, self.at.f)).wait_recv()

    def start(self):
        at = self.at
        self.copy(1, self.own, at.c, at.a)
        self.copy(2, self.own, at.c, at.b)
        self.copy(0, self.own, at.c, at.s)

    def pass_a(self):
        at = self.at
        self.wait(1, at.a)
        self.copy(4, self.blocks.at[at.a], at.a, at.b)
        self.copy(3, self.blocks.at[at.a], at.a, at.s)

    def pass_b(self):
        at = self.at
        self.wait(2, at.b)
        self.copy(5, self.blocks.at[at.b], at.b, at.s)

    def pass_d(self):
        at = self.at
        self.wait(4, at.d)
        self.copy(6, self.blocks.at[at.d], at.d, at.s)

    def wait_other(self, which):
        at = self.at
        i, slot = {
            "own": (0, at.s),
            "a": (3, at.b + at.other),
            "b": (5, at.a + at.other),
            "d": (6, at.d + at.other),
        }[which]
        self.wait(i, slot)

    def finish_sends(self):
        for cp in self.started:
            cp.wait_send()


class PlaneScatter:
    COUNT = 7

    def __init__(self, at, emit, bufs, sems):
        self.at, self.emit = at, emit
        self.out, self.landed = bufs
        self.send, self.recv = sems
        self.started = []

    def copy(self, i, src, mate):
        cp = remote(src, self.landed.at[i], self.send.at[i], self.recv.at[i], (mate, self.at.f))
        cp.start()
        self.started.append(cp)

    def wait(self, i):
        block = self.landed.at[i]
        remote(block, block, self.send.at[i], self.recv.at[i], (self.at.s, self.at.f)).wait_recv()

    def others(self):
        at = self.at
        return (at.d + at.other, at.b + at.other, at.s, at.a + at.other)

    def to_other(self):
        for i, index in enumerate(self.others()):
            self.emit(index, self.out.at[i], [])
            self.copy(i, self.out.at[i], self.at.s)

    def first(self, total):
        at = self.at
        self.wait(0)
        self.emit(at.d, self.out.at[4], [self.landed.at[0]])
        self.copy(4, self.out.at[4], at.a)
        self.wait(1)
        self.emit(at.a, self.out.at[5], [self.landed.at[1]])
        self.copy(5, self.out.at[5], at.a)
        self.wait(2)
        self.emit(at.c, total, [self.landed.at[2]])

    def second(self):
        at = self.at
        self.wait(3)
        self.wait(4)
        self.emit(at.b, self.out.at[6], [self.landed.at[3], self.landed.at[4]])
        self.copy(6, self.out.at[6], at.b)

    def last(self):
        self.wait(5)
        self.wait(6)
        return self.landed.at[5], self.landed.at[6]

    def finish_sends(self):
        for cp in self.started:
            cp.wait_send()


def exchange(at, axis, src_of, dst, slot_of, sems):
    send, recv = sems
    n = at.n_ctx if axis == "ctx" else at.n_fsdp
    started, waits = [], []
    for j in range(1, n):
        if axis == "ctx":
            peer, source, mine = at.ctx_peer(j), at.ctx_source(j), at.c
            device = (peer, at.f)
        else:
            peer, source, mine = at.fsdp_peer(j), at.fsdp_source(j), at.f
            device = (at.c, peer)
        cp = remote(src_of(peer), slot_of(dst, mine), send.at[j], recv.at[j], device)
        cp.start()
        started.append(cp)
        block = slot_of(dst, source)
        waits.append(remote(block, block, send.at[j], recv.at[j], device))
    return started, waits


def turn(values_in, cosine, sine):
    return values_in * cosine + pltpu.roll(values_in, HEAD_PAD // 2, 1) * sine


def store_rows(ref, first, lanes, value):
    block_rows, done = ref.shape[1], 0
    while done < value.shape[0]:
        block, start = divmod(first + done, block_rows)
        count = min(block_rows - start, value.shape[0] - done)
        ref[block, start : start + count, lanes] = value[done : done + count]
        done += count


def tile_emit(lhs_of, rhs_of, width, tile):
    def emit(index, dst, extras):
        lhs = lhs_of(index)

        def column_tile(t, carry):
            columns = pl.ds(pl.multiple_of(t * tile, tile), tile)
            value = rhs_of(lhs, t, columns)
            for extra in extras:
                value = value + extra[:, columns].astype(F32)
            dst[:, columns] = value.astype(dst.dtype)
            return carry

        lax.fori_loop(0, width // tile, column_tile, 0)

    return emit


def forward_kernel(
    n_ctx, n_fsdp,
    x, og, wblk, wout, gt, inv, pairs, expand, cosine, sine,
    ni, nm_all, og_all, q, k, kt, v, ot, ao, lse, wqkv, wo, gains, rm,
    x_all, w_raw, wo_raw, gz, gz_sum, gc, vt, nm_own, total, rs_out, rs_in,
    x_send, x_recv, og_send, og_recv, nm_send, nm_recv, rs_send, rs_recv,
    wc_send, wc_recv, wz_send, wz_recv, oz_send, oz_recv, gz_send, gz_recv, gc_send, gc_recv, local_sem,
):
    at = Place(n_ctx, n_fsdp)
    rows, width = x.shape
    half = rows // 2
    seq_len = rows * n_ctx
    own_rows = w_raw.shape[2]
    at.greet(True)

    gx = PlaneGather(at, x, x_all, (x_send, x_recv))
    gx.start()
    wc_copies, wc_waits = exchange(
        at, "ctx", lambda p: wblk.at[p], w_raw, lambda r, i: r.at[i, at.f], (wc_send, wc_recv)
    )
    gz_copies, gz_waits = exchange(at, "fsdp", lambda p: gt, gz, lambda r, i: r.at[i], (gz_send, gz_recv))
    og_local = pltpu.make_async_copy(og, og_all.at[at.c], local_sem.at[0])
    og_local.start()
    w_raw[at.c, at.f] = wblk[at.c]
    wo_raw[at.f] = wout[...]
    gz[at.f] = gt[...]
    x_all[at.c] = x[...]
    for w in gz_waits:
        w.wait_recv()
    gz_sum[...] = sum(gz[i].astype(F32) for i in range(n_fsdp)).astype(BF)
    gc_copies, gc_waits = exchange(at, "ctx", lambda p: gz_sum, gc, lambda r, i: r.at[i], (gc_send, gc_recv))
    gc[at.c] = gz_sum[...]
    for w in wc_waits:
        w.wait_recv()
    wz_copies, wz_waits = exchange(
        at, "fsdp", lambda p: w_raw.at[:, at.f], w_raw, lambda r, i: r.at[:, i], (wz_send, wz_recv)
    )
    oz_copies, oz_waits = exchange(at, "fsdp", lambda p: wout, wo_raw, lambda r, i: r.at[i], (oz_send, oz_recv))
    for w in gc_waits:
        w.wait_recv()
    gains[...] = sum(gc[i].astype(F32) for i in range(n_ctx))
    gain_one = gains[0:1, :]

    def norm_in(slot):
        def part(r, carry):
            start = pl.multiple_of(r * 48, 16)
            part_rows = x_all[slot, pl.ds(start, 48), :].astype(F32)
            scale = lax.rsqrt(jnp.mean(part_rows * part_rows, axis=-1, keepdims=True) + EPS)
            inside = pl.multiple_of(lax.rem(r, 2) * 48, 16)
            ni[2 * slot + lax.div(r, 2), pl.ds(inside, 48), :] = (part_rows * scale * gain_one).astype(BF)
            return carry

        lax.fori_loop(0, rows // 48, part, 0)

    norm_in(at.c)
    gx.wait_other("own")
    norm_in(at.s)
    gx.pass_a()
    gx.pass_b()
    go = PlaneGather(at, og, og_all, (og_send, og_recv))
    go.start()
    norm_in(at.a)
    norm_in(at.b)
    gx.wait_other("a")
    norm_in(at.b + at.other)
    gx.wait_other("b")
    norm_in(at.a + at.other)
    gx.pass_d()
    norm_in(at.d)
    gx.wait_other("d")
    norm_in(at.d + at.other)

    for w in wz_waits:
        w.wait_recv()

    def widen(i, carry):
        part = w_raw[pl.ds(2 * i, 2)].reshape(2 * n_fsdp * own_rows, w_raw.shape[3])
        start = pl.multiple_of(i * 2 * n_fsdp * own_rows, 128)
        wqkv[pl.ds(start, 2 * n_fsdp * own_rows), :] = dot(part, expand[...]).astype(BF)
        return carry

    lax.fori_loop(0, n_ctx // 2, widen, 0)

    def project(g, carry):
        lhs = jnp.concatenate([ni[inv[4 * g + i]] for i in range(4)], axis=0)
        lin = dot(lhs, wqkv[...])
        span = pl.ds(pl.multiple_of(g * 4 * half, 128), 4 * half)
        cos_part, sin_part = cosine[span, :], sine[span, :]
        q[0, span, :] = turn(lin[:, 0:128], cos_part, sin_part).astype(BF)
        q[1, span, :] = turn(lin[:, 128:256], cos_part, sin_part).astype(BF)
        k_part = turn(lin[:, 256:384], cos_part, sin_part).astype(BF)
        v_part = lin[:, 384:512].astype(BF)
        k[span, :] = k_part
        v[span, :] = v_part
        kt[:, span] = jnp.transpose(k_part.astype(F32)).astype(BF)
        vt[:, span] = jnp.transpose(v_part.astype(F32)).astype(BF)
        return carry

    lax.fori_loop(0, seq_len // (4 * half), project, 0)
    go.pass_a()
    go.pass_b()

    block = 256
    score_scale = HEAD_DIM ** (-0.5) * LOG2E
    for i in range(seq_len // block):
        first = i * block

        def head_step(h, carry, first=first):
            span = slice(first, first + block)
            q_part = q[h, span, :]
            diag = dot(k[span, :], q_part, NT) * score_scale
            key_id = lax.broadcasted_iota(jnp.int32, (block, block), 0)
            query_id = lax.broadcasted_iota(jnp.int32, (block, block), 1)
            diag = jnp.where(key_id <= query_id, diag, NEG_FILL)
            top = jnp.max(diag, axis=0, keepdims=True)
            if first:
                past = dot(k[0:first, :], q_part, NT) * score_scale
                top = jnp.maximum(top, jnp.max(past, axis=0, keepdims=True))
            diag_p = jnp.exp2(diag - top)
            norm = jnp.sum(diag_p, axis=0, keepdims=True)
            acc = dot(vt[:, span], diag_p.astype(BF))
            if first:
                past_p = jnp.exp2(past - top)
                norm = norm + jnp.sum(past_p, axis=0, keepdims=True)
                acc = acc + dot(vt[:, 0:first], past_p.astype(BF))
            acc = acc / norm
            ot[h, :, span] = acc
            lse[h, :, span] = jnp.broadcast_to(top + jnp.log2(norm), (8, block))
            lanes = pl.ds(pl.multiple_of(h * HEAD_PAD, HEAD_PAD), HEAD_PAD)
            store_rows(ao, first, lanes, jnp.transpose(acc).astype(BF))
            return carry

        lax.fori_loop(0, 2, head_step, 0)
        if i == 3:
            go.pass_d()

    for w in oz_waits:
        w.wait_recv()
    raw = wo_raw[...].reshape(2 * HEAD_DIM, width)
    pad_rows = jnp.zeros((HEAD_PAD - HEAD_DIM, width), BF)
    wo[0:96, :] = raw[0:96]
    wo[96:128, :] = pad_rows
    wo[128:224, :] = raw[96:192]
    wo[224:256, :] = pad_rows

    def attn_rows(index):
        pair = pairs[index]
        return jnp.concatenate([ao[pair], ao[2 * n_ctx - 1 - pair]], axis=0)

    emit = tile_emit(attn_rows, lambda lhs, t, cols: dot(lhs, wo[:, cols]), width, 512)
    sc = PlaneScatter(at, emit, (rs_out, rs_in), (rs_send, rs_recv))
    sc.to_other()
    sc.first(total)
    sc.second()
    go.wait_other("own")
    go.wait_other("a")
    go.wait_other("b")
    go.wait_other("d")
    more, most = sc.last()
    gain_two = gains[1:2, :]

    def finish_rows(r, carry):
        span = pl.ds(pl.multiple_of(r * 48, 16), 48)
        mid = x[span, :].astype(F32) + total[span, :] + more[span, :].astype(F32) + most[span, :].astype(F32)
        scale = lax.rsqrt(jnp.mean(mid * mid, axis=-1, keepdims=True) + EPS)
        rm[span, :] = mid
        nm_own[span, :] = (mid * scale * gain_two).astype(BF)
        return carry

    lax.fori_loop(0, rows // 48, finish_rows, 0)
    gn = PlaneGather(at, nm_own, nm_all, (nm_send, nm_recv))
    gn.start()
    nm_local = pltpu.make_async_copy(nm_own, nm_all.at[at.c], local_sem.at[1])
    nm_local.start()
    gn.pass_a()
    gn.pass_b()
    gn.pass_d()
    for which in ("own", "a", "b", "d"):
        gn.wait_other(which)
    og_local.wait()
    nm_local.wait()
    for part in (gx, go, gn, sc):
        part.finish_sends()
    for copies in (wc_copies, wz_copies, oz_copies, gz_copies, gc_copies):
        for cp in copies:
            cp.wait_send()


def middle_kernel(
    n_ctx, n_fsdp,
    nm_all, og_all, weights, rm, og, gains,
    dpack, mlp, gm_all, g_mid, dgain,
    nm, ogv, wgu, wd, hidden, ggu, gm_own, total, rs_out, rs_in,
    rs_send, rs_recv, gm_send, gm_recv, load_sem, local_sem,
):
    at = Place(n_ctx, n_fsdp)
    rows, width = rm.shape
    chunks = width // 128
    part_cols = n_fsdp * 128
    loads = {}

    def load(name, i, src, dst):
        cp = pltpu.make_async_copy(src, dst, load_sem.at[i])
        cp.start()
        loads.setdefault(name, []).append(cp)

    for i in range(n_fsdp):
        load("gu", i, weights.at[i, pl.ds(0, chunks)], wgu.at[:, :, pl.ds(i * 128, 128)])
        load(
            "gu", n_fsdp + i, weights.at[i, pl.ds(chunks, chunks)],
            wgu.at[:, :, pl.ds(part_cols + i * 128, 128)],
        )
    load("nm", 2 * n_fsdp, nm_all, nm)
    load("og", 2 * n_fsdp + 1, og_all, ogv)
    for i in range(chunks):
        load("wd", 2 * n_fsdp + 2 + i, weights.at[:, 2 * chunks + i], wd.at[:, :, pl.ds(i * 128, 128)])
    at.greet(False)
    for name in ("gu", "nm", "og", "wd"):
        for cp in loads[name]:
            cp.wait()

    order = [at.d + at.other, at.b + at.other, at.s, at.a + at.other, at.d, at.a, at.c, at.b]

    def feed(i, carry):
        nm_part = nm[pl.ds(2 * i, 2)].reshape(2 * rows, width)
        og_part = ogv[pl.ds(2 * i, 2)].reshape(2 * rows, width)
        both = dot(nm_part, wgu[...].reshape(width, 2 * part_cols))
        gate, up = both[:, :part_cols], both[:, part_cols:]
        g_hidden = dot(og_part, wd[...].reshape(part_cols, width), NT)
        sigma = 1.0 / (1.0 + jnp.exp(-gate))
        act = gate * sigma
        hidden[pl.ds(2 * i, 2)] = (act * up).astype(BF).reshape(2, rows, part_cols)
        ggu[pl.ds(2 * i, 2), :, 0:part_cols] = (
            (g_hidden * up * sigma * (1.0 + gate * (1.0 - sigma))).astype(BF).reshape(2, rows, part_cols)
        )
        ggu[pl.ds(2 * i, 2), :, part_cols:] = (g_hidden * act).astype(BF).reshape(2, rows, part_cols)
        return carry

    lax.fori_loop(0, n_ctx // 2, feed, 0)

    def emit_rhs(lhs, t, cols):
        part = wgu[pl.ds(t * 4, 4)].reshape(512, 2 * part_cols)
        return dot(lhs, part, NT)

    emit = tile_emit(lambda index: ggu[index], emit_rhs, width, 512)
    sc = PlaneScatter(at, emit, (rs_out, rs_in), (rs_send, rs_recv))
    sc.to_other()
    sc.first(total)

    def down_grad(t, carry):
        cols = pl.ds(pl.multiple_of(t * 256, 256), 256)
        value = dot(
            hidden[...].reshape(n_ctx * rows, part_cols), ogv[:, :, cols].reshape(n_ctx * rows, 256), TN
        ).astype(BF)
        for i in range(n_fsdp):
            for j in range(2):
                dpack[i, 2 * chunks + 2 * t + j] = value[i * 128 : (i + 1) * 128, j * 128 : (j + 1) * 128]
        return carry

    lax.fori_loop(0, width // 256, down_grad, 0)
    sc.second()

    def gate_up_grad(t, carry):
        cols = pl.ds(pl.multiple_of(t * 256, 256), 256)
        value = dot(
            nm[:, :, cols].reshape(n_ctx * rows, 256), ggu[...].reshape(n_ctx * rows, 2 * part_cols), TN
        ).astype(BF)
        for i in range(n_fsdp):
            for j in range(2):
                piece = slice(j * 128, (j + 1) * 128)
                dpack[i, 2 * t + j] = value[piece, i * 128 : (i + 1) * 128]
                dpack[i, chunks + 2 * t + j] = value[piece, part_cols + i * 128 : part_cols + (i + 1) * 128]
        return carry

    lax.fori_loop(0, width // 256, gate_up_grad, 0)

    more, most = sc.last()
    gain_two = gains[1:2, :]

    def finish_rows(r, carry):
        span = pl.ds(pl.multiple_of(r * 48, 16), 48)
        grad = total[span, :] + more[span, :].astype(F32) + most[span, :].astype(F32)
        mid = rm[span, :]
        scale = lax.rsqrt(jnp.mean(mid * mid, axis=-1, keepdims=True) + EPS)
        normed = mid * scale
        scaled = grad * gain_two
        back = og[span, :].astype(F32) + scale * (scaled - normed * jnp.mean(scaled * normed, axis=-1, keepdims=True))
        g_mid[span, :] = back
        gm_own[span, :] = back.astype(BF)
        return carry + jnp.sum((grad * normed).reshape(6, 8, width), axis=0)

    dgain[...] = lax.fori_loop(0, rows // 48, finish_rows, jnp.zeros((8, width), F32))
    gm = PlaneGather(at, gm_own, gm_all, (gm_send, gm_recv))
    gm.start()
    gm_local = pltpu.make_async_copy(gm_own, gm_all.at[at.c], local_sem)
    gm_local.start()

    def down(i, carry):
        part = hidden[pl.ds(2 * i, 2)].reshape(2 * rows, part_cols)
        mlp[pl.ds(2 * i, 2)] = dot(part, wd[...].reshape(part_cols, width)).astype(BF).reshape(2, rows, width)
        return carry

    lax.fori_loop(0, n_ctx // 2, down, 0)
    gm.pass_a()
    gm.pass_b()
    gm.pass_d()
    for which in ("own", "a", "b", "d"):
        gm.wait_other(which)
    gm_local.wait()
    sc.finish_sends()
    gm.finish_sends()


def backward_kernel(
    n_ctx, n_fsdp,
    gm_all, ao, q, k, kt, v, ot, lse, wo, ni, wqkv, x, g_mid, gains, rm, mlp, dgain, inv, pairs, expand, cosine, sine,
    mixed, tgrad, dqkv, dwout, dgain_out,
    ga, gat, delta, dwo, dwo_out, dwo_in, dk, dv, gq, gqc, dw, dw_in, dw_sum, dw_own, mine, mixed_total, total,
    ms_out, ms_in, rs_out, rs_in, dgc, dgz, dg_sum,
    ms_send, ms_recv, rs_send, rs_recv, oz_send, oz_recv, gz_send, gz_recv, gc_send, gc_recv,
    wz_send, wz_recv, wc_send, wc_recv, load_sem,
):
    at = Place(n_ctx, n_fsdp)
    rows, width = x.shape
    half = rows // 2
    seq_len = rows * n_ctx
    own_rows = dw.shape[2]
    loads = []
    for i, index in enumerate((at.d, at.a, at.c, at.b)):
        cp = pltpu.make_async_copy(mlp.at[index], mine.at[i], load_sem.at[i])
        cp.start()
        loads.append(cp)
    at.greet(True)

    ms = PlaneScatter(at, None, (ms_out, ms_in), (ms_send, ms_recv))
    for i, index in enumerate(ms.others()):
        ms.copy(i, mlp.at[index], at.s)
    gc_copies, gc_waits = exchange(at, "ctx", lambda p: dgain, dgc, lambda r, i: r.at[i], (gc_send, gc_recv))
    dgc[at.c] = dgain[...]

    def add_blocks(index, dst, extras):
        i = index

        def part(r, carry):
            span = pl.ds(pl.multiple_of(r * 48, 16), 48)
            value = mine[i, span, :].astype(F32)
            for extra in extras:
                value = value + extra[span, :].astype(F32)
            dst[span, :] = value.astype(dst.dtype)
            return carry

        lax.fori_loop(0, rows // 48, part, 0)

    def attn_grad(g, carry):
        gm_part = jnp.concatenate([gm_all[inv[4 * g + i]] for i in range(4)], axis=0)
        span = pl.ds(pl.multiple_of(g * 4 * half, 128), 4 * half)
        low = dot(gm_part, wo[...], NT).astype(BF)
        for h in range(2):
            part = low[:, h * HEAD_PAD : (h + 1) * HEAD_PAD]
            ga[h, span, :] = part
            turned = jnp.transpose(part.astype(F32))
            gat[h, :, span] = turned.astype(BF)
            delta[h, :, span] = jnp.broadcast_to(
                jnp.sum(turned * ot[h, :, span], axis=0, keepdims=True), (8, 4 * half)
            )
        dwo[...] += dot(ao[pl.ds(4 * g, 4)].reshape(4 * half, 2 * HEAD_PAD), gm_part, TN)
        return carry

    dwo[...] = jnp.zeros_like(dwo)
    lax.fori_loop(0, seq_len // (4 * half), attn_grad, 0)
    low = jnp.concatenate([dwo[0:96, :], dwo[128:224, :]], axis=0).astype(BF)
    dwo_out[...] = low.reshape(dwo_out.shape)
    oz_copies, oz_waits = exchange(
        at, "fsdp", lambda p: dwo_out.at[p], dwo_in, lambda r, i: r.at[i], (oz_send, oz_recv)
    )
    dwo_in[at.f] = dwo_out[at.f]
    for cp in loads:
        cp.wait()
    ms.emit = add_blocks
    ms.wait(0)
    add_blocks(0, ms_out.at[0], [ms_in.at[0]])
    ms.copy(4, ms_out.at[0], at.a)
    ms.wait(1)
    add_blocks(1, ms_out.at[1], [ms_in.at[1]])
    ms.copy(5, ms_out.at[1], at.a)
    ms.wait(2)
    add_blocks(2, mixed_total, [ms_in.at[2]])

    for w in gc_waits:
        w.wait_recv()
    dg_sum[...] = sum(dgc[i] for i in range(n_ctx))
    gz_copies, gz_waits = exchange(at, "fsdp", lambda p: dg_sum, dgz, lambda r, i: r.at[i], (gz_send, gz_recv))
    dgz[at.f] = dg_sum[...]

    dk[...] = jnp.zeros_like(dk)
    dv[...] = jnp.zeros_like(dv)
    block = 256
    plain_scale = HEAD_DIM ** (-0.5)
    score_scale = plain_scale * LOG2E
    for i in range(seq_len // block):
        first = i * block

        def head_step(h, carry, first=first):
            span = slice(first, first + block)
            q_part, ga_part, gat_part = q[h, span, :], ga[h, span, :], gat[h, :, span]
            top = lse[h, 0:1, span]
            shift = delta[h, 0:1, span]

            def piece(keys, masked):
                scores = dot(k[keys, :], q_part, NT) * score_scale - top
                if masked:
                    key_id = lax.broadcasted_iota(jnp.int32, (block, block), 0)
                    query_id = lax.broadcasted_iota(jnp.int32, (block, block), 1)
                    scores = jnp.where(key_id <= query_id, scores, NEG_FILL)
                prob = jnp.exp2(scores)
                grad = (prob * (dot(v[keys, :], gat_part) - shift)).astype(BF)
                dv[keys, :] += dot(prob.astype(BF), ga_part)
                dk[keys, :] += dot(grad, q_part)
                return dot(kt[:, keys], grad)

            turned = piece(span, True)
            if first:
                turned = turned + piece(slice(0, first), False)
            lanes = pl.ds(pl.multiple_of(h * HEAD_PAD, HEAD_PAD), HEAD_PAD)
            grad_q = jnp.transpose(turned) * plain_scale
            store_rows(gq, first, lanes, turn(grad_q, cosine[span, :], -sine[span, :]).astype(BF))
            return carry

        lax.fori_loop(0, 2, head_step, 0)
        if i == 2:
            ms.wait(3)
            ms.wait(4)
            add_blocks(3, ms_out.at[2], [ms_in.at[3], ms_in.at[4]])
            ms.copy(6, ms_out.at[2], at.b)

    def key_rows(g, carry):
        span = pl.ds(pl.multiple_of(g * 4 * half, 128), 4 * half)
        grad_k = turn(dk[span, :] * plain_scale, cosine[span, :], -sine[span, :]).astype(BF)
        gq[pl.ds(4 * g, 4), :, 256:384] = grad_k.reshape(4, half, HEAD_PAD)
        gq[pl.ds(4 * g, 4), :, 384:512] = dv[span, :].astype(BF).reshape(4, half, HEAD_PAD)
        return carry

    lax.fori_loop(0, seq_len // (4 * half), key_rows, 0)

    def to_ctx(slot, carry):
        pair = pairs[slot]
        gqc[2 * slot] = gq[pair]
        gqc[2 * slot + 1] = gq[2 * n_ctx - 1 - pair]
        return carry

    lax.fori_loop(0, n_ctx, to_ctx, 0)

    def weight_grad(t, carry):
        tile = 2 * n_fsdp * own_rows
        cols = pl.ds(pl.multiple_of(t * tile, 128), tile)
        value = dot(ni[:, :, cols].reshape(seq_len, tile), gqc[...].reshape(seq_len, 4 * HEAD_PAD), TN)
        low = dot(value.astype(BF), expand[...], NT).astype(BF)
        dw[pl.ds(2 * t, 2)] = low.reshape(2, n_fsdp, own_rows, low.shape[1])
        return carry

    lax.fori_loop(0, n_ctx // 2, weight_grad, 0)
    wz_copies, wz_waits = exchange(
        at, "fsdp", lambda p: dw.at[:, p], dw_in, lambda r, i: r.at[i], (wz_send, wz_recv)
    )

    def gni_rhs(lhs, t, cols):
        return dot(lhs, wqkv[pl.ds(pl.multiple_of(t * 512, 512), 512), :], NT)

    emit = tile_emit(lambda index: gqc[pl.ds(2 * index, 2)].reshape(rows, 4 * HEAD_PAD), gni_rhs, width, 512)
    sc = PlaneScatter(at, emit, (rs_out, rs_in), (rs_send, rs_recv))
    sc.to_other()
    sc.first(total)

    mixed_more, mixed_most = ms.last()

    def mixed_rows(r, carry):
        span = pl.ds(pl.multiple_of(r * 48, 16), 48)
        value = rm[span, :] + mixed_total[span, :]
        value = value + mixed_more[span, :].astype(F32) + mixed_most[span, :].astype(F32)
        mixed[span, :] = value.astype(BF)
        return carry

    lax.fori_loop(0, rows // 48, mixed_rows, 0)
    for w in oz_waits:
        w.wait_recv()
    dwout[...] = sum(dwo_in[i].astype(F32) for i in range(n_fsdp))
    for w in gz_waits:
        w.wait_recv()
    dgain_out[...] = sum(dgz[i] for i in range(n_fsdp))
    sc.second()

    for w in wz_waits:
        w.wait_recv()
    for i in range(n_ctx):
        value = dw[i, at.f].astype(F32)
        for j in range(1, n_fsdp):
            value = value + dw_in[at.fsdp_source(j), i].astype(F32)
        dw_sum[i] = value.astype(BF)
    wc_copies, wc_waits = exchange(
        at, "ctx", lambda p: dw_sum.at[p], dw_own, lambda r, i: r.at[i], (wc_send, wc_recv)
    )
    dw_own[at.c] = dw_sum[at.c]

    more, most = sc.last()
    gain_one = gains[0:1, :]

    def finish_rows(r, carry):
        span = pl.ds(pl.multiple_of(r * 48, 16), 48)
        grad = total[span, :] + more[span, :].astype(F32) + most[span, :].astype(F32)
        held = x[span, :].astype(F32)
        scale = lax.rsqrt(jnp.mean(held * held, axis=-1, keepdims=True) + EPS)
        normed = held * scale
        scaled = grad * gain_one
        back = g_mid[span, :] + scale * (scaled - normed * jnp.mean(scaled * normed, axis=-1, keepdims=True))
        tgrad[span, :] = back.astype(BF)
        return carry

    lax.fori_loop(0, rows // 48, finish_rows, 0)
    for w in wc_waits:
        w.wait_recv()
    dqkv[...] = dw_own[...]
    for part in (ms, sc):
        part.finish_sends()
    for copies in (oz_copies, gz_copies, gc_copies, wz_copies, wc_copies):
        for cp in copies:
            cp.wait_send()


def head_spread():
    spread = np.zeros((4 * HEAD_DIM, 4 * HEAD_PAD), np.float32)
    for head in range(4):
        for j in range(HEAD_DIM):
            lane = j if head == 3 or j < HEAD_DIM // 2 else j + HEAD_PAD // 2 - HEAD_DIM // 2
            spread[head * HEAD_DIM + j, head * HEAD_PAD + lane] = 1.0
    return spread


def turn_tables(seq_len):
    half_dim = HEAD_DIM // 2
    freqs = THETA ** (-(jnp.arange(half_dim, dtype=F32) * 2.0 / HEAD_DIM))
    angle = jnp.arange(seq_len, dtype=F32)[:, None] * freqs[None, :]
    gap = jnp.zeros((seq_len, HEAD_PAD // 2 - half_dim), F32)
    cosine, sine = jnp.cos(angle), jnp.sin(angle)
    return (
        jnp.concatenate([cosine, gap, cosine, gap], axis=1),
        jnp.concatenate([-sine, gap, sine, gap], axis=1),
    )


def sems(*counts):
    return [pltpu.SemaphoreType.DMA((n,)) for n in counts for _ in range(2)]


VM = pl.BlockSpec(memory_space=pltpu.VMEM)
SM = pl.BlockSpec(memory_space=pltpu.SMEM)
HB = pl.BlockSpec(memory_space=pl.ANY)


def plane(tokens, out_grad, pair_table, attn_gain, w_query, w_key, w_value, w_out, mlp_gain, w_gate, w_up, w_down):
    n_ctx, n_fsdp = lax.axis_size("ctx"), lax.axis_size("fsdp")
    rows, width = tokens.shape
    half = rows // 2
    seq_len = rows * n_ctx
    own_rows = w_query.shape[0]
    chunks = width // 128
    pairs = pair_table[0]
    slots = jnp.stack([pairs, 2 * n_ctx - 1 - pairs], axis=1).reshape(-1)
    ids = jnp.arange(2 * n_ctx, dtype=jnp.int32)
    inv = jnp.sum(jnp.where(slots[None, :] == ids[:, None], ids[None, :], 0), axis=1).astype(jnp.int32)

    packed = jnp.concatenate(
        [
            w_gate.reshape(chunks, 128, 128),
            w_up.reshape(chunks, 128, 128),
            w_down.reshape(128, chunks, 128).transpose(1, 0, 2),
        ],
        axis=0,
    )
    weights = lax.all_gather(packed, "fsdp", axis=0, tiled=False)

    wblk = jnp.concatenate(
        [w.reshape(own_rows, n_ctx, -1) for w in (w_query, w_key, w_value)], axis=2
    ).transpose(1, 0, 2)
    place = (lax.axis_index("ctx") * n_fsdp + lax.axis_index("fsdp")) * own_rows
    gt = jnp.zeros((16, width), BF)
    gt = lax.dynamic_update_slice(gt, jnp.stack([attn_gain, mlp_gain]), (0, place))
    expand = jnp.asarray(head_spread(), BF)
    cosine, sine = turn_tables(seq_len)

    def sds(shape, dtype):
        return jax.ShapeDtypeStruct(shape, dtype)

    blocks = (n_ctx, rows, width)
    vm = pltpu.VMEM
    forward = pl.pallas_call(
        functools.partial(forward_kernel, n_ctx, n_fsdp),
        out_shape=(
            sds((2 * n_ctx, half, width), BF),
            sds(blocks, BF),
            sds(blocks, BF),
            sds((2, seq_len, HEAD_PAD), BF),
            sds((seq_len, HEAD_PAD), BF),
            sds((HEAD_PAD, seq_len), BF),
            sds((seq_len, HEAD_PAD), BF),
            sds((2, HEAD_PAD, seq_len), F32),
            sds((2 * n_ctx, half, 2 * HEAD_PAD), BF),
            sds((2, 8, seq_len), F32),
            sds((width, 4 * HEAD_PAD), BF),
            sds((2 * HEAD_PAD, width), BF),
            sds((16, width), F32),
            sds((rows, width), F32),
        ),
        in_specs=[VM, HB, VM, VM, VM, SM, SM, VM, VM, VM],
        out_specs=(VM, HB, HB) + (VM,) * 11,
        scratch_shapes=[
            vm(blocks, BF),
            vm((n_ctx, n_fsdp, own_rows, 4 * HEAD_DIM), BF),
            vm((n_fsdp, own_rows, width), BF),
            vm((n_fsdp, 16, width), BF),
            vm((16, width), BF),
            vm((n_ctx, 16, width), BF),
            vm((HEAD_PAD, seq_len), BF),
            vm((rows, width), BF),
            vm((rows, width), F32),
            vm((7, rows, width), BF),
            vm((7, rows, width), BF),
            *sems(7, 7, 7, 7, n_ctx, n_fsdp, n_fsdp, n_fsdp, n_ctx),
            pltpu.SemaphoreType.DMA((2,)),
        ],
        compiler_params=pltpu.CompilerParams(
            collective_id=0, has_side_effects=True, vmem_limit_bytes=VMEM_LIMIT
        ),
        name="attention_forward",
    )
    ni, nm_all, og_all, q, k, kt, v, ot, ao, lse, wqkv, wo, gains, rm = forward(
        tokens, out_grad, wblk, w_out, gt, inv, pairs, expand, cosine, sine
    )

    part_cols = n_fsdp * 128
    middle = pl.pallas_call(
        functools.partial(middle_kernel, n_ctx, n_fsdp),
        out_shape=(
            sds((n_fsdp, 3 * chunks, 128, 128), BF),
            sds(blocks, BF),
            sds(blocks, BF),
            sds((rows, width), F32),
            sds((8, width), F32),
        ),
        in_specs=[HB, HB, HB, VM, VM, VM],
        out_specs=(VM, VM, HB, VM, VM),
        scratch_shapes=[
            vm(blocks, BF),
            vm(blocks, BF),
            vm((chunks, 128, 2 * part_cols), BF),
            vm((n_fsdp, 128, width), BF),
            vm((n_ctx, rows, part_cols), BF),
            vm((n_ctx, rows, 2 * part_cols), BF),
            vm((rows, width), BF),
            vm((rows, width), F32),
            vm((7, rows, width), BF),
            vm((7, rows, width), BF),
            *sems(7, 7),
            pltpu.SemaphoreType.DMA((2 * n_fsdp + 2 + chunks,)),
            pltpu.SemaphoreType.DMA,
        ],
        compiler_params=pltpu.CompilerParams(
            collective_id=1, has_side_effects=True, vmem_limit_bytes=VMEM_LIMIT
        ),
        name="feed_forward",
    )
    dpack, mlp, gm_all, g_mid, dgain = middle(nm_all, og_all, weights, rm, out_grad, gains)
    dffn = lax.psum_scatter(dpack, "fsdp", scatter_dimension=0, tiled=False).astype(F32)

    backward = pl.pallas_call(
        functools.partial(backward_kernel, n_ctx, n_fsdp),
        out_shape=(
            sds((rows, width), BF),
            sds((rows, width), BF),
            sds((n_ctx, own_rows, 4 * HEAD_DIM), BF),
            sds((own_rows, width), F32),
            sds((8, width), F32),
        ),
        in_specs=[VM] * 15 + [HB, VM, SM, SM, VM, VM, VM],
        out_specs=(VM,) * 5,
        scratch_shapes=[
            vm((2, seq_len, HEAD_PAD), BF),
            vm((2, HEAD_PAD, seq_len), BF),
            vm((2, 8, seq_len), F32),
            vm((2 * HEAD_PAD, width), F32),
            vm((n_fsdp, own_rows, width), BF),
            vm((n_fsdp, own_rows, width), BF),
            vm((seq_len, HEAD_PAD), F32),
            vm((seq_len, HEAD_PAD), F32),
            vm((2 * n_ctx, half, 4 * HEAD_PAD), BF),
            vm((2 * n_ctx, half, 4 * HEAD_PAD), BF),
            vm((n_ctx, n_fsdp, own_rows, 4 * HEAD_DIM), BF),
            vm((n_fsdp, n_ctx, own_rows, 4 * HEAD_DIM), BF),
            vm((n_ctx, own_rows, 4 * HEAD_DIM), BF),
            vm((n_ctx, own_rows, 4 * HEAD_DIM), BF),
            vm((4, rows, width), BF),
            vm((rows, width), F32),
            vm((rows, width), F32),
            vm((3, rows, width), BF),
            vm((7, rows, width), BF),
            vm((7, rows, width), BF),
            vm((7, rows, width), BF),
            vm((n_ctx, 8, width), F32),
            vm((n_fsdp, 8, width), F32),
            vm((8, width), F32),
            *sems(7, 7, n_fsdp, n_fsdp, n_ctx, n_fsdp, n_ctx),
            pltpu.SemaphoreType.DMA((4,)),
        ],
        compiler_params=pltpu.CompilerParams(
            collective_id=2, has_side_effects=True, vmem_limit_bytes=VMEM_LIMIT
        ),
        name="attention_backward",
    )
    mixed, tokens_grad, dqkv, d_out, d_gain_two = backward(
        gm_all.reshape(2 * n_ctx, half, width), ao, q, k, kt, v, ot, lse, wo, ni, wqkv, tokens, g_mid, gains, rm, mlp,
        dgain, inv, pairs, expand, cosine, sine,
    )
    dqkv = dqkv.astype(F32)
    q_cols, kv_cols = w_query.shape[1] // n_ctx, w_key.shape[1] // n_ctx
    gain_one_grad = jnp.sum(dqkv * wblk.astype(F32), axis=(0, 2)) / attn_gain.astype(F32)
    by_row = dqkv.transpose(1, 0, 2)
    d_query = by_row[:, :, :q_cols].reshape(w_query.shape)
    d_key = by_row[:, :, q_cols : q_cols + kv_cols].reshape(w_key.shape)
    d_value = by_row[:, :, q_cols + kv_cols :].reshape(w_value.shape)
    gain_two_grad = lax.dynamic_slice_in_dim(jnp.sum(d_gain_two, axis=0), place, own_rows, 0)
    d_gate = dffn[:chunks].reshape(w_gate.shape)
    d_up = dffn[chunks : 2 * chunks].reshape(w_up.shape)
    d_down = dffn[2 * chunks :].transpose(1, 0, 2).reshape(w_down.shape)
    return (
        mixed, tokens_grad, gain_one_grad, d_query, d_key, d_value, d_out, gain_two_grad, d_gate, d_up, d_down,
    )


def solution(mesh):
    in_specs = (
        P(("ctx", "fsdp"), None),
        P(("ctx", "fsdp"), None),
        P("fsdp", None),
        P(("ctx", "fsdp")),
        P(("ctx", "fsdp"), None),
        P(("ctx", "fsdp"), None),
        P(("ctx", "fsdp"), None),
        P(("ctx", "fsdp"), None),
        P(("ctx", "fsdp")),
        P(None, ("ctx", "fsdp")),
        P(None, ("ctx", "fsdp")),
        P(("ctx", "fsdp"), None),
    )
    out_specs = (
        P(("ctx", "fsdp"), None),
        P(("ctx", "fsdp"), None),
        P(("ctx", "fsdp")),
        P(("ctx", "fsdp"), None),
        P(("ctx", "fsdp"), None),
        P(("ctx", "fsdp"), None),
        P(("ctx", "fsdp"), None),
        P(("ctx", "fsdp")),
        P(None, ("ctx", "fsdp")),
        P(None, ("ctx", "fsdp")),
        P(("ctx", "fsdp"), None),
    )
    fits = (
        mesh.shape["ctx"] == KV_HEADS
        and mesh.shape["fsdp"] * 128 * KV_HEADS == FEED_WIDTH
        and HEADS == 2 * KV_HEADS
    )
    return jax.shard_map(plane if fits else local, mesh=mesh, in_specs=in_specs, out_specs=out_specs, check_vma=False)
```

```python
import functools
import math

import jax
import jax.numpy as jnp
import numpy as np
from jax import lax
from jax.experimental import pallas as pl
from jax.experimental.pallas import tpu as pltpu
from jax.sharding import PartitionSpec as P

HEADS = 16
KV_HEADS = 8
HEAD_DIM = 96


EPS = 1e-05
THETA = 100000.0
NEG_FILL = -1e30


def rotate(values_in, positions, direction):
    half_dim = values_in.shape[-1] // 2
    freqs = THETA ** (-(jnp.arange(half_dim, dtype=jnp.float32) * 2.0 / values_in.shape[-1]))
    angle = positions.astype(jnp.float32)[:, None] * freqs[None, :]
    cosine = jnp.cos(angle)[:, None, :]
    sine = direction * jnp.sin(angle)[:, None, :]
    first_half = values_in[..., :half_dim]
    second_half = values_in[..., half_dim:]
    return jnp.concatenate(
        [first_half * cosine - second_half * sine, second_half * cosine + first_half * sine],
        axis=-1,
    )


def place_rows(pair_index, tok_rows, block_count):
    half_rows = tok_rows // 2
    offsets = jnp.arange(tok_rows, dtype=jnp.int32)
    early = pair_index * half_rows + offsets
    late = (block_count - 1 - pair_index) * half_rows + offsets - half_rows
    return jnp.where(offsets < half_rows, early, late)


def rms_scale(values_in):
    return lax.rsqrt(jnp.mean(values_in * values_in, axis=-1, keepdims=True) + EPS)


def norm_back(grad_normed, normed, inv_rms, gain):
    scaled = grad_normed * gain
    return inv_rms * (scaled - normed * jnp.mean(scaled * normed, axis=-1, keepdims=True))


def local(
    tokens,
    out_grad,
    pair_table,
    attn_gain,
    w_query,
    w_key,
    w_value,
    w_out,
    mlp_gain,
    w_gate,
    w_up,
    w_down,
):
    tok_rows = tokens.shape[0]
    half_rows = tok_rows // 2
    ctx_count = lax.axis_size("ctx")
    half_count = 2 * ctx_count
    pair_row = pair_table[0]
    my_pos = place_rows(pair_row[lax.axis_index("ctx")], tok_rows, half_count)
    half_blocks = jnp.stack([pair_row, half_count - 1 - pair_row], axis=1).reshape(-1)
    block_ids = jnp.arange(half_count, dtype=jnp.int32)
    inverse = jnp.sum(
        jnp.where(half_blocks[None, :] == block_ids[:, None], block_ids[None, :], 0), axis=1
    )
    group_size = HEADS // KV_HEADS
    score_scale = HEAD_DIM ** (-0.5)
    query_width = HEADS * HEAD_DIM
    kv_width = KV_HEADS * HEAD_DIM
    w_query_all, w_key_all, w_value_all, w_out_all, gain_first, gain_second = (
        lax.all_gather(w_query, ("ctx", "fsdp"), axis=0, tiled=True),
        lax.all_gather(w_key, ("ctx", "fsdp"), axis=0, tiled=True),
        lax.all_gather(w_value, ("ctx", "fsdp"), axis=0, tiled=True),
        lax.all_gather(w_out, ("ctx", "fsdp"), axis=0, tiled=True),
        lax.all_gather(attn_gain, ("ctx", "fsdp"), axis=0, tiled=True),
        lax.all_gather(mlp_gain, ("ctx", "fsdp"), axis=0, tiled=True),
    )
    gain_one = gain_first.astype(jnp.float32)
    gain_two = gain_second.astype(jnp.float32)
    resid_in = tokens.astype(jnp.float32)
    inv_one = rms_scale(resid_in)
    normed_one = resid_in * inv_one
    normed_in = (normed_one * gain_one).astype(jnp.bfloat16)
    query_lin = jnp.dot(normed_in, w_query_all, preferred_element_type=jnp.float32)
    key_lin = jnp.dot(normed_in, w_key_all, preferred_element_type=jnp.float32)
    value_lin = jnp.dot(normed_in, w_value_all, preferred_element_type=jnp.float32)
    query_rot = rotate(query_lin.reshape(tok_rows, HEADS, HEAD_DIM), my_pos, 1.0).astype(
        jnp.bfloat16
    )
    key_rot = (
        rotate(key_lin.reshape(tok_rows, KV_HEADS, HEAD_DIM), my_pos, 1.0)
        .astype(jnp.bfloat16)
        .reshape(tok_rows, kv_width)
    )
    value_low = value_lin.astype(jnp.bfloat16)
    keys_got, values_got = (
        lax.all_gather(key_rot, "ctx", axis=0, tiled=True),
        lax.all_gather(value_low, "ctx", axis=0, tiled=True),
    )
    seq_len = keys_got.shape[0]
    keys_all = jnp.take(keys_got.reshape(half_count, half_rows, kv_width), inverse, axis=0).reshape(
        seq_len, kv_width
    )
    values_all = jnp.take(
        values_got.reshape(half_count, half_rows, kv_width), inverse, axis=0
    ).reshape(seq_len, kv_width)
    key_pos = jnp.arange(seq_len, dtype=jnp.int32)
    key_block = math.gcd(seq_len, 512)
    live_blocks = jnp.max(my_pos) // key_block + 1
    query_grp = query_rot.reshape(tok_rows, KV_HEADS, group_size, HEAD_DIM)

    def block_scores(block_index):
        first_row = block_index * key_block
        key_tile = lax.dynamic_slice_in_dim(keys_all, first_row, key_block, 0).reshape(
            key_block, KV_HEADS, HEAD_DIM
        )
        value_tile = lax.dynamic_slice_in_dim(values_all, first_row, key_block, 0).reshape(
            key_block, KV_HEADS, HEAD_DIM
        )
        scores = (
            jnp.einsum("tkgd,skd->kgts", query_grp, key_tile, preferred_element_type=jnp.float32)
            * score_scale
        )
        visible = (
            lax.dynamic_slice_in_dim(key_pos, first_row, key_block, 0)[None, :] <= my_pos[:, None]
        )
        return (scores, visible, key_tile, value_tile)

    def stats_step(block_index, carry):
        run_max, run_sum = carry
        scores, visible, key_tile, value_tile = block_scores(block_index)
        masked = jnp.where(visible, scores, NEG_FILL)
        new_max = jnp.maximum(run_max, jnp.max(masked, axis=-1))
        weights = jnp.where(visible, jnp.exp(masked - new_max[..., None]), 0.0)
        return (new_max, run_sum * jnp.exp(run_max - new_max) + jnp.sum(weights, axis=-1))

    start_max = jnp.full((KV_HEADS, group_size, tok_rows), NEG_FILL, jnp.float32)
    run_max, run_sum = lax.fori_loop(
        0, live_blocks, stats_step, (start_max, jnp.zeros_like(start_max))
    )
    log_total = run_max + jnp.log(run_sum)

    def probs(scores, visible):
        return jnp.where(visible, jnp.exp(scores - log_total[..., None]), 0.0)

    def output_step(block_index, accum):
        scores, visible, key_tile, value_tile = block_scores(block_index)
        prob_low = probs(scores, visible).astype(jnp.bfloat16)
        return accum + jnp.einsum(
            "kgts,skd->kgtd", prob_low, value_tile, preferred_element_type=jnp.float32
        )

    attn_acc = lax.fori_loop(
        0,
        live_blocks,
        output_step,
        jnp.zeros((KV_HEADS, group_size, tok_rows, HEAD_DIM), jnp.float32),
    )
    attn_low = attn_acc.transpose(2, 0, 1, 3).reshape(tok_rows, query_width).astype(jnp.bfloat16)
    resid_mid = resid_in + jnp.dot(attn_low, w_out_all, preferred_element_type=jnp.float32)
    inv_two = rms_scale(resid_mid)
    normed_two = resid_mid * inv_two
    normed_mid = (normed_two * gain_two).astype(jnp.bfloat16)
    w_gate_part, w_up_part, w_down_part = (
        lax.all_gather(w_gate, ("ctx", "fsdp"), axis=1, tiled=True),
        lax.all_gather(w_up, ("ctx", "fsdp"), axis=1, tiled=True),
        lax.all_gather(w_down, ("ctx", "fsdp"), axis=0, tiled=True),
    )
    gate_lin = jnp.dot(normed_mid, w_gate_part, preferred_element_type=jnp.float32)
    up_lin = jnp.dot(normed_mid, w_up_part, preferred_element_type=jnp.float32)
    sigma = jax.nn.sigmoid(gate_lin)
    activated = gate_lin * sigma
    hidden_low = (activated * up_lin).astype(jnp.bfloat16)
    mlp_branch = jnp.dot(hidden_low, w_down_part, preferred_element_type=jnp.float32)
    mixed = (resid_mid + mlp_branch).astype(jnp.bfloat16)
    grad_top = out_grad.astype(jnp.float32)
    d_down = jnp.einsum("tf,td->fd", hidden_low, out_grad, preferred_element_type=jnp.float32)
    grad_hidden = jnp.einsum("td,fd->tf", out_grad, w_down_part, preferred_element_type=jnp.float32)
    grad_gate = (grad_hidden * up_lin * sigma * (1.0 + gate_lin * (1.0 - sigma))).astype(
        jnp.bfloat16
    )
    grad_up = (grad_hidden * activated).astype(jnp.bfloat16)
    d_gate = jnp.einsum("td,tf->df", normed_mid, grad_gate, preferred_element_type=jnp.float32)
    d_up = jnp.einsum("td,tf->df", normed_mid, grad_up, preferred_element_type=jnp.float32)
    grad_normed_mid = jnp.einsum(
        "tf,df->td", grad_gate, w_gate_part, preferred_element_type=jnp.float32
    ) + jnp.einsum("tf,df->td", grad_up, w_up_part, preferred_element_type=jnp.float32)
    gate_grad_out, up_grad_out, down_grad_out = (
        lax.psum_scatter(d_gate, ("ctx", "fsdp"), scatter_dimension=1, tiled=True),
        lax.psum_scatter(d_up, ("ctx", "fsdp"), scatter_dimension=1, tiled=True),
        lax.psum_scatter(d_down, ("ctx", "fsdp"), scatter_dimension=0, tiled=True),
    )
    d_gain_two = jnp.sum(grad_normed_mid * normed_two, axis=0)
    grad_mid = grad_top + norm_back(grad_normed_mid, normed_two, inv_two, gain_two)
    grad_mid_low = grad_mid.astype(jnp.bfloat16)
    d_out = jnp.einsum("tq,td->qd", attn_low, grad_mid_low, preferred_element_type=jnp.float32)
    grad_attn_low = jnp.einsum(
        "td,qd->tq", grad_mid_low, w_out_all, preferred_element_type=jnp.float32
    ).astype(jnp.bfloat16)
    grad_heads = grad_attn_low.reshape(tok_rows, KV_HEADS, group_size, HEAD_DIM).transpose(
        1, 2, 0, 3
    )
    row_delta = jnp.sum(grad_heads.astype(jnp.float32) * attn_acc, axis=-1)

    def back_step(block_index, carry):
        grad_query, grad_keys, grad_values = carry
        scores, visible, key_tile, value_tile = block_scores(block_index)
        prob_full = probs(scores, visible)
        prob_low = prob_full.astype(jnp.bfloat16)
        grad_prob = jnp.einsum(
            "kgtd,skd->kgts", grad_heads, value_tile, preferred_element_type=jnp.float32
        )
        grad_score = (prob_full * (grad_prob - row_delta[..., None])).astype(jnp.bfloat16)
        grad_query = grad_query + score_scale * jnp.einsum(
            "kgts,skd->kgtd", grad_score, key_tile, preferred_element_type=jnp.float32
        )
        key_part = score_scale * jnp.einsum(
            "kgts,tkgd->skd", grad_score, query_grp, preferred_element_type=jnp.float32
        )
        value_part = jnp.einsum(
            "kgts,kgtd->skd", prob_low, grad_heads, preferred_element_type=jnp.float32
        )
        first_row = block_index * key_block
        grad_keys = lax.dynamic_update_slice_in_dim(
            grad_keys, key_part.reshape(key_block, kv_width), first_row, 0
        )
        grad_values = lax.dynamic_update_slice_in_dim(
            grad_values, value_part.reshape(key_block, kv_width), first_row, 0
        )
        return (grad_query, grad_keys, grad_values)

    empty_keys = jnp.zeros((seq_len, kv_width), jnp.float32)
    grad_query, grad_keys, grad_values = lax.fori_loop(
        0,
        live_blocks,
        back_step,
        (
            jnp.zeros((KV_HEADS, group_size, tok_rows, HEAD_DIM), jnp.float32),
            empty_keys,
            empty_keys,
        ),
    )
    keys_back = jnp.take(
        grad_keys.reshape(half_count, half_rows, kv_width), half_blocks, axis=0
    ).reshape(seq_len, kv_width)
    values_back = jnp.take(
        grad_values.reshape(half_count, half_rows, kv_width), half_blocks, axis=0
    ).reshape(seq_len, kv_width)
    own_keys, own_values = (
        lax.psum_scatter(
            keys_back.astype(jnp.bfloat16), "ctx", scatter_dimension=0, tiled=True
        ).astype(jnp.float32),
        lax.psum_scatter(
            values_back.astype(jnp.bfloat16), "ctx", scatter_dimension=0, tiled=True
        ).astype(jnp.float32),
    )
    grad_query_lin = rotate(
        grad_query.transpose(2, 0, 1, 3).reshape(tok_rows, HEADS, HEAD_DIM), my_pos, -1.0
    )
    grad_query_low = grad_query_lin.reshape(tok_rows, query_width).astype(jnp.bfloat16)
    grad_key_lin = rotate(own_keys.reshape(tok_rows, KV_HEADS, HEAD_DIM), my_pos, -1.0)
    grad_key_low = grad_key_lin.reshape(tok_rows, kv_width).astype(jnp.bfloat16)
    grad_value_low = own_values.astype(jnp.bfloat16)
    d_query = jnp.einsum("td,tq->dq", normed_in, grad_query_low, preferred_element_type=jnp.float32)
    d_key = jnp.einsum("td,tq->dq", normed_in, grad_key_low, preferred_element_type=jnp.float32)
    d_value = jnp.einsum("td,tq->dq", normed_in, grad_value_low, preferred_element_type=jnp.float32)
    grad_normed_in = (
        jnp.einsum("tq,dq->td", grad_query_low, w_query_all, preferred_element_type=jnp.float32)
        + jnp.einsum("tq,dq->td", grad_key_low, w_key_all, preferred_element_type=jnp.float32)
        + jnp.einsum("tq,dq->td", grad_value_low, w_value_all, preferred_element_type=jnp.float32)
    )
    d_gain_one = jnp.sum(grad_normed_in * normed_one, axis=0)
    grad_input = grad_mid + norm_back(grad_normed_in, normed_one, inv_one, gain_one)
    query_grad_out, key_grad_out, value_grad_out, out_grad_out, gain_one_out, gain_two_out = (
        lax.psum_scatter(d_query, ("ctx", "fsdp"), scatter_dimension=0, tiled=True),
        lax.psum_scatter(d_key, ("ctx", "fsdp"), scatter_dimension=0, tiled=True),
        lax.psum_scatter(d_value, ("ctx", "fsdp"), scatter_dimension=0, tiled=True),
        lax.psum_scatter(d_out, ("ctx", "fsdp"), scatter_dimension=0, tiled=True),
        lax.psum_scatter(d_gain_one, ("ctx", "fsdp"), scatter_dimension=0, tiled=True),
        lax.psum_scatter(d_gain_two, ("ctx", "fsdp"), scatter_dimension=0, tiled=True),
    )
    return (
        mixed,
        grad_input.astype(jnp.bfloat16),
        gain_one_out,
        query_grad_out,
        key_grad_out,
        value_grad_out,
        out_grad_out,
        gain_two_out,
        gate_grad_out,
        up_grad_out,
        down_grad_out,
    )


BF = jnp.bfloat16
F32 = jnp.float32
MESH = pl.DeviceIdType.MESH
HEAD_PAD = 128
LOG2E = 1.4426950408889634
VMEM_LIMIT = 58 * 2**20
NT = (((1,), (1,)), ((), ()))
TN = (((0,), (0,)), ((), ()))


def dot(a, b, dims=(((1,), (0,)), ((), ()))):
    return lax.dot_general(a, b, dims, preferred_element_type=F32)


class Place:
    def __init__(self, n_ctx, n_fsdp):
        self.n_ctx, self.n_fsdp = n_ctx, n_fsdp
        self.c, self.f = lax.axis_index("ctx"), lax.axis_index("fsdp")
        core = lax.rem(self.c, 2)
        step_x = 2 - 4 * lax.rem(lax.div(self.c, 2), 2)
        step_y = 4 - 8 * lax.div(self.c, 4)
        self.other = 1 - 2 * core
        self.s = self.c + self.other
        self.a = self.c + step_x * (1 - core) + step_y * core
        self.b = self.c + step_x * core + step_y * (1 - core)
        self.d = self.c + step_x + step_y
        self.f1 = self.f + 1 - 2 * lax.rem(self.f, 2)
        self.f2 = self.f + 2 - 4 * lax.div(self.f, 2)
        self.f3 = n_fsdp - 1 - self.f

    def ctx_peer(self, j):
        return lax.rem(self.c + j, self.n_ctx)

    def ctx_source(self, j):
        return lax.rem(self.c + self.n_ctx - j, self.n_ctx)

    def greet(self, everyone):
        barrier = pltpu.get_barrier_semaphore()
        if everyone:
            mates = [(self.ctx_peer(j), self.f) for j in range(1, self.n_ctx)]
        else:
            mates = [(self.s, self.f), (self.a, self.f), (self.b, self.f)]
        mates += [(self.c, self.f1), (self.c, self.f2)]
        for mate in mates:
            pl.semaphore_signal(barrier, inc=1, device_id=mate, device_id_type=MESH)
        pl.semaphore_wait(barrier, len(mates))


def remote(src, dst, send, recv, device):
    return pltpu.make_async_remote_copy(
        src_ref=src, dst_ref=dst, send_sem=send, recv_sem=recv, device_id=device, device_id_type=MESH
    )


class PlaneGather:
    PIECES = 3
    COUNT = 7 * PIECES

    def __init__(self, at, own, blocks, sems):
        self.at, self.own, self.blocks = at, own, blocks
        self.send, self.recv = sems
        self.rows = own.shape[0] // self.PIECES
        self.started = []

    def piece(self, slot, p):
        return self.blocks.at[slot, pl.ds(p * self.rows, self.rows)]

    def copy(self, i, p, src, slot, mate):
        k = i * self.PIECES + p
        cp = remote(src, self.piece(slot, p), self.send.at[k], self.recv.at[k], (mate, self.at.f))
        cp.start()
        self.started.append(cp)

    def wait(self, i, p, slot):
        k = i * self.PIECES + p
        block = self.piece(slot, p)
        remote(block, block, self.send.at[k], self.recv.at[k], (self.at.s, self.at.f)).wait_recv()

    def start_piece(self, p):
        at = self.at
        src = self.own.at[pl.ds(p * self.rows, self.rows)]
        self.copy(1, p, src, at.c, at.a)
        self.copy(2, p, src, at.c, at.b)
        self.copy(0, p, src, at.c, at.s)

    def start(self):
        for p in range(self.PIECES):
            self.start_piece(p)

    def pass_a(self):
        at = self.at
        for p in range(self.PIECES):
            self.wait(1, p, at.a)
            self.copy(4, p, self.piece(at.a, p), at.a, at.b)
            self.copy(3, p, self.piece(at.a, p), at.a, at.s)

    def pass_b(self):
        at = self.at
        for p in range(self.PIECES):
            self.wait(2, p, at.b)
            self.copy(5, p, self.piece(at.b, p), at.b, at.s)

    def pass_d(self):
        at = self.at
        for p in range(self.PIECES):
            self.wait(4, p, at.d)
            self.copy(6, p, self.piece(at.d, p), at.d, at.s)

    def wait_other(self, which):
        at = self.at
        i, slot = {
            "own": (0, at.s),
            "a": (3, at.b + at.other),
            "b": (5, at.a + at.other),
            "d": (6, at.d + at.other),
        }[which]
        for p in range(self.PIECES):
            self.wait(i, p, slot)

    def finish_sends(self):
        for cp in self.started:
            cp.wait_send()


class PlaneScatter:
    def __init__(self, at, emit, bufs, sems, pieces):
        self.at, self.emit, self.pieces = at, emit, pieces
        self.out, self.landed = bufs
        self.send, self.recv = sems
        self.started = []

    def columns(self, t):
        width = self.landed.shape[2] // self.pieces
        return slice(t * width, (t + 1) * width)

    def copy(self, i, t, src, mate):
        k = i * self.pieces + t
        dst = self.landed.at[i, :, self.columns(t)]
        cp = remote(src, dst, self.send.at[k], self.recv.at[k], (mate, self.at.f))
        cp.start()
        self.started.append(cp)

    def wait(self, i, t):
        k = i * self.pieces + t
        block = self.landed.at[i, :, self.columns(t)]
        remote(block, block, self.send.at[k], self.recv.at[k], (self.at.s, self.at.f)).wait_recv()

    def others(self):
        at = self.at
        return (at.d + at.other, at.b + at.other, at.s, at.a + at.other)

    def to_other(self, i):
        for t in range(self.pieces):
            columns = self.columns(t)
            self.emit(self.others()[i], columns, self.out.at[i], [])
            self.copy(i, t, self.out.at[i, :, columns], self.at.s)

    def onward(self, i, index, extras, mate):
        for t in range(self.pieces):
            columns = self.columns(t)
            for extra in extras:
                self.wait(extra, t)
            self.emit(index, columns, self.out.at[i], [self.landed.at[extra] for extra in extras])
            self.copy(i, t, self.out.at[i, :, columns], mate)

    def first(self, total):
        at = self.at
        self.to_other(0)
        self.to_other(1)
        self.onward(4, at.d, [0], at.a)
        self.onward(5, at.a, [1], at.a)
        self.to_other(3)
        self.to_other(2)
        for t in range(self.pieces):
            self.wait(2, t)
            self.emit(at.c, self.columns(t), total, [self.landed.at[2]])

    def second(self):
        self.onward(6, self.at.b, [3, 4], self.at.b)

    def last(self):
        for i in (5, 6):
            for t in range(self.pieces):
                self.wait(i, t)
        return self.landed.at[5], self.landed.at[6]

    def finish_sends(self):
        for cp in self.started:
            cp.wait_send()


class LineGather:
    COUNT = 3

    def __init__(self, at, own, slot, sems):
        self.at, self.own, self.slot = at, own, slot
        self.send, self.recv = sems
        self.started = []

    def copy(self, i, src, slot, mate):
        cp = remote(src, self.slot(slot), self.send.at[i], self.recv.at[i], (self.at.c, mate))
        cp.start()
        self.started.append(cp)

    def wait(self, i, slot):
        block = self.slot(slot)
        remote(block, block, self.send.at[i], self.recv.at[i], (self.at.c, self.at.f1)).wait_recv()

    def start(self):
        at = self.at
        self.copy(1, self.own, at.f, at.f2)
        self.copy(0, self.own, at.f, at.f1)

    def relay(self):
        at = self.at
        self.wait(1, at.f2)
        self.copy(2, self.slot(at.f2), at.f2, at.f1)

    def finish(self):
        self.wait(0, self.at.f1)
        self.wait(2, self.at.f3)

    def finish_sends(self):
        for cp in self.started:
            cp.wait_send()


class LineScatter:
    COUNT = 3

    def __init__(self, at, part, landed, stage, sems):
        self.at, self.part, self.landed, self.stage = at, part, landed, stage
        self.send, self.recv = sems
        self.started = []

    def copy(self, i, src, mate):
        cp = remote(src, self.landed.at[i], self.send.at[i], self.recv.at[i], (self.at.c, mate))
        cp.start()
        self.started.append(cp)

    def wait(self, i):
        block = self.landed.at[i]
        remote(block, block, self.send.at[i], self.recv.at[i], (self.at.c, self.at.f1)).wait_recv()

    def start(self):
        at = self.at
        self.copy(0, self.part(at.f3), at.f1)
        self.copy(1, self.part(at.f1), at.f1)

    def add(self, dst, refs):
        count = dst.shape[0]
        step = min(count, 128) if len(dst.shape) == 2 else 1

        def piece(i, carry):
            rows = pl.ds(pl.multiple_of(i * step, step), step) if len(dst.shape) == 2 else pl.ds(i, 1)
            value = refs[0][rows].astype(F32)
            for ref in refs[1:]:
                value = value + ref[rows].astype(F32)
            dst[rows] = value.astype(dst.dtype)
            return carry

        lax.fori_loop(0, count // step, piece, 0)

    def relay(self):
        at = self.at
        self.wait(0)
        self.add(self.stage, [self.part(at.f2), self.landed.at[0]])
        self.copy(2, self.stage, at.f2)

    def finish(self, dst):
        self.wait(1)
        self.wait(2)
        self.add(dst, [self.part(self.at.f), self.landed.at[1], self.landed.at[2]])

    def finish_sends(self):
        for cp in self.started:
            cp.wait_send()


def exchange(at, src_of, dst, slot_of, sems):
    send, recv = sems
    started, waits = [], []
    for j in range(1, at.n_ctx):
        peer, source = at.ctx_peer(j), at.ctx_source(j)
        device = (peer, at.f)
        cp = remote(src_of(peer), slot_of(dst, at.c), send.at[j], recv.at[j], device)
        cp.start()
        started.append(cp)
        block = slot_of(dst, source)
        waits.append(remote(block, block, send.at[j], recv.at[j], device))
    return started, waits


def turn(values_in, cosine, sine):
    return values_in * cosine + pltpu.roll(values_in, HEAD_PAD // 2, 1) * sine


def store_rows(ref, first, lanes, value):
    block_rows, done = ref.shape[1], 0
    while done < value.shape[0]:
        block, start = divmod(first + done, block_rows)
        count = min(block_rows - start, value.shape[0] - done)
        ref[block, start : start + count, lanes] = value[done : done + count]
        done += count


def product_emit(lhs_of, rhs_of):
    def emit(index, columns, dst, extras):
        value = rhs_of(lhs_of(index), columns)
        for extra in extras:
            value = value + extra[:, columns].astype(F32)
        dst[:, columns] = value.astype(dst.dtype)

    return emit


def forward_kernel(
    n_ctx, n_fsdp,
    x, og, wq, wk, wv, wout, wg, wu, wd, gain_rows, inv, pairs, expand, cosine, sine,
    ni, nm_all, og_all, wg_all, wu_all, wd_all, q, k, kt, v, ot, ao, lse, wqkv, wo, gains, rm,
    x_all, wblk, w_raw, wo_raw, gt, gz, gz_sum, gc, vt, nm_own, total, rs_out, rs_in,
    x_send, x_recv, og_send, og_recv, nm_send, nm_recv, rs_send, rs_recv,
    wc_send, wc_recv, wz_send, wz_recv, oz_send, oz_recv, gz_send, gz_recv, gc_send, gc_recv,
    fg_send, fg_recv, fu_send, fu_recv, fd_send, fd_recv, local_sem,
):
    at = Place(n_ctx, n_fsdp)
    rows, width = x.shape
    half = rows // 2
    seq_len = rows * n_ctx
    own_rows = w_raw.shape[2]
    local_copies = []
    for i, (src, dst) in enumerate(
        ((og, og_all.at[at.c]), (wg, wg_all.at[at.f]), (wu, wu_all.at[at.f]), (wd, wd_all.at[at.f]))
    ):
        cp = pltpu.make_async_copy(src, dst, local_sem.at[i])
        cp.start()
        local_copies.append(cp)
    q_cols, kv_cols = wq.shape[1] // n_ctx, wk.shape[1] // n_ctx
    for i in range(n_ctx):
        parts = (wq[:, i * q_cols : (i + 1) * q_cols], *(w[:, i * kv_cols : (i + 1) * kv_cols] for w in (wk, wv)))
        wblk[i] = jnp.concatenate(parts, axis=1)
    place = (at.c * n_fsdp + at.f) * own_rows
    from_lane = lax.broadcasted_iota(jnp.int32, (128, width), 0)
    to_lane = lax.broadcasted_iota(jnp.int32, (128, width), 1)
    spread = jnp.where((to_lane == from_lane + place) & (from_lane < own_rows), 1.0, 0.0).astype(BF)
    gt[...] = dot(gain_rows[...], spread).astype(BF)
    at.greet(True)

    wc_copies, wc_waits = exchange(
        at, lambda p: wblk.at[p], w_raw, lambda r, i: r.at[i, at.f], (wc_send, wc_recv)
    )
    zg = LineGather(at, gt, lambda i: gz.at[i], (gz_send, gz_recv))
    zg.start()
    gx = PlaneGather(at, x, x_all, (x_send, x_recv))
    gx.start()
    zo = LineGather(at, wout, lambda i: wo_raw.at[i], (oz_send, oz_recv))
    zo.start()
    w_raw[at.c, at.f] = wblk[at.c]
    wo_raw[at.f] = wout[...]
    gz[at.f] = gt[...]
    x_all[at.c] = x[...]
    zg.relay()
    zg.finish()
    gz_sum[...] = sum(gz[i].astype(F32) for i in range(n_fsdp)).astype(BF)
    gc_copies, gc_waits = exchange(at, lambda p: gz_sum, gc, lambda r, i: r.at[i], (gc_send, gc_recv))
    gc[at.c] = gz_sum[...]
    for w in wc_waits:
        w.wait_recv()
    zw = LineGather(at, w_raw.at[:, at.f], lambda i: w_raw.at[:, i], (wz_send, wz_recv))
    zw.start()
    for w in gc_waits:
        w.wait_recv()
    gains[...] = sum(gc[i].astype(F32) for i in range(n_ctx))
    gain_one = gains[0:1, :]

    def norm_in(slot):
        def part(r, carry):
            start = pl.multiple_of(r * 48, 16)
            part_rows = x_all[slot, pl.ds(start, 48), :].astype(F32)
            scale = lax.rsqrt(jnp.mean(part_rows * part_rows, axis=-1, keepdims=True) + EPS)
            inside = pl.multiple_of(lax.rem(r, 2) * 48, 16)
            ni[2 * slot + lax.div(r, 2), pl.ds(inside, 48), :] = (part_rows * scale * gain_one).astype(BF)
            return carry

        lax.fori_loop(0, rows // 48, part, 0)

    norm_in(at.c)
    gx.wait_other("own")
    norm_in(at.s)
    gx.pass_a()
    gx.pass_b()
    zw.relay()
    zo.relay()
    ffn = [
        LineGather(at, own, lambda i, every=every: every.at[i], pair)
        for own, every, pair in (
            (wg, wg_all, (fg_send, fg_recv)), (wu, wu_all, (fu_send, fu_recv)), (wd, wd_all, (fd_send, fd_recv))
        )
    ]
    for part in ffn:
        part.start()
    go = PlaneGather(at, og, og_all, (og_send, og_recv))
    go.start()
    norm_in(at.a)
    norm_in(at.b)
    gx.wait_other("a")
    norm_in(at.b + at.other)
    gx.wait_other("b")
    norm_in(at.a + at.other)
    gx.pass_d()
    norm_in(at.d)
    gx.wait_other("d")
    norm_in(at.d + at.other)

    zw.finish()

    def widen(i, carry):
        part = w_raw[pl.ds(2 * i, 2)].reshape(2 * n_fsdp * own_rows, w_raw.shape[3])
        start = pl.multiple_of(i * 2 * n_fsdp * own_rows, 128)
        wqkv[pl.ds(start, 2 * n_fsdp * own_rows), :] = dot(part, expand[...]).astype(BF)
        return carry

    lax.fori_loop(0, n_ctx // 2, widen, 0)

    def project(g, carry):
        lhs = jnp.concatenate([ni[inv[4 * g + i]] for i in range(4)], axis=0)
        lin = dot(lhs, wqkv[...])
        span = pl.ds(pl.multiple_of(g * 4 * half, 128), 4 * half)
        cos_part, sin_part = cosine[span, :], sine[span, :]
        q[0, span, :] = turn(lin[:, 0:128], cos_part, sin_part).astype(BF)
        q[1, span, :] = turn(lin[:, 128:256], cos_part, sin_part).astype(BF)
        k_part = turn(lin[:, 256:384], cos_part, sin_part).astype(BF)
        v_part = lin[:, 384:512].astype(BF)
        k[span, :] = k_part
        v[span, :] = v_part
        kt[:, span] = jnp.transpose(k_part.astype(F32)).astype(BF)
        vt[:, span] = jnp.transpose(v_part.astype(F32)).astype(BF)
        return carry

    lax.fori_loop(0, seq_len // (4 * half), project, 0)
    go.pass_a()
    go.pass_b()

    block = 256
    score_scale = HEAD_DIM ** (-0.5) * LOG2E
    for i in range(seq_len // block):
        first = i * block

        def head_step(h, carry, first=first):
            span = slice(first, first + block)
            q_part = q[h, span, :]
            diag = dot(k[span, :], q_part, NT) * score_scale
            key_id = lax.broadcasted_iota(jnp.int32, (block, block), 0)
            query_id = lax.broadcasted_iota(jnp.int32, (block, block), 1)
            diag = jnp.where(key_id <= query_id, diag, NEG_FILL)
            top = jnp.max(diag, axis=0, keepdims=True)
            if first:
                past = dot(k[0:first, :], q_part, NT) * score_scale
                top = jnp.maximum(top, jnp.max(past, axis=0, keepdims=True))
            diag_p = jnp.exp2(diag - top)
            norm = jnp.sum(diag_p, axis=0, keepdims=True)
            acc = dot(vt[:, span], diag_p.astype(BF))
            if first:
                past_p = jnp.exp2(past - top)
                norm = norm + jnp.sum(past_p, axis=0, keepdims=True)
                acc = acc + dot(vt[:, 0:first], past_p.astype(BF))
            acc = acc / norm
            ot[h, :, span] = acc
            lse[h, :, span] = jnp.broadcast_to(top + jnp.log2(norm), (8, block))
            lanes = pl.ds(pl.multiple_of(h * HEAD_PAD, HEAD_PAD), HEAD_PAD)
            store_rows(ao, first, lanes, jnp.transpose(acc).astype(BF))
            return carry

        lax.fori_loop(0, 2, head_step, 0)
        if i == 3:
            go.pass_d()

    zo.finish()
    ffn[0].relay()
    raw = wo_raw[...].reshape(2 * HEAD_DIM, width)
    pad_rows = jnp.zeros((HEAD_PAD - HEAD_DIM, width), BF)
    wo[0:96, :] = raw[0:96]
    wo[96:128, :] = pad_rows
    wo[128:224, :] = raw[96:192]
    wo[224:256, :] = pad_rows

    def attn_rows(index):
        pair = pairs[index]
        return jnp.concatenate([ao[pair], ao[2 * n_ctx - 1 - pair]], axis=0)

    emit = product_emit(attn_rows, lambda lhs, columns: dot(lhs, wo[:, columns]))
    sc = PlaneScatter(at, emit, (rs_out, rs_in), (rs_send, rs_recv), 3)
    sc.first(total)
    sc.second()
    ffn[1].relay()
    go.wait_other("own")
    go.wait_other("a")
    go.wait_other("b")
    go.wait_other("d")
    more, most = sc.last()
    gain_two = gains[1:2, :]

    gn = PlaneGather(at, nm_own, nm_all, (nm_send, nm_recv))
    for p in range(gn.PIECES):
        span = slice(p * gn.rows, (p + 1) * gn.rows)
        mid = x[span, :].astype(F32) + total[span, :] + more[span, :].astype(F32) + most[span, :].astype(F32)
        scale = lax.rsqrt(jnp.mean(mid * mid, axis=-1, keepdims=True) + EPS)
        rm[span, :] = mid
        nm_own[span, :] = (mid * scale * gain_two).astype(BF)
        gn.start_piece(p)
    nm_local = pltpu.make_async_copy(nm_own, nm_all.at[at.c], local_sem.at[4])
    nm_local.start()
    local_copies.append(nm_local)
    ffn[2].relay()
    gn.pass_a()
    gn.pass_b()
    gn.pass_d()
    for which in ("own", "a", "b", "d"):
        gn.wait_other(which)
    for part in ffn:
        part.finish()
    for cp in local_copies:
        cp.wait()
    for part in (gx, go, gn, sc, zg, zo, zw, *ffn):
        part.finish_sends()
    for copies in (wc_copies, gc_copies):
        for cp in copies:
            cp.wait_send()


def middle_kernel(
    n_ctx, n_fsdp,
    nm_all, og_all, wg_all, wu_all, wd_all, rm, og, gains,
    d_gate, d_down, du, mlp, gm_all, g_mid, dgain,
    nm, ogv, wgu, wd, hidden, ggu, dg, dd, dg_in, dd_in, dg_stage, dd_stage, gm_own, total, rs_out, rs_in,
    rs_send, rs_recv, gm_send, gm_recv, zg_send, zg_recv, zd_send, zd_recv, load_sem, local_sem,
):
    at = Place(n_ctx, n_fsdp)
    rows, width = rm.shape
    part_cols = n_fsdp * 128
    loads = {}

    def load(name, i, src, dst):
        cp = pltpu.make_async_copy(src, dst, load_sem.at[i])
        cp.start()
        loads.setdefault(name, []).append(cp)

    for i in range(n_fsdp):
        load("gu", i, wg_all.at[i], wgu.at[:, pl.ds(i * 128, 128)])
        load("gu", n_fsdp + i, wu_all.at[i], wgu.at[:, pl.ds(part_cols + i * 128, 128)])
    load("nm", 2 * n_fsdp, nm_all, nm)
    load("wd", 2 * n_fsdp + 1, wd_all, wd)
    load("og", 2 * n_fsdp + 2, og_all, ogv)
    at.greet(False)
    for name in ("gu", "nm", "og", "wd"):
        for cp in loads[name]:
            cp.wait()

    def feed(i, carry):
        nm_part = nm[pl.ds(2 * i, 2)].reshape(2 * rows, width)
        og_part = ogv[pl.ds(2 * i, 2)].reshape(2 * rows, width)
        both = dot(nm_part, wgu[...])
        gate, up = both[:, :part_cols], both[:, part_cols:]
        g_hidden = dot(og_part, wd[...].reshape(part_cols, width), NT)
        sigma = 1.0 / (1.0 + jnp.exp(-gate))
        act = gate * sigma
        hidden[pl.ds(2 * i, 2)] = (act * up).astype(BF).reshape(2, rows, part_cols)
        ggu[pl.ds(2 * i, 2), :, 0:part_cols] = (
            (g_hidden * up * sigma * (1.0 + gate * (1.0 - sigma))).astype(BF).reshape(2, rows, part_cols)
        )
        ggu[pl.ds(2 * i, 2), :, part_cols:] = (g_hidden * act).astype(BF).reshape(2, rows, part_cols)
        return carry

    lax.fori_loop(0, n_ctx // 2, feed, 0)

    emit = product_emit(lambda index: ggu[index], lambda lhs, columns: dot(lhs, wgu[columns, :], NT))
    sc = PlaneScatter(at, emit, (rs_out, rs_in), (rs_send, rs_recv), 3)
    sc.first(total)

    def down_grad(t, carry):
        cols = pl.ds(pl.multiple_of(t * 256, 256), 256)
        value = dot(
            hidden[...].reshape(n_ctx * rows, part_cols), ogv[:, :, cols].reshape(n_ctx * rows, 256), TN
        ).astype(BF)
        dd[:, :, cols] = value.reshape(n_fsdp, 128, 256)
        return carry

    lax.fori_loop(0, width // 256, down_grad, 0)
    zd = LineScatter(at, lambda i: dd.at[i], dd_in, dd_stage, (zd_send, zd_recv))
    zd.start()
    sc.second()

    def gate_up_grad(t, carry):
        cols = pl.ds(pl.multiple_of(t * 256, 256), 256)
        value = dot(
            nm[:, :, cols].reshape(n_ctx * rows, 256), ggu[...].reshape(n_ctx * rows, 2 * part_cols), TN
        ).astype(BF)
        for i in range(n_fsdp):
            dg[i, cols, :] = value[:, i * 128 : (i + 1) * 128]
            du[i, cols, :] = value[:, part_cols + i * 128 : part_cols + (i + 1) * 128]
        return carry

    lax.fori_loop(0, width // 256, gate_up_grad, 0)
    zg = LineScatter(at, lambda i: dg.at[i], dg_in, dg_stage, (zg_send, zg_recv))
    zg.start()
    zd.relay()

    more, most = sc.last()
    gain_two = gains[1:2, :]

    gm = PlaneGather(at, gm_own, gm_all, (gm_send, gm_recv))
    gain_part = jnp.zeros((8, width), F32)
    for p in range(gm.PIECES):
        span = slice(p * gm.rows, (p + 1) * gm.rows)
        grad = total[span, :] + more[span, :].astype(F32) + most[span, :].astype(F32)
        mid = rm[span, :]
        scale = lax.rsqrt(jnp.mean(mid * mid, axis=-1, keepdims=True) + EPS)
        normed = mid * scale
        scaled = grad * gain_two
        back = og[span, :].astype(F32) + scale * (scaled - normed * jnp.mean(scaled * normed, axis=-1, keepdims=True))
        g_mid[span, :] = back
        gm_own[span, :] = back.astype(BF)
        gm.start_piece(p)
        gain_part = gain_part + jnp.sum((grad * normed).reshape(gm.rows // 8, 8, width), axis=0)
    dgain[...] = gain_part
    gm_local = pltpu.make_async_copy(gm_own, gm_all.at[at.c], local_sem)
    gm_local.start()

    def down(i, carry):
        part = hidden[pl.ds(2 * i, 2)].reshape(2 * rows, part_cols)
        mlp[pl.ds(2 * i, 2)] = dot(part, wd[...].reshape(part_cols, width)).astype(BF).reshape(2, rows, width)
        return carry

    lax.fori_loop(0, n_ctx // 2, down, 0)
    gm.pass_a()
    gm.pass_b()
    zg.relay()
    gm.pass_d()
    for which in ("own", "a", "b", "d"):
        gm.wait_other(which)
    gm_local.wait()
    zd.finish(d_down)
    zg.finish(d_gate)
    for part in (sc, gm, zd, zg):
        part.finish_sends()


def backward_kernel(
    n_ctx, n_fsdp,
    gm_all, ao, q, k, kt, v, ot, lse, wo, ni, wqkv, x, g_mid, gains, rm, mlp, dgain, du, inv, pairs, expand, cosine, sine,
    mixed, tgrad, dqkv, dwout, dgain_out, d_up,
    ga, gat, delta, dwo, dwo_out, dwo_in, dwo_stage, du_in, du_stage, dk, dv, gq, gqc, dw, dw_in, dw_stage, dw_sum, dw_own, mine, mixed_total, total,
    ms_out, ms_in, rs_out, rs_in, dgc, dgz, dg_sum,
    ms_send, ms_recv, rs_send, rs_recv, oz_send, oz_recv, gz_send, gz_recv, gc_send, gc_recv,
    wz_send, wz_recv, wc_send, wc_recv, zu_send, zu_recv, load_sem,
):
    at = Place(n_ctx, n_fsdp)
    rows, width = x.shape
    half = rows // 2
    seq_len = rows * n_ctx
    own_rows = dw.shape[2]
    loads = []
    for i, index in enumerate((at.d, at.a, at.c, at.b)):
        cp = pltpu.make_async_copy(mlp.at[index], mine.at[i], load_sem.at[i])
        cp.start()
        loads.append(cp)
    at.greet(True)

    ms = PlaneScatter(at, None, (ms_out, ms_in), (ms_send, ms_recv), 1)
    for i, index in enumerate(ms.others()):
        ms.copy(i, 0, mlp.at[index], at.s)
    zu = LineScatter(at, lambda i: du.at[i], du_in, du_stage, (zu_send, zu_recv))
    zu.start()
    gc_copies, gc_waits = exchange(at, lambda p: dgain, dgc, lambda r, i: r.at[i], (gc_send, gc_recv))
    dgc[at.c] = dgain[...]

    def add_blocks(index, dst, extras):
        i = index

        def part(r, carry):
            span = pl.ds(pl.multiple_of(r * 48, 16), 48)
            value = mine[i, span, :].astype(F32)
            for extra in extras:
                value = value + extra[span, :].astype(F32)
            dst[span, :] = value.astype(dst.dtype)
            return carry

        lax.fori_loop(0, rows // 48, part, 0)

    def attn_grad(g, carry):
        gm_part = jnp.concatenate([gm_all[inv[4 * g + i]] for i in range(4)], axis=0)
        span = pl.ds(pl.multiple_of(g * 4 * half, 128), 4 * half)
        low = dot(gm_part, wo[...], NT).astype(BF)
        for h in range(2):
            part = low[:, h * HEAD_PAD : (h + 1) * HEAD_PAD]
            ga[h, span, :] = part
            turned = jnp.transpose(part.astype(F32))
            gat[h, :, span] = turned.astype(BF)
            delta[h, :, span] = jnp.broadcast_to(
                jnp.sum(turned * ot[h, :, span], axis=0, keepdims=True), (8, 4 * half)
            )
        dwo[...] += dot(ao[pl.ds(4 * g, 4)].reshape(4 * half, 2 * HEAD_PAD), gm_part, TN)
        return carry

    dwo[...] = jnp.zeros_like(dwo)
    lax.fori_loop(0, seq_len // (4 * half), attn_grad, 0)
    low = jnp.concatenate([dwo[0:96, :], dwo[128:224, :]], axis=0).astype(BF)
    dwo_out[...] = low.reshape(dwo_out.shape)
    zo = LineScatter(at, lambda i: dwo_out.at[i], dwo_in, dwo_stage, (oz_send, oz_recv))
    zo.start()
    for cp in loads:
        cp.wait()
    ms.wait(0, 0)
    add_blocks(0, ms_out.at[0], [ms_in.at[0]])
    ms.copy(4, 0, ms_out.at[0], at.a)
    ms.wait(1, 0)
    add_blocks(1, ms_out.at[1], [ms_in.at[1]])
    ms.copy(5, 0, ms_out.at[1], at.a)
    ms.wait(2, 0)
    add_blocks(2, mixed_total, [ms_in.at[2]])

    for w in gc_waits:
        w.wait_recv()
    dg_sum[...] = sum(dgc[i] for i in range(n_ctx))
    zg = LineGather(at, dg_sum, lambda i: dgz.at[i], (gz_send, gz_recv))
    zg.start()
    dgz[at.f] = dg_sum[...]

    dk[...] = jnp.zeros_like(dk)
    dv[...] = jnp.zeros_like(dv)
    block = 256
    plain_scale = HEAD_DIM ** (-0.5)
    score_scale = plain_scale * LOG2E
    for i in range(seq_len // block):
        first = i * block

        def head_step(h, carry, first=first):
            span = slice(first, first + block)
            q_part, ga_part, gat_part = q[h, span, :], ga[h, span, :], gat[h, :, span]
            top = lse[h, 0:1, span]
            shift = delta[h, 0:1, span]

            def piece(keys, masked):
                scores = dot(k[keys, :], q_part, NT) * score_scale - top
                if masked:
                    key_id = lax.broadcasted_iota(jnp.int32, (block, block), 0)
                    query_id = lax.broadcasted_iota(jnp.int32, (block, block), 1)
                    scores = jnp.where(key_id <= query_id, scores, NEG_FILL)
                prob = jnp.exp2(scores)
                grad = (prob * (dot(v[keys, :], gat_part) - shift)).astype(BF)
                dv[keys, :] += dot(prob.astype(BF), ga_part)
                dk[keys, :] += dot(grad, q_part)
                return dot(kt[:, keys], grad)

            turned = piece(span, True)
            if first:
                turned = turned + piece(slice(0, first), False)
            lanes = pl.ds(pl.multiple_of(h * HEAD_PAD, HEAD_PAD), HEAD_PAD)
            grad_q = jnp.transpose(turned) * plain_scale
            store_rows(gq, first, lanes, turn(grad_q, cosine[span, :], -sine[span, :]).astype(BF))
            return carry

        lax.fori_loop(0, 2, head_step, 0)
        if i == 2:
            ms.wait(3, 0)
            ms.wait(4, 0)
            add_blocks(3, ms_out.at[2], [ms_in.at[3], ms_in.at[4]])
            ms.copy(6, 0, ms_out.at[2], at.b)
            zu.relay()
            zo.relay()
            zg.relay()

    def key_rows(g, carry):
        span = pl.ds(pl.multiple_of(g * 4 * half, 128), 4 * half)
        grad_k = turn(dk[span, :] * plain_scale, cosine[span, :], -sine[span, :]).astype(BF)
        gq[pl.ds(4 * g, 4), :, 256:384] = grad_k.reshape(4, half, HEAD_PAD)
        gq[pl.ds(4 * g, 4), :, 384:512] = dv[span, :].astype(BF).reshape(4, half, HEAD_PAD)
        return carry

    lax.fori_loop(0, seq_len // (4 * half), key_rows, 0)

    def to_ctx(slot, carry):
        pair = pairs[slot]
        gqc[2 * slot] = gq[pair]
        gqc[2 * slot + 1] = gq[2 * n_ctx - 1 - pair]
        return carry

    lax.fori_loop(0, n_ctx, to_ctx, 0)

    def weight_grad(t, carry):
        tile = 2 * n_fsdp * own_rows
        cols = pl.ds(pl.multiple_of(t * tile, 128), tile)
        value = dot(ni[:, :, cols].reshape(seq_len, tile), gqc[...].reshape(seq_len, 4 * HEAD_PAD), TN)
        low = dot(value.astype(BF), expand[...], NT).astype(BF)
        dw[pl.ds(2 * t, 2)] = low.reshape(2, n_fsdp, own_rows, low.shape[1])
        return carry

    lax.fori_loop(0, n_ctx // 2, weight_grad, 0)
    zw = LineScatter(at, lambda i: dw.at[:, i], dw_in, dw_stage, (wz_send, wz_recv))
    zw.start()

    emit = product_emit(
        lambda index: gqc[pl.ds(2 * index, 2)].reshape(rows, 4 * HEAD_PAD),
        lambda lhs, columns: dot(lhs, wqkv[columns, :], NT),
    )
    sc = PlaneScatter(at, emit, (rs_out, rs_in), (rs_send, rs_recv), 3)
    sc.first(total)

    mixed_more, mixed_most = ms.last()

    def mixed_rows(r, carry):
        span = pl.ds(pl.multiple_of(r * 48, 16), 48)
        value = rm[span, :] + mixed_total[span, :]
        value = value + mixed_more[span, :].astype(F32) + mixed_most[span, :].astype(F32)
        mixed[span, :] = value.astype(BF)
        return carry

    lax.fori_loop(0, rows // 48, mixed_rows, 0)
    zw.relay()
    zu.finish(d_up)
    zo.finish(dwout)
    zg.finish()
    dgain_out[...] = sum(dgz[i] for i in range(n_fsdp))
    sc.second()

    zw.finish(dw_sum)
    wc_copies, wc_waits = exchange(
        at, lambda p: dw_sum.at[p], dw_own, lambda r, i: r.at[i], (wc_send, wc_recv)
    )
    dw_own[at.c] = dw_sum[at.c]

    more, most = sc.last()
    gain_one = gains[0:1, :]

    def finish_rows(r, carry):
        span = pl.ds(pl.multiple_of(r * 48, 16), 48)
        grad = total[span, :] + more[span, :].astype(F32) + most[span, :].astype(F32)
        held = x[span, :].astype(F32)
        scale = lax.rsqrt(jnp.mean(held * held, axis=-1, keepdims=True) + EPS)
        normed = held * scale
        scaled = grad * gain_one
        back = g_mid[span, :] + scale * (scaled - normed * jnp.mean(scaled * normed, axis=-1, keepdims=True))
        tgrad[span, :] = back.astype(BF)
        return carry

    lax.fori_loop(0, rows // 48, finish_rows, 0)
    for w in wc_waits:
        w.wait_recv()
    dqkv[...] = dw_own[...]
    for part in (ms, sc, zu, zo, zg, zw):
        part.finish_sends()
    for copies in (gc_copies, wc_copies):
        for cp in copies:
            cp.wait_send()


def head_spread():
    spread = np.zeros((4 * HEAD_DIM, 4 * HEAD_PAD), np.float32)
    for head in range(4):
        for j in range(HEAD_DIM):
            lane = j if head == 3 or j < HEAD_DIM // 2 else j + HEAD_PAD // 2 - HEAD_DIM // 2
            spread[head * HEAD_DIM + j, head * HEAD_PAD + lane] = 1.0
    return spread


def turn_tables(seq_len):
    half_dim = HEAD_DIM // 2
    freqs = np.float32(THETA) ** (-(np.arange(half_dim, dtype=np.float32) * np.float32(2.0 / HEAD_DIM)))
    angle = np.arange(seq_len, dtype=np.float32)[:, None] * freqs[None, :].astype(np.float32)
    gap = np.zeros((seq_len, HEAD_PAD // 2 - half_dim), np.float32)
    cosine, sine = np.cos(angle).astype(np.float32), np.sin(angle).astype(np.float32)
    return (
        np.concatenate([cosine, gap, cosine, gap], axis=1),
        np.concatenate([-sine, gap, sine, gap], axis=1),
    )


def tail_kernel(
    n_ctx, n_fsdp,
    dqkv, wq, wk, wv, gain_rows, dgain, mixed_in, tgrad_in, dwout_in, dgate_in, dup_in, ddown_in,
    dq, dk, dv, gain_one, gain_two, mixed, tgrad, dwout, dgate, dup, ddown, sem,
):
    pairs = (
        (mixed_in, mixed), (tgrad_in, tgrad), (dwout_in, dwout), (dgate_in, dgate), (dup_in, dup), (ddown_in, ddown)
    )
    copies = [pltpu.make_async_copy(src, dst, sem.at[i]) for i, (src, dst) in enumerate(pairs)]
    for cp in copies:
        cp.start()
    own_rows = wq.shape[0]
    q_cols, kv_cols = wq.shape[1] // n_ctx, wk.shape[1] // n_ctx
    got = [dqkv[i].astype(F32) for i in range(n_ctx)]
    query = jnp.concatenate([g[:, :q_cols] for g in got], axis=1)
    key = jnp.concatenate([g[:, q_cols : q_cols + kv_cols] for g in got], axis=1)
    value = jnp.concatenate([g[:, q_cols + kv_cols :] for g in got], axis=1)
    dq[...] = query
    dk[...] = key
    dv[...] = value
    both = sum(
        jnp.sum(g * w[...].astype(F32), axis=1, keepdims=True) for g, w in ((query, wq), (key, wk), (value, wv))
    )
    row = jnp.transpose(jnp.broadcast_to(both, (own_rows, 128)))[0:1, :]
    gain_one[...] = row / gain_rows[0:1, :own_rows].astype(F32)
    place = (lax.axis_index("ctx") * n_fsdp + lax.axis_index("fsdp")) * own_rows
    width = dgain.shape[1]
    gain = jnp.broadcast_to(jnp.sum(dgain[...], axis=0, keepdims=True), (8, width))
    gain_two[...] = pltpu.roll(gain, width - place, 1)[0:1, :own_rows]
    for cp in copies:
        cp.wait()


def sems(*counts):
    return [pltpu.SemaphoreType.DMA((n,)) for n in counts for _ in range(2)]


VM = pl.BlockSpec(memory_space=pltpu.VMEM)
SM = pl.BlockSpec(memory_space=pltpu.SMEM)
HB = pl.BlockSpec(memory_space=pl.ANY)


def plane(tokens, out_grad, pair_table, attn_gain, w_query, w_key, w_value, w_out, mlp_gain, w_gate, w_up, w_down):
    n_ctx, n_fsdp = lax.axis_size("ctx"), lax.axis_size("fsdp")
    rows, width = tokens.shape
    half = rows // 2
    seq_len = rows * n_ctx
    own_rows = w_query.shape[0]
    pairs = pair_table[0]
    slots = jnp.stack([pairs, 2 * n_ctx - 1 - pairs], axis=1).reshape(-1)
    ids = jnp.arange(2 * n_ctx, dtype=jnp.int32)
    inv = jnp.sum(jnp.where(slots[None, :] == ids[:, None], ids[None, :], 0), axis=1).astype(jnp.int32)

    gain_rows = jnp.pad(jnp.stack([attn_gain, mlp_gain]), ((0, 14), (0, 128 - own_rows)))
    expand = jnp.asarray(head_spread(), BF)
    cosine, sine = (jnp.asarray(table) for table in turn_tables(seq_len))

    def sds(shape, dtype):
        return jax.ShapeDtypeStruct(shape, dtype)

    blocks = (n_ctx, rows, width)
    vm = pltpu.VMEM
    forward = pl.pallas_call(
        functools.partial(forward_kernel, n_ctx, n_fsdp),
        out_shape=(
            sds((2 * n_ctx, half, width), BF),
            sds(blocks, BF),
            sds(blocks, BF),
            sds((n_fsdp, *w_gate.shape), BF),
            sds((n_fsdp, *w_up.shape), BF),
            sds((n_fsdp, *w_down.shape), BF),
            sds((2, seq_len, HEAD_PAD), BF),
            sds((seq_len, HEAD_PAD), BF),
            sds((HEAD_PAD, seq_len), BF),
            sds((seq_len, HEAD_PAD), BF),
            sds((2, HEAD_PAD, seq_len), F32),
            sds((2 * n_ctx, half, 2 * HEAD_PAD), BF),
            sds((2, 8, seq_len), F32),
            sds((width, 4 * HEAD_PAD), BF),
            sds((2 * HEAD_PAD, width), BF),
            sds((16, width), F32),
            sds((rows, width), F32),
        ),
        in_specs=[VM, HB, VM, VM, VM, VM, HB, HB, HB, VM, SM, SM, VM, VM, VM],
        out_specs=(VM, HB, HB, HB, HB, HB) + (VM,) * 11,
        scratch_shapes=[
            vm(blocks, BF),
            vm((n_ctx, own_rows, 4 * HEAD_DIM), BF),
            vm((n_ctx, n_fsdp, own_rows, 4 * HEAD_DIM), BF),
            vm((n_fsdp, own_rows, width), BF),
            vm((16, width), BF),
            vm((n_fsdp, 16, width), BF),
            vm((16, width), BF),
            vm((n_ctx, 16, width), BF),
            vm((HEAD_PAD, seq_len), BF),
            vm((rows, width), BF),
            vm((rows, width), F32),
            vm((7, rows, width), BF),
            vm((7, rows, width), BF),
            *sems(21, 21, 21, 21, n_ctx, 3, 3, 3, n_ctx, 3, 3, 3),
            pltpu.SemaphoreType.DMA((5,)),
        ],
        compiler_params=pltpu.CompilerParams(
            collective_id=0, has_side_effects=True, vmem_limit_bytes=VMEM_LIMIT
        ),
        name="attention_forward",
    )
    ni, nm_all, og_all, wg_all, wu_all, wd_all, q, k, kt, v, ot, ao, lse, wqkv, wo, gains, rm = forward(
        tokens, out_grad, w_query, w_key, w_value, w_out, w_gate, w_up, w_down, gain_rows, inv, pairs, expand, cosine, sine
    )

    part_cols = n_fsdp * 128
    middle = pl.pallas_call(
        functools.partial(middle_kernel, n_ctx, n_fsdp),
        out_shape=(
            sds(w_gate.shape, F32),
            sds(w_down.shape, F32),
            sds((n_fsdp, *w_up.shape), BF),
            sds(blocks, BF),
            sds(blocks, BF),
            sds((rows, width), F32),
            sds((8, width), F32),
        ),
        in_specs=[HB, HB, HB, HB, HB, VM, VM, VM],
        out_specs=(VM, VM, VM, VM, HB, VM, VM),
        scratch_shapes=[
            vm(blocks, BF),
            vm(blocks, BF),
            vm((width, 2 * part_cols), BF),
            vm((n_fsdp, 128, width), BF),
            vm((n_ctx, rows, part_cols), BF),
            vm((n_ctx, rows, 2 * part_cols), BF),
            vm((n_fsdp, *w_gate.shape), BF),
            vm((n_fsdp, *w_down.shape), BF),
            vm((3, *w_gate.shape), BF),
            vm((3, *w_down.shape), BF),
            vm(w_gate.shape, BF),
            vm(w_down.shape, BF),
            vm((rows, width), BF),
            vm((rows, width), F32),
            vm((7, rows, width), BF),
            vm((7, rows, width), BF),
            *sems(21, 21, 3, 3),
            pltpu.SemaphoreType.DMA((2 * n_fsdp + 3,)),
            pltpu.SemaphoreType.DMA,
        ],
        compiler_params=pltpu.CompilerParams(
            collective_id=1, has_side_effects=True, vmem_limit_bytes=VMEM_LIMIT
        ),
        name="feed_forward",
    )
    d_gate, d_down, du, mlp, gm_all, g_mid, dgain = middle(
        nm_all, og_all, wg_all, wu_all, wd_all, rm, out_grad, gains
    )

    backward = pl.pallas_call(
        functools.partial(backward_kernel, n_ctx, n_fsdp),
        out_shape=(
            sds((rows, width), BF),
            sds((rows, width), BF),
            sds((n_ctx, own_rows, 4 * HEAD_DIM), BF),
            sds((own_rows, width), F32),
            sds((8, width), F32),
            sds(w_up.shape, F32),
        ),
        in_specs=[VM] * 15 + [HB, VM, VM, SM, SM, VM, VM, VM],
        out_specs=(VM,) * 6,
        scratch_shapes=[
            vm((2, seq_len, HEAD_PAD), BF),
            vm((2, HEAD_PAD, seq_len), BF),
            vm((2, 8, seq_len), F32),
            vm((2 * HEAD_PAD, width), F32),
            vm((n_fsdp, own_rows, width), BF),
            vm((3, own_rows, width), BF),
            vm((own_rows, width), BF),
            vm((3, *w_up.shape), BF),
            vm(w_up.shape, BF),
            vm((seq_len, HEAD_PAD), F32),
            vm((seq_len, HEAD_PAD), F32),
            vm((2 * n_ctx, half, 4 * HEAD_PAD), BF),
            vm((2 * n_ctx, half, 4 * HEAD_PAD), BF),
            vm((n_ctx, n_fsdp, own_rows, 4 * HEAD_DIM), BF),
            vm((3, n_ctx, own_rows, 4 * HEAD_DIM), BF),
            vm((n_ctx, own_rows, 4 * HEAD_DIM), BF),
            vm((n_ctx, own_rows, 4 * HEAD_DIM), BF),
            vm((n_ctx, own_rows, 4 * HEAD_DIM), BF),
            vm((4, rows, width), BF),
            vm((rows, width), F32),
            vm((rows, width), F32),
            vm((3, rows, width), BF),
            vm((7, rows, width), BF),
            vm((7, rows, width), BF),
            vm((7, rows, width), BF),
            vm((n_ctx, 8, width), F32),
            vm((n_fsdp, 8, width), F32),
            vm((8, width), F32),
            *sems(7, 21, 3, 3, n_ctx, 3, n_ctx, 3),
            pltpu.SemaphoreType.DMA((4,)),
        ],
        compiler_params=pltpu.CompilerParams(
            collective_id=2, has_side_effects=True, vmem_limit_bytes=VMEM_LIMIT
        ),
        name="attention_backward",
    )
    mixed, tokens_grad, dqkv, d_out, d_gain_two, d_up = backward(
        gm_all.reshape(2 * n_ctx, half, width), ao, q, k, kt, v, ot, lse, wo, ni, wqkv, tokens, g_mid, gains, rm, mlp,
        dgain, du, inv, pairs, expand, cosine, sine,
    )
    tail = pl.pallas_call(
        functools.partial(tail_kernel, n_ctx, n_fsdp),
        out_shape=(
            sds(w_query.shape, F32),
            sds(w_key.shape, F32),
            sds(w_value.shape, F32),
            sds((1, own_rows), F32),
            sds((1, own_rows), F32),
            sds((rows, width), BF),
            sds((rows, width), BF),
            sds(w_out.shape, F32),
            sds(w_gate.shape, F32),
            sds(w_up.shape, F32),
            sds(w_down.shape, F32),
        ),
        in_specs=[VM] * 12,
        out_specs=(VM,) * 5 + (HB,) * 6,
        scratch_shapes=[pltpu.SemaphoreType.DMA((6,))],
        compiler_params=pltpu.CompilerParams(vmem_limit_bytes=16 * 2**20),
        name="layouts",
    )
    d_query, d_key, d_value, gain_one_grad, gain_two_grad, mixed, tokens_grad, d_out, d_gate, d_up, d_down = tail(
        dqkv, w_query, w_key, w_value, gain_rows, d_gain_two, mixed, tokens_grad, d_out, d_gate, d_up, d_down
    )
    return (
        mixed, tokens_grad, gain_one_grad.reshape(-1), d_query, d_key, d_value, d_out, gain_two_grad.reshape(-1),
        d_gate, d_up, d_down,
    )


def solution(mesh):
    in_specs = (
        P(("ctx", "fsdp"), None),
        P(("ctx", "fsdp"), None),
        P("fsdp", None),
        P(("ctx", "fsdp")),
        P(("ctx", "fsdp"), None),
        P(("ctx", "fsdp"), None),
        P(("ctx", "fsdp"), None),
        P(("ctx", "fsdp"), None),
        P(("ctx", "fsdp")),
        P(None, ("ctx", "fsdp")),
        P(None, ("ctx", "fsdp")),
        P(("ctx", "fsdp"), None),
    )
    out_specs = (
        P(("ctx", "fsdp"), None),
        P(("ctx", "fsdp"), None),
        P(("ctx", "fsdp")),
        P(("ctx", "fsdp"), None),
        P(("ctx", "fsdp"), None),
        P(("ctx", "fsdp"), None),
        P(("ctx", "fsdp"), None),
        P(("ctx", "fsdp")),
        P(None, ("ctx", "fsdp")),
        P(None, ("ctx", "fsdp")),
        P(("ctx", "fsdp"), None),
    )
    fits = (
        mesh.shape["ctx"] == KV_HEADS
        and mesh.shape["fsdp"] == 4
        and HEADS == 2 * KV_HEADS
    )
    return jax.shard_map(plane if fits else local, mesh=mesh, in_specs=in_specs, out_specs=out_specs, check_vma=False)
```

```python
import functools
import math

import jax
import jax.numpy as jnp
import numpy as np
from jax import lax
from jax.experimental import pallas as pl
from jax.experimental.pallas import tpu as pltpu
from jax.sharding import PartitionSpec as P

HEADS = 16
KV_HEADS = 8
HEAD_DIM = 96


EPS = 1e-05
THETA = 100000.0
NEG_FILL = -1e30


def rotate(values_in, positions, direction):
    half_dim = values_in.shape[-1] // 2
    freqs = THETA ** (-(jnp.arange(half_dim, dtype=jnp.float32) * 2.0 / values_in.shape[-1]))
    angle = positions.astype(jnp.float32)[:, None] * freqs[None, :]
    cosine = jnp.cos(angle)[:, None, :]
    sine = direction * jnp.sin(angle)[:, None, :]
    first_half = values_in[..., :half_dim]
    second_half = values_in[..., half_dim:]
    return jnp.concatenate(
        [first_half * cosine - second_half * sine, second_half * cosine + first_half * sine],
        axis=-1,
    )


def place_rows(pair_index, tok_rows, block_count):
    half_rows = tok_rows // 2
    offsets = jnp.arange(tok_rows, dtype=jnp.int32)
    early = pair_index * half_rows + offsets
    late = (block_count - 1 - pair_index) * half_rows + offsets - half_rows
    return jnp.where(offsets < half_rows, early, late)


def rms_scale(values_in):
    return lax.rsqrt(jnp.mean(values_in * values_in, axis=-1, keepdims=True) + EPS)


def norm_back(grad_normed, normed, inv_rms, gain):
    scaled = grad_normed * gain
    return inv_rms * (scaled - normed * jnp.mean(scaled * normed, axis=-1, keepdims=True))


def local(
    tokens,
    out_grad,
    pair_table,
    attn_gain,
    w_query,
    w_key,
    w_value,
    w_out,
    mlp_gain,
    w_gate,
    w_up,
    w_down,
):
    tok_rows = tokens.shape[0]
    half_rows = tok_rows // 2
    ctx_count = lax.axis_size("ctx")
    half_count = 2 * ctx_count
    pair_row = pair_table[0]
    my_pos = place_rows(pair_row[lax.axis_index("ctx")], tok_rows, half_count)
    half_blocks = jnp.stack([pair_row, half_count - 1 - pair_row], axis=1).reshape(-1)
    block_ids = jnp.arange(half_count, dtype=jnp.int32)
    inverse = jnp.sum(
        jnp.where(half_blocks[None, :] == block_ids[:, None], block_ids[None, :], 0), axis=1
    )
    group_size = HEADS // KV_HEADS
    score_scale = HEAD_DIM ** (-0.5)
    query_width = HEADS * HEAD_DIM
    kv_width = KV_HEADS * HEAD_DIM
    w_query_all, w_key_all, w_value_all, w_out_all, gain_first, gain_second = (
        lax.all_gather(w_query, ("ctx", "fsdp"), axis=0, tiled=True),
        lax.all_gather(w_key, ("ctx", "fsdp"), axis=0, tiled=True),
        lax.all_gather(w_value, ("ctx", "fsdp"), axis=0, tiled=True),
        lax.all_gather(w_out, ("ctx", "fsdp"), axis=0, tiled=True),
        lax.all_gather(attn_gain, ("ctx", "fsdp"), axis=0, tiled=True),
        lax.all_gather(mlp_gain, ("ctx", "fsdp"), axis=0, tiled=True),
    )
    gain_one = gain_first.astype(jnp.float32)
    gain_two = gain_second.astype(jnp.float32)
    resid_in = tokens.astype(jnp.float32)
    inv_one = rms_scale(resid_in)
    normed_one = resid_in * inv_one
    normed_in = (normed_one * gain_one).astype(jnp.bfloat16)
    query_lin = jnp.dot(normed_in, w_query_all, preferred_element_type=jnp.float32)
    key_lin = jnp.dot(normed_in, w_key_all, preferred_element_type=jnp.float32)
    value_lin = jnp.dot(normed_in, w_value_all, preferred_element_type=jnp.float32)
    query_rot = rotate(query_lin.reshape(tok_rows, HEADS, HEAD_DIM), my_pos, 1.0).astype(
        jnp.bfloat16
    )
    key_rot = (
        rotate(key_lin.reshape(tok_rows, KV_HEADS, HEAD_DIM), my_pos, 1.0)
        .astype(jnp.bfloat16)
        .reshape(tok_rows, kv_width)
    )
    value_low = value_lin.astype(jnp.bfloat16)
    keys_got, values_got = (
        lax.all_gather(key_rot, "ctx", axis=0, tiled=True),
        lax.all_gather(value_low, "ctx", axis=0, tiled=True),
    )
    seq_len = keys_got.shape[0]
    keys_all = jnp.take(keys_got.reshape(half_count, half_rows, kv_width), inverse, axis=0).reshape(
        seq_len, kv_width
    )
    values_all = jnp.take(
        values_got.reshape(half_count, half_rows, kv_width), inverse, axis=0
    ).reshape(seq_len, kv_width)
    key_pos = jnp.arange(seq_len, dtype=jnp.int32)
    key_block = math.gcd(seq_len, 512)
    live_blocks = jnp.max(my_pos) // key_block + 1
    query_grp = query_rot.reshape(tok_rows, KV_HEADS, group_size, HEAD_DIM)

    def block_scores(block_index):
        first_row = block_index * key_block
        key_tile = lax.dynamic_slice_in_dim(keys_all, first_row, key_block, 0).reshape(
            key_block, KV_HEADS, HEAD_DIM
        )
        value_tile = lax.dynamic_slice_in_dim(values_all, first_row, key_block, 0).reshape(
            key_block, KV_HEADS, HEAD_DIM
        )
        scores = (
            jnp.einsum("tkgd,skd->kgts", query_grp, key_tile, preferred_element_type=jnp.float32)
            * score_scale
        )
        visible = (
            lax.dynamic_slice_in_dim(key_pos, first_row, key_block, 0)[None, :] <= my_pos[:, None]
        )
        return (scores, visible, key_tile, value_tile)

    def stats_step(block_index, carry):
        run_max, run_sum = carry
        scores, visible, key_tile, value_tile = block_scores(block_index)
        masked = jnp.where(visible, scores, NEG_FILL)
        new_max = jnp.maximum(run_max, jnp.max(masked, axis=-1))
        weights = jnp.where(visible, jnp.exp(masked - new_max[..., None]), 0.0)
        return (new_max, run_sum * jnp.exp(run_max - new_max) + jnp.sum(weights, axis=-1))

    start_max = jnp.full((KV_HEADS, group_size, tok_rows), NEG_FILL, jnp.float32)
    run_max, run_sum = lax.fori_loop(
        0, live_blocks, stats_step, (start_max, jnp.zeros_like(start_max))
    )
    log_total = run_max + jnp.log(run_sum)

    def probs(scores, visible):
        return jnp.where(visible, jnp.exp(scores - log_total[..., None]), 0.0)

    def output_step(block_index, accum):
        scores, visible, key_tile, value_tile = block_scores(block_index)
        prob_low = probs(scores, visible).astype(jnp.bfloat16)
        return accum + jnp.einsum(
            "kgts,skd->kgtd", prob_low, value_tile, preferred_element_type=jnp.float32
        )

    attn_acc = lax.fori_loop(
        0,
        live_blocks,
        output_step,
        jnp.zeros((KV_HEADS, group_size, tok_rows, HEAD_DIM), jnp.float32),
    )
    attn_low = attn_acc.transpose(2, 0, 1, 3).reshape(tok_rows, query_width).astype(jnp.bfloat16)
    resid_mid = resid_in + jnp.dot(attn_low, w_out_all, preferred_element_type=jnp.float32)
    inv_two = rms_scale(resid_mid)
    normed_two = resid_mid * inv_two
    normed_mid = (normed_two * gain_two).astype(jnp.bfloat16)
    w_gate_part, w_up_part, w_down_part = (
        lax.all_gather(w_gate, ("ctx", "fsdp"), axis=1, tiled=True),
        lax.all_gather(w_up, ("ctx", "fsdp"), axis=1, tiled=True),
        lax.all_gather(w_down, ("ctx", "fsdp"), axis=0, tiled=True),
    )
    gate_lin = jnp.dot(normed_mid, w_gate_part, preferred_element_type=jnp.float32)
    up_lin = jnp.dot(normed_mid, w_up_part, preferred_element_type=jnp.float32)
    sigma = jax.nn.sigmoid(gate_lin)
    activated = gate_lin * sigma
    hidden_low = (activated * up_lin).astype(jnp.bfloat16)
    mlp_branch = jnp.dot(hidden_low, w_down_part, preferred_element_type=jnp.float32)
    mixed = (resid_mid + mlp_branch).astype(jnp.bfloat16)
    grad_top = out_grad.astype(jnp.float32)
    d_down = jnp.einsum("tf,td->fd", hidden_low, out_grad, preferred_element_type=jnp.float32)
    grad_hidden = jnp.einsum("td,fd->tf", out_grad, w_down_part, preferred_element_type=jnp.float32)
    grad_gate = (grad_hidden * up_lin * sigma * (1.0 + gate_lin * (1.0 - sigma))).astype(
        jnp.bfloat16
    )
    grad_up = (grad_hidden * activated).astype(jnp.bfloat16)
    d_gate = jnp.einsum("td,tf->df", normed_mid, grad_gate, preferred_element_type=jnp.float32)
    d_up = jnp.einsum("td,tf->df", normed_mid, grad_up, preferred_element_type=jnp.float32)
    grad_normed_mid = jnp.einsum(
        "tf,df->td", grad_gate, w_gate_part, preferred_element_type=jnp.float32
    ) + jnp.einsum("tf,df->td", grad_up, w_up_part, preferred_element_type=jnp.float32)
    gate_grad_out, up_grad_out, down_grad_out = (
        lax.psum_scatter(d_gate, ("ctx", "fsdp"), scatter_dimension=1, tiled=True),
        lax.psum_scatter(d_up, ("ctx", "fsdp"), scatter_dimension=1, tiled=True),
        lax.psum_scatter(d_down, ("ctx", "fsdp"), scatter_dimension=0, tiled=True),
    )
    d_gain_two = jnp.sum(grad_normed_mid * normed_two, axis=0)
    grad_mid = grad_top + norm_back(grad_normed_mid, normed_two, inv_two, gain_two)
    grad_mid_low = grad_mid.astype(jnp.bfloat16)
    d_out = jnp.einsum("tq,td->qd", attn_low, grad_mid_low, preferred_element_type=jnp.float32)
    grad_attn_low = jnp.einsum(
        "td,qd->tq", grad_mid_low, w_out_all, preferred_element_type=jnp.float32
    ).astype(jnp.bfloat16)
    grad_heads = grad_attn_low.reshape(tok_rows, KV_HEADS, group_size, HEAD_DIM).transpose(
        1, 2, 0, 3
    )
    row_delta = jnp.sum(grad_heads.astype(jnp.float32) * attn_acc, axis=-1)

    def back_step(block_index, carry):
        grad_query, grad_keys, grad_values = carry
        scores, visible, key_tile, value_tile = block_scores(block_index)
        prob_full = probs(scores, visible)
        prob_low = prob_full.astype(jnp.bfloat16)
        grad_prob = jnp.einsum(
            "kgtd,skd->kgts", grad_heads, value_tile, preferred_element_type=jnp.float32
        )
        grad_score = (prob_full * (grad_prob - row_delta[..., None])).astype(jnp.bfloat16)
        grad_query = grad_query + score_scale * jnp.einsum(
            "kgts,skd->kgtd", grad_score, key_tile, preferred_element_type=jnp.float32
        )
        key_part = score_scale * jnp.einsum(
            "kgts,tkgd->skd", grad_score, query_grp, preferred_element_type=jnp.float32
        )
        value_part = jnp.einsum(
            "kgts,kgtd->skd", prob_low, grad_heads, preferred_element_type=jnp.float32
        )
        first_row = block_index * key_block
        grad_keys = lax.dynamic_update_slice_in_dim(
            grad_keys, key_part.reshape(key_block, kv_width), first_row, 0
        )
        grad_values = lax.dynamic_update_slice_in_dim(
            grad_values, value_part.reshape(key_block, kv_width), first_row, 0
        )
        return (grad_query, grad_keys, grad_values)

    empty_keys = jnp.zeros((seq_len, kv_width), jnp.float32)
    grad_query, grad_keys, grad_values = lax.fori_loop(
        0,
        live_blocks,
        back_step,
        (
            jnp.zeros((KV_HEADS, group_size, tok_rows, HEAD_DIM), jnp.float32),
            empty_keys,
            empty_keys,
        ),
    )
    keys_back = jnp.take(
        grad_keys.reshape(half_count, half_rows, kv_width), half_blocks, axis=0
    ).reshape(seq_len, kv_width)
    values_back = jnp.take(
        grad_values.reshape(half_count, half_rows, kv_width), half_blocks, axis=0
    ).reshape(seq_len, kv_width)
    own_keys, own_values = (
        lax.psum_scatter(
            keys_back.astype(jnp.bfloat16), "ctx", scatter_dimension=0, tiled=True
        ).astype(jnp.float32),
        lax.psum_scatter(
            values_back.astype(jnp.bfloat16), "ctx", scatter_dimension=0, tiled=True
        ).astype(jnp.float32),
    )
    grad_query_lin = rotate(
        grad_query.transpose(2, 0, 1, 3).reshape(tok_rows, HEADS, HEAD_DIM), my_pos, -1.0
    )
    grad_query_low = grad_query_lin.reshape(tok_rows, query_width).astype(jnp.bfloat16)
    grad_key_lin = rotate(own_keys.reshape(tok_rows, KV_HEADS, HEAD_DIM), my_pos, -1.0)
    grad_key_low = grad_key_lin.reshape(tok_rows, kv_width).astype(jnp.bfloat16)
    grad_value_low = own_values.astype(jnp.bfloat16)
    d_query = jnp.einsum("td,tq->dq", normed_in, grad_query_low, preferred_element_type=jnp.float32)
    d_key = jnp.einsum("td,tq->dq", normed_in, grad_key_low, preferred_element_type=jnp.float32)
    d_value = jnp.einsum("td,tq->dq", normed_in, grad_value_low, preferred_element_type=jnp.float32)
    grad_normed_in = (
        jnp.einsum("tq,dq->td", grad_query_low, w_query_all, preferred_element_type=jnp.float32)
        + jnp.einsum("tq,dq->td", grad_key_low, w_key_all, preferred_element_type=jnp.float32)
        + jnp.einsum("tq,dq->td", grad_value_low, w_value_all, preferred_element_type=jnp.float32)
    )
    d_gain_one = jnp.sum(grad_normed_in * normed_one, axis=0)
    grad_input = grad_mid + norm_back(grad_normed_in, normed_one, inv_one, gain_one)
    query_grad_out, key_grad_out, value_grad_out, out_grad_out, gain_one_out, gain_two_out = (
        lax.psum_scatter(d_query, ("ctx", "fsdp"), scatter_dimension=0, tiled=True),
        lax.psum_scatter(d_key, ("ctx", "fsdp"), scatter_dimension=0, tiled=True),
        lax.psum_scatter(d_value, ("ctx", "fsdp"), scatter_dimension=0, tiled=True),
        lax.psum_scatter(d_out, ("ctx", "fsdp"), scatter_dimension=0, tiled=True),
        lax.psum_scatter(d_gain_one, ("ctx", "fsdp"), scatter_dimension=0, tiled=True),
        lax.psum_scatter(d_gain_two, ("ctx", "fsdp"), scatter_dimension=0, tiled=True),
    )
    return (
        mixed,
        grad_input.astype(jnp.bfloat16),
        gain_one_out,
        query_grad_out,
        key_grad_out,
        value_grad_out,
        out_grad_out,
        gain_two_out,
        gate_grad_out,
        up_grad_out,
        down_grad_out,
    )


BF = jnp.bfloat16
F32 = jnp.float32
MESH = pl.DeviceIdType.MESH
HEAD_PAD = 128
LOG2E = 1.4426950408889634
VMEM_LIMIT = 58 * 2**20
FRONT_VMEM_LIMIT = 61 * 2**20
NT = (((1,), (1,)), ((), ()))
TN = (((0,), (0,)), ((), ()))


def dot(a, b, dims=(((1,), (0,)), ((), ()))):
    return lax.dot_general(a, b, dims, preferred_element_type=F32)


class Place:
    def __init__(self, n_ctx, n_fsdp):
        self.n_ctx, self.n_fsdp = n_ctx, n_fsdp
        self.c, self.f = lax.axis_index("ctx"), lax.axis_index("fsdp")
        core = lax.rem(self.c, 2)
        step_x = 2 - 4 * lax.rem(lax.div(self.c, 2), 2)
        step_y = 4 - 8 * lax.div(self.c, 4)
        self.other = 1 - 2 * core
        self.s = self.c + self.other
        self.a = self.c + step_x * (1 - core) + step_y * core
        self.b = self.c + step_x * core + step_y * (1 - core)
        self.d = self.c + step_x + step_y
        self.f1 = self.f + 1 - 2 * lax.rem(self.f, 2)
        self.f2 = self.f + 2 - 4 * lax.div(self.f, 2)
        self.f3 = n_fsdp - 1 - self.f

    def ctx_peer(self, j):
        return lax.rem(self.c + j, self.n_ctx)

    def ctx_source(self, j):
        return lax.rem(self.c + self.n_ctx - j, self.n_ctx)

    def greet(self, everyone):
        barrier = pltpu.get_barrier_semaphore()
        if everyone:
            mates = [(self.ctx_peer(j), self.f) for j in range(1, self.n_ctx)]
        else:
            mates = [(self.s, self.f), (self.a, self.f), (self.b, self.f)]
        mates += [(self.c, self.f1), (self.c, self.f2)]
        for mate in mates:
            pl.semaphore_signal(barrier, inc=1, device_id=mate, device_id_type=MESH)
        self.mates = len(mates)

    def wait_greeted(self):
        pl.semaphore_wait(pltpu.get_barrier_semaphore(), self.mates)


def remote(src, dst, send, recv, device):
    return pltpu.make_async_remote_copy(
        src_ref=src, dst_ref=dst, send_sem=send, recv_sem=recv, device_id=device, device_id_type=MESH
    )


class LocalCopies:
    def __init__(self, sems):
        self.sems, self.count, self.named = sems, 0, {}

    def start(self, name, src, dst):
        cp = pltpu.make_async_copy(src, dst, self.sems.at[self.count])
        cp.start()
        self.count += 1
        self.named.setdefault(name, []).append(cp)

    def wait(self, *names):
        for name in names:
            for cp in self.named.pop(name):
                cp.wait()

    def wait_all(self):
        self.wait(*list(self.named))


class PlaneGather:
    PIECES = 3
    COUNT = 7 * PIECES

    def __init__(self, at, own, blocks, sems):
        self.at, self.own, self.blocks = at, own, blocks
        self.send, self.recv = sems
        self.rows = own.shape[0] // self.PIECES
        self.started = []

    def piece(self, slot, p):
        return self.blocks.at[slot, pl.ds(p * self.rows, self.rows)]

    def copy(self, i, p, src, slot, mate):
        k = i * self.PIECES + p
        cp = remote(src, self.piece(slot, p), self.send.at[k], self.recv.at[k], (mate, self.at.f))
        cp.start()
        self.started.append(cp)

    def wait(self, i, p, slot):
        k = i * self.PIECES + p
        block = self.piece(slot, p)
        remote(block, block, self.send.at[k], self.recv.at[k], (self.at.s, self.at.f)).wait_recv()

    def start_piece(self, p):
        at = self.at
        src = self.own.at[pl.ds(p * self.rows, self.rows)]
        self.copy(1, p, src, at.c, at.a)
        self.copy(2, p, src, at.c, at.b)
        self.copy(0, p, src, at.c, at.s)

    def start(self):
        for p in range(self.PIECES):
            self.start_piece(p)

    def pass_a(self):
        at = self.at
        for p in range(self.PIECES):
            self.wait(1, p, at.a)
            self.copy(4, p, self.piece(at.a, p), at.a, at.b)
            self.copy(3, p, self.piece(at.a, p), at.a, at.s)

    def pass_b(self):
        at = self.at
        for p in range(self.PIECES):
            self.wait(2, p, at.b)
            self.copy(5, p, self.piece(at.b, p), at.b, at.s)

    def pass_d(self):
        at = self.at
        for p in range(self.PIECES):
            self.wait(4, p, at.d)
            self.copy(6, p, self.piece(at.d, p), at.d, at.s)

    def wait_other(self, which):
        at = self.at
        i, slot = {
            "own": (0, at.s),
            "a": (3, at.b + at.other),
            "b": (5, at.a + at.other),
            "d": (6, at.d + at.other),
        }[which]
        for p in range(self.PIECES):
            self.wait(i, p, slot)

    def finish_sends(self):
        for cp in self.started:
            cp.wait_send()


class PlaneScatter:
    def __init__(self, at, emit, bufs, sems, pieces):
        self.at, self.emit, self.pieces = at, emit, pieces
        self.out, self.landed = bufs
        self.send, self.recv = sems
        self.started = []

    def columns(self, t):
        width = self.landed.shape[2] // self.pieces
        return slice(t * width, (t + 1) * width)

    def copy(self, i, t, src, mate):
        k = i * self.pieces + t
        dst = self.landed.at[i, :, self.columns(t)]
        cp = remote(src, dst, self.send.at[k], self.recv.at[k], (mate, self.at.f))
        cp.start()
        self.started.append(cp)

    def wait(self, i, t):
        k = i * self.pieces + t
        block = self.landed.at[i, :, self.columns(t)]
        remote(block, block, self.send.at[k], self.recv.at[k], (self.at.s, self.at.f)).wait_recv()

    def others(self):
        at = self.at
        return (at.d + at.other, at.b + at.other, at.s, at.a + at.other)

    def to_other(self, i):
        for t in range(self.pieces):
            columns = self.columns(t)
            self.emit(self.others()[i], columns, self.out.at[i], [])
            self.copy(i, t, self.out.at[i, :, columns], self.at.s)

    def onward(self, i, index, extras, mate):
        for t in range(self.pieces):
            columns = self.columns(t)
            for extra in extras:
                self.wait(extra, t)
            self.emit(index, columns, self.out.at[i], [self.landed.at[extra] for extra in extras])
            self.copy(i, t, self.out.at[i, :, columns], mate)

    def first(self, total):
        at = self.at
        self.to_other(0)
        self.to_other(1)
        self.onward(4, at.d, [0], at.a)
        self.onward(5, at.a, [1], at.a)
        self.to_other(3)
        self.to_other(2)
        for t in range(self.pieces):
            self.wait(2, t)
            self.emit(at.c, self.columns(t), total, [self.landed.at[2]])

    def second(self):
        self.onward(6, self.at.b, [3, 4], self.at.b)

    def last(self):
        for i in (5, 6):
            for t in range(self.pieces):
                self.wait(i, t)
        return self.landed.at[5], self.landed.at[6]

    def finish_sends(self):
        for cp in self.started:
            cp.wait_send()


class LineGather:
    COUNT = 3

    def __init__(self, at, own, slot, sems):
        self.at, self.own, self.slot = at, own, slot
        self.send, self.recv = sems
        self.started = []

    def copy(self, i, src, slot, mate):
        cp = remote(src, self.slot(slot), self.send.at[i], self.recv.at[i], (self.at.c, mate))
        cp.start()
        self.started.append(cp)

    def wait(self, i, slot):
        block = self.slot(slot)
        remote(block, block, self.send.at[i], self.recv.at[i], (self.at.c, self.at.f1)).wait_recv()

    def start(self):
        at = self.at
        self.copy(1, self.own, at.f, at.f2)
        self.copy(0, self.own, at.f, at.f1)

    def relay(self):
        at = self.at
        self.wait(1, at.f2)
        self.copy(2, self.slot(at.f2), at.f2, at.f1)

    def finish(self):
        self.wait(0, self.at.f1)
        self.wait(2, self.at.f3)

    def finish_sends(self):
        for cp in self.started:
            cp.wait_send()


class LineScatter:
    COUNT = 3

    def __init__(self, at, part, landed, sems):
        self.at, self.part, self.landed = at, part, landed
        self.send, self.recv = sems
        self.started = []

    def copy(self, i, src, mate):
        cp = remote(src, self.landed.at[i], self.send.at[i], self.recv.at[i], (self.at.c, mate))
        cp.start()
        self.started.append(cp)

    def wait(self, i):
        block = self.landed.at[i]
        remote(block, block, self.send.at[i], self.recv.at[i], (self.at.c, self.at.f1)).wait_recv()

    def start(self):
        at = self.at
        self.copy(0, self.part(at.f3), at.f1)
        self.copy(1, self.part(at.f1), at.f1)

    def add(self, dst, refs):
        count = dst.shape[0]
        step = min(count, 128) if len(dst.shape) == 2 else 1

        def piece(i, carry):
            rows = pl.ds(pl.multiple_of(i * step, step), step) if len(dst.shape) == 2 else pl.ds(i, 1)
            value = refs[0][rows].astype(F32)
            for ref in refs[1:]:
                value = value + ref[rows].astype(F32)
            dst[rows] = value.astype(dst.dtype)
            return carry

        lax.fori_loop(0, count // step, piece, 0)

    def relay(self):
        at = self.at
        self.wait(0)
        self.add(self.part(at.f2), [self.part(at.f2), self.landed.at[0]])
        self.copy(2, self.part(at.f2), at.f2)

    def finish(self, dst):
        self.wait(1)
        self.wait(2)
        self.add(dst, [self.part(self.at.f), self.landed.at[1], self.landed.at[2]])

    def finish_sends(self):
        for cp in self.started:
            cp.wait_send()


def exchange(at, src_of, dst, slot_of, sems):
    send, recv = sems
    started, waits = [], []
    for j in range(1, at.n_ctx):
        peer, source = at.ctx_peer(j), at.ctx_source(j)
        device = (peer, at.f)
        cp = remote(src_of(peer), slot_of(dst, at.c), send.at[j], recv.at[j], device)
        cp.start()
        started.append(cp)
        block = slot_of(dst, source)
        waits.append(remote(block, block, send.at[j], recv.at[j], device))
    return started, waits


def turn(values_in, cosine, sine):
    return values_in * cosine + pltpu.roll(values_in, HEAD_PAD // 2, 1) * sine


def store_rows(ref, first, lanes, value):
    block_rows, done = ref.shape[1], 0
    while done < value.shape[0]:
        block, start = divmod(first + done, block_rows)
        count = min(block_rows - start, value.shape[0] - done)
        ref[block, start : start + count, lanes] = value[done : done + count]
        done += count


def product_emit(lhs_of, rhs_of):
    def emit(index, columns, dst, extras):
        value = rhs_of(lhs_of(index), columns)
        for extra in extras:
            value = value + extra[:, columns].astype(F32)
        dst[:, columns] = value.astype(dst.dtype)

    return emit


def front_kernel(
    n_ctx, n_fsdp,
    x, og, wq, wk, wv, wout, wg, wu, wd_own, gain_rows, inv, pairs, expand, cosine, sine,
    d_gate, d_down, dgain,
    ni_out, heads_out, kt_out, ot_out, ao_out, lse_out, wqkv_out, wo_out, gains_out, rm_out, du_out, mlp_out, gm_all, g_mid_out,
    ni, heads, kt, vt, ot, ao, lse, wqkv, wo, gains, rm, x_all, wblk, w_raw, wo_raw, gt, gz, gz_sum, gc, nm_own, total,
    rs_out, rs_in, nm, ogv, wgu, wd, dd, du, dg_in, dd_in,
    x_send, x_recv, og_send, og_recv, rs_send, rs_recv,
    wc_send, wc_recv, wz_send, wz_recv, oz_send, oz_recv, gz_send, gz_recv, gc_send, gc_recv,
    fg_send, fg_recv, fu_send, fu_recv, fd_send, fd_recv, zg_send, zg_recv, zd_send, zd_recv, local_sem,
):
    at = Place(n_ctx, n_fsdp)
    rows, width = x.shape
    half = rows // 2
    seq_len = rows * n_ctx
    own_rows = w_raw.shape[2]
    at.greet(True)
    local = LocalCopies(local_sem)
    part_cols = n_fsdp * 128

    def gate_slot(i):
        return wgu.at[:, pl.ds(pl.multiple_of(i * 128, 128), 128)]

    def up_slot(i):
        return wgu.at[:, pl.ds(pl.multiple_of(part_cols + i * 128, 128), 128)]

    for src, dst in ((og, ogv.at[at.c]), (wg, gate_slot(at.f)), (wu, up_slot(at.f)), (wd_own, wd.at[at.f])):
        local.start("own", src, dst)
    q_cols, kv_cols = wq.shape[1] // n_ctx, wk.shape[1] // n_ctx
    for i in range(n_ctx):
        parts = (wq[:, i * q_cols : (i + 1) * q_cols], *(w[:, i * kv_cols : (i + 1) * kv_cols] for w in (wk, wv)))
        wblk[i] = jnp.concatenate(parts, axis=1)
    place = (at.c * n_fsdp + at.f) * own_rows
    from_lane = lax.broadcasted_iota(jnp.int32, (128, width), 0)
    to_lane = lax.broadcasted_iota(jnp.int32, (128, width), 1)
    spread = jnp.where((to_lane == from_lane + place) & (from_lane < own_rows), 1.0, 0.0).astype(BF)
    gt[...] = dot(gain_rows[...], spread).astype(BF)
    at.wait_greeted()

    wc_copies, wc_waits = exchange(
        at, lambda p: wblk.at[p], w_raw, lambda r, i: r.at[i, at.f], (wc_send, wc_recv)
    )
    zt = LineGather(at, gt, lambda i: gz.at[i], (gz_send, gz_recv))
    zt.start()
    gx = PlaneGather(at, x, x_all, (x_send, x_recv))
    gx.start()
    zo = LineGather(at, wout, lambda i: wo_raw.at[i], (oz_send, oz_recv))
    zo.start()
    w_raw[at.c, at.f] = wblk[at.c]
    wo_raw[at.f] = wout[...]
    gz[at.f] = gt[...]
    x_all[at.c] = x[...]
    zt.relay()
    zt.finish()
    gz_sum[...] = sum(gz[i].astype(F32) for i in range(n_fsdp)).astype(BF)
    gc_copies, gc_waits = exchange(at, lambda p: gz_sum, gc, lambda r, i: r.at[i], (gc_send, gc_recv))
    gc[at.c] = gz_sum[...]
    for w in wc_waits:
        w.wait_recv()
    zw = LineGather(at, w_raw.at[:, at.f], lambda i: w_raw.at[:, i], (wz_send, wz_recv))
    zw.start()
    for w in gc_waits:
        w.wait_recv()
    gains[...] = sum(gc[i].astype(F32) for i in range(n_ctx))
    gain_one = gains[0:1, :]

    def norm_in(slot):
        def part(r, carry):
            start = pl.multiple_of(r * 48, 16)
            part_rows = x_all[slot, pl.ds(start, 48), :].astype(F32)
            scale = lax.rsqrt(jnp.mean(part_rows * part_rows, axis=-1, keepdims=True) + EPS)
            inside = pl.multiple_of(lax.rem(r, 2) * 48, 16)
            ni[2 * slot + lax.div(r, 2), pl.ds(inside, 48), :] = (part_rows * scale * gain_one).astype(BF)
            return carry

        lax.fori_loop(0, rows // 48, part, 0)

    norm_in(at.c)
    gx.wait_other("own")
    norm_in(at.s)
    gx.pass_a()
    gx.pass_b()
    zw.relay()
    zo.relay()
    ffn = [
        LineGather(at, wg, gate_slot, (fg_send, fg_recv)),
        LineGather(at, wu, up_slot, (fu_send, fu_recv)),
        LineGather(at, wd_own, lambda i: wd.at[i], (fd_send, fd_recv)),
    ]
    for part in ffn:
        part.start()
    go = PlaneGather(at, og, ogv, (og_send, og_recv))
    go.start()
    norm_in(at.a)
    norm_in(at.b)
    gx.wait_other("a")
    norm_in(at.b + at.other)
    gx.wait_other("b")
    norm_in(at.a + at.other)
    gx.pass_d()
    norm_in(at.d)
    gx.wait_other("d")
    norm_in(at.d + at.other)

    local.start("ni", ni, ni_out)
    local.start("out", gains, gains_out)
    zw.finish()

    def widen(i, carry):
        part = w_raw[pl.ds(2 * i, 2)].reshape(2 * n_fsdp * own_rows, w_raw.shape[3])
        start = pl.multiple_of(i * 2 * n_fsdp * own_rows, 128)
        wqkv[pl.ds(start, 2 * n_fsdp * own_rows), :] = dot(part, expand[...]).astype(BF)
        return carry

    lax.fori_loop(0, n_ctx // 2, widen, 0)

    def project(g, carry):
        lhs = jnp.concatenate([ni[inv[4 * g + i]] for i in range(4)], axis=0)
        lin = dot(lhs, wqkv[...])
        span = pl.ds(pl.multiple_of(g * 4 * half, 128), 4 * half)
        cos_part, sin_part = cosine[span, :], sine[span, :]
        heads[0, span, :] = turn(lin[:, 0:128], cos_part, sin_part).astype(BF)
        heads[1, span, :] = turn(lin[:, 128:256], cos_part, sin_part).astype(BF)
        k_part = turn(lin[:, 256:384], cos_part, sin_part).astype(BF)
        v_part = lin[:, 384:512].astype(BF)
        heads[2, span, :] = k_part
        heads[3, span, :] = v_part
        kt[:, span] = jnp.transpose(k_part.astype(F32)).astype(BF)
        vt[:, span] = jnp.transpose(v_part.astype(F32)).astype(BF)
        return carry

    lax.fori_loop(0, seq_len // (4 * half), project, 0)
    local.start("heads", heads, heads_out)
    for src, dst in ((kt, kt_out), (wqkv, wqkv_out)):
        local.start("out", src, dst)

    block = 256
    score_scale = HEAD_DIM ** (-0.5) * LOG2E
    for i in range(seq_len // block):
        first = i * block

        def head_step(h, carry, first=first):
            span = slice(first, first + block)
            q_part = heads[h, span, :]
            diag = dot(heads[2, span, :], q_part, NT) * score_scale
            key_id = lax.broadcasted_iota(jnp.int32, (block, block), 0)
            query_id = lax.broadcasted_iota(jnp.int32, (block, block), 1)
            diag = jnp.where(key_id <= query_id, diag, NEG_FILL)
            top = jnp.max(diag, axis=0, keepdims=True)
            if first:
                past = dot(heads[2, 0:first, :], q_part, NT) * score_scale
                top = jnp.maximum(top, jnp.max(past, axis=0, keepdims=True))
            diag_p = jnp.exp2(diag - top)
            norm = jnp.sum(diag_p, axis=0, keepdims=True)
            acc = dot(vt[:, span], diag_p.astype(BF))
            if first:
                past_p = jnp.exp2(past - top)
                norm = norm + jnp.sum(past_p, axis=0, keepdims=True)
                acc = acc + dot(vt[:, 0:first], past_p.astype(BF))
            acc = acc / norm
            ot[h, :, span] = acc
            lse[h, :, span] = jnp.broadcast_to(top + jnp.log2(norm), (8, block))
            lanes = pl.ds(pl.multiple_of(h * HEAD_PAD, HEAD_PAD), HEAD_PAD)
            store_rows(ao, first, lanes, jnp.transpose(acc).astype(BF))
            return carry

        lax.fori_loop(0, 2, head_step, 0)
        if i == 4:
            go.pass_a()
            go.pass_b()

    for src, dst in ((ot, ot_out), (ao, ao_out), (lse, lse_out)):
        local.start("out", src, dst)
    zo.finish()
    ffn[0].relay()
    raw = wo_raw[...].reshape(2 * HEAD_DIM, width)
    pad_rows = jnp.zeros((HEAD_PAD - HEAD_DIM, width), BF)
    wo[0:96, :] = raw[0:96]
    wo[96:128, :] = pad_rows
    wo[128:224, :] = raw[96:192]
    wo[224:256, :] = pad_rows
    local.start("out", wo, wo_out)

    def attn_rows(index):
        pair = pairs[index]
        return jnp.concatenate([ao[pair], ao[2 * n_ctx - 1 - pair]], axis=0)

    emit = product_emit(attn_rows, lambda lhs, columns: dot(lhs, wo[:, columns]))
    sc = PlaneScatter(at, emit, (rs_out, rs_in), (rs_send, rs_recv), 3)
    sc.first(total)
    go.pass_d()
    sc.second()
    ffn[1].relay()
    go.wait_other("own")
    go.wait_other("a")
    go.wait_other("b")
    go.wait_other("d")
    more, most = sc.last()
    gain_two = gains[1:2, :]

    gx.finish_sends()
    gn = PlaneGather(at, nm_own, nm, (x_send, x_recv))
    for p in range(gn.PIECES):
        span = slice(p * gn.rows, (p + 1) * gn.rows)
        mid = x[span, :].astype(F32) + total[span, :] + more[span, :].astype(F32) + most[span, :].astype(F32)
        scale = lax.rsqrt(jnp.mean(mid * mid, axis=-1, keepdims=True) + EPS)
        rm[span, :] = mid
        normed_mid = (mid * scale * gain_two).astype(BF)
        nm_own[span, :] = normed_mid
        gn.start_piece(p)
        nm[at.c, span, :] = normed_mid
    local.start("rm", rm, rm_out)
    ffn[2].relay()
    gn.pass_a()
    gn.pass_b()
    sc.finish_sends()
    local.wait("own")
    for part in ffn:
        part.finish()
    gn.pass_d()

    def feed(mate):
        i = lax.div(mate, 2)
        nm_part = nm[pl.ds(2 * i, 2)].reshape(2 * rows, width)
        og_part = ogv[pl.ds(2 * i, 2)].reshape(2 * rows, width)
        both = dot(nm_part, wgu[...])
        gate, up = both[:, :part_cols], both[:, part_cols:]
        g_hidden = dot(og_part, wd[...].reshape(part_cols, width), NT)
        sigma = 1.0 / (1.0 + jnp.exp(-gate))
        act = gate * sigma
        g_gate = g_hidden * up * sigma * (1.0 + gate * (1.0 - sigma))
        for start, value in ((0, act * up), (part_cols, g_gate), (2 * part_cols, g_hidden * act)):
            x_all[pl.ds(2 * i, 2), :, start : start + part_cols] = value.astype(BF).reshape(2, rows, part_cols)

    gn.wait_other("own")
    feed(at.c)
    gn.wait_other("b")
    feed(at.a)
    gn.wait_other("a")
    feed(at.b)
    gn.wait_other("d")
    feed(at.d)
    local.wait("heads", "ni")
    dg = heads

    for i in range(part_cols // 256):
        value = dot(
            x_all[:, :, i * 256 : (i + 1) * 256].reshape(n_ctx * rows, 256), ogv[...].reshape(n_ctx * rows, width), TN
        )
        dd[2 * i : 2 * i + 2] = value.astype(BF).reshape(2, 128, width)
    zd = LineScatter(at, lambda i: dd.at[i], dd_in, (zd_send, zd_recv))
    zd.start()
    emit = product_emit(lambda index: x_all[index, :, part_cols:], lambda lhs, columns: dot(lhs, wgu[columns, :], NT))
    sc = PlaneScatter(at, emit, (rs_out, rs_in), (rs_send, rs_recv), 3)
    sc.first(total)

    def gate_up_grad(t, carry):
        cols = pl.ds(pl.multiple_of(t * 256, 256), 256)
        value = dot(
            nm[:, :, cols].reshape(n_ctx * rows, 256), x_all[:, :, part_cols:].reshape(n_ctx * rows, 2 * part_cols), TN
        ).astype(BF)
        for i in range(n_fsdp):
            dg[i, cols, :] = value[:, i * 128 : (i + 1) * 128]
            du[i, cols, :] = value[:, part_cols + i * 128 : part_cols + (i + 1) * 128]
        return carry

    lax.fori_loop(0, width // 256, gate_up_grad, 0)
    zg = LineScatter(at, lambda i: dg.at[i], dg_in, (zg_send, zg_recv))
    zg.start()
    local.start("out", du, du_out)
    sc.second()
    zd.relay()

    more, most = sc.last()
    local.wait("rm")
    gn.finish_sends()
    g_mid, gm_own = rm, nm_own
    gm = PlaneGather(at, gm_own, gm_all, (x_send, x_recv))
    gain_part = jnp.zeros((8, width), F32)
    for p in range(gm.PIECES):
        span = slice(p * gm.rows, (p + 1) * gm.rows)
        grad = total[span, :] + more[span, :].astype(F32) + most[span, :].astype(F32)
        mid = rm[span, :]
        scale = lax.rsqrt(jnp.mean(mid * mid, axis=-1, keepdims=True) + EPS)
        normed = mid * scale
        scaled = grad * gain_two
        back = og[span, :].astype(F32) + scale * (scaled - normed * jnp.mean(scaled * normed, axis=-1, keepdims=True))
        g_mid[span, :] = back
        gm_own[span, :] = back.astype(BF)
        gm.start_piece(p)
        gain_part = gain_part + jnp.sum((grad * normed).reshape(gm.rows // 8, 8, width), axis=0)
    dgain[...] = gain_part
    local.start("out", gm_own, gm_all.at[at.c])
    local.start("out", g_mid, g_mid_out)

    def down(i, carry):
        part = x_all[pl.ds(2 * i, 2), :, 0:part_cols].reshape(2 * rows, part_cols)
        ni[pl.ds(4 * i, 4)] = dot(part, wd[...].reshape(part_cols, width)).astype(BF).reshape(4, half, width)
        return carry

    lax.fori_loop(0, n_ctx // 2, down, 0)
    local.start("out", ni, mlp_out)
    gm.pass_a()
    zg.relay()
    gm.pass_b()
    gm.pass_d()
    for which in ("own", "a", "b", "d"):
        gm.wait_other(which)
    local.wait_all()
    zd.finish(d_down)
    zg.finish(d_gate)
    for part in (go, zt, zo, zw, *ffn, sc, gm, zd, zg):
        part.finish_sends()
    for copies in (wc_copies, gc_copies):
        for cp in copies:
            cp.wait_send()


def backward_kernel(
    n_ctx, n_fsdp,
    gm_in, ao_in, heads_in, kt_in, ot_in, lse_in, wo_in, ni_in, wqkv_in, x_in, g_mid_in, gains_in, rm_in, mlp,
    dgain, du_in_all, inv, pairs, expand_in, cosine_in, sine_in,
    mixed, tgrad, dqkv, dwout, dgain_out, d_up,
    gm_all, ao, heads, kt, ot, lse, wo, ni, wqkv, x, g_mid, gains, rm, du, expand, cosine, sine,
    ga, gat, delta, dwo, dwo_out, dwo_in, du_in, dk, dv, gq, gqc, dw, dw_in, dw_sum, dw_own, mine, mixed_total, total,
    ms_out, ms_in, rs_out, rs_in, dgc, dgz, dg_sum,
    ms_send, ms_recv, rs_send, rs_recv, oz_send, oz_recv, gz_send, gz_recv, gc_send, gc_recv,
    wz_send, wz_recv, wc_send, wc_recv, zu_send, zu_recv, local_sem,
):
    at = Place(n_ctx, n_fsdp)
    rows, width = x.shape
    half = rows // 2
    seq_len = rows * n_ctx
    own_rows = dw.shape[2]
    at.greet(True)
    local = LocalCopies(local_sem)
    for name, src, dst in (
        ("grad", gm_in, gm_all), ("grad", wo_in, wo), ("grad", ao_in, ao), ("grad", ot_in, ot),
        ("attn", heads_in, heads), ("attn", kt_in, kt), ("attn", lse_in, lse),
        ("attn", cosine_in, cosine), ("attn", sine_in, sine),
        ("mlp", mlp.at[at.d], mine.at[0]), ("mlp", mlp.at[at.a], mine.at[1]),
        ("mlp", mlp.at[at.c], mine.at[2]), ("mlp", mlp.at[at.b], mine.at[3]),
        ("weight", ni_in, ni), ("weight", expand_in, expand), ("weight", wqkv_in, wqkv),
        ("up", du_in_all, du), ("last", x_in, x), ("last", g_mid_in, g_mid), ("last", gains_in, gains), ("last", rm_in, rm),
    ):
        local.start(name, src, dst)
    at.wait_greeted()

    ms = PlaneScatter(at, None, (ms_out, ms_in), (ms_send, ms_recv), 1)
    for i, index in enumerate(ms.others()):
        ms.copy(i, 0, mlp.at[index], at.s)
    zu = LineScatter(at, lambda i: du_in_all.at[i], du_in, (zu_send, zu_recv))
    zu.start()
    zu.part = lambda i: du.at[i]
    gc_copies, gc_waits = exchange(at, lambda p: dgain, dgc, lambda r, i: r.at[i], (gc_send, gc_recv))
    dgc[at.c] = dgain[...]

    def add_blocks(index, dst, extras):
        i = index

        def part(r, carry):
            span = pl.ds(pl.multiple_of(r * 48, 16), 48)
            value = mine[i, span, :].astype(F32)
            for extra in extras:
                value = value + extra[span, :].astype(F32)
            dst[span, :] = value.astype(dst.dtype)
            return carry

        lax.fori_loop(0, rows // 48, part, 0)

    def attn_grad(g, carry):
        gm_part = jnp.concatenate([gm_all[inv[4 * g + i]] for i in range(4)], axis=0)
        span = pl.ds(pl.multiple_of(g * 4 * half, 128), 4 * half)
        low = dot(gm_part, wo[...], NT).astype(BF)
        for h in range(2):
            part = low[:, h * HEAD_PAD : (h + 1) * HEAD_PAD]
            ga[h, span, :] = part
            turned = jnp.transpose(part.astype(F32))
            gat[h, :, span] = turned.astype(BF)
            delta[h, :, span] = jnp.broadcast_to(
                jnp.sum(turned * ot[h, :, span], axis=0, keepdims=True), (8, 4 * half)
            )
        dwo[...] += dot(ao[pl.ds(4 * g, 4)].reshape(4 * half, 2 * HEAD_PAD), gm_part, TN)
        return carry

    dwo[...] = jnp.zeros_like(dwo)
    local.wait("grad")
    lax.fori_loop(0, seq_len // (4 * half), attn_grad, 0)
    low = jnp.concatenate([dwo[0:96, :], dwo[128:224, :]], axis=0).astype(BF)
    dwo_out[...] = low.reshape(dwo_out.shape)
    zo = LineScatter(at, lambda i: dwo_out.at[i], dwo_in, (oz_send, oz_recv))
    zo.start()
    local.wait("mlp")
    ms.wait(0, 0)
    add_blocks(0, ms_out.at[0], [ms_in.at[0]])
    ms.copy(4, 0, ms_out.at[0], at.a)
    ms.wait(1, 0)
    add_blocks(1, ms_out.at[1], [ms_in.at[1]])
    ms.copy(5, 0, ms_out.at[1], at.a)
    ms.wait(2, 0)
    add_blocks(2, mixed_total, [ms_in.at[2]])

    for w in gc_waits:
        w.wait_recv()
    dg_sum[...] = sum(dgc[i] for i in range(n_ctx))
    zg = LineGather(at, dg_sum, lambda i: dgz.at[i], (gz_send, gz_recv))
    zg.start()
    dgz[at.f] = dg_sum[...]

    local.wait("attn")
    dk[...] = jnp.zeros_like(dk)
    dv[...] = jnp.zeros_like(dv)
    block = 256
    plain_scale = HEAD_DIM ** (-0.5)
    score_scale = plain_scale * LOG2E
    for i in range(seq_len // block):
        first = i * block

        def head_step(h, carry, first=first):
            span = slice(first, first + block)
            q_part, ga_part, gat_part = heads[h, span, :], ga[h, span, :], gat[h, :, span]
            top = lse[h, 0:1, span]
            shift = delta[h, 0:1, span]

            def piece(keys, masked):
                scores = dot(heads[2, keys, :], q_part, NT) * score_scale - top
                if masked:
                    key_id = lax.broadcasted_iota(jnp.int32, (block, block), 0)
                    query_id = lax.broadcasted_iota(jnp.int32, (block, block), 1)
                    scores = jnp.where(key_id <= query_id, scores, NEG_FILL)
                prob = jnp.exp2(scores)
                grad = (prob * (dot(heads[3, keys, :], gat_part) - shift)).astype(BF)
                dv[keys, :] += dot(prob.astype(BF), ga_part)
                dk[keys, :] += dot(grad, q_part)
                return dot(kt[:, keys], grad)

            turned = piece(span, True)
            if first:
                turned = turned + piece(slice(0, first), False)
            lanes = pl.ds(pl.multiple_of(h * HEAD_PAD, HEAD_PAD), HEAD_PAD)
            grad_q = jnp.transpose(turned) * plain_scale
            store_rows(gq, first, lanes, turn(grad_q, cosine[span, :], -sine[span, :]).astype(BF))
            return carry

        lax.fori_loop(0, 2, head_step, 0)
        if i == 2:
            ms.wait(3, 0)
            ms.wait(4, 0)
            add_blocks(3, ms_out.at[2], [ms_in.at[3], ms_in.at[4]])
            ms.copy(6, 0, ms_out.at[2], at.b)

    def key_rows(g, carry):
        span = pl.ds(pl.multiple_of(g * 4 * half, 128), 4 * half)
        grad_k = turn(dk[span, :] * plain_scale, cosine[span, :], -sine[span, :]).astype(BF)
        gq[pl.ds(4 * g, 4), :, 256:384] = grad_k.reshape(4, half, HEAD_PAD)
        gq[pl.ds(4 * g, 4), :, 384:512] = dv[span, :].astype(BF).reshape(4, half, HEAD_PAD)
        return carry

    lax.fori_loop(0, seq_len // (4 * half), key_rows, 0)

    def to_ctx(slot, carry):
        pair = pairs[slot]
        gqc[2 * slot] = gq[pair]
        gqc[2 * slot + 1] = gq[2 * n_ctx - 1 - pair]
        return carry

    lax.fori_loop(0, n_ctx, to_ctx, 0)
    local.wait("weight", "up", "last")

    def weight_grad(t, carry):
        tile = 2 * n_fsdp * own_rows
        cols = pl.ds(pl.multiple_of(t * tile, 128), tile)
        value = dot(ni[:, :, cols].reshape(seq_len, tile), gqc[...].reshape(seq_len, 4 * HEAD_PAD), TN)
        low = dot(value.astype(BF), expand[...], NT).astype(BF)
        dw[pl.ds(2 * t, 2)] = low.reshape(2, n_fsdp, own_rows, low.shape[1])
        return carry

    lax.fori_loop(0, n_ctx // 2, weight_grad, 0)
    zw = LineScatter(at, lambda i: dw.at[:, i], dw_in, (wz_send, wz_recv))
    zw.start()

    emit = product_emit(
        lambda index: gqc[pl.ds(2 * index, 2)].reshape(rows, 4 * HEAD_PAD),
        lambda lhs, columns: dot(lhs, wqkv[columns, :], NT),
    )
    sc = PlaneScatter(at, emit, (rs_out, rs_in), (rs_send, rs_recv), 3)
    sc.first(total)

    zw.relay()
    zu.relay()
    zo.relay()
    zg.relay()
    sc.second()
    zw.finish(dw_sum)
    wc_copies, wc_waits = exchange(
        at, lambda p: dw_sum.at[p], dw_own, lambda r, i: r.at[i], (wc_send, wc_recv)
    )
    dw_own[at.c] = dw_sum[at.c]
    mixed_more, mixed_most = ms.last()

    def mixed_rows(r, carry):
        span = pl.ds(pl.multiple_of(r * 48, 16), 48)
        value = rm[span, :] + mixed_total[span, :]
        value = value + mixed_more[span, :].astype(F32) + mixed_most[span, :].astype(F32)
        mixed[span, :] = value.astype(BF)
        return carry

    lax.fori_loop(0, rows // 48, mixed_rows, 0)
    zg.finish()
    dgain_out[...] = sum(dgz[i] for i in range(n_fsdp))

    more, most = sc.last()
    gain_one = gains[0:1, :]

    def finish_rows(r, carry):
        span = pl.ds(pl.multiple_of(r * 48, 16), 48)
        grad = total[span, :] + more[span, :].astype(F32) + most[span, :].astype(F32)
        held = x[span, :].astype(F32)
        scale = lax.rsqrt(jnp.mean(held * held, axis=-1, keepdims=True) + EPS)
        normed = held * scale
        scaled = grad * gain_one
        back = g_mid[span, :] + scale * (scaled - normed * jnp.mean(scaled * normed, axis=-1, keepdims=True))
        tgrad[span, :] = back.astype(BF)
        return carry

    lax.fori_loop(0, rows // 48, finish_rows, 0)
    zu.finish(d_up)
    zo.finish(dwout)
    for w in wc_waits:
        w.wait_recv()
    dqkv[...] = dw_own[...]
    for part in (ms, sc, zu, zo, zg, zw):
        part.finish_sends()
    for copies in (gc_copies, wc_copies):
        for cp in copies:
            cp.wait_send()


def head_spread():
    spread = np.zeros((4 * HEAD_DIM, 4 * HEAD_PAD), np.float32)
    for head in range(4):
        for j in range(HEAD_DIM):
            lane = j if head == 3 or j < HEAD_DIM // 2 else j + HEAD_PAD // 2 - HEAD_DIM // 2
            spread[head * HEAD_DIM + j, head * HEAD_PAD + lane] = 1.0
    return spread


def turn_tables(seq_len):
    half_dim = HEAD_DIM // 2
    freqs = np.float32(THETA) ** (-(np.arange(half_dim, dtype=np.float32) * np.float32(2.0 / HEAD_DIM)))
    angle = np.arange(seq_len, dtype=np.float32)[:, None] * freqs[None, :].astype(np.float32)
    gap = np.zeros((seq_len, HEAD_PAD // 2 - half_dim), np.float32)
    cosine, sine = np.cos(angle).astype(np.float32), np.sin(angle).astype(np.float32)
    return (
        np.concatenate([cosine, gap, cosine, gap], axis=1),
        np.concatenate([-sine, gap, sine, gap], axis=1),
    )


def tail_kernel(
    n_ctx, n_fsdp,
    dqkv, wq, wk, wv, gain_rows, dgain, mixed_in, tgrad_in, dwout_in, dgate_in, dup_in, ddown_in,
    dq, dk, dv, gain_one, gain_two, mixed, tgrad, dwout, dgate, dup, ddown, sem,
):
    pairs = (
        (mixed_in, mixed), (tgrad_in, tgrad), (dwout_in, dwout), (dgate_in, dgate), (dup_in, dup), (ddown_in, ddown)
    )
    copies = [pltpu.make_async_copy(src, dst, sem.at[i]) for i, (src, dst) in enumerate(pairs)]
    for cp in copies:
        cp.start()
    own_rows = wq.shape[0]
    q_cols, kv_cols = wq.shape[1] // n_ctx, wk.shape[1] // n_ctx
    got = [dqkv[i].astype(F32) for i in range(n_ctx)]
    query = jnp.concatenate([g[:, :q_cols] for g in got], axis=1)
    key = jnp.concatenate([g[:, q_cols : q_cols + kv_cols] for g in got], axis=1)
    value = jnp.concatenate([g[:, q_cols + kv_cols :] for g in got], axis=1)
    dq[...] = query
    dk[...] = key
    dv[...] = value
    both = sum(
        jnp.sum(g * w[...].astype(F32), axis=1, keepdims=True) for g, w in ((query, wq), (key, wk), (value, wv))
    )
    row = jnp.transpose(jnp.broadcast_to(both, (own_rows, 128)))[0:1, :]
    gain_one[...] = row / gain_rows[0:1, :own_rows].astype(F32)
    place = (lax.axis_index("ctx") * n_fsdp + lax.axis_index("fsdp")) * own_rows
    width = dgain.shape[1]
    gain = jnp.broadcast_to(jnp.sum(dgain[...], axis=0, keepdims=True), (8, width))
    gain_two[...] = pltpu.roll(gain, width - place, 1)[0:1, :own_rows]
    for cp in copies:
        cp.wait()


def sems(*counts):
    return [pltpu.SemaphoreType.DMA((n,)) for n in counts for _ in range(2)]


VM = pl.BlockSpec(memory_space=pltpu.VMEM)
SM = pl.BlockSpec(memory_space=pltpu.SMEM)
HB = pl.BlockSpec(memory_space=pl.ANY)


def plane(tokens, out_grad, pair_table, attn_gain, w_query, w_key, w_value, w_out, mlp_gain, w_gate, w_up, w_down):
    n_ctx, n_fsdp = lax.axis_size("ctx"), lax.axis_size("fsdp")
    rows, width = tokens.shape
    half = rows // 2
    seq_len = rows * n_ctx
    own_rows = w_query.shape[0]
    pairs = pair_table[0]
    slots = jnp.stack([pairs, 2 * n_ctx - 1 - pairs], axis=1).reshape(-1)
    ids = jnp.arange(2 * n_ctx, dtype=jnp.int32)
    inv = jnp.sum(jnp.where(slots[None, :] == ids[:, None], ids[None, :], 0), axis=1).astype(jnp.int32)

    gain_rows = jnp.pad(jnp.stack([attn_gain, mlp_gain]), ((0, 14), (0, 128 - own_rows)))
    expand = jnp.asarray(head_spread(), BF)
    cosine, sine = (jnp.asarray(table) for table in turn_tables(seq_len))

    def sds(shape, dtype):
        return jax.ShapeDtypeStruct(shape, dtype)

    blocks = (n_ctx, rows, width)
    vm = pltpu.VMEM
    part_cols = n_fsdp * 128
    front = pl.pallas_call(
        functools.partial(front_kernel, n_ctx, n_fsdp),
        out_shape=(
            sds(w_gate.shape, F32),
            sds(w_down.shape, F32),
            sds((8, width), F32),
            sds((2 * n_ctx, half, width), BF),
            sds((4, seq_len, HEAD_PAD), BF),
            sds((HEAD_PAD, seq_len), BF),
            sds((2, HEAD_PAD, seq_len), F32),
            sds((2 * n_ctx, half, 2 * HEAD_PAD), BF),
            sds((2, 8, seq_len), F32),
            sds((width, 4 * HEAD_PAD), BF),
            sds((2 * HEAD_PAD, width), BF),
            sds((16, width), F32),
            sds((rows, width), F32),
            sds((n_fsdp, *w_up.shape), BF),
            sds((2 * n_ctx, half, width), BF),
            sds(blocks, BF),
            sds((rows, width), F32),
        ),
        in_specs=[VM] * 6 + [HB] * 3 + [VM, SM, SM, VM, VM, VM],
        out_specs=(VM,) * 3 + (HB,) * 14,
        scratch_shapes=[
            vm((2 * n_ctx, half, width), BF),
            vm((4, seq_len, HEAD_PAD), BF),
            vm((HEAD_PAD, seq_len), BF),
            vm((HEAD_PAD, seq_len), BF),
            vm((2, HEAD_PAD, seq_len), F32),
            vm((2 * n_ctx, half, 2 * HEAD_PAD), BF),
            vm((2, 8, seq_len), F32),
            vm((width, 4 * HEAD_PAD), BF),
            vm((2 * HEAD_PAD, width), BF),
            vm((16, width), F32),
            vm((rows, width), F32),
            vm(blocks, BF),
            vm((n_ctx, own_rows, 4 * HEAD_DIM), BF),
            vm((n_ctx, n_fsdp, own_rows, 4 * HEAD_DIM), BF),
            vm((n_fsdp, own_rows, width), BF),
            vm((16, width), BF),
            vm((n_fsdp, 16, width), BF),
            vm((16, width), BF),
            vm((n_ctx, 16, width), BF),
            vm((rows, width), BF),
            vm((rows, width), F32),
            vm((7, rows, width), BF),
            vm((7, rows, width), BF),
            vm(blocks, BF),
            vm(blocks, BF),
            vm((width, 2 * part_cols), BF),
            vm((n_fsdp, *w_down.shape), BF),
            vm((n_fsdp, *w_down.shape), BF),
            vm((n_fsdp, *w_up.shape), BF),
            vm((3, *w_gate.shape), BF),
            vm((3, *w_down.shape), BF),
            *sems(21, 21, 21, n_ctx, 3, 3, 3, n_ctx, 3, 3, 3, 3, 3),
            pltpu.SemaphoreType.DMA((18,)),
        ],
        compiler_params=pltpu.CompilerParams(
            collective_id=0, has_side_effects=True, vmem_limit_bytes=FRONT_VMEM_LIMIT
        ),
        name="forward_and_feed_forward",
    )
    d_gate, d_down, dgain, ni, heads, kt, ot, ao, lse, wqkv, wo, gains, rm, du, mlp, gm_all, g_mid = front(
        tokens, out_grad, w_query, w_key, w_value, w_out, w_gate, w_up, w_down, gain_rows, inv, pairs, expand, cosine, sine
    )

    backward = pl.pallas_call(
        functools.partial(backward_kernel, n_ctx, n_fsdp),
        out_shape=(
            sds((rows, width), BF),
            sds((rows, width), BF),
            sds((n_ctx, own_rows, 4 * HEAD_DIM), BF),
            sds((own_rows, width), F32),
            sds((8, width), F32),
            sds(w_up.shape, F32),
        ),
        in_specs=[HB] * 14 + [VM, HB, SM, SM, HB, HB, HB],
        out_specs=(VM,) * 6,
        scratch_shapes=[
            vm((2 * n_ctx, half, width), BF),
            vm((2 * n_ctx, half, 2 * HEAD_PAD), BF),
            vm((4, seq_len, HEAD_PAD), BF),
            vm((HEAD_PAD, seq_len), BF),
            vm((2, HEAD_PAD, seq_len), F32),
            vm((2, 8, seq_len), F32),
            vm((2 * HEAD_PAD, width), BF),
            vm((2 * n_ctx, half, width), BF),
            vm((width, 4 * HEAD_PAD), BF),
            vm((rows, width), BF),
            vm((rows, width), F32),
            vm((16, width), F32),
            vm((rows, width), F32),
            vm((n_fsdp, *w_up.shape), BF),
            vm((4 * HEAD_DIM, 4 * HEAD_PAD), BF),
            vm((seq_len, HEAD_PAD), F32),
            vm((seq_len, HEAD_PAD), F32),
            vm((2, seq_len, HEAD_PAD), BF),
            vm((2, HEAD_PAD, seq_len), BF),
            vm((2, 8, seq_len), F32),
            vm((2 * HEAD_PAD, width), F32),
            vm((n_fsdp, own_rows, width), BF),
            vm((3, own_rows, width), BF),
            vm((3, *w_up.shape), BF),
            vm((seq_len, HEAD_PAD), F32),
            vm((seq_len, HEAD_PAD), F32),
            vm((2 * n_ctx, half, 4 * HEAD_PAD), BF),
            vm((2 * n_ctx, half, 4 * HEAD_PAD), BF),
            vm((n_ctx, n_fsdp, own_rows, 4 * HEAD_DIM), BF),
            vm((3, n_ctx, own_rows, 4 * HEAD_DIM), BF),
            vm((n_ctx, own_rows, 4 * HEAD_DIM), BF),
            vm((n_ctx, own_rows, 4 * HEAD_DIM), BF),
            vm((4, rows, width), BF),
            vm((rows, width), F32),
            vm((rows, width), F32),
            vm((3, rows, width), BF),
            vm((7, rows, width), BF),
            vm((7, rows, width), BF),
            vm((7, rows, width), BF),
            vm((n_ctx, 8, width), F32),
            vm((n_fsdp, 8, width), F32),
            vm((8, width), F32),
            *sems(7, 21, 3, 3, n_ctx, 3, n_ctx, 3),
            pltpu.SemaphoreType.DMA((21,)),
        ],
        compiler_params=pltpu.CompilerParams(
            collective_id=1, has_side_effects=True, vmem_limit_bytes=VMEM_LIMIT
        ),
        name="attention_backward",
    )
    mixed, tokens_grad, dqkv, d_out, d_gain_two, d_up = backward(
        gm_all.reshape(2 * n_ctx, half, width), ao, heads, kt, ot, lse, wo, ni, wqkv, tokens, g_mid, gains, rm,
        mlp.reshape(blocks), dgain, du, inv, pairs, expand, cosine, sine,
    )
    tail = pl.pallas_call(
        functools.partial(tail_kernel, n_ctx, n_fsdp),
        out_shape=(
            sds(w_query.shape, F32),
            sds(w_key.shape, F32),
            sds(w_value.shape, F32),
            sds((1, own_rows), F32),
            sds((1, own_rows), F32),
            sds((rows, width), BF),
            sds((rows, width), BF),
            sds(w_out.shape, F32),
            sds(w_gate.shape, F32),
            sds(w_up.shape, F32),
            sds(w_down.shape, F32),
        ),
        in_specs=[VM] * 12,
        out_specs=(VM,) * 5 + (HB,) * 6,
        scratch_shapes=[pltpu.SemaphoreType.DMA((6,))],
        compiler_params=pltpu.CompilerParams(vmem_limit_bytes=VMEM_LIMIT),
        name="layouts",
    )
    d_query, d_key, d_value, gain_one_grad, gain_two_grad, mixed, tokens_grad, d_out, d_gate, d_up, d_down = tail(
        dqkv, w_query, w_key, w_value, gain_rows, d_gain_two, mixed, tokens_grad, d_out, d_gate, d_up, d_down
    )
    return (
        mixed, tokens_grad, gain_one_grad.reshape(-1), d_query, d_key, d_value, d_out, gain_two_grad.reshape(-1),
        d_gate, d_up, d_down,
    )


def solution(mesh):
    in_specs = (
        P(("ctx", "fsdp"), None),
        P(("ctx", "fsdp"), None),
        P("fsdp", None),
        P(("ctx", "fsdp")),
        P(("ctx", "fsdp"), None),
        P(("ctx", "fsdp"), None),
        P(("ctx", "fsdp"), None),
        P(("ctx", "fsdp"), None),
        P(("ctx", "fsdp")),
        P(None, ("ctx", "fsdp")),
        P(None, ("ctx", "fsdp")),
        P(("ctx", "fsdp"), None),
    )
    out_specs = (
        P(("ctx", "fsdp"), None),
        P(("ctx", "fsdp"), None),
        P(("ctx", "fsdp")),
        P(("ctx", "fsdp"), None),
        P(("ctx", "fsdp"), None),
        P(("ctx", "fsdp"), None),
        P(("ctx", "fsdp"), None),
        P(("ctx", "fsdp")),
        P(None, ("ctx", "fsdp")),
        P(None, ("ctx", "fsdp")),
        P(("ctx", "fsdp"), None),
    )
    fits = (
        mesh.shape["ctx"] == KV_HEADS
        and mesh.shape["fsdp"] == 4
        and HEADS == 2 * KV_HEADS
    )
    return jax.shard_map(plane if fits else local, mesh=mesh, in_specs=in_specs, out_specs=out_specs, check_vma=False)
```

```python
import functools
import math

import jax
import jax.numpy as jnp
import numpy as np
from jax import lax
from jax.experimental import pallas as pl
from jax.experimental.pallas import tpu as pltpu
from jax.sharding import PartitionSpec as P

HEADS = 16
KV_HEADS = 8
HEAD_DIM = 96


EPS = 1e-05
THETA = 100000.0
NEG_FILL = -1e30


def rotate(values_in, positions, direction):
    half_dim = values_in.shape[-1] // 2
    freqs = THETA ** (-(jnp.arange(half_dim, dtype=jnp.float32) * 2.0 / values_in.shape[-1]))
    angle = positions.astype(jnp.float32)[:, None] * freqs[None, :]
    cosine = jnp.cos(angle)[:, None, :]
    sine = direction * jnp.sin(angle)[:, None, :]
    first_half = values_in[..., :half_dim]
    second_half = values_in[..., half_dim:]
    return jnp.concatenate(
        [first_half * cosine - second_half * sine, second_half * cosine + first_half * sine],
        axis=-1,
    )


def place_rows(pair_index, tok_rows, block_count):
    half_rows = tok_rows // 2
    offsets = jnp.arange(tok_rows, dtype=jnp.int32)
    early = pair_index * half_rows + offsets
    late = (block_count - 1 - pair_index) * half_rows + offsets - half_rows
    return jnp.where(offsets < half_rows, early, late)


def rms_scale(values_in):
    return lax.rsqrt(jnp.mean(values_in * values_in, axis=-1, keepdims=True) + EPS)


def norm_back(grad_normed, normed, inv_rms, gain):
    scaled = grad_normed * gain
    return inv_rms * (scaled - normed * jnp.mean(scaled * normed, axis=-1, keepdims=True))


def local(
    tokens,
    out_grad,
    pair_table,
    attn_gain,
    w_query,
    w_key,
    w_value,
    w_out,
    mlp_gain,
    w_gate,
    w_up,
    w_down,
):
    tok_rows = tokens.shape[0]
    half_rows = tok_rows // 2
    ctx_count = lax.axis_size("ctx")
    half_count = 2 * ctx_count
    pair_row = pair_table[0]
    my_pos = place_rows(pair_row[lax.axis_index("ctx")], tok_rows, half_count)
    half_blocks = jnp.stack([pair_row, half_count - 1 - pair_row], axis=1).reshape(-1)
    block_ids = jnp.arange(half_count, dtype=jnp.int32)
    inverse = jnp.sum(
        jnp.where(half_blocks[None, :] == block_ids[:, None], block_ids[None, :], 0), axis=1
    )
    group_size = HEADS // KV_HEADS
    score_scale = HEAD_DIM ** (-0.5)
    query_width = HEADS * HEAD_DIM
    kv_width = KV_HEADS * HEAD_DIM
    w_query_all, w_key_all, w_value_all, w_out_all, gain_first, gain_second = (
        lax.all_gather(w_query, ("ctx", "fsdp"), axis=0, tiled=True),
        lax.all_gather(w_key, ("ctx", "fsdp"), axis=0, tiled=True),
        lax.all_gather(w_value, ("ctx", "fsdp"), axis=0, tiled=True),
        lax.all_gather(w_out, ("ctx", "fsdp"), axis=0, tiled=True),
        lax.all_gather(attn_gain, ("ctx", "fsdp"), axis=0, tiled=True),
        lax.all_gather(mlp_gain, ("ctx", "fsdp"), axis=0, tiled=True),
    )
    gain_one = gain_first.astype(jnp.float32)
    gain_two = gain_second.astype(jnp.float32)
    resid_in = tokens.astype(jnp.float32)
    inv_one = rms_scale(resid_in)
    normed_one = resid_in * inv_one
    normed_in = (normed_one * gain_one).astype(jnp.bfloat16)
    query_lin = jnp.dot(normed_in, w_query_all, preferred_element_type=jnp.float32)
    key_lin = jnp.dot(normed_in, w_key_all, preferred_element_type=jnp.float32)
    value_lin = jnp.dot(normed_in, w_value_all, preferred_element_type=jnp.float32)
    query_rot = rotate(query_lin.reshape(tok_rows, HEADS, HEAD_DIM), my_pos, 1.0).astype(
        jnp.bfloat16
    )
    key_rot = (
        rotate(key_lin.reshape(tok_rows, KV_HEADS, HEAD_DIM), my_pos, 1.0)
        .astype(jnp.bfloat16)
        .reshape(tok_rows, kv_width)
    )
    value_low = value_lin.astype(jnp.bfloat16)
    keys_got, values_got = (
        lax.all_gather(key_rot, "ctx", axis=0, tiled=True),
        lax.all_gather(value_low, "ctx", axis=0, tiled=True),
    )
    seq_len = keys_got.shape[0]
    keys_all = jnp.take(keys_got.reshape(half_count, half_rows, kv_width), inverse, axis=0).reshape(
        seq_len, kv_width
    )
    values_all = jnp.take(
        values_got.reshape(half_count, half_rows, kv_width), inverse, axis=0
    ).reshape(seq_len, kv_width)
    key_pos = jnp.arange(seq_len, dtype=jnp.int32)
    key_block = math.gcd(seq_len, 512)
    live_blocks = jnp.max(my_pos) // key_block + 1
    query_grp = query_rot.reshape(tok_rows, KV_HEADS, group_size, HEAD_DIM)

    def block_scores(block_index):
        first_row = block_index * key_block
        key_tile = lax.dynamic_slice_in_dim(keys_all, first_row, key_block, 0).reshape(
            key_block, KV_HEADS, HEAD_DIM
        )
        value_tile = lax.dynamic_slice_in_dim(values_all, first_row, key_block, 0).reshape(
            key_block, KV_HEADS, HEAD_DIM
        )
        scores = (
            jnp.einsum("tkgd,skd->kgts", query_grp, key_tile, preferred_element_type=jnp.float32)
            * score_scale
        )
        visible = (
            lax.dynamic_slice_in_dim(key_pos, first_row, key_block, 0)[None, :] <= my_pos[:, None]
        )
        return (scores, visible, key_tile, value_tile)

    def stats_step(block_index, carry):
        run_max, run_sum = carry
        scores, visible, key_tile, value_tile = block_scores(block_index)
        masked = jnp.where(visible, scores, NEG_FILL)
        new_max = jnp.maximum(run_max, jnp.max(masked, axis=-1))
        weights = jnp.where(visible, jnp.exp(masked - new_max[..., None]), 0.0)
        return (new_max, run_sum * jnp.exp(run_max - new_max) + jnp.sum(weights, axis=-1))

    start_max = jnp.full((KV_HEADS, group_size, tok_rows), NEG_FILL, jnp.float32)
    run_max, run_sum = lax.fori_loop(
        0, live_blocks, stats_step, (start_max, jnp.zeros_like(start_max))
    )
    log_total = run_max + jnp.log(run_sum)

    def probs(scores, visible):
        return jnp.where(visible, jnp.exp(scores - log_total[..., None]), 0.0)

    def output_step(block_index, accum):
        scores, visible, key_tile, value_tile = block_scores(block_index)
        prob_low = probs(scores, visible).astype(jnp.bfloat16)
        return accum + jnp.einsum(
            "kgts,skd->kgtd", prob_low, value_tile, preferred_element_type=jnp.float32
        )

    attn_acc = lax.fori_loop(
        0,
        live_blocks,
        output_step,
        jnp.zeros((KV_HEADS, group_size, tok_rows, HEAD_DIM), jnp.float32),
    )
    attn_low = attn_acc.transpose(2, 0, 1, 3).reshape(tok_rows, query_width).astype(jnp.bfloat16)
    resid_mid = resid_in + jnp.dot(attn_low, w_out_all, preferred_element_type=jnp.float32)
    inv_two = rms_scale(resid_mid)
    normed_two = resid_mid * inv_two
    normed_mid = (normed_two * gain_two).astype(jnp.bfloat16)
    w_gate_part, w_up_part, w_down_part = (
        lax.all_gather(w_gate, ("ctx", "fsdp"), axis=1, tiled=True),
        lax.all_gather(w_up, ("ctx", "fsdp"), axis=1, tiled=True),
        lax.all_gather(w_down, ("ctx", "fsdp"), axis=0, tiled=True),
    )
    gate_lin = jnp.dot(normed_mid, w_gate_part, preferred_element_type=jnp.float32)
    up_lin = jnp.dot(normed_mid, w_up_part, preferred_element_type=jnp.float32)
    sigma = jax.nn.sigmoid(gate_lin)
    activated = gate_lin * sigma
    hidden_low = (activated * up_lin).astype(jnp.bfloat16)
    mlp_branch = jnp.dot(hidden_low, w_down_part, preferred_element_type=jnp.float32)
    mixed = (resid_mid + mlp_branch).astype(jnp.bfloat16)
    grad_top = out_grad.astype(jnp.float32)
    d_down = jnp.einsum("tf,td->fd", hidden_low, out_grad, preferred_element_type=jnp.float32)
    grad_hidden = jnp.einsum("td,fd->tf", out_grad, w_down_part, preferred_element_type=jnp.float32)
    grad_gate = (grad_hidden * up_lin * sigma * (1.0 + gate_lin * (1.0 - sigma))).astype(
        jnp.bfloat16
    )
    grad_up = (grad_hidden * activated).astype(jnp.bfloat16)
    d_gate = jnp.einsum("td,tf->df", normed_mid, grad_gate, preferred_element_type=jnp.float32)
    d_up = jnp.einsum("td,tf->df", normed_mid, grad_up, preferred_element_type=jnp.float32)
    grad_normed_mid = jnp.einsum(
        "tf,df->td", grad_gate, w_gate_part, preferred_element_type=jnp.float32
    ) + jnp.einsum("tf,df->td", grad_up, w_up_part, preferred_element_type=jnp.float32)
    gate_grad_out, up_grad_out, down_grad_out = (
        lax.psum_scatter(d_gate, ("ctx", "fsdp"), scatter_dimension=1, tiled=True),
        lax.psum_scatter(d_up, ("ctx", "fsdp"), scatter_dimension=1, tiled=True),
        lax.psum_scatter(d_down, ("ctx", "fsdp"), scatter_dimension=0, tiled=True),
    )
    d_gain_two = jnp.sum(grad_normed_mid * normed_two, axis=0)
    grad_mid = grad_top + norm_back(grad_normed_mid, normed_two, inv_two, gain_two)
    grad_mid_low = grad_mid.astype(jnp.bfloat16)
    d_out = jnp.einsum("tq,td->qd", attn_low, grad_mid_low, preferred_element_type=jnp.float32)
    grad_attn_low = jnp.einsum(
        "td,qd->tq", grad_mid_low, w_out_all, preferred_element_type=jnp.float32
    ).astype(jnp.bfloat16)
    grad_heads = grad_attn_low.reshape(tok_rows, KV_HEADS, group_size, HEAD_DIM).transpose(
        1, 2, 0, 3
    )
    row_delta = jnp.sum(grad_heads.astype(jnp.float32) * attn_acc, axis=-1)

    def back_step(block_index, carry):
        grad_query, grad_keys, grad_values = carry
        scores, visible, key_tile, value_tile = block_scores(block_index)
        prob_full = probs(scores, visible)
        prob_low = prob_full.astype(jnp.bfloat16)
        grad_prob = jnp.einsum(
            "kgtd,skd->kgts", grad_heads, value_tile, preferred_element_type=jnp.float32
        )
        grad_score = (prob_full * (grad_prob - row_delta[..., None])).astype(jnp.bfloat16)
        grad_query = grad_query + score_scale * jnp.einsum(
            "kgts,skd->kgtd", grad_score, key_tile, preferred_element_type=jnp.float32
        )
        key_part = score_scale * jnp.einsum(
            "kgts,tkgd->skd", grad_score, query_grp, preferred_element_type=jnp.float32
        )
        value_part = jnp.einsum(
            "kgts,kgtd->skd", prob_low, grad_heads, preferred_element_type=jnp.float32
        )
        first_row = block_index * key_block
        grad_keys = lax.dynamic_update_slice_in_dim(
            grad_keys, key_part.reshape(key_block, kv_width), first_row, 0
        )
        grad_values = lax.dynamic_update_slice_in_dim(
            grad_values, value_part.reshape(key_block, kv_width), first_row, 0
        )
        return (grad_query, grad_keys, grad_values)

    empty_keys = jnp.zeros((seq_len, kv_width), jnp.float32)
    grad_query, grad_keys, grad_values = lax.fori_loop(
        0,
        live_blocks,
        back_step,
        (
            jnp.zeros((KV_HEADS, group_size, tok_rows, HEAD_DIM), jnp.float32),
            empty_keys,
            empty_keys,
        ),
    )
    keys_back = jnp.take(
        grad_keys.reshape(half_count, half_rows, kv_width), half_blocks, axis=0
    ).reshape(seq_len, kv_width)
    values_back = jnp.take(
        grad_values.reshape(half_count, half_rows, kv_width), half_blocks, axis=0
    ).reshape(seq_len, kv_width)
    own_keys, own_values = (
        lax.psum_scatter(
            keys_back.astype(jnp.bfloat16), "ctx", scatter_dimension=0, tiled=True
        ).astype(jnp.float32),
        lax.psum_scatter(
            values_back.astype(jnp.bfloat16), "ctx", scatter_dimension=0, tiled=True
        ).astype(jnp.float32),
    )
    grad_query_lin = rotate(
        grad_query.transpose(2, 0, 1, 3).reshape(tok_rows, HEADS, HEAD_DIM), my_pos, -1.0
    )
    grad_query_low = grad_query_lin.reshape(tok_rows, query_width).astype(jnp.bfloat16)
    grad_key_lin = rotate(own_keys.reshape(tok_rows, KV_HEADS, HEAD_DIM), my_pos, -1.0)
    grad_key_low = grad_key_lin.reshape(tok_rows, kv_width).astype(jnp.bfloat16)
    grad_value_low = own_values.astype(jnp.bfloat16)
    d_query = jnp.einsum("td,tq->dq", normed_in, grad_query_low, preferred_element_type=jnp.float32)
    d_key = jnp.einsum("td,tq->dq", normed_in, grad_key_low, preferred_element_type=jnp.float32)
    d_value = jnp.einsum("td,tq->dq", normed_in, grad_value_low, preferred_element_type=jnp.float32)
    grad_normed_in = (
        jnp.einsum("tq,dq->td", grad_query_low, w_query_all, preferred_element_type=jnp.float32)
        + jnp.einsum("tq,dq->td", grad_key_low, w_key_all, preferred_element_type=jnp.float32)
        + jnp.einsum("tq,dq->td", grad_value_low, w_value_all, preferred_element_type=jnp.float32)
    )
    d_gain_one = jnp.sum(grad_normed_in * normed_one, axis=0)
    grad_input = grad_mid + norm_back(grad_normed_in, normed_one, inv_one, gain_one)
    query_grad_out, key_grad_out, value_grad_out, out_grad_out, gain_one_out, gain_two_out = (
        lax.psum_scatter(d_query, ("ctx", "fsdp"), scatter_dimension=0, tiled=True),
        lax.psum_scatter(d_key, ("ctx", "fsdp"), scatter_dimension=0, tiled=True),
        lax.psum_scatter(d_value, ("ctx", "fsdp"), scatter_dimension=0, tiled=True),
        lax.psum_scatter(d_out, ("ctx", "fsdp"), scatter_dimension=0, tiled=True),
        lax.psum_scatter(d_gain_one, ("ctx", "fsdp"), scatter_dimension=0, tiled=True),
        lax.psum_scatter(d_gain_two, ("ctx", "fsdp"), scatter_dimension=0, tiled=True),
    )
    return (
        mixed,
        grad_input.astype(jnp.bfloat16),
        gain_one_out,
        query_grad_out,
        key_grad_out,
        value_grad_out,
        out_grad_out,
        gain_two_out,
        gate_grad_out,
        up_grad_out,
        down_grad_out,
    )


BF = jnp.bfloat16
F32 = jnp.float32
MESH = pl.DeviceIdType.MESH
HEAD_PAD = 128
LOG2E = 1.4426950408889634
VMEM_LIMIT = 58 * 2**20
FRONT_VMEM_LIMIT = 61 * 2**20
NT = (((1,), (1,)), ((), ()))
TN = (((0,), (0,)), ((), ()))


def dot(a, b, dims=(((1,), (0,)), ((), ()))):
    return lax.dot_general(a, b, dims, preferred_element_type=F32)


class Place:
    def __init__(self, n_ctx, n_fsdp):
        self.n_ctx, self.n_fsdp = n_ctx, n_fsdp
        self.c, self.f = lax.axis_index("ctx"), lax.axis_index("fsdp")
        core = lax.rem(self.c, 2)
        step_x = 2 - 4 * lax.rem(lax.div(self.c, 2), 2)
        step_y = 4 - 8 * lax.div(self.c, 4)
        self.other = 1 - 2 * core
        self.s = self.c + self.other
        self.a = self.c + step_x * (1 - core) + step_y * core
        self.b = self.c + step_x * core + step_y * (1 - core)
        self.d = self.c + step_x + step_y
        self.f1 = self.f + 1 - 2 * lax.rem(self.f, 2)
        self.f2 = self.f + 2 - 4 * lax.div(self.f, 2)
        self.f3 = n_fsdp - 1 - self.f

    def ctx_peer(self, j):
        return lax.rem(self.c + j, self.n_ctx)

    def ctx_source(self, j):
        return lax.rem(self.c + self.n_ctx - j, self.n_ctx)

    def greet(self, everyone):
        barrier = pltpu.get_barrier_semaphore()
        if everyone:
            mates = [(self.ctx_peer(j), self.f) for j in range(1, self.n_ctx)]
        else:
            mates = [(self.s, self.f), (self.a, self.f), (self.b, self.f)]
        mates += [(self.c, self.f1), (self.c, self.f2)]
        for mate in mates:
            pl.semaphore_signal(barrier, inc=1, device_id=mate, device_id_type=MESH)
        self.mates = len(mates)

    def wait_greeted(self):
        pl.semaphore_wait(pltpu.get_barrier_semaphore(), self.mates)


def remote(src, dst, send, recv, device):
    return pltpu.make_async_remote_copy(
        src_ref=src, dst_ref=dst, send_sem=send, recv_sem=recv, device_id=device, device_id_type=MESH
    )


class LocalCopies:
    def __init__(self, sems):
        self.sems, self.count, self.named = sems, 0, {}

    def start(self, name, src, dst):
        cp = pltpu.make_async_copy(src, dst, self.sems.at[self.count])
        cp.start()
        self.count += 1
        self.named.setdefault(name, []).append(cp)

    def wait(self, *names):
        for name in names:
            for cp in self.named.pop(name):
                cp.wait()

    def wait_all(self):
        self.wait(*list(self.named))


class PlaneGather:
    PIECES = 3
    COUNT = 7 * PIECES

    def __init__(self, at, own, blocks, sems):
        self.at, self.own, self.blocks = at, own, blocks
        self.send, self.recv = sems
        self.rows = own.shape[0] // self.PIECES
        self.started = []

    def piece(self, slot, p):
        return self.blocks.at[slot, pl.ds(p * self.rows, self.rows)]

    def copy(self, i, p, src, slot, mate):
        k = i * self.PIECES + p
        cp = remote(src, self.piece(slot, p), self.send.at[k], self.recv.at[k], (mate, self.at.f))
        cp.start()
        self.started.append(cp)

    def wait(self, i, p, slot):
        k = i * self.PIECES + p
        block = self.piece(slot, p)
        remote(block, block, self.send.at[k], self.recv.at[k], (self.at.s, self.at.f)).wait_recv()

    def start_piece(self, p):
        at = self.at
        src = self.own.at[pl.ds(p * self.rows, self.rows)]
        self.copy(1, p, src, at.c, at.a)
        self.copy(2, p, src, at.c, at.b)
        self.copy(0, p, src, at.c, at.s)

    def start(self):
        for p in range(self.PIECES):
            self.start_piece(p)

    def pass_a(self):
        at = self.at
        for p in range(self.PIECES):
            self.wait(1, p, at.a)
            self.copy(4, p, self.piece(at.a, p), at.a, at.b)
            self.copy(3, p, self.piece(at.a, p), at.a, at.s)

    def pass_b(self):
        at = self.at
        for p in range(self.PIECES):
            self.wait(2, p, at.b)
            self.copy(5, p, self.piece(at.b, p), at.b, at.s)

    def pass_d(self):
        at = self.at
        for p in range(self.PIECES):
            self.wait(4, p, at.d)
            self.copy(6, p, self.piece(at.d, p), at.d, at.s)

    def wait_other(self, which):
        at = self.at
        i, slot = {
            "own": (0, at.s),
            "a": (3, at.b + at.other),
            "b": (5, at.a + at.other),
            "d": (6, at.d + at.other),
        }[which]
        for p in range(self.PIECES):
            self.wait(i, p, slot)

    def finish_sends(self):
        for cp in self.started:
            cp.wait_send()


class PlaneScatter:
    def __init__(self, at, emit, bufs, sems, pieces):
        self.at, self.emit, self.pieces = at, emit, pieces
        self.out, self.landed = bufs
        self.send, self.recv = sems
        self.started = []

    def columns(self, t):
        width = self.landed.shape[2] // self.pieces
        return slice(t * width, (t + 1) * width)

    def copy(self, i, t, src, mate):
        k = i * self.pieces + t
        dst = self.landed.at[i, :, self.columns(t)]
        cp = remote(src, dst, self.send.at[k], self.recv.at[k], (mate, self.at.f))
        cp.start()
        self.started.append(cp)

    def wait(self, i, t):
        k = i * self.pieces + t
        block = self.landed.at[i, :, self.columns(t)]
        remote(block, block, self.send.at[k], self.recv.at[k], (self.at.s, self.at.f)).wait_recv()

    def others(self):
        at = self.at
        return (at.d + at.other, at.b + at.other, at.s, at.a + at.other)

    def to_other(self, i):
        for t in range(self.pieces):
            columns = self.columns(t)
            self.emit(self.others()[i], columns, self.out.at[i], [])
            self.copy(i, t, self.out.at[i, :, columns], self.at.s)

    def onward(self, i, index, extras, mate):
        for t in range(self.pieces):
            columns = self.columns(t)
            for extra in extras:
                self.wait(extra, t)
            self.emit(index, columns, self.out.at[i], [self.landed.at[extra] for extra in extras])
            self.copy(i, t, self.out.at[i, :, columns], mate)

    def first(self, total):
        at = self.at
        self.to_other(0)
        self.to_other(1)
        self.onward(4, at.d, [0], at.a)
        self.onward(5, at.a, [1], at.a)
        self.to_other(3)
        self.to_other(2)
        for t in range(self.pieces):
            self.wait(2, t)
            self.emit(at.c, self.columns(t), total, [self.landed.at[2]])

    def second(self):
        self.onward(6, self.at.b, [3, 4], self.at.b)

    def last(self):
        for i in (5, 6):
            for t in range(self.pieces):
                self.wait(i, t)
        return self.landed.at[5], self.landed.at[6]

    def finish_sends(self):
        for cp in self.started:
            cp.wait_send()


class LineGather:
    COUNT = 3

    def __init__(self, at, own, slot, sems):
        self.at, self.own, self.slot = at, own, slot
        self.send, self.recv = sems
        self.started = []

    def copy(self, i, src, slot, mate):
        cp = remote(src, self.slot(slot), self.send.at[i], self.recv.at[i], (self.at.c, mate))
        cp.start()
        self.started.append(cp)

    def wait(self, i, slot):
        block = self.slot(slot)
        remote(block, block, self.send.at[i], self.recv.at[i], (self.at.c, self.at.f1)).wait_recv()

    def start(self):
        at = self.at
        self.copy(1, self.own, at.f, at.f2)
        self.copy(0, self.own, at.f, at.f1)

    def relay(self):
        at = self.at
        self.wait(1, at.f2)
        self.copy(2, self.slot(at.f2), at.f2, at.f1)

    def finish(self):
        self.wait(0, self.at.f1)
        self.wait(2, self.at.f3)

    def finish_sends(self):
        for cp in self.started:
            cp.wait_send()


class LineScatter:
    COUNT = 3

    def __init__(self, at, part, landed, sems, base=0):
        self.at, self.part, self.landed, self.base = at, part, landed, base
        self.send, self.recv = sems
        self.started = []

    def copy(self, i, src, mate):
        k = self.base + i
        cp = remote(src, self.landed.at[i], self.send.at[k], self.recv.at[k], (self.at.c, mate))
        cp.start()
        self.started.append(cp)

    def wait(self, i):
        k = self.base + i
        block = self.landed.at[i]
        remote(block, block, self.send.at[k], self.recv.at[k], (self.at.c, self.at.f1)).wait_recv()

    def start(self):
        at = self.at
        self.copy(0, self.part(at.f3), at.f1)
        self.copy(1, self.part(at.f1), at.f1)

    def add(self, dst, refs):
        count = dst.shape[0]
        step = min(count, 128) if len(dst.shape) == 2 else 1

        def piece(i, carry):
            rows = pl.ds(pl.multiple_of(i * step, step), step) if len(dst.shape) == 2 else pl.ds(i, 1)
            value = refs[0][rows].astype(F32)
            for ref in refs[1:]:
                value = value + ref[rows].astype(F32)
            dst[rows] = value.astype(dst.dtype)
            return carry

        lax.fori_loop(0, count // step, piece, 0)

    def relay(self):
        at = self.at
        self.wait(0)
        self.add(self.part(at.f2), [self.part(at.f2), self.landed.at[0]])
        self.copy(2, self.part(at.f2), at.f2)

    def finish(self, dst):
        self.wait(1)
        self.wait(2)
        self.add(dst, [self.part(self.at.f), self.landed.at[1], self.landed.at[2]])

    def finish_sends(self):
        for cp in self.started:
            cp.wait_send()


def exchange(at, src_of, dst, slot_of, sems):
    send, recv = sems
    started, waits = [], []
    for j in range(1, at.n_ctx):
        peer, source = at.ctx_peer(j), at.ctx_source(j)
        device = (peer, at.f)
        cp = remote(src_of(peer), slot_of(dst, at.c), send.at[j], recv.at[j], device)
        cp.start()
        started.append(cp)
        block = slot_of(dst, source)
        waits.append(remote(block, block, send.at[j], recv.at[j], device))
    return started, waits


def turn(values_in, cosine, sine):
    return values_in * cosine + pltpu.roll(values_in, HEAD_PAD // 2, 1) * sine


def store_rows(ref, first, lanes, value):
    block_rows, done = ref.shape[1], 0
    while done < value.shape[0]:
        block, start = divmod(first + done, block_rows)
        count = min(block_rows - start, value.shape[0] - done)
        ref[block, start : start + count, lanes] = value[done : done + count]
        done += count


def product_emit(lhs_of, rhs_of):
    def emit(index, columns, dst, extras):
        value = rhs_of(lhs_of(index), columns)
        for extra in extras:
            value = value + extra[:, columns].astype(F32)
        dst[:, columns] = value.astype(dst.dtype)

    return emit


def front_kernel(
    n_ctx, n_fsdp,
    x, og, wq, wk, wv, wout, wg, wu, wd_own, gain_a, gain_b, inv, pairs, expand, cosine, sine,
    d_gate, d_down, dgain,
    ni_out, heads_out, kt_out, ot_out, ao_out, lse_out, wqkv_out, wo_out, gains_out, rm_out, du_out, mlp_out, gm_all, g_mid_out,
    ni, heads, kt, vt, ot, ao, lse, wqkv, wo, gains, rm, x_all, wblk, w_raw, wo_raw, gt, gz, gz_sum, gc, nm_own, total,
    rs_out, rs_in, nm, ogv, wgu, wd, dd, du, dg_in, dd_in,
    x_send, x_recv, og_send, og_recv, rs_send, rs_recv,
    wc_send, wc_recv, wz_send, wz_recv, oz_send, oz_recv, gz_send, gz_recv, gc_send, gc_recv,
    fg_send, fg_recv, fu_send, fu_recv, fd_send, fd_recv, zg_send, zg_recv, zd_send, zd_recv, local_sem,
):
    at = Place(n_ctx, n_fsdp)
    rows, width = x.shape
    half = rows // 2
    seq_len = rows * n_ctx
    own_rows = w_raw.shape[2]
    at.greet(True)
    local = LocalCopies(local_sem)
    part_cols = n_fsdp * 128

    def gate_slot(i):
        return wgu.at[:, pl.ds(pl.multiple_of(i * 128, 128), 128)]

    def up_slot(i):
        return wgu.at[:, pl.ds(pl.multiple_of(part_cols + i * 128, 128), 128)]

    for src, dst in ((og, ogv.at[at.c]), (wg, gate_slot(at.f)), (wu, up_slot(at.f)), (wd_own, wd.at[at.f])):
        local.start("own", src, dst)
    q_cols, kv_cols = wq.shape[1] // n_ctx, wk.shape[1] // n_ctx
    for i in range(n_ctx):
        parts = (wq[:, i * q_cols : (i + 1) * q_cols], *(w[:, i * kv_cols : (i + 1) * kv_cols] for w in (wk, wv)))
        wblk[i] = jnp.concatenate(parts, axis=1)
    place = (at.c * n_fsdp + at.f) * own_rows
    from_lane = lax.broadcasted_iota(jnp.int32, (own_rows, width), 0)
    to_lane = lax.broadcasted_iota(jnp.int32, (own_rows, width), 1)
    spread = jnp.where(to_lane == from_lane + place, 1.0, 0.0).astype(BF)
    row = lax.broadcasted_iota(jnp.int32, (16, width), 0)
    spread_gains = [dot(jnp.broadcast_to(g[...], (16, own_rows)), spread) for g in (gain_a, gain_b)]
    gt[...] = jnp.where(row == 0, spread_gains[0], jnp.where(row == 1, spread_gains[1], 0.0)).astype(BF)
    at.wait_greeted()

    wc_copies, wc_waits = exchange(
        at, lambda p: wblk.at[p], w_raw, lambda r, i: r.at[i, at.f], (wc_send, wc_recv)
    )
    zt = LineGather(at, gt, lambda i: gz.at[i], (gz_send, gz_recv))
    zt.start()
    gx = PlaneGather(at, x, x_all, (x_send, x_recv))
    gx.start()
    zo = LineGather(at, wout, lambda i: wo_raw.at[i], (oz_send, oz_recv))
    zo.start()
    w_raw[at.c, at.f] = wblk[at.c]
    wo_raw[at.f] = wout[...]
    gz[at.f] = gt[...]
    x_all[at.c] = x[...]
    zt.relay()
    zt.finish()
    gz_sum[...] = sum(gz[i].astype(F32) for i in range(n_fsdp)).astype(BF)
    gc_copies, gc_waits = exchange(at, lambda p: gz_sum, gc, lambda r, i: r.at[i], (gc_send, gc_recv))
    gc[at.c] = gz_sum[...]
    for w in wc_waits:
        w.wait_recv()
    zw = LineGather(at, w_raw.at[:, at.f], lambda i: w_raw.at[:, i], (wz_send, wz_recv))
    zw.start()
    gx.pass_a()
    gx.pass_b()
    zw.relay()
    zo.relay()
    ffn = [
        LineGather(at, wg, gate_slot, (fg_send, fg_recv)),
        LineGather(at, wu, up_slot, (fu_send, fu_recv)),
        LineGather(at, wd_own, lambda i: wd.at[i], (fd_send, fd_recv)),
    ]
    for part in ffn:
        part.start()
    go = PlaneGather(at, og, ogv, (og_send, og_recv))
    go.start()
    for w in gc_waits:
        w.wait_recv()
    gains[...] = sum(gc[i].astype(F32) for i in range(n_ctx))
    gain_one = gains[0:1, :]

    def norm_in(slot):
        def part(r, carry):
            start = pl.multiple_of(r * 48, 16)
            part_rows = x_all[slot, pl.ds(start, 48), :].astype(F32)
            scale = lax.rsqrt(jnp.mean(part_rows * part_rows, axis=-1, keepdims=True) + EPS)
            inside = pl.multiple_of(lax.rem(r, 2) * 48, 16)
            ni[2 * slot + lax.div(r, 2), pl.ds(inside, 48), :] = (part_rows * scale * gain_one).astype(BF)
            return carry

        lax.fori_loop(0, rows // 48, part, 0)

    norm_in(at.c)
    gx.wait_other("own")
    norm_in(at.s)
    norm_in(at.a)
    norm_in(at.b)
    gx.pass_d()
    norm_in(at.d)
    gx.wait_other("a")
    norm_in(at.b + at.other)
    gx.wait_other("b")
    norm_in(at.a + at.other)
    gx.wait_other("d")
    norm_in(at.d + at.other)
    local.start("ni", ni, ni_out)
    local.start("out", gains, gains_out)
    zw.finish()

    def widen(i, carry):
        part = w_raw[pl.ds(2 * i, 2)].reshape(2 * n_fsdp * own_rows, w_raw.shape[3])
        start = pl.multiple_of(i * 2 * n_fsdp * own_rows, 128)
        wqkv[pl.ds(start, 2 * n_fsdp * own_rows), :] = dot(part, expand[...]).astype(BF)
        return carry

    lax.fori_loop(0, n_ctx // 2, widen, 0)

    def project(g, carry):
        lhs = jnp.concatenate([ni[inv[4 * g + i]] for i in range(4)], axis=0)
        lin = dot(lhs, wqkv[...])
        span = pl.ds(pl.multiple_of(g * 4 * half, 128), 4 * half)
        cos_part, sin_part = cosine[span, :], sine[span, :]
        heads[0, span, :] = turn(lin[:, 0:128], cos_part, sin_part).astype(BF)
        heads[1, span, :] = turn(lin[:, 128:256], cos_part, sin_part).astype(BF)
        k_part = turn(lin[:, 256:384], cos_part, sin_part).astype(BF)
        v_part = lin[:, 384:512].astype(BF)
        heads[2, span, :] = k_part
        heads[3, span, :] = v_part
        kt[:, span] = jnp.transpose(k_part.astype(F32)).astype(BF)
        vt[:, span] = jnp.transpose(v_part.astype(F32)).astype(BF)
        return carry

    lax.fori_loop(0, seq_len // (4 * half), project, 0)
    local.start("heads", heads, heads_out)
    for src, dst in ((kt, kt_out), (wqkv, wqkv_out)):
        local.start("out", src, dst)

    block = 256
    score_scale = HEAD_DIM ** (-0.5) * LOG2E
    for i in range(seq_len // block):
        first = i * block

        def head_step(h, carry, first=first):
            span = slice(first, first + block)
            q_part = heads[h, span, :]
            diag = dot(heads[2, span, :], q_part, NT) * score_scale
            key_id = lax.broadcasted_iota(jnp.int32, (block, block), 0)
            query_id = lax.broadcasted_iota(jnp.int32, (block, block), 1)
            diag = jnp.where(key_id <= query_id, diag, NEG_FILL)
            top = jnp.max(diag, axis=0, keepdims=True)
            if first:
                past = dot(heads[2, 0:first, :], q_part, NT) * score_scale
                top = jnp.maximum(top, jnp.max(past, axis=0, keepdims=True))
            diag_p = jnp.exp2(diag - top)
            norm = jnp.sum(diag_p, axis=0, keepdims=True)
            acc = dot(vt[:, span], diag_p.astype(BF))
            if first:
                past_p = jnp.exp2(past - top)
                norm = norm + jnp.sum(past_p, axis=0, keepdims=True)
                acc = acc + dot(vt[:, 0:first], past_p.astype(BF))
            acc = acc / norm
            ot[h, :, span] = acc
            lse[h, :, span] = jnp.broadcast_to(top + jnp.log2(norm), (8, block))
            lanes = pl.ds(pl.multiple_of(h * HEAD_PAD, HEAD_PAD), HEAD_PAD)
            store_rows(ao, first, lanes, jnp.transpose(acc).astype(BF))
            return carry

        lax.fori_loop(0, 2, head_step, 0)
        if i == 4:
            go.pass_a()
            go.pass_b()

    for src, dst in ((ot, ot_out), (ao, ao_out), (lse, lse_out)):
        local.start("out", src, dst)
    zo.finish()
    ffn[0].relay()
    raw = wo_raw[...].reshape(2 * HEAD_DIM, width)
    pad_rows = jnp.zeros((HEAD_PAD - HEAD_DIM, width), BF)
    wo[0:96, :] = raw[0:96]
    wo[96:128, :] = pad_rows
    wo[128:224, :] = raw[96:192]
    wo[224:256, :] = pad_rows
    local.start("out", wo, wo_out)

    def attn_rows(index):
        pair = pairs[index]
        return jnp.concatenate([ao[pair], ao[2 * n_ctx - 1 - pair]], axis=0)

    emit = product_emit(attn_rows, lambda lhs, columns: dot(lhs, wo[:, columns]))
    sc = PlaneScatter(at, emit, (rs_out, rs_in), (rs_send, rs_recv), 3)
    sc.first(total)
    go.pass_d()
    sc.second()
    ffn[1].relay()
    go.wait_other("own")
    go.wait_other("a")
    go.wait_other("b")
    go.wait_other("d")
    more, most = sc.last()
    gain_two = gains[1:2, :]

    gx.finish_sends()
    gn = PlaneGather(at, nm_own, nm, (x_send, x_recv))
    for p in range(gn.PIECES):
        span = slice(p * gn.rows, (p + 1) * gn.rows)
        mid = x[span, :].astype(F32) + total[span, :] + more[span, :].astype(F32) + most[span, :].astype(F32)
        scale = lax.rsqrt(jnp.mean(mid * mid, axis=-1, keepdims=True) + EPS)
        rm[span, :] = mid
        normed_mid = (mid * scale * gain_two).astype(BF)
        nm_own[span, :] = normed_mid
        gn.start_piece(p)
        nm[at.c, span, :] = normed_mid
    local.start("rm", rm, rm_out)
    ffn[2].relay()
    gn.pass_a()
    gn.pass_b()
    sc.finish_sends()
    local.wait("own")
    for part in ffn[:2]:
        part.finish()
    gn.pass_d()

    def feed(mate):
        i = lax.div(mate, 2)
        both = dot(nm[pl.ds(2 * i, 2)].reshape(2 * rows, width), wgu[...])
        gate, up = both[:, :part_cols], both[:, part_cols:]
        sigma = 1.0 / (1.0 + jnp.exp(-gate))
        act = gate * sigma
        from_gate = up * sigma * (1.0 + gate * (1.0 - sigma))
        for start, value in ((0, act * up), (part_cols, from_gate), (2 * part_cols, act)):
            x_all[pl.ds(2 * i, 2), :, start : start + part_cols] = value.astype(BF).reshape(2, rows, part_cols)

    def feed_back(i, carry):
        g_hidden = dot(ogv[pl.ds(2 * i, 2)].reshape(2 * rows, width), wd[...].reshape(part_cols, width), NT)
        for start in (part_cols, 2 * part_cols):
            factor = x_all[pl.ds(2 * i, 2), :, start : start + part_cols].reshape(2 * rows, part_cols).astype(F32)
            x_all[pl.ds(2 * i, 2), :, start : start + part_cols] = (
                (g_hidden * factor).astype(BF).reshape(2, rows, part_cols)
            )
        return carry

    gn.wait_other("own")
    feed(at.c)
    gn.wait_other("b")
    feed(at.a)
    gn.wait_other("a")
    feed(at.b)
    gn.wait_other("d")
    feed(at.d)
    local.wait("heads", "ni")
    dg = heads

    for i in range(part_cols // 256):
        value = dot(
            x_all[:, :, i * 256 : (i + 1) * 256].reshape(n_ctx * rows, 256), ogv[...].reshape(n_ctx * rows, width), TN
        )
        dd[2 * i : 2 * i + 2] = value.astype(BF).reshape(2, 128, width)
    zd = LineScatter(at, lambda i: dd.at[i], dd_in, (zd_send, zd_recv))
    zd.start()
    ffn[2].finish()
    lax.fori_loop(0, n_ctx // 2, feed_back, 0)
    emit = product_emit(lambda index: x_all[index, :, part_cols:], lambda lhs, columns: dot(lhs, wgu[columns, :], NT))
    sc = PlaneScatter(at, emit, (rs_out, rs_in), (rs_send, rs_recv), 3)
    sc.first(total)
    zd.relay()

    def gate_up_grad(t, carry):
        cols = pl.ds(pl.multiple_of(t * 256, 256), 256)
        value = dot(
            nm[:, :, cols].reshape(n_ctx * rows, 256), x_all[:, :, part_cols:].reshape(n_ctx * rows, 2 * part_cols), TN
        ).astype(BF)
        for i in range(n_fsdp):
            dg[i, cols, :] = value[:, i * 128 : (i + 1) * 128]
            du[i, cols, :] = value[:, part_cols + i * 128 : part_cols + (i + 1) * 128]
        return carry

    zg = []
    for part in range(2):
        lax.fori_loop(part * width // 512, (part + 1) * width // 512, gate_up_grad, 0)
        half_rows = pl.ds(part * width // 2, width // 2)
        zg.append(
            LineScatter(
                at, lambda i, h=half_rows: dg.at[i, h], dg_in.at[:, half_rows], (zg_send, zg_recv), 3 * part
            )
        )
        zg[part].start()
    local.start("out", du, du_out)
    sc.second()

    more, most = sc.last()
    local.wait("rm")
    gn.finish_sends()
    g_mid, gm_own = rm, nm_own
    gm = PlaneGather(at, gm_own, gm_all, (x_send, x_recv))
    gain_part = jnp.zeros((8, width), F32)
    for p in range(gm.PIECES):
        span = slice(p * gm.rows, (p + 1) * gm.rows)
        grad = total[span, :] + more[span, :].astype(F32) + most[span, :].astype(F32)
        mid = rm[span, :]
        scale = lax.rsqrt(jnp.mean(mid * mid, axis=-1, keepdims=True) + EPS)
        normed = mid * scale
        scaled = grad * gain_two
        back = og[span, :].astype(F32) + scale * (scaled - normed * jnp.mean(scaled * normed, axis=-1, keepdims=True))
        g_mid[span, :] = back
        gm_own[span, :] = back.astype(BF)
        gm.start_piece(p)
        gain_part = gain_part + jnp.sum((grad * normed).reshape(gm.rows // 8, 8, width), axis=0)
    dgain[...] = gain_part
    local.start("out", gm_own, gm_all.at[at.c])
    local.start("out", g_mid, g_mid_out)

    zg[0].relay()

    def down(i, carry):
        part = x_all[pl.ds(2 * i, 2), :, 0:part_cols].reshape(2 * rows, part_cols)
        ni[pl.ds(4 * i, 4)] = dot(part, wd[...].reshape(part_cols, width)).astype(BF).reshape(4, half, width)
        return carry

    lax.fori_loop(0, n_ctx // 2, down, 0)
    local.start("out", ni, mlp_out)
    zg[1].relay()
    gm.pass_a()
    gm.pass_b()
    gm.pass_d()
    for which in ("own", "a", "b", "d"):
        gm.wait_other(which)
    local.wait_all()
    zd.finish(d_down)
    for part in range(2):
        zg[part].finish(d_gate.at[pl.ds(part * width // 2, width // 2)])
    for part in (go, zt, zo, zw, *ffn, sc, gm, zd, *zg):
        part.finish_sends()
    for copies in (wc_copies, gc_copies):
        for cp in copies:
            cp.wait_send()


def backward_kernel(
    n_ctx, n_fsdp,
    gm_in, ao_in, heads_in, kt_in, ot_in, lse_in, wo_in, ni_in, wqkv_in, x_in, g_mid_in, gains_in, rm_in, mlp,
    dgain, du_in_all, inv, pairs, expand_in, cosine_in, sine_in,
    mixed, tgrad, dqkv, dwout, dgain_out, d_up,
    gm_all, ao, heads, kt, ot, lse, wo, ni, wqkv, x, g_mid, gains, rm, du, expand, cosine, sine,
    ga, gat, delta, dwo, dwo_out, dwo_in, du_in, dk, dv, gq, gqc, dw, dw_in, dw_sum, dw_own, mine, mixed_total, total,
    ms_out, ms_in, rs_out, rs_in, dgc, dgz, dg_sum,
    ms_send, ms_recv, rs_send, rs_recv, oz_send, oz_recv, gz_send, gz_recv, gc_send, gc_recv,
    wz_send, wz_recv, wc_send, wc_recv, zu_send, zu_recv, local_sem,
):
    at = Place(n_ctx, n_fsdp)
    rows, width = x.shape
    half = rows // 2
    seq_len = rows * n_ctx
    own_rows = dw.shape[2]
    at.greet(True)
    local = LocalCopies(local_sem)
    for name, src, dst in (
        ("grad", gm_in, gm_all), ("grad", wo_in, wo), ("grad", ao_in, ao), ("grad", ot_in, ot),
        ("attn", heads_in, heads), ("attn", kt_in, kt), ("attn", lse_in, lse),
        ("attn", cosine_in, cosine), ("attn", sine_in, sine),
        ("mlp", mlp.at[at.d], mine.at[0]), ("mlp", mlp.at[at.a], mine.at[1]),
        ("mlp", mlp.at[at.c], mine.at[2]), ("mlp", mlp.at[at.b], mine.at[3]),
        ("weight", ni_in, ni), ("weight", expand_in, expand), ("weight", wqkv_in, wqkv),
        ("up", du_in_all, du), ("last", x_in, x), ("last", g_mid_in, g_mid), ("last", gains_in, gains), ("last", rm_in, rm),
    ):
        local.start(name, src, dst)
    at.wait_greeted()

    ms = PlaneScatter(at, None, (ms_out, ms_in), (ms_send, ms_recv), 1)
    for i, index in enumerate(ms.others()):
        ms.copy(i, 0, mlp.at[index], at.s)
    zu = LineScatter(at, lambda i: du_in_all.at[i], du_in, (zu_send, zu_recv))
    zu.start()
    zu.part = lambda i: du.at[i]
    gc_copies, gc_waits = exchange(at, lambda p: dgain, dgc, lambda r, i: r.at[i], (gc_send, gc_recv))
    dgc[at.c] = dgain[...]

    def add_blocks(index, dst, extras):
        i = index

        def part(r, carry):
            span = pl.ds(pl.multiple_of(r * 48, 16), 48)
            value = mine[i, span, :].astype(F32)
            for extra in extras:
                value = value + extra[span, :].astype(F32)
            dst[span, :] = value.astype(dst.dtype)
            return carry

        lax.fori_loop(0, rows // 48, part, 0)

    def attn_grad(g, carry):
        gm_part = jnp.concatenate([gm_all[inv[4 * g + i]] for i in range(4)], axis=0)
        span = pl.ds(pl.multiple_of(g * 4 * half, 128), 4 * half)
        low = dot(gm_part, wo[...], NT).astype(BF)
        for h in range(2):
            part = low[:, h * HEAD_PAD : (h + 1) * HEAD_PAD]
            ga[h, span, :] = part
            turned = jnp.transpose(part.astype(F32))
            gat[h, :, span] = turned.astype(BF)
            delta[h, :, span] = jnp.broadcast_to(
                jnp.sum(turned * ot[h, :, span], axis=0, keepdims=True), (8, 4 * half)
            )
        dwo[...] += dot(ao[pl.ds(4 * g, 4)].reshape(4 * half, 2 * HEAD_PAD), gm_part, TN)
        return carry

    dwo[...] = jnp.zeros_like(dwo)
    local.wait("grad")
    lax.fori_loop(0, seq_len // (4 * half), attn_grad, 0)
    low = jnp.concatenate([dwo[0:96, :], dwo[128:224, :]], axis=0).astype(BF)
    dwo_out[...] = low.reshape(dwo_out.shape)
    zo = LineScatter(at, lambda i: dwo_out.at[i], dwo_in, (oz_send, oz_recv))
    zo.start()
    local.wait("mlp")
    ms.wait(0, 0)
    add_blocks(0, ms_out.at[0], [ms_in.at[0]])
    ms.copy(4, 0, ms_out.at[0], at.a)
    ms.wait(1, 0)
    add_blocks(1, ms_out.at[1], [ms_in.at[1]])
    ms.copy(5, 0, ms_out.at[1], at.a)
    ms.wait(2, 0)
    add_blocks(2, mixed_total, [ms_in.at[2]])

    for w in gc_waits:
        w.wait_recv()
    dg_sum[...] = sum(dgc[i] for i in range(n_ctx))
    zg = LineGather(at, dg_sum, lambda i: dgz.at[i], (gz_send, gz_recv))
    zg.start()
    dgz[at.f] = dg_sum[...]

    local.wait("attn")
    dk[...] = jnp.zeros_like(dk)
    dv[...] = jnp.zeros_like(dv)
    block = 256
    plain_scale = HEAD_DIM ** (-0.5)
    score_scale = plain_scale * LOG2E
    for i in range(seq_len // block):
        first = i * block

        def head_step(h, carry, first=first):
            span = slice(first, first + block)
            q_part, ga_part, gat_part = heads[h, span, :], ga[h, span, :], gat[h, :, span]
            top = lse[h, 0:1, span]
            shift = delta[h, 0:1, span]

            def piece(keys, masked):
                scores = dot(heads[2, keys, :], q_part, NT) * score_scale - top
                if masked:
                    key_id = lax.broadcasted_iota(jnp.int32, (block, block), 0)
                    query_id = lax.broadcasted_iota(jnp.int32, (block, block), 1)
                    scores = jnp.where(key_id <= query_id, scores, NEG_FILL)
                prob = jnp.exp2(scores)
                grad = (prob * (dot(heads[3, keys, :], gat_part) - shift)).astype(BF)
                dv[keys, :] += dot(prob.astype(BF), ga_part)
                dk[keys, :] += dot(grad, q_part)
                return dot(kt[:, keys], grad)

            turned = piece(span, True)
            if first:
                turned = turned + piece(slice(0, first), False)
            lanes = pl.ds(pl.multiple_of(h * HEAD_PAD, HEAD_PAD), HEAD_PAD)
            grad_q = jnp.transpose(turned) * plain_scale
            store_rows(gq, first, lanes, turn(grad_q, cosine[span, :], -sine[span, :]).astype(BF))
            return carry

        lax.fori_loop(0, 2, head_step, 0)
        if i == 2:
            ms.wait(3, 0)
            ms.wait(4, 0)
            add_blocks(3, ms_out.at[2], [ms_in.at[3], ms_in.at[4]])
            ms.copy(6, 0, ms_out.at[2], at.b)
        if i == 4:
            local.wait("up")
            zu.relay()

    zo.relay()

    def key_rows(g, carry):
        span = pl.ds(pl.multiple_of(g * 4 * half, 128), 4 * half)
        grad_k = turn(dk[span, :] * plain_scale, cosine[span, :], -sine[span, :]).astype(BF)
        gq[pl.ds(4 * g, 4), :, 256:384] = grad_k.reshape(4, half, HEAD_PAD)
        gq[pl.ds(4 * g, 4), :, 384:512] = dv[span, :].astype(BF).reshape(4, half, HEAD_PAD)
        return carry

    lax.fori_loop(0, seq_len // (4 * half), key_rows, 0)

    def to_ctx(slot, carry):
        pair = pairs[slot]
        gqc[2 * slot] = gq[pair]
        gqc[2 * slot + 1] = gq[2 * n_ctx - 1 - pair]
        return carry

    lax.fori_loop(0, n_ctx, to_ctx, 0)
    local.wait("weight", "last")

    def weight_grad(t, carry):
        tile = 2 * n_fsdp * own_rows
        cols = pl.ds(pl.multiple_of(t * tile, 128), tile)
        value = dot(ni[:, :, cols].reshape(seq_len, tile), gqc[...].reshape(seq_len, 4 * HEAD_PAD), TN)
        low = dot(value.astype(BF), expand[...], NT).astype(BF)
        dw[pl.ds(2 * t, 2)] = low.reshape(2, n_fsdp, own_rows, low.shape[1])
        return carry

    zw = []
    for part in range(2):
        lax.fori_loop(part * n_ctx // 4, (part + 1) * n_ctx // 4, weight_grad, 0)
        rows_of = pl.ds(part * n_ctx // 2, n_ctx // 2)
        zw.append(
            LineScatter(
                at, lambda i, r=rows_of: dw.at[r, i], dw_in.at[:, rows_of], (wz_send, wz_recv), 3 * part
            )
        )
        zw[part].start()

    emit = product_emit(
        lambda index: gqc[pl.ds(2 * index, 2)].reshape(rows, 4 * HEAD_PAD),
        lambda lhs, columns: dot(lhs, wqkv[columns, :], NT),
    )
    sc = PlaneScatter(at, emit, (rs_out, rs_in), (rs_send, rs_recv), 3)
    sc.first(total)
    sc.second()
    zw[0].relay()
    zw[1].relay()
    zg.relay()
    for part in range(2):
        zw[part].finish(dw_sum.at[pl.ds(part * n_ctx // 2, n_ctx // 2)])
    wc_copies, wc_waits = exchange(
        at, lambda p: dw_sum.at[p], dw_own, lambda r, i: r.at[i], (wc_send, wc_recv)
    )
    dw_own[at.c] = dw_sum[at.c]
    mixed_more, mixed_most = ms.last()

    def mixed_rows(r, carry):
        span = pl.ds(pl.multiple_of(r * 48, 16), 48)
        value = rm[span, :] + mixed_total[span, :]
        value = value + mixed_more[span, :].astype(F32) + mixed_most[span, :].astype(F32)
        mixed[span, :] = value.astype(BF)
        return carry

    lax.fori_loop(0, rows // 48, mixed_rows, 0)
    zg.finish()
    dgain_out[...] = sum(dgz[i] for i in range(n_fsdp))

    more, most = sc.last()
    gain_one = gains[0:1, :]

    def finish_rows(r, carry):
        span = pl.ds(pl.multiple_of(r * 48, 16), 48)
        grad = total[span, :] + more[span, :].astype(F32) + most[span, :].astype(F32)
        held = x[span, :].astype(F32)
        scale = lax.rsqrt(jnp.mean(held * held, axis=-1, keepdims=True) + EPS)
        normed = held * scale
        scaled = grad * gain_one
        back = g_mid[span, :] + scale * (scaled - normed * jnp.mean(scaled * normed, axis=-1, keepdims=True))
        tgrad[span, :] = back.astype(BF)
        return carry

    lax.fori_loop(0, rows // 48, finish_rows, 0)
    zu.finish(d_up)
    zo.finish(dwout)
    for w in wc_waits:
        w.wait_recv()
    dqkv[...] = dw_own[...]
    for part in (ms, sc, zu, zo, zg, *zw):
        part.finish_sends()
    for copies in (gc_copies, wc_copies):
        for cp in copies:
            cp.wait_send()


def head_spread():
    spread = np.zeros((4 * HEAD_DIM, 4 * HEAD_PAD), np.float32)
    for head in range(4):
        for j in range(HEAD_DIM):
            lane = j if head == 3 or j < HEAD_DIM // 2 else j + HEAD_PAD // 2 - HEAD_DIM // 2
            spread[head * HEAD_DIM + j, head * HEAD_PAD + lane] = 1.0
    return spread


def turn_tables(seq_len):
    half_dim = HEAD_DIM // 2
    freqs = np.float32(THETA) ** (-(np.arange(half_dim, dtype=np.float32) * np.float32(2.0 / HEAD_DIM)))
    angle = np.arange(seq_len, dtype=np.float32)[:, None] * freqs[None, :].astype(np.float32)
    gap = np.zeros((seq_len, HEAD_PAD // 2 - half_dim), np.float32)
    cosine, sine = np.cos(angle).astype(np.float32), np.sin(angle).astype(np.float32)
    return (
        np.concatenate([cosine, gap, cosine, gap], axis=1),
        np.concatenate([-sine, gap, sine, gap], axis=1),
    )


def tail_kernel(
    n_ctx, n_fsdp,
    dqkv, wq, wk, wv, gain_a, dgain, mixed_in, tgrad_in, dwout_in, dgate_in, dup_in, ddown_in,
    dq, dk, dv, gain_one, gain_two, mixed, tgrad, dwout, dgate, dup, ddown,
    mixed_held, tgrad_held, dwout_held, dgate_held, dup_held, ddown_held, sem,
):
    moves = (
        (mixed_in, mixed_held, mixed), (tgrad_in, tgrad_held, tgrad), (dwout_in, dwout_held, dwout),
        (dgate_in, dgate_held, dgate), (dup_in, dup_held, dup), (ddown_in, ddown_held, ddown),
    )
    loads = [pltpu.make_async_copy(src, held, sem.at[i]) for i, (src, held, _) in enumerate(moves)]
    for cp in loads:
        cp.start()
    stores = []
    for i, (_, held, dst) in enumerate(moves):
        loads[i].wait()
        stores.append(pltpu.make_async_copy(held, dst, sem.at[len(moves) + i]))
        stores[i].start()
    own_rows = wq.shape[0]
    q_cols, kv_cols = wq.shape[1] // n_ctx, wk.shape[1] // n_ctx
    got = [dqkv[i].astype(F32) for i in range(n_ctx)]
    query = jnp.concatenate([g[:, :q_cols] for g in got], axis=1)
    key = jnp.concatenate([g[:, q_cols : q_cols + kv_cols] for g in got], axis=1)
    value = jnp.concatenate([g[:, q_cols + kv_cols :] for g in got], axis=1)
    dq[...] = query
    dk[...] = key
    dv[...] = value
    both = sum(
        jnp.sum(g * w[...].astype(F32), axis=1, keepdims=True) for g, w in ((query, wq), (key, wk), (value, wv))
    )
    row = jnp.transpose(jnp.broadcast_to(both, (own_rows, 128)))[0:1, :]
    gain_one[...] = row / gain_a[...].astype(F32)
    place = (lax.axis_index("ctx") * n_fsdp + lax.axis_index("fsdp")) * own_rows
    width = dgain.shape[1]
    gain = jnp.broadcast_to(jnp.sum(dgain[...], axis=0, keepdims=True), (8, width))
    gain_two[...] = pltpu.roll(gain, width - place, 1)[0:1, :own_rows]
    for cp in stores:
        cp.wait()


def sems(*counts):
    return [pltpu.SemaphoreType.DMA((n,)) for n in counts for _ in range(2)]


VM = pl.BlockSpec(memory_space=pltpu.VMEM)
SM = pl.BlockSpec(memory_space=pltpu.SMEM)
HB = pl.BlockSpec(memory_space=pl.ANY)


def plane(tokens, out_grad, pair_table, attn_gain, w_query, w_key, w_value, w_out, mlp_gain, w_gate, w_up, w_down):
    n_ctx, n_fsdp = lax.axis_size("ctx"), lax.axis_size("fsdp")
    rows, width = tokens.shape
    half = rows // 2
    seq_len = rows * n_ctx
    own_rows = w_query.shape[0]
    pairs = pair_table[0]
    ids = jnp.arange(2 * n_ctx, dtype=jnp.int32)[:, None]
    early = 2 * jnp.arange(n_ctx, dtype=jnp.int32)[None, :]
    late_or_not = jnp.where(2 * n_ctx - 1 - pairs[None, :] == ids, early + 1, 0)
    inv = jnp.sum(jnp.where(pairs[None, :] == ids, early, late_or_not), axis=1)

    gain_a, gain_b = attn_gain.reshape(1, own_rows), mlp_gain.reshape(1, own_rows)
    expand = jnp.asarray(head_spread(), BF)
    cosine, sine = (jnp.asarray(table) for table in turn_tables(seq_len))

    def sds(shape, dtype):
        return jax.ShapeDtypeStruct(shape, dtype)

    blocks = (n_ctx, rows, width)
    vm = pltpu.VMEM
    part_cols = n_fsdp * 128
    front = pl.pallas_call(
        functools.partial(front_kernel, n_ctx, n_fsdp),
        out_shape=(
            sds(w_gate.shape, F32),
            sds(w_down.shape, F32),
            sds((8, width), F32),
            sds((2 * n_ctx, half, width), BF),
            sds((4, seq_len, HEAD_PAD), BF),
            sds((HEAD_PAD, seq_len), BF),
            sds((2, HEAD_PAD, seq_len), F32),
            sds((2 * n_ctx, half, 2 * HEAD_PAD), BF),
            sds((2, 8, seq_len), F32),
            sds((width, 4 * HEAD_PAD), BF),
            sds((2 * HEAD_PAD, width), BF),
            sds((16, width), F32),
            sds((rows, width), F32),
            sds((n_fsdp, *w_up.shape), BF),
            sds((2 * n_ctx, half, width), BF),
            sds(blocks, BF),
            sds((rows, width), F32),
        ),
        in_specs=[VM] * 6 + [HB] * 3 + [VM, VM, SM, SM, VM, VM, VM],
        out_specs=(VM,) * 3 + (HB,) * 14,
        scratch_shapes=[
            vm((2 * n_ctx, half, width), BF),
            vm((4, seq_len, HEAD_PAD), BF),
            vm((HEAD_PAD, seq_len), BF),
            vm((HEAD_PAD, seq_len), BF),
            vm((2, HEAD_PAD, seq_len), F32),
            vm((2 * n_ctx, half, 2 * HEAD_PAD), BF),
            vm((2, 8, seq_len), F32),
            vm((width, 4 * HEAD_PAD), BF),
            vm((2 * HEAD_PAD, width), BF),
            vm((16, width), F32),
            vm((rows, width), F32),
            vm(blocks, BF),
            vm((n_ctx, own_rows, 4 * HEAD_DIM), BF),
            vm((n_ctx, n_fsdp, own_rows, 4 * HEAD_DIM), BF),
            vm((n_fsdp, own_rows, width), BF),
            vm((16, width), BF),
            vm((n_fsdp, 16, width), BF),
            vm((16, width), BF),
            vm((n_ctx, 16, width), BF),
            vm((rows, width), BF),
            vm((rows, width), F32),
            vm((7, rows, width), BF),
            vm((7, rows, width), BF),
            vm(blocks, BF),
            vm(blocks, BF),
            vm((width, 2 * part_cols), BF),
            vm((n_fsdp, *w_down.shape), BF),
            vm((n_fsdp, *w_down.shape), BF),
            vm((n_fsdp, *w_up.shape), BF),
            vm((3, *w_gate.shape), BF),
            vm((3, *w_down.shape), BF),
            *sems(21, 21, 21, n_ctx, 3, 3, 3, n_ctx, 3, 3, 3, 6, 3),
            pltpu.SemaphoreType.DMA((18,)),
        ],
        compiler_params=pltpu.CompilerParams(
            collective_id=0, has_side_effects=True, vmem_limit_bytes=FRONT_VMEM_LIMIT
        ),
        name="forward_and_feed_forward",
    )
    d_gate, d_down, dgain, ni, heads, kt, ot, ao, lse, wqkv, wo, gains, rm, du, mlp, gm_all, g_mid = front(
        tokens, out_grad, w_query, w_key, w_value, w_out, w_gate, w_up, w_down, gain_a, gain_b, inv, pairs, expand, cosine, sine
    )

    backward = pl.pallas_call(
        functools.partial(backward_kernel, n_ctx, n_fsdp),
        out_shape=(
            sds((rows, width), BF),
            sds((rows, width), BF),
            sds((n_ctx, own_rows, 4 * HEAD_DIM), BF),
            sds((own_rows, width), F32),
            sds((8, width), F32),
            sds(w_up.shape, F32),
        ),
        in_specs=[HB] * 14 + [VM, HB, SM, SM, HB, HB, HB],
        out_specs=(VM,) * 6,
        scratch_shapes=[
            vm((2 * n_ctx, half, width), BF),
            vm((2 * n_ctx, half, 2 * HEAD_PAD), BF),
            vm((4, seq_len, HEAD_PAD), BF),
            vm((HEAD_PAD, seq_len), BF),
            vm((2, HEAD_PAD, seq_len), F32),
            vm((2, 8, seq_len), F32),
            vm((2 * HEAD_PAD, width), BF),
            vm((2 * n_ctx, half, width), BF),
            vm((width, 4 * HEAD_PAD), BF),
            vm((rows, width), BF),
            vm((rows, width), F32),
            vm((16, width), F32),
            vm((rows, width), F32),
            vm((n_fsdp, *w_up.shape), BF),
            vm((4 * HEAD_DIM, 4 * HEAD_PAD), BF),
            vm((seq_len, HEAD_PAD), F32),
            vm((seq_len, HEAD_PAD), F32),
            vm((2, seq_len, HEAD_PAD), BF),
            vm((2, HEAD_PAD, seq_len), BF),
            vm((2, 8, seq_len), F32),
            vm((2 * HEAD_PAD, width), F32),
            vm((n_fsdp, own_rows, width), BF),
            vm((3, own_rows, width), BF),
            vm((3, *w_up.shape), BF),
            vm((seq_len, HEAD_PAD), F32),
            vm((seq_len, HEAD_PAD), F32),
            vm((2 * n_ctx, half, 4 * HEAD_PAD), BF),
            vm((2 * n_ctx, half, 4 * HEAD_PAD), BF),
            vm((n_ctx, n_fsdp, own_rows, 4 * HEAD_DIM), BF),
            vm((3, n_ctx, own_rows, 4 * HEAD_DIM), BF),
            vm((n_ctx, own_rows, 4 * HEAD_DIM), BF),
            vm((n_ctx, own_rows, 4 * HEAD_DIM), BF),
            vm((4, rows, width), BF),
            vm((rows, width), F32),
            vm((rows, width), F32),
            vm((3, rows, width), BF),
            vm((7, rows, width), BF),
            vm((7, rows, width), BF),
            vm((7, rows, width), BF),
            vm((n_ctx, 8, width), F32),
            vm((n_fsdp, 8, width), F32),
            vm((8, width), F32),
            *sems(7, 21, 3, 3, n_ctx, 6, n_ctx, 3),
            pltpu.SemaphoreType.DMA((21,)),
        ],
        compiler_params=pltpu.CompilerParams(
            collective_id=1, has_side_effects=True, vmem_limit_bytes=VMEM_LIMIT
        ),
        name="attention_backward",
    )
    mixed, tokens_grad, dqkv, d_out, d_gain_two, d_up = backward(
        gm_all.reshape(2 * n_ctx, half, width), ao, heads, kt, ot, lse, wo, ni, wqkv, tokens, g_mid, gains, rm,
        mlp.reshape(blocks), dgain, du, inv, pairs, expand, cosine, sine,
    )
    tail = pl.pallas_call(
        functools.partial(tail_kernel, n_ctx, n_fsdp),
        out_shape=(
            sds(w_query.shape, F32),
            sds(w_key.shape, F32),
            sds(w_value.shape, F32),
            sds((1, own_rows), F32),
            sds((1, own_rows), F32),
            sds((rows, width), BF),
            sds((rows, width), BF),
            sds(w_out.shape, F32),
            sds(w_gate.shape, F32),
            sds(w_up.shape, F32),
            sds(w_down.shape, F32),
        ),
        in_specs=[VM] * 6 + [HB] * 6,
        out_specs=(VM,) * 5 + (HB,) * 6,
        scratch_shapes=[
            vm((rows, width), BF),
            vm((rows, width), BF),
            vm(w_out.shape, F32),
            vm(w_gate.shape, F32),
            vm(w_up.shape, F32),
            vm(w_down.shape, F32),
            pltpu.SemaphoreType.DMA((12,)),
        ],
        compiler_params=pltpu.CompilerParams(vmem_limit_bytes=VMEM_LIMIT),
        name="layouts",
    )
    d_query, d_key, d_value, gain_one_grad, gain_two_grad, mixed, tokens_grad, d_out, d_gate, d_up, d_down = tail(
        dqkv, w_query, w_key, w_value, gain_a, d_gain_two, mixed, tokens_grad, d_out, d_gate, d_up, d_down
    )
    return (
        mixed, tokens_grad, gain_one_grad.reshape(-1), d_query, d_key, d_value, d_out, gain_two_grad.reshape(-1),
        d_gate, d_up, d_down,
    )


def solution(mesh):
    in_specs = (
        P(("ctx", "fsdp"), None),
        P(("ctx", "fsdp"), None),
        P("fsdp", None),
        P(("ctx", "fsdp")),
        P(("ctx", "fsdp"), None),
        P(("ctx", "fsdp"), None),
        P(("ctx", "fsdp"), None),
        P(("ctx", "fsdp"), None),
        P(("ctx", "fsdp")),
        P(None, ("ctx", "fsdp")),
        P(None, ("ctx", "fsdp")),
        P(("ctx", "fsdp"), None),
    )
    out_specs = (
        P(("ctx", "fsdp"), None),
        P(("ctx", "fsdp"), None),
        P(("ctx", "fsdp")),
        P(("ctx", "fsdp"), None),
        P(("ctx", "fsdp"), None),
        P(("ctx", "fsdp"), None),
        P(("ctx", "fsdp"), None),
        P(("ctx", "fsdp")),
        P(None, ("ctx", "fsdp")),
        P(None, ("ctx", "fsdp")),
        P(("ctx", "fsdp"), None),
    )
    fits = (
        mesh.shape["ctx"] == KV_HEADS
        and mesh.shape["fsdp"] == 4
        and HEADS == 2 * KV_HEADS
    )
    return jax.shard_map(plane if fits else local, mesh=mesh, in_specs=in_specs, out_specs=out_specs, check_vma=False)
```

```python
import functools
import math

import jax
import jax.numpy as jnp
import numpy as np
from jax import lax
from jax.experimental import pallas as pl
from jax.experimental.pallas import tpu as pltpu
from jax.sharding import PartitionSpec as P

HEADS = 16
KV_HEADS = 8
HEAD_DIM = 96


EPS = 1e-05
THETA = 100000.0
NEG_FILL = -1e30


def rotate(values_in, positions, direction):
    half_dim = values_in.shape[-1] // 2
    freqs = THETA ** (-(jnp.arange(half_dim, dtype=jnp.float32) * 2.0 / values_in.shape[-1]))
    angle = positions.astype(jnp.float32)[:, None] * freqs[None, :]
    cosine = jnp.cos(angle)[:, None, :]
    sine = direction * jnp.sin(angle)[:, None, :]
    first_half = values_in[..., :half_dim]
    second_half = values_in[..., half_dim:]
    return jnp.concatenate(
        [first_half * cosine - second_half * sine, second_half * cosine + first_half * sine],
        axis=-1,
    )


def place_rows(pair_index, tok_rows, block_count):
    half_rows = tok_rows // 2
    offsets = jnp.arange(tok_rows, dtype=jnp.int32)
    early = pair_index * half_rows + offsets
    late = (block_count - 1 - pair_index) * half_rows + offsets - half_rows
    return jnp.where(offsets < half_rows, early, late)


def rms_scale(values_in):
    return lax.rsqrt(jnp.mean(values_in * values_in, axis=-1, keepdims=True) + EPS)


def norm_back(grad_normed, normed, inv_rms, gain):
    scaled = grad_normed * gain
    return inv_rms * (scaled - normed * jnp.mean(scaled * normed, axis=-1, keepdims=True))


def local(
    tokens,
    out_grad,
    pair_table,
    attn_gain,
    w_query,
    w_key,
    w_value,
    w_out,
    mlp_gain,
    w_gate,
    w_up,
    w_down,
):
    tok_rows = tokens.shape[0]
    half_rows = tok_rows // 2
    ctx_count = lax.axis_size("ctx")
    half_count = 2 * ctx_count
    pair_row = pair_table[0]
    my_pos = place_rows(pair_row[lax.axis_index("ctx")], tok_rows, half_count)
    half_blocks = jnp.stack([pair_row, half_count - 1 - pair_row], axis=1).reshape(-1)
    block_ids = jnp.arange(half_count, dtype=jnp.int32)
    inverse = jnp.sum(
        jnp.where(half_blocks[None, :] == block_ids[:, None], block_ids[None, :], 0), axis=1
    )
    group_size = HEADS // KV_HEADS
    score_scale = HEAD_DIM ** (-0.5)
    query_width = HEADS * HEAD_DIM
    kv_width = KV_HEADS * HEAD_DIM
    w_query_all, w_key_all, w_value_all, w_out_all, gain_first, gain_second = (
        lax.all_gather(w_query, ("ctx", "fsdp"), axis=0, tiled=True),
        lax.all_gather(w_key, ("ctx", "fsdp"), axis=0, tiled=True),
        lax.all_gather(w_value, ("ctx", "fsdp"), axis=0, tiled=True),
        lax.all_gather(w_out, ("ctx", "fsdp"), axis=0, tiled=True),
        lax.all_gather(attn_gain, ("ctx", "fsdp"), axis=0, tiled=True),
        lax.all_gather(mlp_gain, ("ctx", "fsdp"), axis=0, tiled=True),
    )
    gain_one = gain_first.astype(jnp.float32)
    gain_two = gain_second.astype(jnp.float32)
    resid_in = tokens.astype(jnp.float32)
    inv_one = rms_scale(resid_in)
    normed_one = resid_in * inv_one
    normed_in = (normed_one * gain_one).astype(jnp.bfloat16)
    query_lin = jnp.dot(normed_in, w_query_all, preferred_element_type=jnp.float32)
    key_lin = jnp.dot(normed_in, w_key_all, preferred_element_type=jnp.float32)
    value_lin = jnp.dot(normed_in, w_value_all, preferred_element_type=jnp.float32)
    query_rot = rotate(query_lin.reshape(tok_rows, HEADS, HEAD_DIM), my_pos, 1.0).astype(
        jnp.bfloat16
    )
    key_rot = (
        rotate(key_lin.reshape(tok_rows, KV_HEADS, HEAD_DIM), my_pos, 1.0)
        .astype(jnp.bfloat16)
        .reshape(tok_rows, kv_width)
    )
    value_low = value_lin.astype(jnp.bfloat16)
    keys_got, values_got = (
        lax.all_gather(key_rot, "ctx", axis=0, tiled=True),
        lax.all_gather(value_low, "ctx", axis=0, tiled=True),
    )
    seq_len = keys_got.shape[0]
    keys_all = jnp.take(keys_got.reshape(half_count, half_rows, kv_width), inverse, axis=0).reshape(
        seq_len, kv_width
    )
    values_all = jnp.take(
        values_got.reshape(half_count, half_rows, kv_width), inverse, axis=0
    ).reshape(seq_len, kv_width)
    key_pos = jnp.arange(seq_len, dtype=jnp.int32)
    key_block = math.gcd(seq_len, 512)
    live_blocks = jnp.max(my_pos) // key_block + 1
    query_grp = query_rot.reshape(tok_rows, KV_HEADS, group_size, HEAD_DIM)

    def block_scores(block_index):
        first_row = block_index * key_block
        key_tile = lax.dynamic_slice_in_dim(keys_all, first_row, key_block, 0).reshape(
            key_block, KV_HEADS, HEAD_DIM
        )
        value_tile = lax.dynamic_slice_in_dim(values_all, first_row, key_block, 0).reshape(
            key_block, KV_HEADS, HEAD_DIM
        )
        scores = (
            jnp.einsum("tkgd,skd->kgts", query_grp, key_tile, preferred_element_type=jnp.float32)
            * score_scale
        )
        visible = (
            lax.dynamic_slice_in_dim(key_pos, first_row, key_block, 0)[None, :] <= my_pos[:, None]
        )
        return (scores, visible, key_tile, value_tile)

    def stats_step(block_index, carry):
        run_max, run_sum = carry
        scores, visible, key_tile, value_tile = block_scores(block_index)
        masked = jnp.where(visible, scores, NEG_FILL)
        new_max = jnp.maximum(run_max, jnp.max(masked, axis=-1))
        weights = jnp.where(visible, jnp.exp(masked - new_max[..., None]), 0.0)
        return (new_max, run_sum * jnp.exp(run_max - new_max) + jnp.sum(weights, axis=-1))

    start_max = jnp.full((KV_HEADS, group_size, tok_rows), NEG_FILL, jnp.float32)
    run_max, run_sum = lax.fori_loop(
        0, live_blocks, stats_step, (start_max, jnp.zeros_like(start_max))
    )
    log_total = run_max + jnp.log(run_sum)

    def probs(scores, visible):
        return jnp.where(visible, jnp.exp(scores - log_total[..., None]), 0.0)

    def output_step(block_index, accum):
        scores, visible, key_tile, value_tile = block_scores(block_index)
        prob_low = probs(scores, visible).astype(jnp.bfloat16)
        return accum + jnp.einsum(
            "kgts,skd->kgtd", prob_low, value_tile, preferred_element_type=jnp.float32
        )

    attn_acc = lax.fori_loop(
        0,
        live_blocks,
        output_step,
        jnp.zeros((KV_HEADS, group_size, tok_rows, HEAD_DIM), jnp.float32),
    )
    attn_low = attn_acc.transpose(2, 0, 1, 3).reshape(tok_rows, query_width).astype(jnp.bfloat16)
    resid_mid = resid_in + jnp.dot(attn_low, w_out_all, preferred_element_type=jnp.float32)
    inv_two = rms_scale(resid_mid)
    normed_two = resid_mid * inv_two
    normed_mid = (normed_two * gain_two).astype(jnp.bfloat16)
    w_gate_part, w_up_part, w_down_part = (
        lax.all_gather(w_gate, ("ctx", "fsdp"), axis=1, tiled=True),
        lax.all_gather(w_up, ("ctx", "fsdp"), axis=1, tiled=True),
        lax.all_gather(w_down, ("ctx", "fsdp"), axis=0, tiled=True),
    )
    gate_lin = jnp.dot(normed_mid, w_gate_part, preferred_element_type=jnp.float32)
    up_lin = jnp.dot(normed_mid, w_up_part, preferred_element_type=jnp.float32)
    sigma = jax.nn.sigmoid(gate_lin)
    activated = gate_lin * sigma
    hidden_low = (activated * up_lin).astype(jnp.bfloat16)
    mlp_branch = jnp.dot(hidden_low, w_down_part, preferred_element_type=jnp.float32)
    mixed = (resid_mid + mlp_branch).astype(jnp.bfloat16)
    grad_top = out_grad.astype(jnp.float32)
    d_down = jnp.einsum("tf,td->fd", hidden_low, out_grad, preferred_element_type=jnp.float32)
    grad_hidden = jnp.einsum("td,fd->tf", out_grad, w_down_part, preferred_element_type=jnp.float32)
    grad_gate = (grad_hidden * up_lin * sigma * (1.0 + gate_lin * (1.0 - sigma))).astype(
        jnp.bfloat16
    )
    grad_up = (grad_hidden * activated).astype(jnp.bfloat16)
    d_gate = jnp.einsum("td,tf->df", normed_mid, grad_gate, preferred_element_type=jnp.float32)
    d_up = jnp.einsum("td,tf->df", normed_mid, grad_up, preferred_element_type=jnp.float32)
    grad_normed_mid = jnp.einsum(
        "tf,df->td", grad_gate, w_gate_part, preferred_element_type=jnp.float32
    ) + jnp.einsum("tf,df->td", grad_up, w_up_part, preferred_element_type=jnp.float32)
    gate_grad_out, up_grad_out, down_grad_out = (
        lax.psum_scatter(d_gate, ("ctx", "fsdp"), scatter_dimension=1, tiled=True),
        lax.psum_scatter(d_up, ("ctx", "fsdp"), scatter_dimension=1, tiled=True),
        lax.psum_scatter(d_down, ("ctx", "fsdp"), scatter_dimension=0, tiled=True),
    )
    d_gain_two = jnp.sum(grad_normed_mid * normed_two, axis=0)
    grad_mid = grad_top + norm_back(grad_normed_mid, normed_two, inv_two, gain_two)
    grad_mid_low = grad_mid.astype(jnp.bfloat16)
    d_out = jnp.einsum("tq,td->qd", attn_low, grad_mid_low, preferred_element_type=jnp.float32)
    grad_attn_low = jnp.einsum(
        "td,qd->tq", grad_mid_low, w_out_all, preferred_element_type=jnp.float32
    ).astype(jnp.bfloat16)
    grad_heads = grad_attn_low.reshape(tok_rows, KV_HEADS, group_size, HEAD_DIM).transpose(
        1, 2, 0, 3
    )
    row_delta = jnp.sum(grad_heads.astype(jnp.float32) * attn_acc, axis=-1)

    def back_step(block_index, carry):
        grad_query, grad_keys, grad_values = carry
        scores, visible, key_tile, value_tile = block_scores(block_index)
        prob_full = probs(scores, visible)
        prob_low = prob_full.astype(jnp.bfloat16)
        grad_prob = jnp.einsum(
            "kgtd,skd->kgts", grad_heads, value_tile, preferred_element_type=jnp.float32
        )
        grad_score = (prob_full * (grad_prob - row_delta[..., None])).astype(jnp.bfloat16)
        grad_query = grad_query + score_scale * jnp.einsum(
            "kgts,skd->kgtd", grad_score, key_tile, preferred_element_type=jnp.float32
        )
        key_part = score_scale * jnp.einsum(
            "kgts,tkgd->skd", grad_score, query_grp, preferred_element_type=jnp.float32
        )
        value_part = jnp.einsum(
            "kgts,kgtd->skd", prob_low, grad_heads, preferred_element_type=jnp.float32
        )
        first_row = block_index * key_block
        grad_keys = lax.dynamic_update_slice_in_dim(
            grad_keys, key_part.reshape(key_block, kv_width), first_row, 0
        )
        grad_values = lax.dynamic_update_slice_in_dim(
            grad_values, value_part.reshape(key_block, kv_width), first_row, 0
        )
        return (grad_query, grad_keys, grad_values)

    empty_keys = jnp.zeros((seq_len, kv_width), jnp.float32)
    grad_query, grad_keys, grad_values = lax.fori_loop(
        0,
        live_blocks,
        back_step,
        (
            jnp.zeros((KV_HEADS, group_size, tok_rows, HEAD_DIM), jnp.float32),
            empty_keys,
            empty_keys,
        ),
    )
    keys_back = jnp.take(
        grad_keys.reshape(half_count, half_rows, kv_width), half_blocks, axis=0
    ).reshape(seq_len, kv_width)
    values_back = jnp.take(
        grad_values.reshape(half_count, half_rows, kv_width), half_blocks, axis=0
    ).reshape(seq_len, kv_width)
    own_keys, own_values = (
        lax.psum_scatter(
            keys_back.astype(jnp.bfloat16), "ctx", scatter_dimension=0, tiled=True
        ).astype(jnp.float32),
        lax.psum_scatter(
            values_back.astype(jnp.bfloat16), "ctx", scatter_dimension=0, tiled=True
        ).astype(jnp.float32),
    )
    grad_query_lin = rotate(
        grad_query.transpose(2, 0, 1, 3).reshape(tok_rows, HEADS, HEAD_DIM), my_pos, -1.0
    )
    grad_query_low = grad_query_lin.reshape(tok_rows, query_width).astype(jnp.bfloat16)
    grad_key_lin = rotate(own_keys.reshape(tok_rows, KV_HEADS, HEAD_DIM), my_pos, -1.0)
    grad_key_low = grad_key_lin.reshape(tok_rows, kv_width).astype(jnp.bfloat16)
    grad_value_low = own_values.astype(jnp.bfloat16)
    d_query = jnp.einsum("td,tq->dq", normed_in, grad_query_low, preferred_element_type=jnp.float32)
    d_key = jnp.einsum("td,tq->dq", normed_in, grad_key_low, preferred_element_type=jnp.float32)
    d_value = jnp.einsum("td,tq->dq", normed_in, grad_value_low, preferred_element_type=jnp.float32)
    grad_normed_in = (
        jnp.einsum("tq,dq->td", grad_query_low, w_query_all, preferred_element_type=jnp.float32)
        + jnp.einsum("tq,dq->td", grad_key_low, w_key_all, preferred_element_type=jnp.float32)
        + jnp.einsum("tq,dq->td", grad_value_low, w_value_all, preferred_element_type=jnp.float32)
    )
    d_gain_one = jnp.sum(grad_normed_in * normed_one, axis=0)
    grad_input = grad_mid + norm_back(grad_normed_in, normed_one, inv_one, gain_one)
    query_grad_out, key_grad_out, value_grad_out, out_grad_out, gain_one_out, gain_two_out = (
        lax.psum_scatter(d_query, ("ctx", "fsdp"), scatter_dimension=0, tiled=True),
        lax.psum_scatter(d_key, ("ctx", "fsdp"), scatter_dimension=0, tiled=True),
        lax.psum_scatter(d_value, ("ctx", "fsdp"), scatter_dimension=0, tiled=True),
        lax.psum_scatter(d_out, ("ctx", "fsdp"), scatter_dimension=0, tiled=True),
        lax.psum_scatter(d_gain_one, ("ctx", "fsdp"), scatter_dimension=0, tiled=True),
        lax.psum_scatter(d_gain_two, ("ctx", "fsdp"), scatter_dimension=0, tiled=True),
    )
    return (
        mixed,
        grad_input.astype(jnp.bfloat16),
        gain_one_out,
        query_grad_out,
        key_grad_out,
        value_grad_out,
        out_grad_out,
        gain_two_out,
        gate_grad_out,
        up_grad_out,
        down_grad_out,
    )


BF = jnp.bfloat16
F32 = jnp.float32
MESH = pl.DeviceIdType.MESH
HEAD_PAD = 128
LOG2E = 1.4426950408889634
VMEM_LIMIT = 58 * 2**20
FRONT_VMEM_LIMIT = 61 * 2**20
NT = (((1,), (1,)), ((), ()))
TN = (((0,), (0,)), ((), ()))


def dot(a, b, dims=(((1,), (0,)), ((), ()))):
    return lax.dot_general(a, b, dims, preferred_element_type=F32)


class Place:
    def __init__(self, n_ctx, n_fsdp):
        self.n_ctx, self.n_fsdp = n_ctx, n_fsdp
        self.c, self.f = lax.axis_index("ctx"), lax.axis_index("fsdp")
        core = lax.rem(self.c, 2)
        step_x = 2 - 4 * lax.rem(lax.div(self.c, 2), 2)
        step_y = 4 - 8 * lax.div(self.c, 4)
        self.other = 1 - 2 * core
        self.s = self.c + self.other
        self.a = self.c + step_x * (1 - core) + step_y * core
        self.b = self.c + step_x * core + step_y * (1 - core)
        self.d = self.c + step_x + step_y
        self.f1 = self.f + 1 - 2 * lax.rem(self.f, 2)
        self.f2 = self.f + 2 - 4 * lax.div(self.f, 2)
        self.f3 = n_fsdp - 1 - self.f

    def ctx_peer(self, j):
        return lax.rem(self.c + j, self.n_ctx)

    def ctx_source(self, j):
        return lax.rem(self.c + self.n_ctx - j, self.n_ctx)

    def greet(self, everyone):
        barrier = pltpu.get_barrier_semaphore()
        if everyone:
            mates = [(self.ctx_peer(j), self.f) for j in range(1, self.n_ctx)]
        else:
            mates = [(self.s, self.f), (self.a, self.f), (self.b, self.f)]
        mates += [(self.c, self.f1), (self.c, self.f2)]
        for mate in mates:
            pl.semaphore_signal(barrier, inc=1, device_id=mate, device_id_type=MESH)
        self.mates = len(mates)

    def wait_greeted(self):
        pl.semaphore_wait(pltpu.get_barrier_semaphore(), self.mates)


def remote(src, dst, send, recv, device):
    return pltpu.make_async_remote_copy(
        src_ref=src, dst_ref=dst, send_sem=send, recv_sem=recv, device_id=device, device_id_type=MESH
    )


class LocalCopies:
    def __init__(self, sems):
        self.sems, self.count, self.named = sems, 0, {}

    def start(self, name, src, dst):
        cp = pltpu.make_async_copy(src, dst, self.sems.at[self.count])
        cp.start()
        self.count += 1
        self.named.setdefault(name, []).append(cp)

    def wait(self, *names):
        for name in names:
            for cp in self.named.pop(name):
                cp.wait()

    def wait_all(self):
        self.wait(*list(self.named))


class PlaneGather:
    PIECES = 3
    COUNT = 7 * PIECES

    def __init__(self, at, own, blocks, sems):
        self.at, self.own, self.blocks = at, own, blocks
        self.send, self.recv = sems
        self.rows = own.shape[0] // self.PIECES
        self.started = []

    def piece(self, slot, p):
        return self.blocks.at[slot, pl.ds(p * self.rows, self.rows)]

    def copy(self, i, p, src, slot, mate):
        k = i * self.PIECES + p
        cp = remote(src, self.piece(slot, p), self.send.at[k], self.recv.at[k], (mate, self.at.f))
        cp.start()
        self.started.append(cp)

    def wait(self, i, p, slot):
        k = i * self.PIECES + p
        block = self.piece(slot, p)
        remote(block, block, self.send.at[k], self.recv.at[k], (self.at.s, self.at.f)).wait_recv()

    def start_piece(self, p):
        at = self.at
        src = self.own.at[pl.ds(p * self.rows, self.rows)]
        self.copy(1, p, src, at.c, at.a)
        self.copy(2, p, src, at.c, at.b)
        self.copy(0, p, src, at.c, at.s)

    def start(self):
        for p in range(self.PIECES):
            self.start_piece(p)

    def pass_a(self):
        at = self.at
        for p in range(self.PIECES):
            self.wait(1, p, at.a)
            self.copy(4, p, self.piece(at.a, p), at.a, at.b)
            self.copy(3, p, self.piece(at.a, p), at.a, at.s)

    def pass_b(self):
        at = self.at
        for p in range(self.PIECES):
            self.wait(2, p, at.b)
            self.copy(5, p, self.piece(at.b, p), at.b, at.s)

    def pass_d(self):
        at = self.at
        for p in range(self.PIECES):
            self.wait(4, p, at.d)
            self.copy(6, p, self.piece(at.d, p), at.d, at.s)

    def wait_other(self, which):
        at = self.at
        i, slot = {
            "own": (0, at.s),
            "a": (3, at.b + at.other),
            "b": (5, at.a + at.other),
            "d": (6, at.d + at.other),
        }[which]
        for p in range(self.PIECES):
            self.wait(i, p, slot)

    def finish_sends(self):
        for cp in self.started:
            cp.wait_send()


class PlaneScatter:
    def __init__(self, at, emit, bufs, sems, pieces):
        self.at, self.emit, self.pieces = at, emit, pieces
        self.out, self.landed = bufs
        self.send, self.recv = sems
        self.started = []

    def columns(self, t):
        width = self.landed.shape[2] // self.pieces
        return slice(t * width, (t + 1) * width)

    def copy(self, i, t, src, mate):
        k = i * self.pieces + t
        dst = self.landed.at[i, :, self.columns(t)]
        cp = remote(src, dst, self.send.at[k], self.recv.at[k], (mate, self.at.f))
        cp.start()
        self.started.append(cp)

    def wait(self, i, t):
        k = i * self.pieces + t
        block = self.landed.at[i, :, self.columns(t)]
        remote(block, block, self.send.at[k], self.recv.at[k], (self.at.s, self.at.f)).wait_recv()

    def others(self):
        at = self.at
        return (at.d + at.other, at.b + at.other, at.s, at.a + at.other)

    def to_other(self, i):
        for t in range(self.pieces):
            columns = self.columns(t)
            self.emit(self.others()[i], columns, self.out.at[i], [])
            self.copy(i, t, self.out.at[i, :, columns], self.at.s)

    def onward(self, i, index, extras, mate):
        for t in range(self.pieces):
            columns = self.columns(t)
            for extra in extras:
                self.wait(extra, t)
            self.emit(index, columns, self.out.at[i], [self.landed.at[extra] for extra in extras])
            self.copy(i, t, self.out.at[i, :, columns], mate)

    def first(self, total):
        at = self.at
        self.to_other(0)
        self.to_other(1)
        self.onward(4, at.d, [0], at.a)
        self.onward(5, at.a, [1], at.a)
        self.to_other(3)
        self.to_other(2)
        for t in range(self.pieces):
            self.wait(2, t)
            self.emit(at.c, self.columns(t), total, [self.landed.at[2]])

    def second(self):
        self.onward(6, self.at.b, [3, 4], self.at.b)

    def last(self):
        for i in (5, 6):
            for t in range(self.pieces):
                self.wait(i, t)
        return self.landed.at[5], self.landed.at[6]

    def finish_sends(self):
        for cp in self.started:
            cp.wait_send()


class LineGather:
    COUNT = 3

    def __init__(self, at, own, slot, sems):
        self.at, self.own, self.slot = at, own, slot
        self.send, self.recv = sems
        self.started = []

    def copy(self, i, src, slot, mate):
        cp = remote(src, self.slot(slot), self.send.at[i], self.recv.at[i], (self.at.c, mate))
        cp.start()
        self.started.append(cp)

    def wait(self, i, slot):
        block = self.slot(slot)
        remote(block, block, self.send.at[i], self.recv.at[i], (self.at.c, self.at.f1)).wait_recv()

    def start(self):
        at = self.at
        self.copy(1, self.own, at.f, at.f2)
        self.copy(0, self.own, at.f, at.f1)

    def relay(self):
        at = self.at
        self.wait(1, at.f2)
        self.copy(2, self.slot(at.f2), at.f2, at.f1)

    def finish(self):
        self.wait(0, self.at.f1)
        self.wait(2, self.at.f3)

    def finish_sends(self):
        for cp in self.started:
            cp.wait_send()


class LineScatter:
    COUNT = 3

    def __init__(self, at, part, landed, sems, base=0):
        self.at, self.part, self.landed, self.base = at, part, landed, base
        self.send, self.recv = sems
        self.started = []

    def copy(self, i, src, mate):
        k = self.base + i
        cp = remote(src, self.landed.at[i], self.send.at[k], self.recv.at[k], (self.at.c, mate))
        cp.start()
        self.started.append(cp)

    def wait(self, i):
        k = self.base + i
        block = self.landed.at[i]
        remote(block, block, self.send.at[k], self.recv.at[k], (self.at.c, self.at.f1)).wait_recv()

    def start(self):
        at = self.at
        self.copy(0, self.part(at.f3), at.f1)

    def rest(self):
        self.copy(1, self.part(self.at.f1), self.at.f1)

    def add(self, dst, refs):
        count = dst.shape[0]
        step = min(count, 128) if len(dst.shape) == 2 else 1

        def piece(i, carry):
            rows = pl.ds(pl.multiple_of(i * step, step), step) if len(dst.shape) == 2 else pl.ds(i, 1)
            value = refs[0][rows].astype(F32)
            for ref in refs[1:]:
                value = value + ref[rows].astype(F32)
            dst[rows] = value.astype(dst.dtype)
            return carry

        lax.fori_loop(0, count // step, piece, 0)

    def relay(self):
        self.wait(0)
        self.pass_on()

    def pass_on(self):
        at = self.at
        self.add(self.part(at.f2), [self.part(at.f2), self.landed.at[0]])
        self.copy(2, self.part(at.f2), at.f2)

    def finish(self, dst):
        self.wait(1)
        self.wait(2)
        self.add(dst, [self.part(self.at.f), self.landed.at[1], self.landed.at[2]])

    def finish_sends(self):
        for cp in self.started:
            cp.wait_send()


def exchange(at, src_of, dst, slot_of, sems):
    send, recv = sems
    started, waits = [], []
    for j in range(1, at.n_ctx):
        peer, source = at.ctx_peer(j), at.ctx_source(j)
        device = (peer, at.f)
        cp = remote(src_of(peer), slot_of(dst, at.c), send.at[j], recv.at[j], device)
        cp.start()
        started.append(cp)
        block = slot_of(dst, source)
        waits.append(remote(block, block, send.at[j], recv.at[j], device))
    return started, waits


def turn(values_in, cosine, sine):
    return values_in * cosine + pltpu.roll(values_in, HEAD_PAD // 2, 1) * sine


def store_rows(ref, first, lanes, value):
    block_rows, done = ref.shape[1], 0
    while done < value.shape[0]:
        block, start = divmod(first + done, block_rows)
        count = min(block_rows - start, value.shape[0] - done)
        ref[block, start : start + count, lanes] = value[done : done + count]
        done += count


def product_emit(lhs_of, rhs_of):
    def emit(index, columns, dst, extras):
        value = rhs_of(lhs_of(index), columns)
        for extra in extras:
            value = value + extra[:, columns].astype(F32)
        dst[:, columns] = value.astype(dst.dtype)

    return emit


def front_kernel(
    n_ctx, n_fsdp,
    x, og, wq, wk, wv, wout, wg, wu, wd_own, gain_a, gain_b, inv, pairs, expand, cosine, sine,
    d_gate, d_down, dgain,
    ni_out, heads_out, kt_out, ot_out, ao_out, lse_out, wqkv_out, wo_out, gains_out, rm_out, du_out, mlp_out, gm_all, g_mid_out,
    du_first,
    ni, heads, kt, vt, ot, ao, lse, wqkv, wo, gains, rm, x_all, wblk, w_raw, wo_raw, gt, gz, gz_sum, gc, nm_own, total,
    rs_out, rs_in, nm, ogv, wgu, wd, dd, du, dg_in, dd_in,
    x_send, x_recv, og_send, og_recv, rs_send, rs_recv,
    wc_send, wc_recv, wz_send, wz_recv, oz_send, oz_recv, gz_send, gz_recv, gc_send, gc_recv,
    fg_send, fg_recv, fu_send, fu_recv, fd_send, fd_recv, zg_send, zg_recv, zd_send, zd_recv, up_send, up_recv, local_sem,
):
    at = Place(n_ctx, n_fsdp)
    rows, width = x.shape
    half = rows // 2
    seq_len = rows * n_ctx
    own_rows = w_raw.shape[2]
    at.greet(True)
    local = LocalCopies(local_sem)
    part_cols = n_fsdp * 128

    def gate_slot(i):
        return wgu.at[:, pl.ds(pl.multiple_of(i * 128, 128), 128)]

    def up_slot(i):
        return wgu.at[:, pl.ds(pl.multiple_of(part_cols + i * 128, 128), 128)]

    for src, dst in ((og, ogv.at[at.c]), (wg, gate_slot(at.f)), (wu, up_slot(at.f)), (wd_own, wd.at[at.f])):
        local.start("own", src, dst)
    q_cols, kv_cols = wq.shape[1] // n_ctx, wk.shape[1] // n_ctx
    for i in range(n_ctx):
        parts = (wq[:, i * q_cols : (i + 1) * q_cols], *(w[:, i * kv_cols : (i + 1) * kv_cols] for w in (wk, wv)))
        wblk[i] = jnp.concatenate(parts, axis=1)
    place = (at.c * n_fsdp + at.f) * own_rows
    from_lane = lax.broadcasted_iota(jnp.int32, (own_rows, width), 0)
    to_lane = lax.broadcasted_iota(jnp.int32, (own_rows, width), 1)
    spread = jnp.where(to_lane == from_lane + place, 1.0, 0.0).astype(BF)
    row = lax.broadcasted_iota(jnp.int32, (16, width), 0)
    spread_gains = [dot(jnp.broadcast_to(g[...], (16, own_rows)), spread) for g in (gain_a, gain_b)]
    gt[...] = jnp.where(row == 0, spread_gains[0], jnp.where(row == 1, spread_gains[1], 0.0)).astype(BF)
    at.wait_greeted()

    wc_copies, wc_waits = exchange(
        at, lambda p: wblk.at[p], w_raw, lambda r, i: r.at[i, at.f], (wc_send, wc_recv)
    )
    zt = LineGather(at, gt, lambda i: gz.at[i], (gz_send, gz_recv))
    zt.start()
    gx = PlaneGather(at, x, x_all, (x_send, x_recv))
    gx.start()
    zo = LineGather(at, wout, lambda i: wo_raw.at[i], (oz_send, oz_recv))
    zo.start()
    w_raw[at.c, at.f] = wblk[at.c]
    wo_raw[at.f] = wout[...]
    gz[at.f] = gt[...]
    x_all[at.c] = x[...]
    zt.relay()
    zt.finish()
    gz_sum[...] = sum(gz[i].astype(F32) for i in range(n_fsdp)).astype(BF)
    gc_copies, gc_waits = exchange(at, lambda p: gz_sum, gc, lambda r, i: r.at[i], (gc_send, gc_recv))
    gc[at.c] = gz_sum[...]
    for w in wc_waits:
        w.wait_recv()
    zw = LineGather(at, w_raw.at[:, at.f], lambda i: w_raw.at[:, i], (wz_send, wz_recv))
    zw.start()
    gx.pass_a()
    gx.pass_b()
    zw.relay()
    zo.relay()
    ffn = [
        LineGather(at, wg, gate_slot, (fg_send, fg_recv)),
        LineGather(at, wu, up_slot, (fu_send, fu_recv)),
        LineGather(at, wd_own, lambda i: wd.at[i], (fd_send, fd_recv)),
    ]
    ffn[0].start()
    go = PlaneGather(at, og, ogv, (og_send, og_recv))
    go.start()
    for w in gc_waits:
        w.wait_recv()
    gains[...] = sum(gc[i].astype(F32) for i in range(n_ctx))
    gain_one = gains[0:1, :]

    def norm_in(slot):
        def part(r, carry):
            start = pl.multiple_of(r * 48, 16)
            part_rows = x_all[slot, pl.ds(start, 48), :].astype(F32)
            scale = lax.rsqrt(jnp.mean(part_rows * part_rows, axis=-1, keepdims=True) + EPS)
            inside = pl.multiple_of(lax.rem(r, 2) * 48, 16)
            ni[2 * slot + lax.div(r, 2), pl.ds(inside, 48), :] = (part_rows * scale * gain_one).astype(BF)
            return carry

        lax.fori_loop(0, rows // 48, part, 0)

    norm_in(at.c)
    gx.wait_other("own")
    norm_in(at.s)
    norm_in(at.a)
    norm_in(at.b)
    gx.pass_d()
    norm_in(at.d)
    gx.wait_other("a")
    norm_in(at.b + at.other)
    gx.wait_other("b")
    norm_in(at.a + at.other)
    gx.wait_other("d")
    norm_in(at.d + at.other)
    local.start("ni", ni, ni_out)
    ffn[1].start()
    local.start("out", gains, gains_out)
    zw.finish()

    def widen(i, carry):
        part = w_raw[pl.ds(2 * i, 2)].reshape(2 * n_fsdp * own_rows, w_raw.shape[3])
        start = pl.multiple_of(i * 2 * n_fsdp * own_rows, 128)
        wqkv[pl.ds(start, 2 * n_fsdp * own_rows), :] = dot(part, expand[...]).astype(BF)
        return carry

    lax.fori_loop(0, n_ctx // 2, widen, 0)

    def project(g, carry):
        lhs = jnp.concatenate([ni[inv[4 * g + i]] for i in range(4)], axis=0)
        lin = dot(lhs, wqkv[...])
        span = pl.ds(pl.multiple_of(g * 4 * half, 128), 4 * half)
        cos_part, sin_part = cosine[span, :], sine[span, :]
        heads[0, span, :] = turn(lin[:, 0:128], cos_part, sin_part).astype(BF)
        heads[1, span, :] = turn(lin[:, 128:256], cos_part, sin_part).astype(BF)
        k_part = turn(lin[:, 256:384], cos_part, sin_part).astype(BF)
        v_part = lin[:, 384:512].astype(BF)
        heads[2, span, :] = k_part
        heads[3, span, :] = v_part
        kt[:, span] = jnp.transpose(k_part.astype(F32)).astype(BF)
        vt[:, span] = jnp.transpose(v_part.astype(F32)).astype(BF)
        return carry

    lax.fori_loop(0, seq_len // (4 * half), project, 0)
    local.start("heads", heads, heads_out)
    for src, dst in ((kt, kt_out), (wqkv, wqkv_out)):
        local.start("out", src, dst)

    block = 256
    score_scale = HEAD_DIM ** (-0.5) * LOG2E
    for i in range(seq_len // block):
        first = i * block

        def head_step(h, carry, first=first):
            span = slice(first, first + block)
            q_part = heads[h, span, :]
            diag = dot(heads[2, span, :], q_part, NT) * score_scale
            key_id = lax.broadcasted_iota(jnp.int32, (block, block), 0)
            query_id = lax.broadcasted_iota(jnp.int32, (block, block), 1)
            diag = jnp.where(key_id <= query_id, diag, NEG_FILL)
            top = jnp.max(diag, axis=0, keepdims=True)
            if first:
                past = dot(heads[2, 0:first, :], q_part, NT) * score_scale
                top = jnp.maximum(top, jnp.max(past, axis=0, keepdims=True))
            diag_p = jnp.exp2(diag - top)
            norm = jnp.sum(diag_p, axis=0, keepdims=True)
            acc = dot(vt[:, span], diag_p.astype(BF))
            if first:
                past_p = jnp.exp2(past - top)
                norm = norm + jnp.sum(past_p, axis=0, keepdims=True)
                acc = acc + dot(vt[:, 0:first], past_p.astype(BF))
            acc = acc / norm
            ot[h, :, span] = acc
            lse[h, :, span] = jnp.broadcast_to(top + jnp.log2(norm), (8, block))
            lanes = pl.ds(pl.multiple_of(h * HEAD_PAD, HEAD_PAD), HEAD_PAD)
            store_rows(ao, first, lanes, jnp.transpose(acc).astype(BF))
            return carry

        lax.fori_loop(0, 2, head_step, 0)
        if i == 4:
            go.pass_a()
            go.pass_b()

    for src, dst in ((ot, ot_out), (ao, ao_out), (lse, lse_out)):
        local.start("out", src, dst)
    zo.finish()
    ffn[0].relay()
    ffn[2].start()
    raw = wo_raw[...].reshape(2 * HEAD_DIM, width)
    pad_rows = jnp.zeros((HEAD_PAD - HEAD_DIM, width), BF)
    wo[0:96, :] = raw[0:96]
    wo[96:128, :] = pad_rows
    wo[128:224, :] = raw[96:192]
    wo[224:256, :] = pad_rows
    local.start("out", wo, wo_out)

    def attn_rows(index):
        pair = pairs[index]
        return jnp.concatenate([ao[pair], ao[2 * n_ctx - 1 - pair]], axis=0)

    emit = product_emit(attn_rows, lambda lhs, columns: dot(lhs, wo[:, columns]))
    sc = PlaneScatter(at, emit, (rs_out, rs_in), (rs_send, rs_recv), 3)
    sc.first(total)
    go.pass_d()
    sc.second()
    ffn[1].relay()
    go.wait_other("own")
    go.wait_other("a")
    go.wait_other("b")
    go.wait_other("d")
    more, most = sc.last()
    gain_two = gains[1:2, :]

    gx.finish_sends()
    gn = PlaneGather(at, nm_own, nm, (x_send, x_recv))
    for p in range(gn.PIECES):
        span = slice(p * gn.rows, (p + 1) * gn.rows)
        mid = x[span, :].astype(F32) + total[span, :] + more[span, :].astype(F32) + most[span, :].astype(F32)
        scale = lax.rsqrt(jnp.mean(mid * mid, axis=-1, keepdims=True) + EPS)
        rm[span, :] = mid
        normed_mid = (mid * scale * gain_two).astype(BF)
        nm_own[span, :] = normed_mid
        gn.start_piece(p)
        nm[at.c, span, :] = normed_mid
    local.start("rm", rm, rm_out)
    ffn[2].relay()
    gn.pass_a()
    gn.pass_b()
    sc.finish_sends()
    local.wait("own")
    for part in ffn[:2]:
        part.finish()
    gn.pass_d()

    def feed(mate):
        i = lax.div(mate, 2)
        both = dot(nm[pl.ds(2 * i, 2)].reshape(2 * rows, width), wgu[...])
        gate, up = both[:, :part_cols], both[:, part_cols:]
        sigma = 1.0 / (1.0 + jnp.exp(-gate))
        act = gate * sigma
        from_gate = up * sigma * (1.0 + gate * (1.0 - sigma))
        for start, value in ((0, act * up), (part_cols, from_gate), (2 * part_cols, act)):
            x_all[pl.ds(2 * i, 2), :, start : start + part_cols] = value.astype(BF).reshape(2, rows, part_cols)

    def feed_back(i, carry):
        g_hidden = dot(ogv[pl.ds(2 * i, 2)].reshape(2 * rows, width), wd[...].reshape(part_cols, width), NT)
        for start in (part_cols, 2 * part_cols):
            factor = x_all[pl.ds(2 * i, 2), :, start : start + part_cols].reshape(2 * rows, part_cols).astype(F32)
            x_all[pl.ds(2 * i, 2), :, start : start + part_cols] = (
                (g_hidden * factor).astype(BF).reshape(2, rows, part_cols)
            )
        return carry

    gn.wait_other("own")
    feed(at.c)
    gn.wait_other("b")
    feed(at.a)
    gn.wait_other("a")
    feed(at.b)
    gn.wait_other("d")
    feed(at.d)
    local.wait("heads", "ni")
    dg = heads

    for i in range(part_cols // 256):
        value = dot(
            x_all[:, :, i * 256 : (i + 1) * 256].reshape(n_ctx * rows, 256), ogv[...].reshape(n_ctx * rows, width), TN
        )
        dd[2 * i : 2 * i + 2] = value.astype(BF).reshape(2, 128, width)
    zd = LineScatter(at, lambda i: dd.at[i], dd_in, (zd_send, zd_recv))
    zd.start()
    zd.rest()
    ffn[2].finish()
    lax.fori_loop(0, n_ctx // 2, feed_back, 0)
    emit = product_emit(lambda index: x_all[index, :, part_cols:], lambda lhs, columns: dot(lhs, wgu[columns, :], NT))
    sc = PlaneScatter(at, emit, (rs_out, rs_in), (rs_send, rs_recv), 3)
    sc.first(total)

    def gate_up_grad(t, carry):
        cols = pl.ds(pl.multiple_of(t * 256, 256), 256)
        value = dot(
            nm[:, :, cols].reshape(n_ctx * rows, 256), x_all[:, :, part_cols:].reshape(n_ctx * rows, 2 * part_cols), TN
        ).astype(BF)
        for i in range(n_fsdp):
            dg[i, cols, :] = value[:, i * 128 : (i + 1) * 128]
            du[i, cols, :] = value[:, part_cols + i * 128 : part_cols + (i + 1) * 128]
        return carry

    zg = []
    for part in range(2):
        lax.fori_loop(part * width // 512, (part + 1) * width // 512, gate_up_grad, 0)
        half_rows = pl.ds(part * width // 2, width // 2)
        zg.append(
            LineScatter(
                at, lambda i, h=half_rows: dg.at[i, h], dg_in.at[:, half_rows], (zg_send, zg_recv), 3 * part
            )
        )
        zg[part].start()
        zg[part].rest()
        if part == 0:
            zd.relay()
    local.start("out", du, du_out)
    sc.second()

    more, most = sc.last()
    local.wait("rm")
    gn.finish_sends()
    g_mid, gm_own = rm, nm_own
    gm = PlaneGather(at, gm_own, gm_all, (x_send, x_recv))
    gain_part = jnp.zeros((8, width), F32)
    for p in range(gm.PIECES):
        span = slice(p * gm.rows, (p + 1) * gm.rows)
        grad = total[span, :] + more[span, :].astype(F32) + most[span, :].astype(F32)
        mid = rm[span, :]
        scale = lax.rsqrt(jnp.mean(mid * mid, axis=-1, keepdims=True) + EPS)
        normed = mid * scale
        scaled = grad * gain_two
        back = og[span, :].astype(F32) + scale * (scaled - normed * jnp.mean(scaled * normed, axis=-1, keepdims=True))
        g_mid[span, :] = back
        gm_own[span, :] = back.astype(BF)
        gm.start_piece(p)
        gain_part = gain_part + jnp.sum((grad * normed).reshape(gm.rows // 8, 8, width), axis=0)
    dgain[...] = gain_part
    local.start("out", gm_own, gm_all.at[at.c])
    local.start("out", g_mid, g_mid_out)

    zg[0].relay()

    def down(i, carry):
        part = x_all[pl.ds(2 * i, 2), :, 0:part_cols].reshape(2 * rows, part_cols)
        ni[pl.ds(4 * i, 4)] = dot(part, wd[...].reshape(part_cols, width)).astype(BF).reshape(4, half, width)
        return carry

    lax.fori_loop(0, n_ctx // 2, down, 0)
    local.start("out", ni, mlp_out)
    zg[1].relay()
    gm.pass_a()
    gm.pass_b()
    up_ahead = remote(du.at[at.f3], du_first, up_send.at[0], up_recv.at[0], (at.c, at.f1))
    up_ahead.start()
    gm.pass_d()
    for which in ("own", "a", "b", "d"):
        gm.wait_other(which)
    local.wait_all()
    up_ahead.wait()
    zd.finish(d_down)
    for part in range(2):
        zg[part].finish(d_gate.at[pl.ds(part * width // 2, width // 2)])
    for part in (go, zt, zo, zw, *ffn, sc, gm, zd, *zg):
        part.finish_sends()
    for copies in (wc_copies, gc_copies):
        for cp in copies:
            cp.wait_send()


def backward_kernel(
    n_ctx, n_fsdp,
    gm_in, ao_in, heads_in, kt_in, ot_in, lse_in, wo_in, ni_in, wqkv_in, x_in, g_mid_in, gains_in, rm_in, mlp,
    dgain, du_in_all, du_first, inv, pairs, expand_in, cosine_in, sine_in,
    mixed, tgrad, dqkv, dwout, dgain_out, d_up,
    gm_all, ao, heads, kt, ot, lse, wo, ni, wqkv, x, g_mid, gains, rm, du, expand, cosine, sine,
    ga, gat, delta, dwo, dwo_out, dwo_in, du_in, dk, dv, gq, gqc, dw, dw_in, dw_sum, dw_own, mine, mixed_total, total,
    ms_out, ms_in, rs_out, rs_in, dgc, dgz, dg_sum,
    ms_send, ms_recv, rs_send, rs_recv, oz_send, oz_recv, gz_send, gz_recv, gc_send, gc_recv,
    wz_send, wz_recv, wc_send, wc_recv, zu_send, zu_recv, local_sem,
):
    at = Place(n_ctx, n_fsdp)
    rows, width = x.shape
    half = rows // 2
    seq_len = rows * n_ctx
    own_rows = dw.shape[2]
    at.greet(True)
    local = LocalCopies(local_sem)
    for name, src, dst in (
        ("grad", gm_in, gm_all), ("grad", wo_in, wo), ("grad", ao_in, ao), ("grad", ot_in, ot),
        ("attn", heads_in, heads), ("attn", kt_in, kt), ("attn", lse_in, lse),
        ("attn", cosine_in, cosine), ("attn", sine_in, sine),
        ("mlp", mlp.at[at.d], mine.at[0]), ("mlp", mlp.at[at.a], mine.at[1]),
        ("mlp", mlp.at[at.c], mine.at[2]), ("mlp", mlp.at[at.b], mine.at[3]),
        ("weight", ni_in, ni), ("weight", expand_in, expand), ("weight", wqkv_in, wqkv),
        ("up", du_in_all, du), ("up", du_first, du_in.at[0]), ("last", x_in, x), ("last", g_mid_in, g_mid), ("last", gains_in, gains), ("last", rm_in, rm),
    ):
        local.start(name, src, dst)
    at.wait_greeted()

    ms = PlaneScatter(at, None, (ms_out, ms_in), (ms_send, ms_recv), 1)
    for i, index in enumerate(ms.others()):
        ms.copy(i, 0, mlp.at[index], at.s)
    zu = LineScatter(at, lambda i: du_in_all.at[i], du_in, (zu_send, zu_recv))
    zu.rest()
    zu.part = lambda i: du.at[i]
    gc_copies, gc_waits = exchange(at, lambda p: dgain, dgc, lambda r, i: r.at[i], (gc_send, gc_recv))
    dgc[at.c] = dgain[...]

    def add_blocks(index, dst, extras):
        i = index

        def part(r, carry):
            span = pl.ds(pl.multiple_of(r * 48, 16), 48)
            value = mine[i, span, :].astype(F32)
            for extra in extras:
                value = value + extra[span, :].astype(F32)
            dst[span, :] = value.astype(dst.dtype)
            return carry

        lax.fori_loop(0, rows // 48, part, 0)

    def attn_grad(g, carry):
        gm_part = jnp.concatenate([gm_all[inv[4 * g + i]] for i in range(4)], axis=0)
        span = pl.ds(pl.multiple_of(g * 4 * half, 128), 4 * half)
        low = dot(gm_part, wo[...], NT).astype(BF)
        for h in range(2):
            part = low[:, h * HEAD_PAD : (h + 1) * HEAD_PAD]
            ga[h, span, :] = part
            turned = jnp.transpose(part.astype(F32))
            gat[h, :, span] = turned.astype(BF)
            delta[h, :, span] = jnp.broadcast_to(
                jnp.sum(turned * ot[h, :, span], axis=0, keepdims=True), (8, 4 * half)
            )
        dwo[...] += dot(ao[pl.ds(4 * g, 4)].reshape(4 * half, 2 * HEAD_PAD), gm_part, TN)
        return carry

    dwo[...] = jnp.zeros_like(dwo)
    local.wait("up")
    zu.pass_on()
    local.wait("grad")
    lax.fori_loop(0, seq_len // (4 * half), attn_grad, 0)
    low = jnp.concatenate([dwo[0:96, :], dwo[128:224, :]], axis=0).astype(BF)
    dwo_out[...] = low.reshape(dwo_out.shape)
    zo = LineScatter(at, lambda i: dwo_out.at[i], dwo_in, (oz_send, oz_recv))
    zo.start()
    zo.rest()
    local.wait("mlp")
    ms.wait(0, 0)
    add_blocks(0, ms_out.at[0], [ms_in.at[0]])
    ms.copy(4, 0, ms_out.at[0], at.a)
    ms.wait(1, 0)
    add_blocks(1, ms_out.at[1], [ms_in.at[1]])
    ms.copy(5, 0, ms_out.at[1], at.a)
    ms.wait(2, 0)
    add_blocks(2, mixed_total, [ms_in.at[2]])

    for w in gc_waits:
        w.wait_recv()
    dg_sum[...] = sum(dgc[i] for i in range(n_ctx))
    zg = LineGather(at, dg_sum, lambda i: dgz.at[i], (gz_send, gz_recv))
    zg.start()
    dgz[at.f] = dg_sum[...]

    local.wait("attn")
    dk[...] = jnp.zeros_like(dk)
    dv[...] = jnp.zeros_like(dv)
    block = 256
    plain_scale = HEAD_DIM ** (-0.5)
    score_scale = plain_scale * LOG2E
    for i in range(seq_len // block):
        first = i * block

        def head_step(h, carry, first=first):
            span = slice(first, first + block)
            q_part, ga_part, gat_part = heads[h, span, :], ga[h, span, :], gat[h, :, span]
            top = lse[h, 0:1, span]
            shift = delta[h, 0:1, span]

            def piece(keys, masked):
                scores = dot(heads[2, keys, :], q_part, NT) * score_scale - top
                if masked:
                    key_id = lax.broadcasted_iota(jnp.int32, (block, block), 0)
                    query_id = lax.broadcasted_iota(jnp.int32, (block, block), 1)
                    scores = jnp.where(key_id <= query_id, scores, NEG_FILL)
                prob = jnp.exp2(scores)
                grad = (prob * (dot(heads[3, keys, :], gat_part) - shift)).astype(BF)
                dv[keys, :] += dot(prob.astype(BF), ga_part)
                dk[keys, :] += dot(grad, q_part)
                return dot(kt[:, keys], grad)

            turned = piece(span, True)
            if first:
                turned = turned + piece(slice(0, first), False)
            lanes = pl.ds(pl.multiple_of(h * HEAD_PAD, HEAD_PAD), HEAD_PAD)
            grad_q = jnp.transpose(turned) * plain_scale
            store_rows(gq, first, lanes, turn(grad_q, cosine[span, :], -sine[span, :]).astype(BF))
            return carry

        lax.fori_loop(0, 2, head_step, 0)
        if i == 2:
            ms.wait(3, 0)
            ms.wait(4, 0)
            add_blocks(3, ms_out.at[2], [ms_in.at[3], ms_in.at[4]])
            ms.copy(6, 0, ms_out.at[2], at.b)
    zo.relay()

    def key_rows(g, carry):
        span = pl.ds(pl.multiple_of(g * 4 * half, 128), 4 * half)
        grad_k = turn(dk[span, :] * plain_scale, cosine[span, :], -sine[span, :]).astype(BF)
        gq[pl.ds(4 * g, 4), :, 256:384] = grad_k.reshape(4, half, HEAD_PAD)
        gq[pl.ds(4 * g, 4), :, 384:512] = dv[span, :].astype(BF).reshape(4, half, HEAD_PAD)
        return carry

    lax.fori_loop(0, seq_len // (4 * half), key_rows, 0)

    def to_ctx(slot, carry):
        pair = pairs[slot]
        gqc[2 * slot] = gq[pair]
        gqc[2 * slot + 1] = gq[2 * n_ctx - 1 - pair]
        return carry

    lax.fori_loop(0, n_ctx, to_ctx, 0)
    local.wait("weight", "last")

    def weight_grad(t, carry):
        tile = 2 * n_fsdp * own_rows
        cols = pl.ds(pl.multiple_of(t * tile, 128), tile)
        value = dot(ni[:, :, cols].reshape(seq_len, tile), gqc[...].reshape(seq_len, 4 * HEAD_PAD), TN)
        low = dot(value.astype(BF), expand[...], NT).astype(BF)
        dw[pl.ds(2 * t, 2)] = low.reshape(2, n_fsdp, own_rows, low.shape[1])
        return carry

    zw = []
    for part in range(2):
        lax.fori_loop(part * n_ctx // 4, (part + 1) * n_ctx // 4, weight_grad, 0)
        rows_of = pl.ds(part * n_ctx // 2, n_ctx // 2)
        zw.append(
            LineScatter(
                at, lambda i, r=rows_of: dw.at[r, i], dw_in.at[:, rows_of], (wz_send, wz_recv), 3 * part
            )
        )
        zw[part].start()
        zw[part].rest()

    emit = product_emit(
        lambda index: gqc[pl.ds(2 * index, 2)].reshape(rows, 4 * HEAD_PAD),
        lambda lhs, columns: dot(lhs, wqkv[columns, :], NT),
    )
    sc = PlaneScatter(at, emit, (rs_out, rs_in), (rs_send, rs_recv), 3)
    sc.first(total)
    sc.second()
    zw[0].relay()
    zw[1].relay()
    zg.relay()
    for part in range(2):
        zw[part].finish(dw_sum.at[pl.ds(part * n_ctx // 2, n_ctx // 2)])
    wc_copies, wc_waits = exchange(
        at, lambda p: dw_sum.at[p], dw_own, lambda r, i: r.at[i], (wc_send, wc_recv)
    )
    dw_own[at.c] = dw_sum[at.c]
    mixed_more, mixed_most = ms.last()

    def mixed_rows(r, carry):
        span = pl.ds(pl.multiple_of(r * 48, 16), 48)
        value = rm[span, :] + mixed_total[span, :]
        value = value + mixed_more[span, :].astype(F32) + mixed_most[span, :].astype(F32)
        mixed[span, :] = value.astype(BF)
        return carry

    lax.fori_loop(0, rows // 48, mixed_rows, 0)
    zg.finish()
    dgain_out[...] = sum(dgz[i] for i in range(n_fsdp))

    more, most = sc.last()
    gain_one = gains[0:1, :]

    def finish_rows(r, carry):
        span = pl.ds(pl.multiple_of(r * 48, 16), 48)
        grad = total[span, :] + more[span, :].astype(F32) + most[span, :].astype(F32)
        held = x[span, :].astype(F32)
        scale = lax.rsqrt(jnp.mean(held * held, axis=-1, keepdims=True) + EPS)
        normed = held * scale
        scaled = grad * gain_one
        back = g_mid[span, :] + scale * (scaled - normed * jnp.mean(scaled * normed, axis=-1, keepdims=True))
        tgrad[span, :] = back.astype(BF)
        return carry

    lax.fori_loop(0, rows // 48, finish_rows, 0)
    zu.finish(d_up)
    zo.finish(dwout)
    for w in wc_waits:
        w.wait_recv()
    dqkv[...] = dw_own[...]
    for part in (ms, sc, zu, zo, zg, *zw):
        part.finish_sends()
    for copies in (gc_copies, wc_copies):
        for cp in copies:
            cp.wait_send()


def head_spread():
    spread = np.zeros((4 * HEAD_DIM, 4 * HEAD_PAD), np.float32)
    for head in range(4):
        for j in range(HEAD_DIM):
            lane = j if head == 3 or j < HEAD_DIM // 2 else j + HEAD_PAD // 2 - HEAD_DIM // 2
            spread[head * HEAD_DIM + j, head * HEAD_PAD + lane] = 1.0
    return spread


def turn_tables(seq_len):
    half_dim = HEAD_DIM // 2
    freqs = np.float32(THETA) ** (-(np.arange(half_dim, dtype=np.float32) * np.float32(2.0 / HEAD_DIM)))
    angle = np.arange(seq_len, dtype=np.float32)[:, None] * freqs[None, :].astype(np.float32)
    gap = np.zeros((seq_len, HEAD_PAD // 2 - half_dim), np.float32)
    cosine, sine = np.cos(angle).astype(np.float32), np.sin(angle).astype(np.float32)
    return (
        np.concatenate([cosine, gap, cosine, gap], axis=1),
        np.concatenate([-sine, gap, sine, gap], axis=1),
    )


def tail_kernel(
    n_ctx, n_fsdp,
    dqkv, wq, wk, wv, gain_a, dgain, mixed_in, tgrad_in, dwout_in, dgate_in, dup_in, ddown_in,
    dq, dk, dv, gain_one, gain_two, mixed, tgrad, dwout, dgate, dup, ddown,
    mixed_held, tgrad_held, dwout_held, dgate_held, dup_held, ddown_held, sem,
):
    moves = (
        (mixed_in, mixed_held, mixed), (tgrad_in, tgrad_held, tgrad), (dwout_in, dwout_held, dwout),
        (dgate_in, dgate_held, dgate), (dup_in, dup_held, dup), (ddown_in, ddown_held, ddown),
    )
    loads = [pltpu.make_async_copy(src, held, sem.at[i]) for i, (src, held, _) in enumerate(moves)]
    for cp in loads:
        cp.start()
    stores = []
    for i, (_, held, dst) in enumerate(moves):
        loads[i].wait()
        stores.append(pltpu.make_async_copy(held, dst, sem.at[len(moves) + i]))
        stores[i].start()
    own_rows = wq.shape[0]
    q_cols, kv_cols = wq.shape[1] // n_ctx, wk.shape[1] // n_ctx
    got = [dqkv[i].astype(F32) for i in range(n_ctx)]
    query = jnp.concatenate([g[:, :q_cols] for g in got], axis=1)
    key = jnp.concatenate([g[:, q_cols : q_cols + kv_cols] for g in got], axis=1)
    value = jnp.concatenate([g[:, q_cols + kv_cols :] for g in got], axis=1)
    dq[...] = query
    dk[...] = key
    dv[...] = value
    both = sum(
        jnp.sum(g * w[...].astype(F32), axis=1, keepdims=True) for g, w in ((query, wq), (key, wk), (value, wv))
    )
    row = jnp.transpose(jnp.broadcast_to(both, (own_rows, 128)))[0:1, :]
    gain_one[...] = row / gain_a[...].astype(F32)
    place = (lax.axis_index("ctx") * n_fsdp + lax.axis_index("fsdp")) * own_rows
    width = dgain.shape[1]
    gain = jnp.broadcast_to(jnp.sum(dgain[...], axis=0, keepdims=True), (8, width))
    gain_two[...] = pltpu.roll(gain, width - place, 1)[0:1, :own_rows]
    for cp in stores:
        cp.wait()


def sems(*counts):
    return [pltpu.SemaphoreType.DMA((n,)) for n in counts for _ in range(2)]


VM = pl.BlockSpec(memory_space=pltpu.VMEM)
SM = pl.BlockSpec(memory_space=pltpu.SMEM)
HB = pl.BlockSpec(memory_space=pl.ANY)


def plane(tokens, out_grad, pair_table, attn_gain, w_query, w_key, w_value, w_out, mlp_gain, w_gate, w_up, w_down):
    n_ctx, n_fsdp = lax.axis_size("ctx"), lax.axis_size("fsdp")
    rows, width = tokens.shape
    half = rows // 2
    seq_len = rows * n_ctx
    own_rows = w_query.shape[0]
    pairs = pair_table[0]
    ids = jnp.arange(2 * n_ctx, dtype=jnp.int32)[:, None]
    early = 2 * jnp.arange(n_ctx, dtype=jnp.int32)[None, :]
    late_or_not = jnp.where(2 * n_ctx - 1 - pairs[None, :] == ids, early + 1, 0)
    inv = jnp.sum(jnp.where(pairs[None, :] == ids, early, late_or_not), axis=1)

    gain_a, gain_b = attn_gain.reshape(1, own_rows), mlp_gain.reshape(1, own_rows)
    expand = jnp.asarray(head_spread(), BF)
    cosine, sine = (jnp.asarray(table) for table in turn_tables(seq_len))

    def sds(shape, dtype):
        return jax.ShapeDtypeStruct(shape, dtype)

    blocks = (n_ctx, rows, width)
    vm = pltpu.VMEM
    part_cols = n_fsdp * 128
    front = pl.pallas_call(
        functools.partial(front_kernel, n_ctx, n_fsdp),
        out_shape=(
            sds(w_gate.shape, F32),
            sds(w_down.shape, F32),
            sds((8, width), F32),
            sds((2 * n_ctx, half, width), BF),
            sds((4, seq_len, HEAD_PAD), BF),
            sds((HEAD_PAD, seq_len), BF),
            sds((2, HEAD_PAD, seq_len), F32),
            sds((2 * n_ctx, half, 2 * HEAD_PAD), BF),
            sds((2, 8, seq_len), F32),
            sds((width, 4 * HEAD_PAD), BF),
            sds((2 * HEAD_PAD, width), BF),
            sds((16, width), F32),
            sds((rows, width), F32),
            sds((n_fsdp, *w_up.shape), BF),
            sds((2 * n_ctx, half, width), BF),
            sds(blocks, BF),
            sds((rows, width), F32),
            sds(w_up.shape, BF),
        ),
        in_specs=[VM] * 6 + [HB] * 3 + [VM, VM, SM, SM, VM, VM, VM],
        out_specs=(VM,) * 3 + (HB,) * 15,
        scratch_shapes=[
            vm((2 * n_ctx, half, width), BF),
            vm((4, seq_len, HEAD_PAD), BF),
            vm((HEAD_PAD, seq_len), BF),
            vm((HEAD_PAD, seq_len), BF),
            vm((2, HEAD_PAD, seq_len), F32),
            vm((2 * n_ctx, half, 2 * HEAD_PAD), BF),
            vm((2, 8, seq_len), F32),
            vm((width, 4 * HEAD_PAD), BF),
            vm((2 * HEAD_PAD, width), BF),
            vm((16, width), F32),
            vm((rows, width), F32),
            vm(blocks, BF),
            vm((n_ctx, own_rows, 4 * HEAD_DIM), BF),
            vm((n_ctx, n_fsdp, own_rows, 4 * HEAD_DIM), BF),
            vm((n_fsdp, own_rows, width), BF),
            vm((16, width), BF),
            vm((n_fsdp, 16, width), BF),
            vm((16, width), BF),
            vm((n_ctx, 16, width), BF),
            vm((rows, width), BF),
            vm((rows, width), F32),
            vm((7, rows, width), BF),
            vm((7, rows, width), BF),
            vm(blocks, BF),
            vm(blocks, BF),
            vm((width, 2 * part_cols), BF),
            vm((n_fsdp, *w_down.shape), BF),
            vm((n_fsdp, *w_down.shape), BF),
            vm((n_fsdp, *w_up.shape), BF),
            vm((3, *w_gate.shape), BF),
            vm((3, *w_down.shape), BF),
            *sems(21, 21, 21, n_ctx, 3, 3, 3, n_ctx, 3, 3, 3, 6, 3, 1),
            pltpu.SemaphoreType.DMA((18,)),
        ],
        compiler_params=pltpu.CompilerParams(
            collective_id=0, has_side_effects=True, vmem_limit_bytes=FRONT_VMEM_LIMIT
        ),
        name="forward_and_feed_forward",
    )
    d_gate, d_down, dgain, ni, heads, kt, ot, ao, lse, wqkv, wo, gains, rm, du, mlp, gm_all, g_mid, du_first = front(
        tokens, out_grad, w_query, w_key, w_value, w_out, w_gate, w_up, w_down, gain_a, gain_b, inv, pairs, expand, cosine, sine
    )

    backward = pl.pallas_call(
        functools.partial(backward_kernel, n_ctx, n_fsdp),
        out_shape=(
            sds((rows, width), BF),
            sds((rows, width), BF),
            sds((n_ctx, own_rows, 4 * HEAD_DIM), BF),
            sds((own_rows, width), F32),
            sds((8, width), F32),
            sds(w_up.shape, F32),
        ),
        in_specs=[HB] * 14 + [VM, HB, HB, SM, SM, HB, HB, HB],
        out_specs=(VM,) * 6,
        scratch_shapes=[
            vm((2 * n_ctx, half, width), BF),
            vm((2 * n_ctx, half, 2 * HEAD_PAD), BF),
            vm((4, seq_len, HEAD_PAD), BF),
            vm((HEAD_PAD, seq_len), BF),
            vm((2, HEAD_PAD, seq_len), F32),
            vm((2, 8, seq_len), F32),
            vm((2 * HEAD_PAD, width), BF),
            vm((2 * n_ctx, half, width), BF),
            vm((width, 4 * HEAD_PAD), BF),
            vm((rows, width), BF),
            vm((rows, width), F32),
            vm((16, width), F32),
            vm((rows, width), F32),
            vm((n_fsdp, *w_up.shape), BF),
            vm((4 * HEAD_DIM, 4 * HEAD_PAD), BF),
            vm((seq_len, HEAD_PAD), F32),
            vm((seq_len, HEAD_PAD), F32),
            vm((2, seq_len, HEAD_PAD), BF),
            vm((2, HEAD_PAD, seq_len), BF),
            vm((2, 8, seq_len), F32),
            vm((2 * HEAD_PAD, width), F32),
            vm((n_fsdp, own_rows, width), BF),
            vm((3, own_rows, width), BF),
            vm((3, *w_up.shape), BF),
            vm((seq_len, HEAD_PAD), F32),
            vm((seq_len, HEAD_PAD), F32),
            vm((2 * n_ctx, half, 4 * HEAD_PAD), BF),
            vm((2 * n_ctx, half, 4 * HEAD_PAD), BF),
            vm((n_ctx, n_fsdp, own_rows, 4 * HEAD_DIM), BF),
            vm((3, n_ctx, own_rows, 4 * HEAD_DIM), BF),
            vm((n_ctx, own_rows, 4 * HEAD_DIM), BF),
            vm((n_ctx, own_rows, 4 * HEAD_DIM), BF),
            vm((4, rows, width), BF),
            vm((rows, width), F32),
            vm((rows, width), F32),
            vm((3, rows, width), BF),
            vm((7, rows, width), BF),
            vm((7, rows, width), BF),
            vm((7, rows, width), BF),
            vm((n_ctx, 8, width), F32),
            vm((n_fsdp, 8, width), F32),
            vm((8, width), F32),
            *sems(7, 21, 3, 3, n_ctx, 6, n_ctx, 3),
            pltpu.SemaphoreType.DMA((22,)),
        ],
        compiler_params=pltpu.CompilerParams(
            collective_id=1, has_side_effects=True, vmem_limit_bytes=VMEM_LIMIT
        ),
        name="attention_backward",
    )
    mixed, tokens_grad, dqkv, d_out, d_gain_two, d_up = backward(
        gm_all.reshape(2 * n_ctx, half, width), ao, heads, kt, ot, lse, wo, ni, wqkv, tokens, g_mid, gains, rm,
        mlp.reshape(blocks), dgain, du, du_first, inv, pairs, expand, cosine, sine,
    )
    tail = pl.pallas_call(
        functools.partial(tail_kernel, n_ctx, n_fsdp),
        out_shape=(
            sds(w_query.shape, F32),
            sds(w_key.shape, F32),
            sds(w_value.shape, F32),
            sds((1, own_rows), F32),
            sds((1, own_rows), F32),
            sds((rows, width), BF),
            sds((rows, width), BF),
            sds(w_out.shape, F32),
            sds(w_gate.shape, F32),
            sds(w_up.shape, F32),
            sds(w_down.shape, F32),
        ),
        in_specs=[VM] * 6 + [HB] * 6,
        out_specs=(VM,) * 5 + (HB,) * 6,
        scratch_shapes=[
            vm((rows, width), BF),
            vm((rows, width), BF),
            vm(w_out.shape, F32),
            vm(w_gate.shape, F32),
            vm(w_up.shape, F32),
            vm(w_down.shape, F32),
            pltpu.SemaphoreType.DMA((12,)),
        ],
        compiler_params=pltpu.CompilerParams(vmem_limit_bytes=VMEM_LIMIT),
        name="layouts",
    )
    d_query, d_key, d_value, gain_one_grad, gain_two_grad, mixed, tokens_grad, d_out, d_gate, d_up, d_down = tail(
        dqkv, w_query, w_key, w_value, gain_a, d_gain_two, mixed, tokens_grad, d_out, d_gate, d_up, d_down
    )
    return (
        mixed, tokens_grad, gain_one_grad.reshape(-1), d_query, d_key, d_value, d_out, gain_two_grad.reshape(-1),
        d_gate, d_up, d_down,
    )


def solution(mesh):
    in_specs = (
        P(("ctx", "fsdp"), None),
        P(("ctx", "fsdp"), None),
        P("fsdp", None),
        P(("ctx", "fsdp")),
        P(("ctx", "fsdp"), None),
        P(("ctx", "fsdp"), None),
        P(("ctx", "fsdp"), None),
        P(("ctx", "fsdp"), None),
        P(("ctx", "fsdp")),
        P(None, ("ctx", "fsdp")),
        P(None, ("ctx", "fsdp")),
        P(("ctx", "fsdp"), None),
    )
    out_specs = (
        P(("ctx", "fsdp"), None),
        P(("ctx", "fsdp"), None),
        P(("ctx", "fsdp")),
        P(("ctx", "fsdp"), None),
        P(("ctx", "fsdp"), None),
        P(("ctx", "fsdp"), None),
        P(("ctx", "fsdp"), None),
        P(("ctx", "fsdp")),
        P(None, ("ctx", "fsdp")),
        P(None, ("ctx", "fsdp")),
        P(("ctx", "fsdp"), None),
    )
    fits = (
        mesh.shape["ctx"] == KV_HEADS
        and mesh.shape["fsdp"] == 4
        and HEADS == 2 * KV_HEADS
    )
    return jax.shard_map(plane if fits else local, mesh=mesh, in_specs=in_specs, out_specs=out_specs, check_vma=False)
```

```python
import functools
import math

import jax
import jax.numpy as jnp
import numpy as np
from jax import lax
from jax.experimental import pallas as pl
from jax.experimental.pallas import tpu as pltpu
from jax.sharding import PartitionSpec as P

HEADS = 16
KV_HEADS = 8
HEAD_DIM = 96


EPS = 1e-05
THETA = 100000.0
NEG_FILL = -1e30


def rotate(values_in, positions, direction):
    half_dim = values_in.shape[-1] // 2
    freqs = THETA ** (-(jnp.arange(half_dim, dtype=jnp.float32) * 2.0 / values_in.shape[-1]))
    angle = positions.astype(jnp.float32)[:, None] * freqs[None, :]
    cosine = jnp.cos(angle)[:, None, :]
    sine = direction * jnp.sin(angle)[:, None, :]
    first_half = values_in[..., :half_dim]
    second_half = values_in[..., half_dim:]
    return jnp.concatenate(
        [first_half * cosine - second_half * sine, second_half * cosine + first_half * sine],
        axis=-1,
    )


def place_rows(pair_index, tok_rows, block_count):
    half_rows = tok_rows // 2
    offsets = jnp.arange(tok_rows, dtype=jnp.int32)
    early = pair_index * half_rows + offsets
    late = (block_count - 1 - pair_index) * half_rows + offsets - half_rows
    return jnp.where(offsets < half_rows, early, late)


def rms_scale(values_in):
    return lax.rsqrt(jnp.mean(values_in * values_in, axis=-1, keepdims=True) + EPS)


def norm_back(grad_normed, normed, inv_rms, gain):
    scaled = grad_normed * gain
    return inv_rms * (scaled - normed * jnp.mean(scaled * normed, axis=-1, keepdims=True))


def local(
    tokens,
    out_grad,
    pair_table,
    attn_gain,
    w_query,
    w_key,
    w_value,
    w_out,
    mlp_gain,
    w_gate,
    w_up,
    w_down,
):
    tok_rows = tokens.shape[0]
    half_rows = tok_rows // 2
    ctx_count = lax.axis_size("ctx")
    half_count = 2 * ctx_count
    pair_row = pair_table[0]
    my_pos = place_rows(pair_row[lax.axis_index("ctx")], tok_rows, half_count)
    half_blocks = jnp.stack([pair_row, half_count - 1 - pair_row], axis=1).reshape(-1)
    block_ids = jnp.arange(half_count, dtype=jnp.int32)
    inverse = jnp.sum(
        jnp.where(half_blocks[None, :] == block_ids[:, None], block_ids[None, :], 0), axis=1
    )
    group_size = HEADS // KV_HEADS
    score_scale = HEAD_DIM ** (-0.5)
    query_width = HEADS * HEAD_DIM
    kv_width = KV_HEADS * HEAD_DIM
    w_query_all, w_key_all, w_value_all, w_out_all, gain_first, gain_second = (
        lax.all_gather(w_query, ("ctx", "fsdp"), axis=0, tiled=True),
        lax.all_gather(w_key, ("ctx", "fsdp"), axis=0, tiled=True),
        lax.all_gather(w_value, ("ctx", "fsdp"), axis=0, tiled=True),
        lax.all_gather(w_out, ("ctx", "fsdp"), axis=0, tiled=True),
        lax.all_gather(attn_gain, ("ctx", "fsdp"), axis=0, tiled=True),
        lax.all_gather(mlp_gain, ("ctx", "fsdp"), axis=0, tiled=True),
    )
    gain_one = gain_first.astype(jnp.float32)
    gain_two = gain_second.astype(jnp.float32)
    resid_in = tokens.astype(jnp.float32)
    inv_one = rms_scale(resid_in)
    normed_one = resid_in * inv_one
    normed_in = (normed_one * gain_one).astype(jnp.bfloat16)
    query_lin = jnp.dot(normed_in, w_query_all, preferred_element_type=jnp.float32)
    key_lin = jnp.dot(normed_in, w_key_all, preferred_element_type=jnp.float32)
    value_lin = jnp.dot(normed_in, w_value_all, preferred_element_type=jnp.float32)
    query_rot = rotate(query_lin.reshape(tok_rows, HEADS, HEAD_DIM), my_pos, 1.0).astype(
        jnp.bfloat16
    )
    key_rot = (
        rotate(key_lin.reshape(tok_rows, KV_HEADS, HEAD_DIM), my_pos, 1.0)
        .astype(jnp.bfloat16)
        .reshape(tok_rows, kv_width)
    )
    value_low = value_lin.astype(jnp.bfloat16)
    keys_got, values_got = (
        lax.all_gather(key_rot, "ctx", axis=0, tiled=True),
        lax.all_gather(value_low, "ctx", axis=0, tiled=True),
    )
    seq_len = keys_got.shape[0]
    keys_all = jnp.take(keys_got.reshape(half_count, half_rows, kv_width), inverse, axis=0).reshape(
        seq_len, kv_width
    )
    values_all = jnp.take(
        values_got.reshape(half_count, half_rows, kv_width), inverse, axis=0
    ).reshape(seq_len, kv_width)
    key_pos = jnp.arange(seq_len, dtype=jnp.int32)
    key_block = math.gcd(seq_len, 512)
    live_blocks = jnp.max(my_pos) // key_block + 1
    query_grp = query_rot.reshape(tok_rows, KV_HEADS, group_size, HEAD_DIM)

    def block_scores(block_index):
        first_row = block_index * key_block
        key_tile = lax.dynamic_slice_in_dim(keys_all, first_row, key_block, 0).reshape(
            key_block, KV_HEADS, HEAD_DIM
        )
        value_tile = lax.dynamic_slice_in_dim(values_all, first_row, key_block, 0).reshape(
            key_block, KV_HEADS, HEAD_DIM
        )
        scores = (
            jnp.einsum("tkgd,skd->kgts", query_grp, key_tile, preferred_element_type=jnp.float32)
            * score_scale
        )
        visible = (
            lax.dynamic_slice_in_dim(key_pos, first_row, key_block, 0)[None, :] <= my_pos[:, None]
        )
        return (scores, visible, key_tile, value_tile)

    def stats_step(block_index, carry):
        run_max, run_sum = carry
        scores, visible, key_tile, value_tile = block_scores(block_index)
        masked = jnp.where(visible, scores, NEG_FILL)
        new_max = jnp.maximum(run_max, jnp.max(masked, axis=-1))
        weights = jnp.where(visible, jnp.exp(masked - new_max[..., None]), 0.0)
        return (new_max, run_sum * jnp.exp(run_max - new_max) + jnp.sum(weights, axis=-1))

    start_max = jnp.full((KV_HEADS, group_size, tok_rows), NEG_FILL, jnp.float32)
    run_max, run_sum = lax.fori_loop(
        0, live_blocks, stats_step, (start_max, jnp.zeros_like(start_max))
    )
    log_total = run_max + jnp.log(run_sum)

    def probs(scores, visible):
        return jnp.where(visible, jnp.exp(scores - log_total[..., None]), 0.0)

    def output_step(block_index, accum):
        scores, visible, key_tile, value_tile = block_scores(block_index)
        prob_low = probs(scores, visible).astype(jnp.bfloat16)
        return accum + jnp.einsum(
            "kgts,skd->kgtd", prob_low, value_tile, preferred_element_type=jnp.float32
        )

    attn_acc = lax.fori_loop(
        0,
        live_blocks,
        output_step,
        jnp.zeros((KV_HEADS, group_size, tok_rows, HEAD_DIM), jnp.float32),
    )
    attn_low = attn_acc.transpose(2, 0, 1, 3).reshape(tok_rows, query_width).astype(jnp.bfloat16)
    resid_mid = resid_in + jnp.dot(attn_low, w_out_all, preferred_element_type=jnp.float32)
    inv_two = rms_scale(resid_mid)
    normed_two = resid_mid * inv_two
    normed_mid = (normed_two * gain_two).astype(jnp.bfloat16)
    w_gate_part, w_up_part, w_down_part = (
        lax.all_gather(w_gate, ("ctx", "fsdp"), axis=1, tiled=True),
        lax.all_gather(w_up, ("ctx", "fsdp"), axis=1, tiled=True),
        lax.all_gather(w_down, ("ctx", "fsdp"), axis=0, tiled=True),
    )
    gate_lin = jnp.dot(normed_mid, w_gate_part, preferred_element_type=jnp.float32)
    up_lin = jnp.dot(normed_mid, w_up_part, preferred_element_type=jnp.float32)
    sigma = jax.nn.sigmoid(gate_lin)
    activated = gate_lin * sigma
    hidden_low = (activated * up_lin).astype(jnp.bfloat16)
    mlp_branch = jnp.dot(hidden_low, w_down_part, preferred_element_type=jnp.float32)
    mixed = (resid_mid + mlp_branch).astype(jnp.bfloat16)
    grad_top = out_grad.astype(jnp.float32)
    d_down = jnp.einsum("tf,td->fd", hidden_low, out_grad, preferred_element_type=jnp.float32)
    grad_hidden = jnp.einsum("td,fd->tf", out_grad, w_down_part, preferred_element_type=jnp.float32)
    grad_gate = (grad_hidden * up_lin * sigma * (1.0 + gate_lin * (1.0 - sigma))).astype(
        jnp.bfloat16
    )
    grad_up = (grad_hidden * activated).astype(jnp.bfloat16)
    d_gate = jnp.einsum("td,tf->df", normed_mid, grad_gate, preferred_element_type=jnp.float32)
    d_up = jnp.einsum("td,tf->df", normed_mid, grad_up, preferred_element_type=jnp.float32)
    grad_normed_mid = jnp.einsum(
        "tf,df->td", grad_gate, w_gate_part, preferred_element_type=jnp.float32
    ) + jnp.einsum("tf,df->td", grad_up, w_up_part, preferred_element_type=jnp.float32)
    gate_grad_out, up_grad_out, down_grad_out = (
        lax.psum_scatter(d_gate, ("ctx", "fsdp"), scatter_dimension=1, tiled=True),
        lax.psum_scatter(d_up, ("ctx", "fsdp"), scatter_dimension=1, tiled=True),
        lax.psum_scatter(d_down, ("ctx", "fsdp"), scatter_dimension=0, tiled=True),
    )
    d_gain_two = jnp.sum(grad_normed_mid * normed_two, axis=0)
    grad_mid = grad_top + norm_back(grad_normed_mid, normed_two, inv_two, gain_two)
    grad_mid_low = grad_mid.astype(jnp.bfloat16)
    d_out = jnp.einsum("tq,td->qd", attn_low, grad_mid_low, preferred_element_type=jnp.float32)
    grad_attn_low = jnp.einsum(
        "td,qd->tq", grad_mid_low, w_out_all, preferred_element_type=jnp.float32
    ).astype(jnp.bfloat16)
    grad_heads = grad_attn_low.reshape(tok_rows, KV_HEADS, group_size, HEAD_DIM).transpose(
        1, 2, 0, 3
    )
    row_delta = jnp.sum(grad_heads.astype(jnp.float32) * attn_acc, axis=-1)

    def back_step(block_index, carry):
        grad_query, grad_keys, grad_values = carry
        scores, visible, key_tile, value_tile = block_scores(block_index)
        prob_full = probs(scores, visible)
        prob_low = prob_full.astype(jnp.bfloat16)
        grad_prob = jnp.einsum(
            "kgtd,skd->kgts", grad_heads, value_tile, preferred_element_type=jnp.float32
        )
        grad_score = (prob_full * (grad_prob - row_delta[..., None])).astype(jnp.bfloat16)
        grad_query = grad_query + score_scale * jnp.einsum(
            "kgts,skd->kgtd", grad_score, key_tile, preferred_element_type=jnp.float32
        )
        key_part = score_scale * jnp.einsum(
            "kgts,tkgd->skd", grad_score, query_grp, preferred_element_type=jnp.float32
        )
        value_part = jnp.einsum(
            "kgts,kgtd->skd", prob_low, grad_heads, preferred_element_type=jnp.float32
        )
        first_row = block_index * key_block
        grad_keys = lax.dynamic_update_slice_in_dim(
            grad_keys, key_part.reshape(key_block, kv_width), first_row, 0
        )
        grad_values = lax.dynamic_update_slice_in_dim(
            grad_values, value_part.reshape(key_block, kv_width), first_row, 0
        )
        return (grad_query, grad_keys, grad_values)

    empty_keys = jnp.zeros((seq_len, kv_width), jnp.float32)
    grad_query, grad_keys, grad_values = lax.fori_loop(
        0,
        live_blocks,
        back_step,
        (
            jnp.zeros((KV_HEADS, group_size, tok_rows, HEAD_DIM), jnp.float32),
            empty_keys,
            empty_keys,
        ),
    )
    keys_back = jnp.take(
        grad_keys.reshape(half_count, half_rows, kv_width), half_blocks, axis=0
    ).reshape(seq_len, kv_width)
    values_back = jnp.take(
        grad_values.reshape(half_count, half_rows, kv_width), half_blocks, axis=0
    ).reshape(seq_len, kv_width)
    own_keys, own_values = (
        lax.psum_scatter(
            keys_back.astype(jnp.bfloat16), "ctx", scatter_dimension=0, tiled=True
        ).astype(jnp.float32),
        lax.psum_scatter(
            values_back.astype(jnp.bfloat16), "ctx", scatter_dimension=0, tiled=True
        ).astype(jnp.float32),
    )
    grad_query_lin = rotate(
        grad_query.transpose(2, 0, 1, 3).reshape(tok_rows, HEADS, HEAD_DIM), my_pos, -1.0
    )
    grad_query_low = grad_query_lin.reshape(tok_rows, query_width).astype(jnp.bfloat16)
    grad_key_lin = rotate(own_keys.reshape(tok_rows, KV_HEADS, HEAD_DIM), my_pos, -1.0)
    grad_key_low = grad_key_lin.reshape(tok_rows, kv_width).astype(jnp.bfloat16)
    grad_value_low = own_values.astype(jnp.bfloat16)
    d_query = jnp.einsum("td,tq->dq", normed_in, grad_query_low, preferred_element_type=jnp.float32)
    d_key = jnp.einsum("td,tq->dq", normed_in, grad_key_low, preferred_element_type=jnp.float32)
    d_value = jnp.einsum("td,tq->dq", normed_in, grad_value_low, preferred_element_type=jnp.float32)
    grad_normed_in = (
        jnp.einsum("tq,dq->td", grad_query_low, w_query_all, preferred_element_type=jnp.float32)
        + jnp.einsum("tq,dq->td", grad_key_low, w_key_all, preferred_element_type=jnp.float32)
        + jnp.einsum("tq,dq->td", grad_value_low, w_value_all, preferred_element_type=jnp.float32)
    )
    d_gain_one = jnp.sum(grad_normed_in * normed_one, axis=0)
    grad_input = grad_mid + norm_back(grad_normed_in, normed_one, inv_one, gain_one)
    query_grad_out, key_grad_out, value_grad_out, out_grad_out, gain_one_out, gain_two_out = (
        lax.psum_scatter(d_query, ("ctx", "fsdp"), scatter_dimension=0, tiled=True),
        lax.psum_scatter(d_key, ("ctx", "fsdp"), scatter_dimension=0, tiled=True),
        lax.psum_scatter(d_value, ("ctx", "fsdp"), scatter_dimension=0, tiled=True),
        lax.psum_scatter(d_out, ("ctx", "fsdp"), scatter_dimension=0, tiled=True),
        lax.psum_scatter(d_gain_one, ("ctx", "fsdp"), scatter_dimension=0, tiled=True),
        lax.psum_scatter(d_gain_two, ("ctx", "fsdp"), scatter_dimension=0, tiled=True),
    )
    return (
        mixed,
        grad_input.astype(jnp.bfloat16),
        gain_one_out,
        query_grad_out,
        key_grad_out,
        value_grad_out,
        out_grad_out,
        gain_two_out,
        gate_grad_out,
        up_grad_out,
        down_grad_out,
    )


BF = jnp.bfloat16
F32 = jnp.float32
MESH = pl.DeviceIdType.MESH
HEAD_PAD = 128
LOG2E = 1.4426950408889634
VMEM_LIMIT = 58 * 2**20
FRONT_VMEM_LIMIT = 61 * 2**20
NT = (((1,), (1,)), ((), ()))
TN = (((0,), (0,)), ((), ()))


def dot(a, b, dims=(((1,), (0,)), ((), ()))):
    return lax.dot_general(a, b, dims, preferred_element_type=F32)


class Place:
    def __init__(self, n_ctx, n_fsdp):
        self.n_ctx, self.n_fsdp = n_ctx, n_fsdp
        self.c, self.f = lax.axis_index("ctx"), lax.axis_index("fsdp")
        core = lax.rem(self.c, 2)
        step_x = 2 - 4 * lax.rem(lax.div(self.c, 2), 2)
        step_y = 4 - 8 * lax.div(self.c, 4)
        self.other = 1 - 2 * core
        self.s = self.c + self.other
        self.a = self.c + step_x * (1 - core) + step_y * core
        self.b = self.c + step_x * core + step_y * (1 - core)
        self.d = self.c + step_x + step_y
        self.f1 = self.f + 1 - 2 * lax.rem(self.f, 2)
        self.f2 = self.f + 2 - 4 * lax.div(self.f, 2)
        self.f3 = n_fsdp - 1 - self.f

    def ctx_peer(self, j):
        return lax.rem(self.c + j, self.n_ctx)

    def ctx_source(self, j):
        return lax.rem(self.c + self.n_ctx - j, self.n_ctx)

    def greet(self, everyone):
        barrier = pltpu.get_barrier_semaphore()
        if everyone:
            mates = [(self.ctx_peer(j), self.f) for j in range(1, self.n_ctx)]
        else:
            mates = [(self.s, self.f), (self.a, self.f), (self.b, self.f)]
        mates += [(self.c, self.f1), (self.c, self.f2)]
        for mate in mates:
            pl.semaphore_signal(barrier, inc=1, device_id=mate, device_id_type=MESH)
        self.mates = len(mates)

    def wait_greeted(self):
        pl.semaphore_wait(pltpu.get_barrier_semaphore(), self.mates)


def block_slots(pairs, inv, n_ctx):
    for block in range(2 * n_ctx):
        slot = jnp.int32(0)
        for i in range(n_ctx):
            pair = pairs[0, i]
            slot = jnp.maximum(slot, jnp.where(pair == block, 2 * i, 0))
            slot = jnp.maximum(slot, jnp.where(2 * n_ctx - 1 - pair == block, 2 * i + 1, 0))
        inv[block] = slot


def remote(src, dst, send, recv, device):
    return pltpu.make_async_remote_copy(
        src_ref=src, dst_ref=dst, send_sem=send, recv_sem=recv, device_id=device, device_id_type=MESH
    )


class LocalCopies:
    def __init__(self, sems):
        self.sems, self.count, self.named = sems, 0, {}

    def start(self, name, src, dst):
        cp = pltpu.make_async_copy(src, dst, self.sems.at[self.count])
        cp.start()
        self.count += 1
        self.named.setdefault(name, []).append(cp)

    def wait(self, *names):
        for name in names:
            for cp in self.named.pop(name):
                cp.wait()

    def wait_all(self):
        self.wait(*list(self.named))


class PlaneGather:
    PIECES = 3
    COUNT = 7 * PIECES

    def __init__(self, at, own, blocks, sems):
        self.at, self.own, self.blocks = at, own, blocks
        self.send, self.recv = sems
        self.rows = own.shape[0] // self.PIECES
        self.started = []

    def piece(self, slot, p):
        return self.blocks.at[slot, pl.ds(p * self.rows, self.rows)]

    def copy(self, i, p, src, slot, mate):
        k = i * self.PIECES + p
        cp = remote(src, self.piece(slot, p), self.send.at[k], self.recv.at[k], (mate, self.at.f))
        cp.start()
        self.started.append(cp)

    def wait(self, i, p, slot):
        k = i * self.PIECES + p
        block = self.piece(slot, p)
        remote(block, block, self.send.at[k], self.recv.at[k], (self.at.s, self.at.f)).wait_recv()

    def start_piece(self, p):
        at = self.at
        src = self.own.at[pl.ds(p * self.rows, self.rows)]
        self.copy(1, p, src, at.c, at.a)
        self.copy(2, p, src, at.c, at.b)
        self.copy(0, p, src, at.c, at.s)

    def start(self):
        for p in range(self.PIECES):
            self.start_piece(p)

    def pass_a(self):
        at = self.at
        for p in range(self.PIECES):
            self.wait(1, p, at.a)
            self.copy(4, p, self.piece(at.a, p), at.a, at.b)
            self.copy(3, p, self.piece(at.a, p), at.a, at.s)

    def pass_b(self):
        at = self.at
        for p in range(self.PIECES):
            self.wait(2, p, at.b)
            self.copy(5, p, self.piece(at.b, p), at.b, at.s)

    def pass_d(self):
        at = self.at
        for p in range(self.PIECES):
            self.wait(4, p, at.d)
            self.copy(6, p, self.piece(at.d, p), at.d, at.s)

    def wait_other(self, which):
        at = self.at
        i, slot = {
            "own": (0, at.s),
            "a": (3, at.b + at.other),
            "b": (5, at.a + at.other),
            "d": (6, at.d + at.other),
        }[which]
        for p in range(self.PIECES):
            self.wait(i, p, slot)

    def finish_sends(self):
        for cp in self.started:
            cp.wait_send()


class PlaneScatter:
    def __init__(self, at, emit, bufs, sems, pieces):
        self.at, self.emit, self.pieces = at, emit, pieces
        self.out, self.landed = bufs
        self.send, self.recv = sems
        self.started = []

    def columns(self, t):
        width = self.landed.shape[2] // self.pieces
        return slice(t * width, (t + 1) * width)

    def copy(self, i, t, src, mate):
        k = i * self.pieces + t
        dst = self.landed.at[i, :, self.columns(t)]
        cp = remote(src, dst, self.send.at[k], self.recv.at[k], (mate, self.at.f))
        cp.start()
        self.started.append(cp)

    def wait(self, i, t):
        k = i * self.pieces + t
        block = self.landed.at[i, :, self.columns(t)]
        remote(block, block, self.send.at[k], self.recv.at[k], (self.at.s, self.at.f)).wait_recv()

    def others(self):
        at = self.at
        return (at.d + at.other, at.b + at.other, at.s, at.a + at.other)

    def to_other(self, i):
        for t in range(self.pieces):
            columns = self.columns(t)
            self.emit(self.others()[i], columns, self.out.at[i], [])
            self.copy(i, t, self.out.at[i, :, columns], self.at.s)

    def onward(self, i, index, extras, mate):
        for t in range(self.pieces):
            columns = self.columns(t)
            for extra in extras:
                self.wait(extra, t)
            self.emit(index, columns, self.out.at[i], [self.landed.at[extra] for extra in extras])
            self.copy(i, t, self.out.at[i, :, columns], mate)

    def first(self, total):
        at = self.at
        self.to_other(0)
        self.to_other(1)
        self.onward(4, at.d, [0], at.a)
        self.onward(5, at.a, [1], at.a)
        self.to_other(3)
        self.to_other(2)
        for t in range(self.pieces):
            self.wait(2, t)
            self.emit(at.c, self.columns(t), total, [self.landed.at[2]])

    def second(self):
        self.onward(6, self.at.b, [3, 4], self.at.b)

    def last(self):
        for i in (5, 6):
            for t in range(self.pieces):
                self.wait(i, t)
        return self.landed.at[5], self.landed.at[6]

    def finish_sends(self):
        for cp in self.started:
            cp.wait_send()


class LineGather:
    COUNT = 3

    def __init__(self, at, own, slot, sems):
        self.at, self.own, self.slot = at, own, slot
        self.send, self.recv = sems
        self.started = []

    def copy(self, i, src, slot, mate):
        cp = remote(src, self.slot(slot), self.send.at[i], self.recv.at[i], (self.at.c, mate))
        cp.start()
        self.started.append(cp)

    def wait(self, i, slot):
        block = self.slot(slot)
        remote(block, block, self.send.at[i], self.recv.at[i], (self.at.c, self.at.f1)).wait_recv()

    def start_far(self):
        self.copy(1, self.own, self.at.f, self.at.f2)

    def start_near(self):
        self.copy(0, self.own, self.at.f, self.at.f1)

    def start(self):
        self.start_far()
        self.start_near()

    def relay(self):
        at = self.at
        self.wait(1, at.f2)
        self.copy(2, self.slot(at.f2), at.f2, at.f1)

    def finish(self):
        self.wait(0, self.at.f1)
        self.wait(2, self.at.f3)

    def finish_sends(self):
        for cp in self.started:
            cp.wait_send()


class LineScatter:
    COUNT = 3

    def __init__(self, at, part, landed, sems, base=0):
        self.at, self.part, self.landed, self.base = at, part, landed, base
        self.send, self.recv = sems
        self.started = []

    def copy(self, i, src, mate):
        k = self.base + i
        cp = remote(src, self.landed.at[i], self.send.at[k], self.recv.at[k], (self.at.c, mate))
        cp.start()
        self.started.append(cp)

    def wait(self, i):
        k = self.base + i
        block = self.landed.at[i]
        remote(block, block, self.send.at[k], self.recv.at[k], (self.at.c, self.at.f1)).wait_recv()

    def start(self):
        at = self.at
        self.copy(0, self.part(at.f3), at.f1)

    def rest(self):
        self.copy(1, self.part(self.at.f1), self.at.f1)

    def add(self, dst, refs):
        count = dst.shape[0]
        step = min(count, 128) if len(dst.shape) == 2 else 1

        def piece(i, carry):
            rows = pl.ds(pl.multiple_of(i * step, step), step) if len(dst.shape) == 2 else pl.ds(i, 1)
            value = refs[0][rows].astype(F32)
            for ref in refs[1:]:
                value = value + ref[rows].astype(F32)
            dst[rows] = value.astype(dst.dtype)
            return carry

        lax.fori_loop(0, count // step, piece, 0)

    def relay(self):
        self.wait(0)
        self.pass_on()

    def pass_on(self):
        at = self.at
        self.add(self.part(at.f2), [self.part(at.f2), self.landed.at[0]])
        self.copy(2, self.part(at.f2), at.f2)

    def finish(self, dst):
        self.wait(1)
        self.wait(2)
        self.add(dst, [self.part(self.at.f), self.landed.at[1], self.landed.at[2]])

    def finish_sends(self):
        for cp in self.started:
            cp.wait_send()


def exchange(at, src_of, dst, slot_of, sems):
    send, recv = sems
    started, waits = [], []
    for j in range(1, at.n_ctx):
        peer, source = at.ctx_peer(j), at.ctx_source(j)
        device = (peer, at.f)
        cp = remote(src_of(peer), slot_of(dst, at.c), send.at[j], recv.at[j], device)
        cp.start()
        started.append(cp)
        block = slot_of(dst, source)
        waits.append(remote(block, block, send.at[j], recv.at[j], device))
    return started, waits


def turn(values_in, cosine, sine):
    return values_in * cosine + pltpu.roll(values_in, HEAD_PAD // 2, 1) * sine


def store_rows(ref, first, lanes, value):
    block_rows, done = ref.shape[1], 0
    while done < value.shape[0]:
        block, start = divmod(first + done, block_rows)
        count = min(block_rows - start, value.shape[0] - done)
        ref[block, start : start + count, lanes] = value[done : done + count]
        done += count


def product_emit(lhs_of, rhs_of):
    def emit(index, columns, dst, extras):
        value = rhs_of(lhs_of(index), columns)
        for extra in extras:
            value = value + extra[:, columns].astype(F32)
        dst[:, columns] = value.astype(dst.dtype)

    return emit


def front_kernel(
    n_ctx, n_fsdp,
    x, og, wq, wk, wv, wout, wg, wu, wd_own, gain_a, gain_b, pairs, expand_in, cosine_in, sine_in,
    d_gate, d_down, dgain,
    ni_out, heads_out, kt_out, ot_out, ao_out, lse_out, wqkv_out, wo_out, gains_out, rm_out, du_out, mlp_out, gm_all, g_mid_out,
    du_first,
    ni, heads, kt, vt, ot, ao, lse, wqkv, wo, gains, rm, x_all, wblk, w_raw, wo_raw, gt, gz, gz_sum, gc, nm_own, total,
    rs_out, rs_in, nm, ogv, wgu, wd, dd, du, dg_in, dd_in,
    x_send, x_recv, og_send, og_recv, rs_send, rs_recv,
    wc_send, wc_recv, wz_send, wz_recv, oz_send, oz_recv, gz_send, gz_recv, gc_send, gc_recv,
    fg_send, fg_recv, fu_send, fu_recv, fd_send, fd_recv, zg_send, zg_recv, zd_send, zd_recv, up_send, up_recv, local_sem, inv, expand, cosine, sine,
):
    at = Place(n_ctx, n_fsdp)
    rows, width = x.shape
    half = rows // 2
    seq_len = rows * n_ctx
    own_rows = w_raw.shape[2]
    at.greet(True)
    local = LocalCopies(local_sem)
    part_cols = n_fsdp * 128

    def gate_slot(i):
        return wgu.at[:, pl.ds(pl.multiple_of(i * 128, 128), 128)]

    def up_slot(i):
        return wgu.at[:, pl.ds(pl.multiple_of(part_cols + i * 128, 128), 128)]

    for src, dst in ((og, ogv.at[at.c]), (wg, gate_slot(at.f)), (wu, up_slot(at.f)), (wd_own, wd.at[at.f])):
        local.start("own", src, dst)
    for src, dst in ((expand_in, expand), (cosine_in, cosine), (sine_in, sine)):
        local.start("tables", src, dst)
    q_cols, kv_cols = wq.shape[1] // n_ctx, wk.shape[1] // n_ctx
    for i in range(n_ctx):
        parts = (wq[:, i * q_cols : (i + 1) * q_cols], *(w[:, i * kv_cols : (i + 1) * kv_cols] for w in (wk, wv)))
        wblk[i] = jnp.concatenate(parts, axis=1)
    place = (at.c * n_fsdp + at.f) * own_rows
    from_lane = lax.broadcasted_iota(jnp.int32, (own_rows, width), 0)
    to_lane = lax.broadcasted_iota(jnp.int32, (own_rows, width), 1)
    spread = jnp.where(to_lane == from_lane + place, 1.0, 0.0).astype(BF)
    row = lax.broadcasted_iota(jnp.int32, (16, width), 0)
    spread_gains = [dot(jnp.broadcast_to(g[...], (16, own_rows)), spread) for g in (gain_a, gain_b)]
    gt[...] = jnp.where(row == 0, spread_gains[0], jnp.where(row == 1, spread_gains[1], 0.0)).astype(BF)
    at.wait_greeted()

    wc_copies, wc_waits = exchange(
        at, lambda p: wblk.at[p], w_raw, lambda r, i: r.at[i, at.f], (wc_send, wc_recv)
    )
    zt = LineGather(at, gt, lambda i: gz.at[i], (gz_send, gz_recv))
    zt.start()
    gx = PlaneGather(at, x, x_all, (x_send, x_recv))
    gx.start()
    zo = LineGather(at, wout, lambda i: wo_raw.at[i], (oz_send, oz_recv))
    zo.start()
    w_raw[at.c, at.f] = wblk[at.c]
    wo_raw[at.f] = wout[...]
    gz[at.f] = gt[...]
    x_all[at.c] = x[...]
    zt.relay()
    zt.finish()
    gz_sum[...] = sum(gz[i].astype(F32) for i in range(n_fsdp)).astype(BF)
    gc_copies, gc_waits = exchange(at, lambda p: gz_sum, gc, lambda r, i: r.at[i], (gc_send, gc_recv))
    gc[at.c] = gz_sum[...]
    for w in wc_waits:
        w.wait_recv()
    zw = LineGather(at, w_raw.at[:, at.f], lambda i: w_raw.at[:, i], (wz_send, wz_recv))
    zw.start()
    gx.pass_a()
    gx.pass_b()
    zw.relay()
    zo.relay()
    ffn = [
        LineGather(at, wg, gate_slot, (fg_send, fg_recv)),
        LineGather(at, wu, up_slot, (fu_send, fu_recv)),
        LineGather(at, wd_own, lambda i: wd.at[i], (fd_send, fd_recv)),
    ]
    ffn[0].start_far()
    go = PlaneGather(at, og, ogv, (og_send, og_recv))
    go.start()
    for w in gc_waits:
        w.wait_recv()
    gains[...] = sum(gc[i].astype(F32) for i in range(n_ctx))
    gain_one = gains[0:1, :]

    def norm_in(slot):
        def part(r, carry):
            start = pl.multiple_of(r * 48, 16)
            part_rows = x_all[slot, pl.ds(start, 48), :].astype(F32)
            scale = lax.rsqrt(jnp.mean(part_rows * part_rows, axis=-1, keepdims=True) + EPS)
            inside = pl.multiple_of(lax.rem(r, 2) * 48, 16)
            ni[2 * slot + lax.div(r, 2), pl.ds(inside, 48), :] = (part_rows * scale * gain_one).astype(BF)
            return carry

        lax.fori_loop(0, rows // 48, part, 0)

    block_slots(pairs, inv, n_ctx)
    norm_in(at.c)
    gx.wait_other("own")
    norm_in(at.s)
    norm_in(at.a)
    norm_in(at.b)
    gx.pass_d()
    norm_in(at.d)
    gx.wait_other("a")
    norm_in(at.b + at.other)
    gx.wait_other("b")
    norm_in(at.a + at.other)
    gx.wait_other("d")
    norm_in(at.d + at.other)
    local.start("ni", ni, ni_out)
    ffn[0].start_near()
    ffn[1].start_far()
    local.start("out", gains, gains_out)
    local.wait("tables")
    zw.finish()

    def widen(i, carry):
        part = w_raw[pl.ds(2 * i, 2)].reshape(2 * n_fsdp * own_rows, w_raw.shape[3])
        start = pl.multiple_of(i * 2 * n_fsdp * own_rows, 128)
        wqkv[pl.ds(start, 2 * n_fsdp * own_rows), :] = dot(part, expand[...]).astype(BF)
        return carry

    lax.fori_loop(0, n_ctx // 2, widen, 0)

    def project(g, carry):
        lhs = jnp.concatenate([ni[inv[4 * g + i]] for i in range(4)], axis=0)
        lin = dot(lhs, wqkv[...])
        span = pl.ds(pl.multiple_of(g * 4 * half, 128), 4 * half)
        cos_part, sin_part = cosine[span, :], sine[span, :]
        heads[0, span, :] = turn(lin[:, 0:128], cos_part, sin_part).astype(BF)
        heads[1, span, :] = turn(lin[:, 128:256], cos_part, sin_part).astype(BF)
        k_part = turn(lin[:, 256:384], cos_part, sin_part).astype(BF)
        v_part = lin[:, 384:512].astype(BF)
        heads[2, span, :] = k_part
        heads[3, span, :] = v_part
        kt[:, span] = jnp.transpose(k_part.astype(F32)).astype(BF)
        vt[:, span] = jnp.transpose(v_part.astype(F32)).astype(BF)
        return carry

    lax.fori_loop(0, seq_len // (4 * half), project, 0)
    local.start("heads", heads, heads_out)
    for src, dst in ((kt, kt_out), (wqkv, wqkv_out)):
        local.start("out", src, dst)

    block = 256
    score_scale = HEAD_DIM ** (-0.5) * LOG2E
    for i in range(seq_len // block):
        first = i * block

        def head_step(h, carry, first=first):
            span = slice(first, first + block)
            q_part = heads[h, span, :]
            diag = dot(heads[2, span, :], q_part, NT) * score_scale
            key_id = lax.broadcasted_iota(jnp.int32, (block, block), 0)
            query_id = lax.broadcasted_iota(jnp.int32, (block, block), 1)
            diag = jnp.where(key_id <= query_id, diag, NEG_FILL)
            top = jnp.max(diag, axis=0, keepdims=True)
            if first:
                past = dot(heads[2, 0:first, :], q_part, NT) * score_scale
                top = jnp.maximum(top, jnp.max(past, axis=0, keepdims=True))
            diag_p = jnp.exp2(diag - top)
            norm = jnp.sum(diag_p, axis=0, keepdims=True)
            acc = dot(vt[:, span], diag_p.astype(BF))
            if first:
                past_p = jnp.exp2(past - top)
                norm = norm + jnp.sum(past_p, axis=0, keepdims=True)
                acc = acc + dot(vt[:, 0:first], past_p.astype(BF))
            acc = acc / norm
            ot[h, :, span] = acc
            lse[h, :, span] = jnp.broadcast_to(top + jnp.log2(norm), (8, block))
            lanes = pl.ds(pl.multiple_of(h * HEAD_PAD, HEAD_PAD), HEAD_PAD)
            store_rows(ao, first, lanes, jnp.transpose(acc).astype(BF))
            return carry

        lax.fori_loop(0, 2, head_step, 0)
        if i == 4:
            go.pass_a()
            go.pass_b()

    for src, dst in ((ot, ot_out), (ao, ao_out), (lse, lse_out)):
        local.start("out", src, dst)
    zo.finish()
    ffn[0].relay()
    ffn[1].start_near()
    ffn[2].start_far()
    raw = wo_raw[...].reshape(2 * HEAD_DIM, width)
    pad_rows = jnp.zeros((HEAD_PAD - HEAD_DIM, width), BF)
    wo[0:96, :] = raw[0:96]
    wo[96:128, :] = pad_rows
    wo[128:224, :] = raw[96:192]
    wo[224:256, :] = pad_rows
    local.start("out", wo, wo_out)

    def attn_rows(index):
        pair = pairs[0, index]
        return jnp.concatenate([ao[pair], ao[2 * n_ctx - 1 - pair]], axis=0)

    emit = product_emit(attn_rows, lambda lhs, columns: dot(lhs, wo[:, columns]))
    sc = PlaneScatter(at, emit, (rs_out, rs_in), (rs_send, rs_recv), 3)
    sc.first(total)
    go.pass_d()
    sc.second()
    ffn[1].relay()
    ffn[2].start_near()
    go.wait_other("own")
    go.wait_other("a")
    go.wait_other("b")
    go.wait_other("d")
    more, most = sc.last()
    gain_two = gains[1:2, :]

    gx.finish_sends()
    gn = PlaneGather(at, nm_own, nm, (x_send, x_recv))
    for p in range(gn.PIECES):
        span = slice(p * gn.rows, (p + 1) * gn.rows)
        mid = x[span, :].astype(F32) + total[span, :] + more[span, :].astype(F32) + most[span, :].astype(F32)
        scale = lax.rsqrt(jnp.mean(mid * mid, axis=-1, keepdims=True) + EPS)
        rm[span, :] = mid
        normed_mid = (mid * scale * gain_two).astype(BF)
        nm_own[span, :] = normed_mid
        gn.start_piece(p)
        nm[at.c, span, :] = normed_mid
    local.start("rm", rm, rm_out)
    ffn[2].relay()
    gn.pass_a()
    gn.pass_b()
    sc.finish_sends()
    local.wait("own")
    for part in ffn[:2]:
        part.finish()
    gn.pass_d()

    def feed(mate):
        i = lax.div(mate, 2)
        both = dot(nm[pl.ds(2 * i, 2)].reshape(2 * rows, width), wgu[...])
        gate, up = both[:, :part_cols], both[:, part_cols:]
        sigma = 1.0 / (1.0 + jnp.exp(-gate))
        act = gate * sigma
        from_gate = up * sigma * (1.0 + gate * (1.0 - sigma))
        for start, value in ((0, act * up), (part_cols, from_gate), (2 * part_cols, act)):
            x_all[pl.ds(2 * i, 2), :, start : start + part_cols] = value.astype(BF).reshape(2, rows, part_cols)

    def feed_back(i, carry):
        g_hidden = dot(ogv[pl.ds(2 * i, 2)].reshape(2 * rows, width), wd[...].reshape(part_cols, width), NT)
        for start in (part_cols, 2 * part_cols):
            factor = x_all[pl.ds(2 * i, 2), :, start : start + part_cols].reshape(2 * rows, part_cols).astype(F32)
            x_all[pl.ds(2 * i, 2), :, start : start + part_cols] = (
                (g_hidden * factor).astype(BF).reshape(2, rows, part_cols)
            )
        return carry

    gn.wait_other("own")
    feed(at.c)
    gn.wait_other("b")
    feed(at.a)
    gn.wait_other("a")
    feed(at.b)
    gn.wait_other("d")
    feed(at.d)
    local.wait("heads", "ni")
    dg = heads

    for i in range(part_cols // 256):
        value = dot(
            x_all[:, :, i * 256 : (i + 1) * 256].reshape(n_ctx * rows, 256), ogv[...].reshape(n_ctx * rows, width), TN
        )
        dd[2 * i : 2 * i + 2] = value.astype(BF).reshape(2, 128, width)
    zd = LineScatter(at, lambda i: dd.at[i], dd_in, (zd_send, zd_recv))
    zd.start()
    zd.rest()
    ffn[2].finish()
    lax.fori_loop(0, n_ctx // 2, feed_back, 0)
    emit = product_emit(lambda index: x_all[index, :, part_cols:], lambda lhs, columns: dot(lhs, wgu[columns, :], NT))
    sc = PlaneScatter(at, emit, (rs_out, rs_in), (rs_send, rs_recv), 3)
    sc.first(total)

    def gate_up_grad(t, carry):
        cols = pl.ds(pl.multiple_of(t * 256, 256), 256)
        value = dot(
            nm[:, :, cols].reshape(n_ctx * rows, 256), x_all[:, :, part_cols:].reshape(n_ctx * rows, 2 * part_cols), TN
        ).astype(BF)
        for i in range(n_fsdp):
            dg[i, cols, :] = value[:, i * 128 : (i + 1) * 128]
            du[i, cols, :] = value[:, part_cols + i * 128 : part_cols + (i + 1) * 128]
        return carry

    zg = []
    for part in range(2):
        lax.fori_loop(part * width // 512, (part + 1) * width // 512, gate_up_grad, 0)
        half_rows = pl.ds(part * width // 2, width // 2)
        zg.append(
            LineScatter(
                at, lambda i, h=half_rows: dg.at[i, h], dg_in.at[:, half_rows], (zg_send, zg_recv), 3 * part
            )
        )
        zg[part].start()
        zg[part].rest()
        if part == 0:
            zd.relay()
    local.start("out", du, du_out)
    sc.second()

    more, most = sc.last()
    local.wait("rm")
    gn.finish_sends()
    g_mid, gm_own = rm, nm_own
    gm = PlaneGather(at, gm_own, gm_all, (x_send, x_recv))
    gain_part = jnp.zeros((8, width), F32)
    for p in range(gm.PIECES):
        span = slice(p * gm.rows, (p + 1) * gm.rows)
        grad = total[span, :] + more[span, :].astype(F32) + most[span, :].astype(F32)
        mid = rm[span, :]
        scale = lax.rsqrt(jnp.mean(mid * mid, axis=-1, keepdims=True) + EPS)
        normed = mid * scale
        scaled = grad * gain_two
        back = og[span, :].astype(F32) + scale * (scaled - normed * jnp.mean(scaled * normed, axis=-1, keepdims=True))
        g_mid[span, :] = back
        gm_own[span, :] = back.astype(BF)
        gm.start_piece(p)
        gain_part = gain_part + jnp.sum((grad * normed).reshape(gm.rows // 8, 8, width), axis=0)
    dgain[...] = gain_part
    local.start("out", gm_own, gm_all.at[at.c])
    local.start("out", g_mid, g_mid_out)

    zg[0].relay()

    def down(i, carry):
        part = x_all[pl.ds(2 * i, 2), :, 0:part_cols].reshape(2 * rows, part_cols)
        ni[pl.ds(4 * i, 4)] = dot(part, wd[...].reshape(part_cols, width)).astype(BF).reshape(4, half, width)
        return carry

    lax.fori_loop(0, n_ctx // 2, down, 0)
    local.start("out", ni, mlp_out)
    zg[1].relay()
    gm.pass_a()
    gm.pass_b()
    up_ahead = remote(du.at[at.f3], du_first, up_send.at[0], up_recv.at[0], (at.c, at.f1))
    up_ahead.start()
    gm.pass_d()
    for which in ("own", "a", "b", "d"):
        gm.wait_other(which)
    local.wait_all()
    up_ahead.wait()
    zd.finish(d_down)
    for part in range(2):
        zg[part].finish(d_gate.at[pl.ds(part * width // 2, width // 2)])
    for part in (go, zt, zo, zw, *ffn, sc, gm, zd, *zg):
        part.finish_sends()
    for copies in (wc_copies, gc_copies):
        for cp in copies:
            cp.wait_send()


def backward_kernel(
    n_ctx, n_fsdp,
    gm_in, ao_in, heads_in, kt_in, ot_in, lse_in, wo_in, ni_in, wqkv_in, x_in, g_mid_in, gains_in, rm_in, mlp,
    dgain, du_in_all, du_first, pairs, expand_in, cosine_in, sine_in,
    mixed, tgrad, dqkv, dwout, dgain_out, d_up,
    gm_all, ao, heads, kt, ot, lse, wo, ni, wqkv, x, g_mid, gains, rm, du, expand, cosine, sine,
    ga, gat, delta, dwo, dwo_out, dwo_in, du_in, dk, dv, gq, gqc, dw, dw_in, dw_sum, dw_own, mine, mixed_total, total,
    ms_out, ms_in, rs_out, rs_in, dgc, dgz, dg_sum,
    ms_send, ms_recv, rs_send, rs_recv, oz_send, oz_recv, gz_send, gz_recv, gc_send, gc_recv,
    wz_send, wz_recv, wc_send, wc_recv, zu_send, zu_recv, local_sem, inv,
):
    at = Place(n_ctx, n_fsdp)
    rows, width = x.shape
    half = rows // 2
    seq_len = rows * n_ctx
    own_rows = dw.shape[2]
    at.greet(True)
    local = LocalCopies(local_sem)
    for name, src, dst in (
        ("grad", gm_in, gm_all), ("grad", wo_in, wo), ("grad", ao_in, ao), ("grad", ot_in, ot),
        ("attn", heads_in, heads), ("attn", kt_in, kt), ("attn", lse_in, lse),
        ("attn", cosine_in, cosine), ("attn", sine_in, sine),
        ("mlp", mlp.at[at.d], mine.at[0]), ("mlp", mlp.at[at.a], mine.at[1]),
        ("mlp", mlp.at[at.c], mine.at[2]), ("mlp", mlp.at[at.b], mine.at[3]),
        ("weight", ni_in, ni), ("weight", expand_in, expand), ("weight", wqkv_in, wqkv),
        ("up", du_in_all, du), ("up", du_first, du_in.at[0]), ("last", x_in, x), ("last", g_mid_in, g_mid), ("last", gains_in, gains), ("last", rm_in, rm),
    ):
        local.start(name, src, dst)
    at.wait_greeted()

    ms = PlaneScatter(at, None, (ms_out, ms_in), (ms_send, ms_recv), 1)
    for i, index in enumerate(ms.others()):
        ms.copy(i, 0, mlp.at[index], at.s)
    zu = LineScatter(at, lambda i: du_in_all.at[i], du_in, (zu_send, zu_recv))
    zu.rest()
    zu.part = lambda i: du.at[i]
    gc_copies, gc_waits = exchange(at, lambda p: dgain, dgc, lambda r, i: r.at[i], (gc_send, gc_recv))
    dgc[at.c] = dgain[...]

    def add_blocks(index, dst, extras):
        i = index

        def part(r, carry):
            span = pl.ds(pl.multiple_of(r * 48, 16), 48)
            value = mine[i, span, :].astype(F32)
            for extra in extras:
                value = value + extra[span, :].astype(F32)
            dst[span, :] = value.astype(dst.dtype)
            return carry

        lax.fori_loop(0, rows // 48, part, 0)

    def attn_grad(g, carry):
        gm_part = jnp.concatenate([gm_all[inv[4 * g + i]] for i in range(4)], axis=0)
        span = pl.ds(pl.multiple_of(g * 4 * half, 128), 4 * half)
        low = dot(gm_part, wo[...], NT).astype(BF)
        for h in range(2):
            part = low[:, h * HEAD_PAD : (h + 1) * HEAD_PAD]
            ga[h, span, :] = part
            turned = jnp.transpose(part.astype(F32))
            gat[h, :, span] = turned.astype(BF)
            delta[h, :, span] = jnp.broadcast_to(
                jnp.sum(turned * ot[h, :, span], axis=0, keepdims=True), (8, 4 * half)
            )
        dwo[...] += dot(ao[pl.ds(4 * g, 4)].reshape(4 * half, 2 * HEAD_PAD), gm_part, TN)
        return carry

    dwo[...] = jnp.zeros_like(dwo)
    block_slots(pairs, inv, n_ctx)
    local.wait("up")
    zu.pass_on()
    local.wait("grad")
    lax.fori_loop(0, seq_len // (4 * half), attn_grad, 0)
    low = jnp.concatenate([dwo[0:96, :], dwo[128:224, :]], axis=0).astype(BF)
    dwo_out[...] = low.reshape(dwo_out.shape)
    zo = LineScatter(at, lambda i: dwo_out.at[i], dwo_in, (oz_send, oz_recv))
    zo.start()
    zo.rest()
    local.wait("mlp")
    ms.wait(0, 0)
    add_blocks(0, ms_out.at[0], [ms_in.at[0]])
    ms.copy(4, 0, ms_out.at[0], at.a)
    ms.wait(1, 0)
    add_blocks(1, ms_out.at[1], [ms_in.at[1]])
    ms.copy(5, 0, ms_out.at[1], at.a)
    ms.wait(2, 0)
    add_blocks(2, mixed_total, [ms_in.at[2]])

    for w in gc_waits:
        w.wait_recv()
    dg_sum[...] = sum(dgc[i] for i in range(n_ctx))
    zg = LineGather(at, dg_sum, lambda i: dgz.at[i], (gz_send, gz_recv))
    zg.start()
    dgz[at.f] = dg_sum[...]

    local.wait("attn")
    dk[...] = jnp.zeros_like(dk)
    dv[...] = jnp.zeros_like(dv)
    block = 256
    plain_scale = HEAD_DIM ** (-0.5)
    score_scale = plain_scale * LOG2E
    for i in range(seq_len // block):
        first = i * block

        def head_step(h, carry, first=first):
            span = slice(first, first + block)
            q_part, ga_part, gat_part = heads[h, span, :], ga[h, span, :], gat[h, :, span]
            top = lse[h, 0:1, span]
            shift = delta[h, 0:1, span]

            def piece(keys, masked):
                scores = dot(heads[2, keys, :], q_part, NT) * score_scale - top
                if masked:
                    key_id = lax.broadcasted_iota(jnp.int32, (block, block), 0)
                    query_id = lax.broadcasted_iota(jnp.int32, (block, block), 1)
                    scores = jnp.where(key_id <= query_id, scores, NEG_FILL)
                prob = jnp.exp2(scores)
                grad = (prob * (dot(heads[3, keys, :], gat_part) - shift)).astype(BF)
                dv[keys, :] += dot(prob.astype(BF), ga_part)
                dk[keys, :] += dot(grad, q_part)
                return dot(kt[:, keys], grad)

            turned = piece(span, True)
            if first:
                turned = turned + piece(slice(0, first), False)
            lanes = pl.ds(pl.multiple_of(h * HEAD_PAD, HEAD_PAD), HEAD_PAD)
            grad_q = jnp.transpose(turned) * plain_scale
            store_rows(gq, first, lanes, turn(grad_q, cosine[span, :], -sine[span, :]).astype(BF))
            return carry

        lax.fori_loop(0, 2, head_step, 0)
        if i == 2:
            ms.wait(3, 0)
            ms.wait(4, 0)
            add_blocks(3, ms_out.at[2], [ms_in.at[3], ms_in.at[4]])
            ms.copy(6, 0, ms_out.at[2], at.b)
    zo.relay()

    def key_rows(g, carry):
        span = pl.ds(pl.multiple_of(g * 4 * half, 128), 4 * half)
        grad_k = turn(dk[span, :] * plain_scale, cosine[span, :], -sine[span, :]).astype(BF)
        gq[pl.ds(4 * g, 4), :, 256:384] = grad_k.reshape(4, half, HEAD_PAD)
        gq[pl.ds(4 * g, 4), :, 384:512] = dv[span, :].astype(BF).reshape(4, half, HEAD_PAD)
        return carry

    lax.fori_loop(0, seq_len // (4 * half), key_rows, 0)

    def to_ctx(slot, carry):
        pair = pairs[0, slot]
        gqc[2 * slot] = gq[pair]
        gqc[2 * slot + 1] = gq[2 * n_ctx - 1 - pair]
        return carry

    lax.fori_loop(0, n_ctx, to_ctx, 0)
    local.wait("weight", "last")

    def weight_grad(t, carry):
        tile = 2 * n_fsdp * own_rows
        cols = pl.ds(pl.multiple_of(t * tile, 128), tile)
        value = dot(ni[:, :, cols].reshape(seq_len, tile), gqc[...].reshape(seq_len, 4 * HEAD_PAD), TN)
        low = dot(value.astype(BF), expand[...], NT).astype(BF)
        dw[pl.ds(2 * t, 2)] = low.reshape(2, n_fsdp, own_rows, low.shape[1])
        return carry

    zw = []
    for part in range(2):
        lax.fori_loop(part * n_ctx // 4, (part + 1) * n_ctx // 4, weight_grad, 0)
        rows_of = pl.ds(part * n_ctx // 2, n_ctx // 2)
        zw.append(
            LineScatter(
                at, lambda i, r=rows_of: dw.at[r, i], dw_in.at[:, rows_of], (wz_send, wz_recv), 3 * part
            )
        )
        zw[part].start()
        zw[part].rest()

    emit = product_emit(
        lambda index: gqc[pl.ds(2 * index, 2)].reshape(rows, 4 * HEAD_PAD),
        lambda lhs, columns: dot(lhs, wqkv[columns, :], NT),
    )
    sc = PlaneScatter(at, emit, (rs_out, rs_in), (rs_send, rs_recv), 3)
    sc.first(total)
    sc.second()
    zw[0].relay()
    zw[1].relay()
    zg.relay()
    for part in range(2):
        zw[part].finish(dw_sum.at[pl.ds(part * n_ctx // 2, n_ctx // 2)])
    wc_copies, wc_waits = exchange(
        at, lambda p: dw_sum.at[p], dw_own, lambda r, i: r.at[i], (wc_send, wc_recv)
    )
    dw_own[at.c] = dw_sum[at.c]
    mixed_more, mixed_most = ms.last()

    def mixed_rows(r, carry):
        span = pl.ds(pl.multiple_of(r * 48, 16), 48)
        value = rm[span, :] + mixed_total[span, :]
        value = value + mixed_more[span, :].astype(F32) + mixed_most[span, :].astype(F32)
        mixed[span, :] = value.astype(BF)
        return carry

    lax.fori_loop(0, rows // 48, mixed_rows, 0)
    zg.finish()
    dgain_out[...] = sum(dgz[i] for i in range(n_fsdp))

    more, most = sc.last()
    gain_one = gains[0:1, :]

    def finish_rows(r, carry):
        span = pl.ds(pl.multiple_of(r * 48, 16), 48)
        grad = total[span, :] + more[span, :].astype(F32) + most[span, :].astype(F32)
        held = x[span, :].astype(F32)
        scale = lax.rsqrt(jnp.mean(held * held, axis=-1, keepdims=True) + EPS)
        normed = held * scale
        scaled = grad * gain_one
        back = g_mid[span, :] + scale * (scaled - normed * jnp.mean(scaled * normed, axis=-1, keepdims=True))
        tgrad[span, :] = back.astype(BF)
        return carry

    lax.fori_loop(0, rows // 48, finish_rows, 0)
    zu.finish(d_up)
    zo.finish(dwout)
    for w in wc_waits:
        w.wait_recv()
    dqkv[...] = dw_own[...]
    for part in (ms, sc, zu, zo, zg, *zw):
        part.finish_sends()
    for copies in (gc_copies, wc_copies):
        for cp in copies:
            cp.wait_send()


def head_spread():
    spread = np.zeros((4 * HEAD_DIM, 4 * HEAD_PAD), np.float32)
    for head in range(4):
        for j in range(HEAD_DIM):
            lane = j if head == 3 or j < HEAD_DIM // 2 else j + HEAD_PAD // 2 - HEAD_DIM // 2
            spread[head * HEAD_DIM + j, head * HEAD_PAD + lane] = 1.0
    return spread


def turn_tables(seq_len):
    half_dim = HEAD_DIM // 2
    freqs = np.float32(THETA) ** (-(np.arange(half_dim, dtype=np.float32) * np.float32(2.0 / HEAD_DIM)))
    angle = np.arange(seq_len, dtype=np.float32)[:, None] * freqs[None, :].astype(np.float32)
    gap = np.zeros((seq_len, HEAD_PAD // 2 - half_dim), np.float32)
    cosine, sine = np.cos(angle).astype(np.float32), np.sin(angle).astype(np.float32)
    return (
        np.concatenate([cosine, gap, cosine, gap], axis=1),
        np.concatenate([-sine, gap, sine, gap], axis=1),
    )


def tail_kernel(
    n_ctx, n_fsdp,
    dqkv, wq, wk, wv, gain_a, dgain, mixed_in, tgrad_in, dwout_in, dgate_in, dup_in, ddown_in,
    dq, dk, dv, gain_one, gain_two, mixed, tgrad, dwout, dgate, dup, ddown,
    mixed_held, tgrad_held, dwout_held, dgate_held, dup_held, ddown_held, sem,
):
    moves = (
        (mixed_in, mixed_held, mixed), (tgrad_in, tgrad_held, tgrad), (dwout_in, dwout_held, dwout),
        (dgate_in, dgate_held, dgate), (dup_in, dup_held, dup), (ddown_in, ddown_held, ddown),
    )
    loads = [pltpu.make_async_copy(src, held, sem.at[i]) for i, (src, held, _) in enumerate(moves)]
    for cp in loads:
        cp.start()
    stores = []
    for i, (_, held, dst) in enumerate(moves):
        loads[i].wait()
        stores.append(pltpu.make_async_copy(held, dst, sem.at[len(moves) + i]))
        stores[i].start()
    own_rows = wq.shape[0]
    q_cols, kv_cols = wq.shape[1] // n_ctx, wk.shape[1] // n_ctx
    got = [dqkv[i].astype(F32) for i in range(n_ctx)]
    query = jnp.concatenate([g[:, :q_cols] for g in got], axis=1)
    key = jnp.concatenate([g[:, q_cols : q_cols + kv_cols] for g in got], axis=1)
    value = jnp.concatenate([g[:, q_cols + kv_cols :] for g in got], axis=1)
    dq[...] = query
    dk[...] = key
    dv[...] = value
    both = sum(
        jnp.sum(g * w[...].astype(F32), axis=1, keepdims=True) for g, w in ((query, wq), (key, wk), (value, wv))
    )
    row = jnp.transpose(jnp.broadcast_to(both, (own_rows, 128)))[0:1, :]
    gain_one[...] = row / gain_a[...].astype(F32)
    place = (lax.axis_index("ctx") * n_fsdp + lax.axis_index("fsdp")) * own_rows
    width = dgain.shape[1]
    gain = jnp.broadcast_to(jnp.sum(dgain[...], axis=0, keepdims=True), (8, width))
    gain_two[...] = pltpu.roll(gain, width - place, 1)[0:1, :own_rows]
    for cp in stores:
        cp.wait()


def sems(*counts):
    return [pltpu.SemaphoreType.DMA((n,)) for n in counts for _ in range(2)]


VM = pl.BlockSpec(memory_space=pltpu.VMEM)
SM = pl.BlockSpec(memory_space=pltpu.SMEM)
HB = pl.BlockSpec(memory_space=pl.ANY)


def plane(tokens, out_grad, pair_table, attn_gain, w_query, w_key, w_value, w_out, mlp_gain, w_gate, w_up, w_down):
    n_ctx, n_fsdp = lax.axis_size("ctx"), lax.axis_size("fsdp")
    rows, width = tokens.shape
    half = rows // 2
    seq_len = rows * n_ctx
    own_rows = w_query.shape[0]
    gain_a, gain_b = attn_gain.reshape(1, own_rows), mlp_gain.reshape(1, own_rows)
    expand = jnp.asarray(head_spread(), BF)
    cosine, sine = (jnp.asarray(table) for table in turn_tables(seq_len))

    def sds(shape, dtype):
        return jax.ShapeDtypeStruct(shape, dtype)

    blocks = (n_ctx, rows, width)
    vm = pltpu.VMEM
    part_cols = n_fsdp * 128
    front = pl.pallas_call(
        functools.partial(front_kernel, n_ctx, n_fsdp),
        out_shape=(
            sds(w_gate.shape, F32),
            sds(w_down.shape, F32),
            sds((8, width), F32),
            sds((2 * n_ctx, half, width), BF),
            sds((4, seq_len, HEAD_PAD), BF),
            sds((HEAD_PAD, seq_len), BF),
            sds((2, HEAD_PAD, seq_len), F32),
            sds((2 * n_ctx, half, 2 * HEAD_PAD), BF),
            sds((2, 8, seq_len), F32),
            sds((width, 4 * HEAD_PAD), BF),
            sds((2 * HEAD_PAD, width), BF),
            sds((16, width), F32),
            sds((rows, width), F32),
            sds((n_fsdp, *w_up.shape), BF),
            sds((2 * n_ctx, half, width), BF),
            sds(blocks, BF),
            sds((rows, width), F32),
            sds(w_up.shape, BF),
        ),
        in_specs=[VM] * 6 + [HB] * 3 + [VM, VM, SM, HB, HB, HB],
        out_specs=(VM,) * 3 + (HB,) * 15,
        scratch_shapes=[
            vm((2 * n_ctx, half, width), BF),
            vm((4, seq_len, HEAD_PAD), BF),
            vm((HEAD_PAD, seq_len), BF),
            vm((HEAD_PAD, seq_len), BF),
            vm((2, HEAD_PAD, seq_len), F32),
            vm((2 * n_ctx, half, 2 * HEAD_PAD), BF),
            vm((2, 8, seq_len), F32),
            vm((width, 4 * HEAD_PAD), BF),
            vm((2 * HEAD_PAD, width), BF),
            vm((16, width), F32),
            vm((rows, width), F32),
            vm(blocks, BF),
            vm((n_ctx, own_rows, 4 * HEAD_DIM), BF),
            vm((n_ctx, n_fsdp, own_rows, 4 * HEAD_DIM), BF),
            vm((n_fsdp, own_rows, width), BF),
            vm((16, width), BF),
            vm((n_fsdp, 16, width), BF),
            vm((16, width), BF),
            vm((n_ctx, 16, width), BF),
            vm((rows, width), BF),
            vm((rows, width), F32),
            vm((7, rows, width), BF),
            vm((7, rows, width), BF),
            vm(blocks, BF),
            vm(blocks, BF),
            vm((width, 2 * part_cols), BF),
            vm((n_fsdp, *w_down.shape), BF),
            vm((n_fsdp, *w_down.shape), BF),
            vm((n_fsdp, *w_up.shape), BF),
            vm((3, *w_gate.shape), BF),
            vm((3, *w_down.shape), BF),
            *sems(21, 21, 21, n_ctx, 3, 3, 3, n_ctx, 3, 3, 3, 6, 3, 1),
            pltpu.SemaphoreType.DMA((21,)),
            pltpu.SMEM((2 * n_ctx,), jnp.int32),
            vm((4 * HEAD_DIM, 4 * HEAD_PAD), BF),
            vm((seq_len, HEAD_PAD), F32),
            vm((seq_len, HEAD_PAD), F32),
        ],
        compiler_params=pltpu.CompilerParams(
            collective_id=0, has_side_effects=True, vmem_limit_bytes=FRONT_VMEM_LIMIT
        ),
        name="forward_and_feed_forward",
    )
    d_gate, d_down, dgain, ni, heads, kt, ot, ao, lse, wqkv, wo, gains, rm, du, mlp, gm_all, g_mid, du_first = front(
        tokens, out_grad, w_query, w_key, w_value, w_out, w_gate, w_up, w_down, gain_a, gain_b, pair_table, expand, cosine, sine
    )

    backward = pl.pallas_call(
        functools.partial(backward_kernel, n_ctx, n_fsdp),
        out_shape=(
            sds((rows, width), BF),
            sds((rows, width), BF),
            sds((n_ctx, own_rows, 4 * HEAD_DIM), BF),
            sds((own_rows, width), F32),
            sds((8, width), F32),
            sds(w_up.shape, F32),
        ),
        in_specs=[HB] * 14 + [VM, HB, HB, SM, HB, HB, HB],
        out_specs=(VM,) * 6,
        scratch_shapes=[
            vm((2 * n_ctx, half, width), BF),
            vm((2 * n_ctx, half, 2 * HEAD_PAD), BF),
            vm((4, seq_len, HEAD_PAD), BF),
            vm((HEAD_PAD, seq_len), BF),
            vm((2, HEAD_PAD, seq_len), F32),
            vm((2, 8, seq_len), F32),
            vm((2 * HEAD_PAD, width), BF),
            vm((2 * n_ctx, half, width), BF),
            vm((width, 4 * HEAD_PAD), BF),
            vm((rows, width), BF),
            vm((rows, width), F32),
            vm((16, width), F32),
            vm((rows, width), F32),
            vm((n_fsdp, *w_up.shape), BF),
            vm((4 * HEAD_DIM, 4 * HEAD_PAD), BF),
            vm((seq_len, HEAD_PAD), F32),
            vm((seq_len, HEAD_PAD), F32),
            vm((2, seq_len, HEAD_PAD), BF),
            vm((2, HEAD_PAD, seq_len), BF),
            vm((2, 8, seq_len), F32),
            vm((2 * HEAD_PAD, width), F32),
            vm((n_fsdp, own_rows, width), BF),
            vm((3, own_rows, width), BF),
            vm((3, *w_up.shape), BF),
            vm((seq_len, HEAD_PAD), F32),
            vm((seq_len, HEAD_PAD), F32),
            vm((2 * n_ctx, half, 4 * HEAD_PAD), BF),
            vm((2 * n_ctx, half, 4 * HEAD_PAD), BF),
            vm((n_ctx, n_fsdp, own_rows, 4 * HEAD_DIM), BF),
            vm((3, n_ctx, own_rows, 4 * HEAD_DIM), BF),
            vm((n_ctx, own_rows, 4 * HEAD_DIM), BF),
            vm((n_ctx, own_rows, 4 * HEAD_DIM), BF),
            vm((4, rows, width), BF),
            vm((rows, width), F32),
            vm((rows, width), F32),
            vm((3, rows, width), BF),
            vm((7, rows, width), BF),
            vm((7, rows, width), BF),
            vm((7, rows, width), BF),
            vm((n_ctx, 8, width), F32),
            vm((n_fsdp, 8, width), F32),
            vm((8, width), F32),
            *sems(7, 21, 3, 3, n_ctx, 6, n_ctx, 3),
            pltpu.SemaphoreType.DMA((22,)),
            pltpu.SMEM((2 * n_ctx,), jnp.int32),
        ],
        compiler_params=pltpu.CompilerParams(
            collective_id=1, has_side_effects=True, vmem_limit_bytes=VMEM_LIMIT
        ),
        name="attention_backward",
    )
    mixed, tokens_grad, dqkv, d_out, d_gain_two, d_up = backward(
        gm_all.reshape(2 * n_ctx, half, width), ao, heads, kt, ot, lse, wo, ni, wqkv, tokens, g_mid, gains, rm,
        mlp.reshape(blocks), dgain, du, du_first, pair_table, expand, cosine, sine,
    )
    tail = pl.pallas_call(
        functools.partial(tail_kernel, n_ctx, n_fsdp),
        out_shape=(
            sds(w_query.shape, F32),
            sds(w_key.shape, F32),
            sds(w_value.shape, F32),
            sds((1, own_rows), F32),
            sds((1, own_rows), F32),
            sds((rows, width), BF),
            sds((rows, width), BF),
            sds(w_out.shape, F32),
            sds(w_gate.shape, F32),
            sds(w_up.shape, F32),
            sds(w_down.shape, F32),
        ),
        in_specs=[VM] * 6 + [HB] * 6,
        out_specs=(VM,) * 5 + (HB,) * 6,
        scratch_shapes=[
            vm((rows, width), BF),
            vm((rows, width), BF),
            vm(w_out.shape, F32),
            vm(w_gate.shape, F32),
            vm(w_up.shape, F32),
            vm(w_down.shape, F32),
            pltpu.SemaphoreType.DMA((12,)),
        ],
        compiler_params=pltpu.CompilerParams(vmem_limit_bytes=VMEM_LIMIT),
        name="layouts",
    )
    d_query, d_key, d_value, gain_one_grad, gain_two_grad, mixed, tokens_grad, d_out, d_gate, d_up, d_down = tail(
        dqkv, w_query, w_key, w_value, gain_a, d_gain_two, mixed, tokens_grad, d_out, d_gate, d_up, d_down
    )
    return (
        mixed, tokens_grad, gain_one_grad.reshape(-1), d_query, d_key, d_value, d_out, gain_two_grad.reshape(-1),
        d_gate, d_up, d_down,
    )


def solution(mesh):
    in_specs = (
        P(("ctx", "fsdp"), None),
        P(("ctx", "fsdp"), None),
        P("fsdp", None),
        P(("ctx", "fsdp")),
        P(("ctx", "fsdp"), None),
        P(("ctx", "fsdp"), None),
        P(("ctx", "fsdp"), None),
        P(("ctx", "fsdp"), None),
        P(("ctx", "fsdp")),
        P(None, ("ctx", "fsdp")),
        P(None, ("ctx", "fsdp")),
        P(("ctx", "fsdp"), None),
    )
    out_specs = (
        P(("ctx", "fsdp"), None),
        P(("ctx", "fsdp"), None),
        P(("ctx", "fsdp")),
        P(("ctx", "fsdp"), None),
        P(("ctx", "fsdp"), None),
        P(("ctx", "fsdp"), None),
        P(("ctx", "fsdp"), None),
        P(("ctx", "fsdp")),
        P(None, ("ctx", "fsdp")),
        P(None, ("ctx", "fsdp")),
        P(("ctx", "fsdp"), None),
    )
    fits = (
        mesh.shape["ctx"] == KV_HEADS
        and mesh.shape["fsdp"] == 4
        and HEADS == 2 * KV_HEADS
    )
    return jax.shard_map(plane if fits else local, mesh=mesh, in_specs=in_specs, out_specs=out_specs, check_vma=False)
```

```python
import functools
import math

import jax
import jax.numpy as jnp
import numpy as np
from jax import lax
from jax.experimental import pallas as pl
from jax.experimental.pallas import tpu as pltpu
from jax.sharding import PartitionSpec as P

HEADS = 16
KV_HEADS = 8
HEAD_DIM = 96


EPS = 1e-05
THETA = 100000.0
NEG_FILL = -1e30


def rotate(values_in, positions, direction):
    half_dim = values_in.shape[-1] // 2
    freqs = THETA ** (-(jnp.arange(half_dim, dtype=jnp.float32) * 2.0 / values_in.shape[-1]))
    angle = positions.astype(jnp.float32)[:, None] * freqs[None, :]
    cosine = jnp.cos(angle)[:, None, :]
    sine = direction * jnp.sin(angle)[:, None, :]
    first_half = values_in[..., :half_dim]
    second_half = values_in[..., half_dim:]
    return jnp.concatenate(
        [first_half * cosine - second_half * sine, second_half * cosine + first_half * sine],
        axis=-1,
    )


def place_rows(pair_index, tok_rows, block_count):
    half_rows = tok_rows // 2
    offsets = jnp.arange(tok_rows, dtype=jnp.int32)
    early = pair_index * half_rows + offsets
    late = (block_count - 1 - pair_index) * half_rows + offsets - half_rows
    return jnp.where(offsets < half_rows, early, late)


def rms_scale(values_in):
    return lax.rsqrt(jnp.mean(values_in * values_in, axis=-1, keepdims=True) + EPS)


def norm_back(grad_normed, normed, inv_rms, gain):
    scaled = grad_normed * gain
    return inv_rms * (scaled - normed * jnp.mean(scaled * normed, axis=-1, keepdims=True))


def local(
    tokens,
    out_grad,
    pair_table,
    attn_gain,
    w_query,
    w_key,
    w_value,
    w_out,
    mlp_gain,
    w_gate,
    w_up,
    w_down,
):
    tok_rows = tokens.shape[0]
    half_rows = tok_rows // 2
    ctx_count = lax.axis_size("ctx")
    half_count = 2 * ctx_count
    pair_row = pair_table[0]
    my_pos = place_rows(pair_row[lax.axis_index("ctx")], tok_rows, half_count)
    half_blocks = jnp.stack([pair_row, half_count - 1 - pair_row], axis=1).reshape(-1)
    block_ids = jnp.arange(half_count, dtype=jnp.int32)
    inverse = jnp.sum(
        jnp.where(half_blocks[None, :] == block_ids[:, None], block_ids[None, :], 0), axis=1
    )
    group_size = HEADS // KV_HEADS
    score_scale = HEAD_DIM ** (-0.5)
    query_width = HEADS * HEAD_DIM
    kv_width = KV_HEADS * HEAD_DIM
    w_query_all, w_key_all, w_value_all, w_out_all, gain_first, gain_second = (
        lax.all_gather(w_query, ("ctx", "fsdp"), axis=0, tiled=True),
        lax.all_gather(w_key, ("ctx", "fsdp"), axis=0, tiled=True),
        lax.all_gather(w_value, ("ctx", "fsdp"), axis=0, tiled=True),
        lax.all_gather(w_out, ("ctx", "fsdp"), axis=0, tiled=True),
        lax.all_gather(attn_gain, ("ctx", "fsdp"), axis=0, tiled=True),
        lax.all_gather(mlp_gain, ("ctx", "fsdp"), axis=0, tiled=True),
    )
    gain_one = gain_first.astype(jnp.float32)
    gain_two = gain_second.astype(jnp.float32)
    resid_in = tokens.astype(jnp.float32)
    inv_one = rms_scale(resid_in)
    normed_one = resid_in * inv_one
    normed_in = (normed_one * gain_one).astype(jnp.bfloat16)
    query_lin = jnp.dot(normed_in, w_query_all, preferred_element_type=jnp.float32)
    key_lin = jnp.dot(normed_in, w_key_all, preferred_element_type=jnp.float32)
    value_lin = jnp.dot(normed_in, w_value_all, preferred_element_type=jnp.float32)
    query_rot = rotate(query_lin.reshape(tok_rows, HEADS, HEAD_DIM), my_pos, 1.0).astype(
        jnp.bfloat16
    )
    key_rot = (
        rotate(key_lin.reshape(tok_rows, KV_HEADS, HEAD_DIM), my_pos, 1.0)
        .astype(jnp.bfloat16)
        .reshape(tok_rows, kv_width)
    )
    value_low = value_lin.astype(jnp.bfloat16)
    keys_got, values_got = (
        lax.all_gather(key_rot, "ctx", axis=0, tiled=True),
        lax.all_gather(value_low, "ctx", axis=0, tiled=True),
    )
    seq_len = keys_got.shape[0]
    keys_all = jnp.take(keys_got.reshape(half_count, half_rows, kv_width), inverse, axis=0).reshape(
        seq_len, kv_width
    )
    values_all = jnp.take(
        values_got.reshape(half_count, half_rows, kv_width), inverse, axis=0
    ).reshape(seq_len, kv_width)
    key_pos = jnp.arange(seq_len, dtype=jnp.int32)
    key_block = math.gcd(seq_len, 512)
    live_blocks = jnp.max(my_pos) // key_block + 1
    query_grp = query_rot.reshape(tok_rows, KV_HEADS, group_size, HEAD_DIM)

    def block_scores(block_index):
        first_row = block_index * key_block
        key_tile = lax.dynamic_slice_in_dim(keys_all, first_row, key_block, 0).reshape(
            key_block, KV_HEADS, HEAD_DIM
        )
        value_tile = lax.dynamic_slice_in_dim(values_all, first_row, key_block, 0).reshape(
            key_block, KV_HEADS, HEAD_DIM
        )
        scores = (
            jnp.einsum("tkgd,skd->kgts", query_grp, key_tile, preferred_element_type=jnp.float32)
            * score_scale
        )
        visible = (
            lax.dynamic_slice_in_dim(key_pos, first_row, key_block, 0)[None, :] <= my_pos[:, None]
        )
        return (scores, visible, key_tile, value_tile)

    def stats_step(block_index, carry):
        run_max, run_sum = carry
        scores, visible, key_tile, value_tile = block_scores(block_index)
        masked = jnp.where(visible, scores, NEG_FILL)
        new_max = jnp.maximum(run_max, jnp.max(masked, axis=-1))
        weights = jnp.where(visible, jnp.exp(masked - new_max[..., None]), 0.0)
        return (new_max, run_sum * jnp.exp(run_max - new_max) + jnp.sum(weights, axis=-1))

    start_max = jnp.full((KV_HEADS, group_size, tok_rows), NEG_FILL, jnp.float32)
    run_max, run_sum = lax.fori_loop(
        0, live_blocks, stats_step, (start_max, jnp.zeros_like(start_max))
    )
    log_total = run_max + jnp.log(run_sum)

    def probs(scores, visible):
        return jnp.where(visible, jnp.exp(scores - log_total[..., None]), 0.0)

    def output_step(block_index, accum):
        scores, visible, key_tile, value_tile = block_scores(block_index)
        prob_low = probs(scores, visible).astype(jnp.bfloat16)
        return accum + jnp.einsum(
            "kgts,skd->kgtd", prob_low, value_tile, preferred_element_type=jnp.float32
        )

    attn_acc = lax.fori_loop(
        0,
        live_blocks,
        output_step,
        jnp.zeros((KV_HEADS, group_size, tok_rows, HEAD_DIM), jnp.float32),
    )
    attn_low = attn_acc.transpose(2, 0, 1, 3).reshape(tok_rows, query_width).astype(jnp.bfloat16)
    resid_mid = resid_in + jnp.dot(attn_low, w_out_all, preferred_element_type=jnp.float32)
    inv_two = rms_scale(resid_mid)
    normed_two = resid_mid * inv_two
    normed_mid = (normed_two * gain_two).astype(jnp.bfloat16)
    w_gate_part, w_up_part, w_down_part = (
        lax.all_gather(w_gate, ("ctx", "fsdp"), axis=1, tiled=True),
        lax.all_gather(w_up, ("ctx", "fsdp"), axis=1, tiled=True),
        lax.all_gather(w_down, ("ctx", "fsdp"), axis=0, tiled=True),
    )
    gate_lin = jnp.dot(normed_mid, w_gate_part, preferred_element_type=jnp.float32)
    up_lin = jnp.dot(normed_mid, w_up_part, preferred_element_type=jnp.float32)
    sigma = jax.nn.sigmoid(gate_lin)
    activated = gate_lin * sigma
    hidden_low = (activated * up_lin).astype(jnp.bfloat16)
    mlp_branch = jnp.dot(hidden_low, w_down_part, preferred_element_type=jnp.float32)
    mixed = (resid_mid + mlp_branch).astype(jnp.bfloat16)
    grad_top = out_grad.astype(jnp.float32)
    d_down = jnp.einsum("tf,td->fd", hidden_low, out_grad, preferred_element_type=jnp.float32)
    grad_hidden = jnp.einsum("td,fd->tf", out_grad, w_down_part, preferred_element_type=jnp.float32)
    grad_gate = (grad_hidden * up_lin * sigma * (1.0 + gate_lin * (1.0 - sigma))).astype(
        jnp.bfloat16
    )
    grad_up = (grad_hidden * activated).astype(jnp.bfloat16)
    d_gate = jnp.einsum("td,tf->df", normed_mid, grad_gate, preferred_element_type=jnp.float32)
    d_up = jnp.einsum("td,tf->df", normed_mid, grad_up, preferred_element_type=jnp.float32)
    grad_normed_mid = jnp.einsum(
        "tf,df->td", grad_gate, w_gate_part, preferred_element_type=jnp.float32
    ) + jnp.einsum("tf,df->td", grad_up, w_up_part, preferred_element_type=jnp.float32)
    gate_grad_out, up_grad_out, down_grad_out = (
        lax.psum_scatter(d_gate, ("ctx", "fsdp"), scatter_dimension=1, tiled=True),
        lax.psum_scatter(d_up, ("ctx", "fsdp"), scatter_dimension=1, tiled=True),
        lax.psum_scatter(d_down, ("ctx", "fsdp"), scatter_dimension=0, tiled=True),
    )
    d_gain_two = jnp.sum(grad_normed_mid * normed_two, axis=0)
    grad_mid = grad_top + norm_back(grad_normed_mid, normed_two, inv_two, gain_two)
    grad_mid_low = grad_mid.astype(jnp.bfloat16)
    d_out = jnp.einsum("tq,td->qd", attn_low, grad_mid_low, preferred_element_type=jnp.float32)
    grad_attn_low = jnp.einsum(
        "td,qd->tq", grad_mid_low, w_out_all, preferred_element_type=jnp.float32
    ).astype(jnp.bfloat16)
    grad_heads = grad_attn_low.reshape(tok_rows, KV_HEADS, group_size, HEAD_DIM).transpose(
        1, 2, 0, 3
    )
    row_delta = jnp.sum(grad_heads.astype(jnp.float32) * attn_acc, axis=-1)

    def back_step(block_index, carry):
        grad_query, grad_keys, grad_values = carry
        scores, visible, key_tile, value_tile = block_scores(block_index)
        prob_full = probs(scores, visible)
        prob_low = prob_full.astype(jnp.bfloat16)
        grad_prob = jnp.einsum(
            "kgtd,skd->kgts", grad_heads, value_tile, preferred_element_type=jnp.float32
        )
        grad_score = (prob_full * (grad_prob - row_delta[..., None])).astype(jnp.bfloat16)
        grad_query = grad_query + score_scale * jnp.einsum(
            "kgts,skd->kgtd", grad_score, key_tile, preferred_element_type=jnp.float32
        )
        key_part = score_scale * jnp.einsum(
            "kgts,tkgd->skd", grad_score, query_grp, preferred_element_type=jnp.float32
        )
        value_part = jnp.einsum(
            "kgts,kgtd->skd", prob_low, grad_heads, preferred_element_type=jnp.float32
        )
        first_row = block_index * key_block
        grad_keys = lax.dynamic_update_slice_in_dim(
            grad_keys, key_part.reshape(key_block, kv_width), first_row, 0
        )
        grad_values = lax.dynamic_update_slice_in_dim(
            grad_values, value_part.reshape(key_block, kv_width), first_row, 0
        )
        return (grad_query, grad_keys, grad_values)

    empty_keys = jnp.zeros((seq_len, kv_width), jnp.float32)
    grad_query, grad_keys, grad_values = lax.fori_loop(
        0,
        live_blocks,
        back_step,
        (
            jnp.zeros((KV_HEADS, group_size, tok_rows, HEAD_DIM), jnp.float32),
            empty_keys,
            empty_keys,
        ),
    )
    keys_back = jnp.take(
        grad_keys.reshape(half_count, half_rows, kv_width), half_blocks, axis=0
    ).reshape(seq_len, kv_width)
    values_back = jnp.take(
        grad_values.reshape(half_count, half_rows, kv_width), half_blocks, axis=0
    ).reshape(seq_len, kv_width)
    own_keys, own_values = (
        lax.psum_scatter(
            keys_back.astype(jnp.bfloat16), "ctx", scatter_dimension=0, tiled=True
        ).astype(jnp.float32),
        lax.psum_scatter(
            values_back.astype(jnp.bfloat16), "ctx", scatter_dimension=0, tiled=True
        ).astype(jnp.float32),
    )
    grad_query_lin = rotate(
        grad_query.transpose(2, 0, 1, 3).reshape(tok_rows, HEADS, HEAD_DIM), my_pos, -1.0
    )
    grad_query_low = grad_query_lin.reshape(tok_rows, query_width).astype(jnp.bfloat16)
    grad_key_lin = rotate(own_keys.reshape(tok_rows, KV_HEADS, HEAD_DIM), my_pos, -1.0)
    grad_key_low = grad_key_lin.reshape(tok_rows, kv_width).astype(jnp.bfloat16)
    grad_value_low = own_values.astype(jnp.bfloat16)
    d_query = jnp.einsum("td,tq->dq", normed_in, grad_query_low, preferred_element_type=jnp.float32)
    d_key = jnp.einsum("td,tq->dq", normed_in, grad_key_low, preferred_element_type=jnp.float32)
    d_value = jnp.einsum("td,tq->dq", normed_in, grad_value_low, preferred_element_type=jnp.float32)
    grad_normed_in = (
        jnp.einsum("tq,dq->td", grad_query_low, w_query_all, preferred_element_type=jnp.float32)
        + jnp.einsum("tq,dq->td", grad_key_low, w_key_all, preferred_element_type=jnp.float32)
        + jnp.einsum("tq,dq->td", grad_value_low, w_value_all, preferred_element_type=jnp.float32)
    )
    d_gain_one = jnp.sum(grad_normed_in * normed_one, axis=0)
    grad_input = grad_mid + norm_back(grad_normed_in, normed_one, inv_one, gain_one)
    query_grad_out, key_grad_out, value_grad_out, out_grad_out, gain_one_out, gain_two_out = (
        lax.psum_scatter(d_query, ("ctx", "fsdp"), scatter_dimension=0, tiled=True),
        lax.psum_scatter(d_key, ("ctx", "fsdp"), scatter_dimension=0, tiled=True),
        lax.psum_scatter(d_value, ("ctx", "fsdp"), scatter_dimension=0, tiled=True),
        lax.psum_scatter(d_out, ("ctx", "fsdp"), scatter_dimension=0, tiled=True),
        lax.psum_scatter(d_gain_one, ("ctx", "fsdp"), scatter_dimension=0, tiled=True),
        lax.psum_scatter(d_gain_two, ("ctx", "fsdp"), scatter_dimension=0, tiled=True),
    )
    return (
        mixed,
        grad_input.astype(jnp.bfloat16),
        gain_one_out,
        query_grad_out,
        key_grad_out,
        value_grad_out,
        out_grad_out,
        gain_two_out,
        gate_grad_out,
        up_grad_out,
        down_grad_out,
    )


BF = jnp.bfloat16
F32 = jnp.float32
MESH = pl.DeviceIdType.MESH
HEAD_PAD = 128
LOG2E = 1.4426950408889634
VMEM_LIMIT = 58 * 2**20
FRONT_VMEM_LIMIT = 61 * 2**20
NT = (((1,), (1,)), ((), ()))
TN = (((0,), (0,)), ((), ()))


def dot(a, b, dims=(((1,), (0,)), ((), ()))):
    return lax.dot_general(a, b, dims, preferred_element_type=F32)


class Place:
    def __init__(self, n_ctx, n_fsdp):
        self.n_ctx, self.n_fsdp = n_ctx, n_fsdp
        self.c, self.f = lax.axis_index("ctx"), lax.axis_index("fsdp")
        core = lax.rem(self.c, 2)
        step_x = 2 - 4 * lax.rem(lax.div(self.c, 2), 2)
        step_y = 4 - 8 * lax.div(self.c, 4)
        self.other = 1 - 2 * core
        self.s = self.c + self.other
        self.a = self.c + step_x * (1 - core) + step_y * core
        self.b = self.c + step_x * core + step_y * (1 - core)
        self.d = self.c + step_x + step_y
        self.f1 = self.f + 1 - 2 * lax.rem(self.f, 2)
        self.f2 = self.f + 2 - 4 * lax.div(self.f, 2)
        self.f3 = n_fsdp - 1 - self.f

    def ctx_peer(self, j):
        return lax.rem(self.c + j, self.n_ctx)

    def ctx_source(self, j):
        return lax.rem(self.c + self.n_ctx - j, self.n_ctx)

    def greet(self, everyone):
        barrier = pltpu.get_barrier_semaphore()
        if everyone:
            mates = [(self.ctx_peer(j), self.f) for j in range(1, self.n_ctx)]
        else:
            mates = [(self.s, self.f), (self.a, self.f), (self.b, self.f)]
        mates += [(self.c, self.f1), (self.c, self.f2)]
        for mate in mates:
            pl.semaphore_signal(barrier, inc=1, device_id=mate, device_id_type=MESH)
        self.mates = len(mates)

    def wait_greeted(self):
        pl.semaphore_wait(pltpu.get_barrier_semaphore(), self.mates)


def block_slots(pairs, inv, n_ctx):
    for block in range(2 * n_ctx):
        slot = jnp.int32(0)
        for i in range(n_ctx):
            pair = pairs[0, i]
            slot = jnp.maximum(slot, jnp.where(pair == block, 2 * i, 0))
            slot = jnp.maximum(slot, jnp.where(2 * n_ctx - 1 - pair == block, 2 * i + 1, 0))
        inv[block] = slot


def remote(src, dst, send, recv, device):
    return pltpu.make_async_remote_copy(
        src_ref=src, dst_ref=dst, send_sem=send, recv_sem=recv, device_id=device, device_id_type=MESH
    )


class LocalCopies:
    def __init__(self, sems):
        self.sems, self.count, self.named = sems, 0, {}

    def start(self, name, src, dst):
        cp = pltpu.make_async_copy(src, dst, self.sems.at[self.count])
        cp.start()
        self.count += 1
        self.named.setdefault(name, []).append(cp)

    def wait(self, *names):
        for name in names:
            for cp in self.named.pop(name):
                cp.wait()

    def wait_all(self):
        self.wait(*list(self.named))


class PlaneGather:
    PIECES = 3
    COUNT = 7 * PIECES

    def __init__(self, at, own, blocks, sems):
        self.at, self.own, self.blocks = at, own, blocks
        self.send, self.recv = sems
        self.rows = own.shape[0] // self.PIECES
        self.started = []

    def piece(self, slot, p):
        return self.blocks.at[slot, pl.ds(p * self.rows, self.rows)]

    def copy(self, i, p, src, slot, mate):
        k = i * self.PIECES + p
        cp = remote(src, self.piece(slot, p), self.send.at[k], self.recv.at[k], (mate, self.at.f))
        cp.start()
        self.started.append(cp)

    def wait(self, i, p, slot):
        k = i * self.PIECES + p
        block = self.piece(slot, p)
        remote(block, block, self.send.at[k], self.recv.at[k], (self.at.s, self.at.f)).wait_recv()

    def start_piece(self, p):
        at = self.at
        src = self.own.at[pl.ds(p * self.rows, self.rows)]
        self.copy(1, p, src, at.c, at.a)
        self.copy(2, p, src, at.c, at.b)
        self.copy(0, p, src, at.c, at.s)

    def start(self):
        for p in range(self.PIECES):
            self.start_piece(p)

    def pass_a(self):
        at = self.at
        for p in range(self.PIECES):
            self.wait(1, p, at.a)
            self.copy(4, p, self.piece(at.a, p), at.a, at.b)
            self.copy(3, p, self.piece(at.a, p), at.a, at.s)

    def pass_b(self):
        at = self.at
        for p in range(self.PIECES):
            self.wait(2, p, at.b)
            self.copy(5, p, self.piece(at.b, p), at.b, at.s)

    def pass_d(self):
        at = self.at
        for p in range(self.PIECES):
            self.wait(4, p, at.d)
            self.copy(6, p, self.piece(at.d, p), at.d, at.s)

    def wait_other(self, which):
        at = self.at
        i, slot = {
            "own": (0, at.s),
            "a": (3, at.b + at.other),
            "b": (5, at.a + at.other),
            "d": (6, at.d + at.other),
        }[which]
        for p in range(self.PIECES):
            self.wait(i, p, slot)

    def finish_sends(self):
        for cp in self.started:
            cp.wait_send()


class PlaneScatter:
    def __init__(self, at, emit, bufs, sems, pieces):
        self.at, self.emit, self.pieces = at, emit, pieces
        self.out, self.landed = bufs
        self.send, self.recv = sems
        self.started = []

    def columns(self, t):
        width = self.landed.shape[2] // self.pieces
        return slice(t * width, (t + 1) * width)

    def copy(self, i, t, src, mate):
        k = i * self.pieces + t
        dst = self.landed.at[i, :, self.columns(t)]
        cp = remote(src, dst, self.send.at[k], self.recv.at[k], (mate, self.at.f))
        cp.start()
        self.started.append(cp)

    def wait(self, i, t):
        k = i * self.pieces + t
        block = self.landed.at[i, :, self.columns(t)]
        remote(block, block, self.send.at[k], self.recv.at[k], (self.at.s, self.at.f)).wait_recv()

    def others(self):
        at = self.at
        return (at.d + at.other, at.b + at.other, at.s, at.a + at.other)

    def to_other(self, i):
        for t in range(self.pieces):
            columns = self.columns(t)
            self.emit(self.others()[i], columns, self.out.at[i], [])
            self.copy(i, t, self.out.at[i, :, columns], self.at.s)

    def onward(self, i, index, extras, mate):
        for t in range(self.pieces):
            columns = self.columns(t)
            for extra in extras:
                self.wait(extra, t)
            self.emit(index, columns, self.out.at[i], [self.landed.at[extra] for extra in extras])
            self.copy(i, t, self.out.at[i, :, columns], mate)

    def first(self, total):
        at = self.at
        self.to_other(0)
        self.to_other(1)
        self.onward(4, at.d, [0], at.a)
        self.onward(5, at.a, [1], at.a)
        self.to_other(3)
        self.to_other(2)
        for t in range(self.pieces):
            self.wait(2, t)
            self.emit(at.c, self.columns(t), total, [self.landed.at[2]])

    def second(self):
        self.onward(6, self.at.b, [3, 4], self.at.b)

    def last(self):
        for i in (5, 6):
            for t in range(self.pieces):
                self.wait(i, t)
        return self.landed.at[5], self.landed.at[6]

    def finish_sends(self):
        for cp in self.started:
            cp.wait_send()


class LineGather:
    COUNT = 3

    def __init__(self, at, own, slot, sems):
        self.at, self.own, self.slot = at, own, slot
        self.send, self.recv = sems
        self.started = []

    def copy(self, i, src, slot, mate):
        cp = remote(src, self.slot(slot), self.send.at[i], self.recv.at[i], (self.at.c, mate))
        cp.start()
        self.started.append(cp)

    def wait(self, i, slot):
        block = self.slot(slot)
        remote(block, block, self.send.at[i], self.recv.at[i], (self.at.c, self.at.f1)).wait_recv()

    def start_far(self):
        self.copy(1, self.own, self.at.f, self.at.f2)

    def start_near(self):
        self.copy(0, self.own, self.at.f, self.at.f1)

    def start(self):
        self.start_far()
        self.start_near()

    def relay(self):
        at = self.at
        self.wait(1, at.f2)
        self.copy(2, self.slot(at.f2), at.f2, at.f1)

    def finish(self):
        self.wait(0, self.at.f1)
        self.wait(2, self.at.f3)

    def finish_sends(self):
        for cp in self.started:
            cp.wait_send()


class LineScatter:
    COUNT = 3

    def __init__(self, at, part, landed, sems, base=0):
        self.at, self.part, self.landed, self.base = at, part, landed, base
        self.send, self.recv = sems
        self.started = []

    def copy(self, i, src, mate):
        k = self.base + i
        cp = remote(src, self.landed.at[i], self.send.at[k], self.recv.at[k], (self.at.c, mate))
        cp.start()
        self.started.append(cp)

    def wait(self, i):
        k = self.base + i
        block = self.landed.at[i]
        remote(block, block, self.send.at[k], self.recv.at[k], (self.at.c, self.at.f1)).wait_recv()

    def start(self):
        at = self.at
        self.copy(0, self.part(at.f3), at.f1)

    def rest(self):
        self.copy(1, self.part(self.at.f1), self.at.f1)

    def add(self, dst, refs):
        count = dst.shape[0]
        step = min(count, 128) if len(dst.shape) == 2 else 1

        def piece(i, carry):
            rows = pl.ds(pl.multiple_of(i * step, step), step) if len(dst.shape) == 2 else pl.ds(i, 1)
            value = refs[0][rows].astype(F32)
            for ref in refs[1:]:
                value = value + ref[rows].astype(F32)
            dst[rows] = value.astype(dst.dtype)
            return carry

        lax.fori_loop(0, count // step, piece, 0)

    def relay(self):
        self.wait(0)
        self.pass_on()

    def pass_on(self):
        at = self.at
        self.add(self.part(at.f2), [self.part(at.f2), self.landed.at[0]])
        self.copy(2, self.part(at.f2), at.f2)

    def finish(self, dst):
        self.wait(1)
        self.wait(2)
        self.add(dst, [self.part(self.at.f), self.landed.at[1], self.landed.at[2]])

    def finish_sends(self):
        for cp in self.started:
            cp.wait_send()


def exchange(at, src_of, dst, slot_of, sems):
    send, recv = sems
    started, waits = [], []
    for j in range(1, at.n_ctx):
        peer, source = at.ctx_peer(j), at.ctx_source(j)
        device = (peer, at.f)
        cp = remote(src_of(peer), slot_of(dst, at.c), send.at[j], recv.at[j], device)
        cp.start()
        started.append(cp)
        block = slot_of(dst, source)
        waits.append(remote(block, block, send.at[j], recv.at[j], device))
    return started, waits


def turn(values_in, cosine, sine):
    return values_in * cosine + pltpu.roll(values_in, HEAD_PAD // 2, 1) * sine


def store_rows(ref, first, lanes, value):
    block_rows, done = ref.shape[1], 0
    while done < value.shape[0]:
        block, start = divmod(first + done, block_rows)
        count = min(block_rows - start, value.shape[0] - done)
        ref[block, start : start + count, lanes] = value[done : done + count]
        done += count


def product_emit(lhs_of, rhs_of):
    def emit(index, columns, dst, extras):
        value = rhs_of(lhs_of(index), columns)
        for extra in extras:
            value = value + extra[:, columns].astype(F32)
        dst[:, columns] = value.astype(dst.dtype)

    return emit


def front_kernel(
    n_ctx, n_fsdp,
    x, og, wq, wk, wv, wout, wg, wu, wd_own, gain_a, gain_b, pairs, expand_in, cosine_in, sine_in,
    d_gate, d_down, dgain,
    ni_out, heads_out, kt_out, ot_out, ao_out, lse_out, wqkv_out, wo_out, gains_out, rm_out, du_out, mlp_out, gm_all, g_mid_out,
    du_first,
    ni, heads, kt, vt, ot, ao, lse, wqkv, wo, gains, rm, x_all, wblk, w_raw, wo_raw, gt, gz, gz_sum, gc, nm_own, total,
    rs_out, rs_in, nm, ogv, wgu, wd, dd, du, dg_in, dd_in,
    x_send, x_recv, og_send, og_recv, rs_send, rs_recv,
    wc_send, wc_recv, wz_send, wz_recv, oz_send, oz_recv, gz_send, gz_recv, gc_send, gc_recv,
    fg_send, fg_recv, fu_send, fu_recv, fd_send, fd_recv, zg_send, zg_recv, zd_send, zd_recv, up_send, up_recv, local_sem, inv, expand, cosine, sine,
):
    at = Place(n_ctx, n_fsdp)
    rows, width = x.shape
    half = rows // 2
    seq_len = rows * n_ctx
    own_rows = w_raw.shape[2]
    at.greet(True)
    local = LocalCopies(local_sem)
    part_cols = n_fsdp * 128

    def gate_slot(i):
        return wgu.at[:, pl.ds(pl.multiple_of(i * 128, 128), 128)]

    def up_slot(i):
        return wgu.at[:, pl.ds(pl.multiple_of(part_cols + i * 128, 128), 128)]

    for src, dst in ((og, ogv.at[at.c]), (wg, gate_slot(at.f)), (wu, up_slot(at.f)), (wd_own, wd.at[at.f])):
        local.start("own", src, dst)
    for src, dst in ((expand_in, expand), (cosine_in, cosine), (sine_in, sine)):
        local.start("tables", src, dst)
    q_cols, kv_cols = wq.shape[1] // n_ctx, wk.shape[1] // n_ctx
    for i in range(n_ctx):
        parts = (wq[:, i * q_cols : (i + 1) * q_cols], *(w[:, i * kv_cols : (i + 1) * kv_cols] for w in (wk, wv)))
        wblk[i] = jnp.concatenate(parts, axis=1)
    place = (at.c * n_fsdp + at.f) * own_rows
    from_lane = lax.broadcasted_iota(jnp.int32, (own_rows, width), 0)
    to_lane = lax.broadcasted_iota(jnp.int32, (own_rows, width), 1)
    spread = jnp.where(to_lane == from_lane + place, 1.0, 0.0).astype(BF)
    row = lax.broadcasted_iota(jnp.int32, (16, width), 0)
    spread_gains = [dot(jnp.broadcast_to(g[...], (16, own_rows)), spread) for g in (gain_a, gain_b)]
    gt[...] = jnp.where(row == 0, spread_gains[0], jnp.where(row == 1, spread_gains[1], 0.0)).astype(BF)
    at.wait_greeted()

    wc_copies, wc_waits = exchange(
        at, lambda p: wblk.at[p], w_raw, lambda r, i: r.at[i, at.f], (wc_send, wc_recv)
    )
    zt = LineGather(at, gt, lambda i: gz.at[i], (gz_send, gz_recv))
    zt.start()
    gx = PlaneGather(at, x, x_all, (x_send, x_recv))
    gx.start()
    zo = LineGather(at, wout, lambda i: wo_raw.at[i], (oz_send, oz_recv))
    zo.start()
    w_raw[at.c, at.f] = wblk[at.c]
    wo_raw[at.f] = wout[...]
    gz[at.f] = gt[...]
    x_all[at.c] = x[...]
    zt.relay()
    zt.finish()
    gz_sum[...] = sum(gz[i].astype(F32) for i in range(n_fsdp)).astype(BF)
    gc_copies, gc_waits = exchange(at, lambda p: gz_sum, gc, lambda r, i: r.at[i], (gc_send, gc_recv))
    gc[at.c] = gz_sum[...]
    for w in wc_waits:
        w.wait_recv()
    zw = LineGather(at, w_raw.at[:, at.f], lambda i: w_raw.at[:, i], (wz_send, wz_recv))
    zw.start()
    gx.pass_a()
    gx.pass_b()
    zw.relay()
    zo.relay()
    ffn = [
        LineGather(at, wg, gate_slot, (fg_send, fg_recv)),
        LineGather(at, wu, up_slot, (fu_send, fu_recv)),
        LineGather(at, wd_own, lambda i: wd.at[i], (fd_send, fd_recv)),
    ]
    ffn[0].start_far()
    go = PlaneGather(at, og, ogv, (og_send, og_recv))
    go.start()
    for w in gc_waits:
        w.wait_recv()
    gains[...] = sum(gc[i].astype(F32) for i in range(n_ctx))
    gain_one = gains[0:1, :]

    def norm_in(slot):
        def part(r, carry):
            start = pl.multiple_of(r * 48, 16)
            part_rows = x_all[slot, pl.ds(start, 48), :].astype(F32)
            scale = lax.rsqrt(jnp.mean(part_rows * part_rows, axis=-1, keepdims=True) + EPS)
            inside = pl.multiple_of(lax.rem(r, 2) * 48, 16)
            ni[2 * slot + lax.div(r, 2), pl.ds(inside, 48), :] = (part_rows * scale * gain_one).astype(BF)
            return carry

        lax.fori_loop(0, rows // 48, part, 0)

    block_slots(pairs, inv, n_ctx)
    norm_in(at.c)
    gx.wait_other("own")
    norm_in(at.s)
    norm_in(at.a)
    norm_in(at.b)
    gx.pass_d()
    norm_in(at.d)
    gx.wait_other("a")
    norm_in(at.b + at.other)
    gx.wait_other("b")
    norm_in(at.a + at.other)
    gx.wait_other("d")
    norm_in(at.d + at.other)
    local.start("ni", ni, ni_out)
    ffn[0].start_near()
    ffn[1].start_far()
    local.start("out", gains, gains_out)
    local.wait("tables")
    zw.finish()

    def widen(i, carry):
        part = w_raw[pl.ds(2 * i, 2)].reshape(2 * n_fsdp * own_rows, w_raw.shape[3])
        start = pl.multiple_of(i * 2 * n_fsdp * own_rows, 128)
        wqkv[pl.ds(start, 2 * n_fsdp * own_rows), :] = dot(part, expand[...]).astype(BF)
        return carry

    lax.fori_loop(0, n_ctx // 2, widen, 0)

    def project(g, carry):
        lhs = jnp.concatenate([ni[inv[4 * g + i]] for i in range(4)], axis=0)
        lin = dot(lhs, wqkv[...])
        span = pl.ds(pl.multiple_of(g * 4 * half, 128), 4 * half)
        cos_part, sin_part = cosine[span, :], sine[span, :]
        heads[0, span, :] = turn(lin[:, 0:128], cos_part, sin_part).astype(BF)
        heads[1, span, :] = turn(lin[:, 128:256], cos_part, sin_part).astype(BF)
        k_part = turn(lin[:, 256:384], cos_part, sin_part).astype(BF)
        v_part = lin[:, 384:512].astype(BF)
        heads[2, span, :] = k_part
        heads[3, span, :] = v_part
        kt[:, span] = jnp.transpose(k_part.astype(F32)).astype(BF)
        vt[:, span] = jnp.transpose(v_part.astype(F32)).astype(BF)
        return carry

    lax.fori_loop(0, seq_len // (4 * half), project, 0)
    local.start("heads", heads, heads_out)
    for src, dst in ((kt, kt_out), (wqkv, wqkv_out)):
        local.start("out", src, dst)

    block = 256
    score_scale = HEAD_DIM ** (-0.5) * LOG2E
    for i in range(seq_len // block):
        first = i * block

        def head_step(h, carry, first=first):
            span = slice(first, first + block)
            q_part = heads[h, span, :]
            diag = dot(heads[2, span, :], q_part, NT) * score_scale
            key_id = lax.broadcasted_iota(jnp.int32, (block, block), 0)
            query_id = lax.broadcasted_iota(jnp.int32, (block, block), 1)
            diag = jnp.where(key_id <= query_id, diag, NEG_FILL)
            top = jnp.max(diag, axis=0, keepdims=True)
            if first:
                past = dot(heads[2, 0:first, :], q_part, NT) * score_scale
                top = jnp.maximum(top, jnp.max(past, axis=0, keepdims=True))
            diag_p = jnp.exp2(diag - top)
            norm = jnp.sum(diag_p, axis=0, keepdims=True)
            acc = dot(vt[:, span], diag_p.astype(BF))
            if first:
                past_p = jnp.exp2(past - top)
                norm = norm + jnp.sum(past_p, axis=0, keepdims=True)
                acc = acc + dot(vt[:, 0:first], past_p.astype(BF))
            acc = acc / norm
            ot[h, :, span] = acc
            lse[h, :, span] = jnp.broadcast_to(top + jnp.log2(norm), (8, block))
            lanes = pl.ds(pl.multiple_of(h * HEAD_PAD, HEAD_PAD), HEAD_PAD)
            store_rows(ao, first, lanes, jnp.transpose(acc).astype(BF))
            return carry

        lax.fori_loop(0, 2, head_step, 0)
        if i == 4:
            go.pass_a()
            go.pass_b()

    for src, dst in ((ot, ot_out), (ao, ao_out), (lse, lse_out)):
        local.start("out", src, dst)
    zo.finish()
    ffn[0].relay()
    ffn[1].start_near()
    ffn[2].start_far()
    raw = wo_raw[...].reshape(2 * HEAD_DIM, width)
    pad_rows = jnp.zeros((HEAD_PAD - HEAD_DIM, width), BF)
    wo[0:96, :] = raw[0:96]
    wo[96:128, :] = pad_rows
    wo[128:224, :] = raw[96:192]
    wo[224:256, :] = pad_rows
    local.start("out", wo, wo_out)

    def attn_rows(index):
        pair = pairs[0, index]
        return jnp.concatenate([ao[pair], ao[2 * n_ctx - 1 - pair]], axis=0)

    emit = product_emit(attn_rows, lambda lhs, columns: dot(lhs, wo[:, columns]))
    sc = PlaneScatter(at, emit, (rs_out, rs_in), (rs_send, rs_recv), 3)
    sc.first(total)
    go.pass_d()
    sc.second()
    ffn[1].relay()
    ffn[2].start_near()
    go.wait_other("own")
    go.wait_other("a")
    go.wait_other("b")
    go.wait_other("d")
    more, most = sc.last()
    gain_two = gains[1:2, :]

    gx.finish_sends()
    gn = PlaneGather(at, nm_own, nm, (x_send, x_recv))
    for p in range(gn.PIECES):
        span = slice(p * gn.rows, (p + 1) * gn.rows)
        mid = x[span, :].astype(F32) + total[span, :] + more[span, :].astype(F32) + most[span, :].astype(F32)
        scale = lax.rsqrt(jnp.mean(mid * mid, axis=-1, keepdims=True) + EPS)
        rm[span, :] = mid
        normed_mid = (mid * scale * gain_two).astype(BF)
        nm_own[span, :] = normed_mid
        gn.start_piece(p)
        nm[at.c, span, :] = normed_mid
    local.start("rm", rm, rm_out)
    ffn[2].relay()
    gn.pass_a()
    gn.pass_b()
    sc.finish_sends()
    local.wait("own")
    for part in ffn[:2]:
        part.finish()
    gn.pass_d()

    def feed(mate):
        i = lax.div(mate, 2)
        both = dot(nm[pl.ds(2 * i, 2)].reshape(2 * rows, width), wgu[...])
        gate, up = both[:, :part_cols], both[:, part_cols:]
        sigma = 1.0 / (1.0 + jnp.exp(-gate))
        act = gate * sigma
        from_gate = up * sigma * (1.0 + gate * (1.0 - sigma))
        for start, value in ((0, act * up), (part_cols, from_gate), (2 * part_cols, act)):
            x_all[pl.ds(2 * i, 2), :, start : start + part_cols] = value.astype(BF).reshape(2, rows, part_cols)

    def feed_back(i, carry):
        g_hidden = dot(ogv[pl.ds(2 * i, 2)].reshape(2 * rows, width), wd[...].reshape(part_cols, width), NT)
        for start in (part_cols, 2 * part_cols):
            factor = x_all[pl.ds(2 * i, 2), :, start : start + part_cols].reshape(2 * rows, part_cols).astype(F32)
            x_all[pl.ds(2 * i, 2), :, start : start + part_cols] = (
                (g_hidden * factor).astype(BF).reshape(2, rows, part_cols)
            )
        return carry

    gn.wait_other("own")
    feed(at.c)
    gn.wait_other("b")
    feed(at.a)
    gn.wait_other("a")
    feed(at.b)
    gn.wait_other("d")
    feed(at.d)
    local.wait("heads", "ni")
    dg = heads

    for i in range(part_cols // 256):
        value = dot(
            x_all[:, :, i * 256 : (i + 1) * 256].reshape(n_ctx * rows, 256), ogv[...].reshape(n_ctx * rows, width), TN
        )
        dd[2 * i : 2 * i + 2] = value.astype(BF).reshape(2, 128, width)
    zd = LineScatter(at, lambda i: dd.at[i], dd_in, (zd_send, zd_recv))
    zd.start()
    zd.rest()
    ffn[2].finish()
    lax.fori_loop(0, n_ctx // 2, feed_back, 0)
    emit = product_emit(lambda index: x_all[index, :, part_cols:], lambda lhs, columns: dot(lhs, wgu[columns, :], NT))
    sc = PlaneScatter(at, emit, (rs_out, rs_in), (rs_send, rs_recv), 3)
    sc.first(total)

    def gate_up_grad(t, carry):
        cols = pl.ds(pl.multiple_of(t * 256, 256), 256)
        value = dot(
            nm[:, :, cols].reshape(n_ctx * rows, 256), x_all[:, :, part_cols:].reshape(n_ctx * rows, 2 * part_cols), TN
        ).astype(BF)
        for i in range(n_fsdp):
            dg[i, cols, :] = value[:, i * 128 : (i + 1) * 128]
            du[i, cols, :] = value[:, part_cols + i * 128 : part_cols + (i + 1) * 128]
        return carry

    zg = []
    for part in range(2):
        lax.fori_loop(part * width // 512, (part + 1) * width // 512, gate_up_grad, 0)
        half_rows = pl.ds(part * width // 2, width // 2)
        zg.append(
            LineScatter(
                at, lambda i, h=half_rows: dg.at[i, h], dg_in.at[:, half_rows], (zg_send, zg_recv), 3 * part
            )
        )
        zg[part].start()
        zg[part].rest()
        if part == 0:
            zd.relay()
    local.start("out", du, du_out)
    sc.second()

    more, most = sc.last()
    local.wait("rm")
    gn.finish_sends()
    g_mid, gm_own = rm, nm_own
    gm = PlaneGather(at, gm_own, gm_all, (x_send, x_recv))
    gain_part = jnp.zeros((8, width), F32)
    for p in range(gm.PIECES):
        span = slice(p * gm.rows, (p + 1) * gm.rows)
        grad = total[span, :] + more[span, :].astype(F32) + most[span, :].astype(F32)
        mid = rm[span, :]
        scale = lax.rsqrt(jnp.mean(mid * mid, axis=-1, keepdims=True) + EPS)
        normed = mid * scale
        scaled = grad * gain_two
        back = og[span, :].astype(F32) + scale * (scaled - normed * jnp.mean(scaled * normed, axis=-1, keepdims=True))
        g_mid[span, :] = back
        gm_own[span, :] = back.astype(BF)
        gm.start_piece(p)
        gain_part = gain_part + jnp.sum((grad * normed).reshape(gm.rows // 8, 8, width), axis=0)
    dgain[...] = gain_part
    local.start("out", gm_own, gm_all.at[at.c])
    local.start("out", g_mid, g_mid_out)

    zg[0].relay()

    def down(i, carry):
        part = x_all[pl.ds(2 * i, 2), :, 0:part_cols].reshape(2 * rows, part_cols)
        ni[pl.ds(4 * i, 4)] = dot(part, wd[...].reshape(part_cols, width)).astype(BF).reshape(4, half, width)
        return carry

    lax.fori_loop(0, n_ctx // 2, down, 0)
    local.start("out", ni, mlp_out)
    zg[1].relay()
    gm.pass_a()
    gm.pass_b()
    up_ahead = remote(du.at[at.f3], du_first, up_send.at[0], up_recv.at[0], (at.c, at.f1))
    up_ahead.start()
    zd.finish(d_down)
    gm.pass_d()
    for which in ("own", "a", "b", "d"):
        gm.wait_other(which)
    local.wait_all()
    up_ahead.wait()
    for part in range(2):
        zg[part].finish(d_gate.at[pl.ds(part * width // 2, width // 2)])
    for part in (go, zt, zo, zw, *ffn, sc, gm, zd, *zg):
        part.finish_sends()
    for copies in (wc_copies, gc_copies):
        for cp in copies:
            cp.wait_send()


def backward_kernel(
    n_ctx, n_fsdp,
    gm_in, ao_in, heads_in, kt_in, ot_in, lse_in, wo_in, ni_in, wqkv_in, x_in, g_mid_in, gains_in, rm_in, mlp,
    dgain, du_in_all, du_first, pairs, expand_in, cosine_in, sine_in,
    mixed, tgrad, dqkv, dwout, dgain_out, d_up,
    gm_all, ao, heads, kt, ot, lse, wo, ni, wqkv, x, g_mid, gains, rm, du, expand, cosine, sine,
    ga, gat, delta, dwo, dwo_out, dwo_in, du_in, dk, dv, gq, gqc, dw, dw_in, dw_sum, dw_own, mine, mixed_total, total,
    ms_out, ms_in, rs_out, rs_in, dgc, dgz, dg_sum,
    ms_send, ms_recv, rs_send, rs_recv, oz_send, oz_recv, gz_send, gz_recv, gc_send, gc_recv,
    wz_send, wz_recv, wc_send, wc_recv, zu_send, zu_recv, local_sem, inv,
):
    at = Place(n_ctx, n_fsdp)
    rows, width = x.shape
    half = rows // 2
    seq_len = rows * n_ctx
    own_rows = dw.shape[2]
    at.greet(True)
    local = LocalCopies(local_sem)
    for name, src, dst in (
        ("grad", gm_in, gm_all), ("grad", wo_in, wo), ("grad", ao_in, ao), ("grad", ot_in, ot),
        ("attn", heads_in, heads), ("attn", kt_in, kt), ("attn", lse_in, lse),
        ("attn", cosine_in, cosine), ("attn", sine_in, sine),
        ("mlp", mlp.at[at.d], mine.at[0]), ("mlp", mlp.at[at.a], mine.at[1]),
        ("mlp", mlp.at[at.c], mine.at[2]), ("mlp", mlp.at[at.b], mine.at[3]),
        ("weight", ni_in, ni), ("weight", expand_in, expand), ("weight", wqkv_in, wqkv),
        ("up", du_in_all, du), ("up", du_first, du_in.at[0]), ("last", x_in, x), ("last", g_mid_in, g_mid), ("last", gains_in, gains), ("last", rm_in, rm),
    ):
        local.start(name, src, dst)
    at.wait_greeted()

    ms = PlaneScatter(at, None, (ms_out, ms_in), (ms_send, ms_recv), 1)
    for i, index in enumerate(ms.others()):
        ms.copy(i, 0, mlp.at[index], at.s)
    zu = LineScatter(at, lambda i: du_in_all.at[i], du_in, (zu_send, zu_recv))
    zu.rest()
    zu.part = lambda i: du.at[i]
    gc_copies, gc_waits = exchange(at, lambda p: dgain, dgc, lambda r, i: r.at[i], (gc_send, gc_recv))
    dgc[at.c] = dgain[...]

    def add_blocks(index, dst, extras):
        i = index

        def part(r, carry):
            span = pl.ds(pl.multiple_of(r * 48, 16), 48)
            value = mine[i, span, :].astype(F32)
            for extra in extras:
                value = value + extra[span, :].astype(F32)
            dst[span, :] = value.astype(dst.dtype)
            return carry

        lax.fori_loop(0, rows // 48, part, 0)

    def attn_grad(g, carry):
        gm_part = jnp.concatenate([gm_all[inv[4 * g + i]] for i in range(4)], axis=0)
        span = pl.ds(pl.multiple_of(g * 4 * half, 128), 4 * half)
        low = dot(gm_part, wo[...], NT).astype(BF)
        for h in range(2):
            part = low[:, h * HEAD_PAD : (h + 1) * HEAD_PAD]
            ga[h, span, :] = part
            turned = jnp.transpose(part.astype(F32))
            gat[h, :, span] = turned.astype(BF)
            delta[h, :, span] = jnp.broadcast_to(
                jnp.sum(turned * ot[h, :, span], axis=0, keepdims=True), (8, 4 * half)
            )
        dwo[...] += dot(ao[pl.ds(4 * g, 4)].reshape(4 * half, 2 * HEAD_PAD), gm_part, TN)
        return carry

    dwo[...] = jnp.zeros_like(dwo)
    block_slots(pairs, inv, n_ctx)
    local.wait("up")
    zu.pass_on()
    local.wait("grad")
    lax.fori_loop(0, seq_len // (4 * half), attn_grad, 0)
    low = jnp.concatenate([dwo[0:96, :], dwo[128:224, :]], axis=0).astype(BF)
    dwo_out[...] = low.reshape(dwo_out.shape)
    zo = LineScatter(at, lambda i: dwo_out.at[i], dwo_in, (oz_send, oz_recv))
    zo.start()
    zo.rest()
    local.wait("mlp")
    ms.wait(0, 0)
    add_blocks(0, ms_out.at[0], [ms_in.at[0]])
    ms.copy(4, 0, ms_out.at[0], at.a)
    ms.wait(1, 0)
    add_blocks(1, ms_out.at[1], [ms_in.at[1]])
    ms.copy(5, 0, ms_out.at[1], at.a)
    ms.wait(2, 0)
    add_blocks(2, mixed_total, [ms_in.at[2]])

    for w in gc_waits:
        w.wait_recv()
    dg_sum[...] = sum(dgc[i] for i in range(n_ctx))
    zg = LineGather(at, dg_sum, lambda i: dgz.at[i], (gz_send, gz_recv))
    zg.start()
    dgz[at.f] = dg_sum[...]

    local.wait("attn")
    dk[...] = jnp.zeros_like(dk)
    dv[...] = jnp.zeros_like(dv)
    block = 256
    plain_scale = HEAD_DIM ** (-0.5)
    score_scale = plain_scale * LOG2E
    for i in range(seq_len // block):
        first = i * block

        def head_step(h, carry, first=first):
            span = slice(first, first + block)
            q_part, ga_part, gat_part = heads[h, span, :], ga[h, span, :], gat[h, :, span]
            top = lse[h, 0:1, span]
            shift = delta[h, 0:1, span]

            def piece(keys, masked):
                scores = dot(heads[2, keys, :], q_part, NT) * score_scale - top
                if masked:
                    key_id = lax.broadcasted_iota(jnp.int32, (block, block), 0)
                    query_id = lax.broadcasted_iota(jnp.int32, (block, block), 1)
                    scores = jnp.where(key_id <= query_id, scores, NEG_FILL)
                prob = jnp.exp2(scores)
                grad = (prob * (dot(heads[3, keys, :], gat_part) - shift)).astype(BF)
                dv[keys, :] += dot(prob.astype(BF), ga_part)
                dk[keys, :] += dot(grad, q_part)
                return dot(kt[:, keys], grad)

            turned = piece(span, True)
            if first:
                turned = turned + piece(slice(0, first), False)
            lanes = pl.ds(pl.multiple_of(h * HEAD_PAD, HEAD_PAD), HEAD_PAD)
            grad_q = jnp.transpose(turned) * plain_scale
            store_rows(gq, first, lanes, turn(grad_q, cosine[span, :], -sine[span, :]).astype(BF))
            return carry

        lax.fori_loop(0, 2, head_step, 0)
        if i == 2:
            ms.wait(3, 0)
            ms.wait(4, 0)
            add_blocks(3, ms_out.at[2], [ms_in.at[3], ms_in.at[4]])
            ms.copy(6, 0, ms_out.at[2], at.b)
    zo.relay()

    def key_rows(g, carry):
        span = pl.ds(pl.multiple_of(g * 4 * half, 128), 4 * half)
        grad_k = turn(dk[span, :] * plain_scale, cosine[span, :], -sine[span, :]).astype(BF)
        gq[pl.ds(4 * g, 4), :, 256:384] = grad_k.reshape(4, half, HEAD_PAD)
        gq[pl.ds(4 * g, 4), :, 384:512] = dv[span, :].astype(BF).reshape(4, half, HEAD_PAD)
        return carry

    lax.fori_loop(0, seq_len // (4 * half), key_rows, 0)

    def to_ctx(slot, carry):
        pair = pairs[0, slot]
        gqc[2 * slot] = gq[pair]
        gqc[2 * slot + 1] = gq[2 * n_ctx - 1 - pair]
        return carry

    lax.fori_loop(0, n_ctx, to_ctx, 0)
    local.wait("weight", "last")

    def weight_grad(t, carry):
        tile = 2 * n_fsdp * own_rows
        cols = pl.ds(pl.multiple_of(t * tile, 128), tile)
        value = dot(ni[:, :, cols].reshape(seq_len, tile), gqc[...].reshape(seq_len, 4 * HEAD_PAD), TN)
        low = dot(value.astype(BF), expand[...], NT).astype(BF)
        dw[pl.ds(2 * t, 2)] = low.reshape(2, n_fsdp, own_rows, low.shape[1])
        return carry

    zw = []
    for part in range(2):
        lax.fori_loop(part * n_ctx // 4, (part + 1) * n_ctx // 4, weight_grad, 0)
        rows_of = pl.ds(part * n_ctx // 2, n_ctx // 2)
        zw.append(
            LineScatter(
                at, lambda i, r=rows_of: dw.at[r, i], dw_in.at[:, rows_of], (wz_send, wz_recv), 3 * part
            )
        )
        zw[part].start()
        zw[part].rest()

    emit = product_emit(
        lambda index: gqc[pl.ds(2 * index, 2)].reshape(rows, 4 * HEAD_PAD),
        lambda lhs, columns: dot(lhs, wqkv[columns, :], NT),
    )
    sc = PlaneScatter(at, emit, (rs_out, rs_in), (rs_send, rs_recv), 3)
    sc.first(total)
    sc.second()
    zw[0].relay()
    zw[1].relay()
    zg.relay()
    for part in range(2):
        zw[part].finish(dw_sum.at[pl.ds(part * n_ctx // 2, n_ctx // 2)])
    wc_copies, wc_waits = exchange(
        at, lambda p: dw_sum.at[p], dw_own, lambda r, i: r.at[i], (wc_send, wc_recv)
    )
    dw_own[at.c] = dw_sum[at.c]
    mixed_more, mixed_most = ms.last()

    def mixed_rows(r, carry):
        span = pl.ds(pl.multiple_of(r * 48, 16), 48)
        value = rm[span, :] + mixed_total[span, :]
        value = value + mixed_more[span, :].astype(F32) + mixed_most[span, :].astype(F32)
        mixed[span, :] = value.astype(BF)
        return carry

    lax.fori_loop(0, rows // 48, mixed_rows, 0)
    zg.finish()
    dgain_out[...] = sum(dgz[i] for i in range(n_fsdp))

    zu.finish(d_up)
    zo.finish(dwout)
    more, most = sc.last()
    gain_one = gains[0:1, :]

    def finish_rows(r, carry):
        span = pl.ds(pl.multiple_of(r * 48, 16), 48)
        grad = total[span, :] + more[span, :].astype(F32) + most[span, :].astype(F32)
        held = x[span, :].astype(F32)
        scale = lax.rsqrt(jnp.mean(held * held, axis=-1, keepdims=True) + EPS)
        normed = held * scale
        scaled = grad * gain_one
        back = g_mid[span, :] + scale * (scaled - normed * jnp.mean(scaled * normed, axis=-1, keepdims=True))
        tgrad[span, :] = back.astype(BF)
        return carry

    lax.fori_loop(0, rows // 48, finish_rows, 0)
    for w in wc_waits:
        w.wait_recv()
    dqkv[...] = dw_own[...]
    for part in (ms, sc, zu, zo, zg, *zw):
        part.finish_sends()
    for copies in (gc_copies, wc_copies):
        for cp in copies:
            cp.wait_send()


def head_spread():
    spread = np.zeros((4 * HEAD_DIM, 4 * HEAD_PAD), np.float32)
    for head in range(4):
        for j in range(HEAD_DIM):
            lane = j if head == 3 or j < HEAD_DIM // 2 else j + HEAD_PAD // 2 - HEAD_DIM // 2
            spread[head * HEAD_DIM + j, head * HEAD_PAD + lane] = 1.0
    return spread


def turn_tables(seq_len):
    half_dim = HEAD_DIM // 2
    freqs = np.float32(THETA) ** (-(np.arange(half_dim, dtype=np.float32) * np.float32(2.0 / HEAD_DIM)))
    angle = np.arange(seq_len, dtype=np.float32)[:, None] * freqs[None, :].astype(np.float32)
    gap = np.zeros((seq_len, HEAD_PAD // 2 - half_dim), np.float32)
    cosine, sine = np.cos(angle).astype(np.float32), np.sin(angle).astype(np.float32)
    return (
        np.concatenate([cosine, gap, cosine, gap], axis=1),
        np.concatenate([-sine, gap, sine, gap], axis=1),
    )


def tail_kernel(
    n_ctx, n_fsdp,
    dqkv, wq, wk, wv, gain_a, dgain, mixed_in, tgrad_in, dwout_in, dgate_in, dup_in, ddown_in,
    dq, dk, dv, gain_one, gain_two, mixed, tgrad, dwout, dgate, dup, ddown,
    mixed_held, tgrad_held, dwout_held, dgate_held, dup_held, ddown_held, sem,
):
    moves = (
        (mixed_in, mixed_held, mixed), (tgrad_in, tgrad_held, tgrad), (dwout_in, dwout_held, dwout),
        (dgate_in, dgate_held, dgate), (dup_in, dup_held, dup), (ddown_in, ddown_held, ddown),
    )
    loads = [pltpu.make_async_copy(src, held, sem.at[i]) for i, (src, held, _) in enumerate(moves)]
    for cp in loads:
        cp.start()
    stores = []
    for i, (_, held, dst) in enumerate(moves):
        loads[i].wait()
        stores.append(pltpu.make_async_copy(held, dst, sem.at[len(moves) + i]))
        stores[i].start()
    own_rows = wq.shape[0]
    q_cols, kv_cols = wq.shape[1] // n_ctx, wk.shape[1] // n_ctx
    got = [dqkv[i].astype(F32) for i in range(n_ctx)]
    query = jnp.concatenate([g[:, :q_cols] for g in got], axis=1)
    key = jnp.concatenate([g[:, q_cols : q_cols + kv_cols] for g in got], axis=1)
    value = jnp.concatenate([g[:, q_cols + kv_cols :] for g in got], axis=1)
    dq[...] = query
    dk[...] = key
    dv[...] = value
    both = sum(
        jnp.sum(g * w[...].astype(F32), axis=1, keepdims=True) for g, w in ((query, wq), (key, wk), (value, wv))
    )
    row = jnp.transpose(jnp.broadcast_to(both, (own_rows, 128)))[0:1, :]
    gain_one[...] = row / gain_a[...].astype(F32)
    place = (lax.axis_index("ctx") * n_fsdp + lax.axis_index("fsdp")) * own_rows
    width = dgain.shape[1]
    gain = jnp.broadcast_to(jnp.sum(dgain[...], axis=0, keepdims=True), (8, width))
    gain_two[...] = pltpu.roll(gain, width - place, 1)[0:1, :own_rows]
    for cp in stores:
        cp.wait()


def sems(*counts):
    return [pltpu.SemaphoreType.DMA((n,)) for n in counts for _ in range(2)]


VM = pl.BlockSpec(memory_space=pltpu.VMEM)
SM = pl.BlockSpec(memory_space=pltpu.SMEM)
HB = pl.BlockSpec(memory_space=pl.ANY)


def plane(tokens, out_grad, pair_table, attn_gain, w_query, w_key, w_value, w_out, mlp_gain, w_gate, w_up, w_down):
    n_ctx, n_fsdp = lax.axis_size("ctx"), lax.axis_size("fsdp")
    rows, width = tokens.shape
    half = rows // 2
    seq_len = rows * n_ctx
    own_rows = w_query.shape[0]
    gain_a, gain_b = attn_gain.reshape(1, own_rows), mlp_gain.reshape(1, own_rows)
    expand = jnp.asarray(head_spread(), BF)
    cosine, sine = (jnp.asarray(table) for table in turn_tables(seq_len))

    def sds(shape, dtype):
        return jax.ShapeDtypeStruct(shape, dtype)

    blocks = (n_ctx, rows, width)
    vm = pltpu.VMEM
    part_cols = n_fsdp * 128
    front = pl.pallas_call(
        functools.partial(front_kernel, n_ctx, n_fsdp),
        out_shape=(
            sds(w_gate.shape, F32),
            sds(w_down.shape, F32),
            sds((8, width), F32),
            sds((2 * n_ctx, half, width), BF),
            sds((4, seq_len, HEAD_PAD), BF),
            sds((HEAD_PAD, seq_len), BF),
            sds((2, HEAD_PAD, seq_len), F32),
            sds((2 * n_ctx, half, 2 * HEAD_PAD), BF),
            sds((2, 8, seq_len), F32),
            sds((width, 4 * HEAD_PAD), BF),
            sds((2 * HEAD_PAD, width), BF),
            sds((16, width), F32),
            sds((rows, width), F32),
            sds((n_fsdp, *w_up.shape), BF),
            sds((2 * n_ctx, half, width), BF),
            sds(blocks, BF),
            sds((rows, width), F32),
            sds(w_up.shape, BF),
        ),
        in_specs=[VM] * 6 + [HB] * 3 + [VM, VM, SM, HB, HB, HB],
        out_specs=(VM,) * 3 + (HB,) * 15,
        scratch_shapes=[
            vm((2 * n_ctx, half, width), BF),
            vm((4, seq_len, HEAD_PAD), BF),
            vm((HEAD_PAD, seq_len), BF),
            vm((HEAD_PAD, seq_len), BF),
            vm((2, HEAD_PAD, seq_len), F32),
            vm((2 * n_ctx, half, 2 * HEAD_PAD), BF),
            vm((2, 8, seq_len), F32),
            vm((width, 4 * HEAD_PAD), BF),
            vm((2 * HEAD_PAD, width), BF),
            vm((16, width), F32),
            vm((rows, width), F32),
            vm(blocks, BF),
            vm((n_ctx, own_rows, 4 * HEAD_DIM), BF),
            vm((n_ctx, n_fsdp, own_rows, 4 * HEAD_DIM), BF),
            vm((n_fsdp, own_rows, width), BF),
            vm((16, width), BF),
            vm((n_fsdp, 16, width), BF),
            vm((16, width), BF),
            vm((n_ctx, 16, width), BF),
            vm((rows, width), BF),
            vm((rows, width), F32),
            vm((7, rows, width), BF),
            vm((7, rows, width), BF),
            vm(blocks, BF),
            vm(blocks, BF),
            vm((width, 2 * part_cols), BF),
            vm((n_fsdp, *w_down.shape), BF),
            vm((n_fsdp, *w_down.shape), BF),
            vm((n_fsdp, *w_up.shape), BF),
            vm((3, *w_gate.shape), BF),
            vm((3, *w_down.shape), BF),
            *sems(21, 21, 21, n_ctx, 3, 3, 3, n_ctx, 3, 3, 3, 6, 3, 1),
            pltpu.SemaphoreType.DMA((21,)),
            pltpu.SMEM((2 * n_ctx,), jnp.int32),
            vm((4 * HEAD_DIM, 4 * HEAD_PAD), BF),
            vm((seq_len, HEAD_PAD), F32),
            vm((seq_len, HEAD_PAD), F32),
        ],
        compiler_params=pltpu.CompilerParams(
            collective_id=0, has_side_effects=True, vmem_limit_bytes=FRONT_VMEM_LIMIT
        ),
        name="forward_and_feed_forward",
    )
    d_gate, d_down, dgain, ni, heads, kt, ot, ao, lse, wqkv, wo, gains, rm, du, mlp, gm_all, g_mid, du_first = front(
        tokens, out_grad, w_query, w_key, w_value, w_out, w_gate, w_up, w_down, gain_a, gain_b, pair_table, expand, cosine, sine
    )

    backward = pl.pallas_call(
        functools.partial(backward_kernel, n_ctx, n_fsdp),
        out_shape=(
            sds((rows, width), BF),
            sds((rows, width), BF),
            sds((n_ctx, own_rows, 4 * HEAD_DIM), BF),
            sds((own_rows, width), F32),
            sds((8, width), F32),
            sds(w_up.shape, F32),
        ),
        in_specs=[HB] * 14 + [VM, HB, HB, SM, HB, HB, HB],
        out_specs=(VM,) * 6,
        scratch_shapes=[
            vm((2 * n_ctx, half, width), BF),
            vm((2 * n_ctx, half, 2 * HEAD_PAD), BF),
            vm((4, seq_len, HEAD_PAD), BF),
            vm((HEAD_PAD, seq_len), BF),
            vm((2, HEAD_PAD, seq_len), F32),
            vm((2, 8, seq_len), F32),
            vm((2 * HEAD_PAD, width), BF),
            vm((2 * n_ctx, half, width), BF),
            vm((width, 4 * HEAD_PAD), BF),
            vm((rows, width), BF),
            vm((rows, width), F32),
            vm((16, width), F32),
            vm((rows, width), F32),
            vm((n_fsdp, *w_up.shape), BF),
            vm((4 * HEAD_DIM, 4 * HEAD_PAD), BF),
            vm((seq_len, HEAD_PAD), F32),
            vm((seq_len, HEAD_PAD), F32),
            vm((2, seq_len, HEAD_PAD), BF),
            vm((2, HEAD_PAD, seq_len), BF),
            vm((2, 8, seq_len), F32),
            vm((2 * HEAD_PAD, width), F32),
            vm((n_fsdp, own_rows, width), BF),
            vm((3, own_rows, width), BF),
            vm((3, *w_up.shape), BF),
            vm((seq_len, HEAD_PAD), F32),
            vm((seq_len, HEAD_PAD), F32),
            vm((2 * n_ctx, half, 4 * HEAD_PAD), BF),
            vm((2 * n_ctx, half, 4 * HEAD_PAD), BF),
            vm((n_ctx, n_fsdp, own_rows, 4 * HEAD_DIM), BF),
            vm((3, n_ctx, own_rows, 4 * HEAD_DIM), BF),
            vm((n_ctx, own_rows, 4 * HEAD_DIM), BF),
            vm((n_ctx, own_rows, 4 * HEAD_DIM), BF),
            vm((4, rows, width), BF),
            vm((rows, width), F32),
            vm((rows, width), F32),
            vm((3, rows, width), BF),
            vm((7, rows, width), BF),
            vm((7, rows, width), BF),
            vm((7, rows, width), BF),
            vm((n_ctx, 8, width), F32),
            vm((n_fsdp, 8, width), F32),
            vm((8, width), F32),
            *sems(7, 21, 3, 3, n_ctx, 6, n_ctx, 3),
            pltpu.SemaphoreType.DMA((22,)),
            pltpu.SMEM((2 * n_ctx,), jnp.int32),
        ],
        compiler_params=pltpu.CompilerParams(
            collective_id=1, has_side_effects=True, vmem_limit_bytes=VMEM_LIMIT
        ),
        name="attention_backward",
    )
    mixed, tokens_grad, dqkv, d_out, d_gain_two, d_up = backward(
        gm_all.reshape(2 * n_ctx, half, width), ao, heads, kt, ot, lse, wo, ni, wqkv, tokens, g_mid, gains, rm,
        mlp.reshape(blocks), dgain, du, du_first, pair_table, expand, cosine, sine,
    )
    tail = pl.pallas_call(
        functools.partial(tail_kernel, n_ctx, n_fsdp),
        out_shape=(
            sds(w_query.shape, F32),
            sds(w_key.shape, F32),
            sds(w_value.shape, F32),
            sds((1, own_rows), F32),
            sds((1, own_rows), F32),
            sds((rows, width), BF),
            sds((rows, width), BF),
            sds(w_out.shape, F32),
            sds(w_gate.shape, F32),
            sds(w_up.shape, F32),
            sds(w_down.shape, F32),
        ),
        in_specs=[VM] * 6 + [HB] * 6,
        out_specs=(VM,) * 5 + (HB,) * 6,
        scratch_shapes=[
            vm((rows, width), BF),
            vm((rows, width), BF),
            vm(w_out.shape, F32),
            vm(w_gate.shape, F32),
            vm(w_up.shape, F32),
            vm(w_down.shape, F32),
            pltpu.SemaphoreType.DMA((12,)),
        ],
        compiler_params=pltpu.CompilerParams(vmem_limit_bytes=VMEM_LIMIT),
        name="layouts",
    )
    d_query, d_key, d_value, gain_one_grad, gain_two_grad, mixed, tokens_grad, d_out, d_gate, d_up, d_down = tail(
        dqkv, w_query, w_key, w_value, gain_a, d_gain_two, mixed, tokens_grad, d_out, d_gate, d_up, d_down
    )
    return (
        mixed, tokens_grad, gain_one_grad.reshape(-1), d_query, d_key, d_value, d_out, gain_two_grad.reshape(-1),
        d_gate, d_up, d_down,
    )


def solution(mesh):
    in_specs = (
        P(("ctx", "fsdp"), None),
        P(("ctx", "fsdp"), None),
        P("fsdp", None),
        P(("ctx", "fsdp")),
        P(("ctx", "fsdp"), None),
        P(("ctx", "fsdp"), None),
        P(("ctx", "fsdp"), None),
        P(("ctx", "fsdp"), None),
        P(("ctx", "fsdp")),
        P(None, ("ctx", "fsdp")),
        P(None, ("ctx", "fsdp")),
        P(("ctx", "fsdp"), None),
    )
    out_specs = (
        P(("ctx", "fsdp"), None),
        P(("ctx", "fsdp"), None),
        P(("ctx", "fsdp")),
        P(("ctx", "fsdp"), None),
        P(("ctx", "fsdp"), None),
        P(("ctx", "fsdp"), None),
        P(("ctx", "fsdp"), None),
        P(("ctx", "fsdp")),
        P(None, ("ctx", "fsdp")),
        P(None, ("ctx", "fsdp")),
        P(("ctx", "fsdp"), None),
    )
    fits = (
        mesh.shape["ctx"] == KV_HEADS
        and mesh.shape["fsdp"] == 4
        and HEADS == 2 * KV_HEADS
    )
    return jax.shard_map(plane if fits else local, mesh=mesh, in_specs=in_specs, out_specs=out_specs, check_vma=False)
```
